32 devices in a mesh: dp: 16 (over z, x, core), mp: 2 (over y).
Axes of the slice: x: 2, y: 2, z: 4, core: 2. Of those that a mesh axis runs over, the one named last changes fastest.
Arguments:
- tokens: bfloat16 [8192, 768], P('dp'), may hold values from -6 to 6
- segment_ids: int32 [16, 512], P('dp'), may hold values from 0 to 3, never falling along the last dimension, each value on 1 to 256 neighbouring positions
- gain_attn: float32 [768], P('dp'), may hold values from 0.1 to 1.9
- gain_ffn: float32 [768], P('dp'), may hold values from 0.1 to 1.9
- random_scores: float32 [12, 512, 512], P('mp', 'dp'), may hold values from -6 to 6
- w_value: float32 [768, 768], P('dp', 'mp'), may hold values from -0.21875 to 0.21875
- w_output: float32 [768, 768], P('mp', 'dp'), may hold values from -0.875 to 0.875
- w_up: float32 [768, 3072], P('dp', 'mp'), may hold values from -0.21875 to 0.21875
- w_down: float32 [3072, 768], P('mp', 'dp'), may hold values from -0.109375 to 0.109375
- cotangent: bfloat16 [8192, 768], P('dp'), may hold values from -6 to 6
Outputs:
- output: bfloat16 [8192, 768], P('dp')
- grad_tokens: bfloat16 [8192, 768], P('dp')
- grad_gain_attn: float32 [768], P('dp')
- grad_gain_ffn: float32 [768], P('dp')
- grad_scores: float32 [12, 512, 512], P('mp', 'dp')
- grad_value: float32 [768, 768], P('dp', 'mp')
- grad_output: float32 [768, 768], P('mp', 'dp')
- grad_up: float32 [768, 3072], P('dp', 'mp')
- grad_down: float32 [3072, 768], P('mp', 'dp')
The draws below stay inside these ranges and needn't reach their ends.
Inputs may be any that keep to these rules, and one draw needn't show every extreme that they name: `segment_ids`: within each packed row the ids never fall; each of the 4 documents of a row holds 1 to 256 tokens and one holds exactly 256.
All inputs are finite; a program needn't handle non-finite values.
Results may differ from the reference program's by a relative error of at most 0.015.
Values may be sent and summed in bfloat16 or wider, within the bound.
No kernel may reach another device: no remote copies, remote signals or barrier semaphores. Data moves between devices by JAX's collectives and lax.ppermute only.
A program may use at most 128 MiB of HBM per device.

```python
import math
import jax
import jax.numpy as jnp
import numpy as np
from jax import lax

D = 768
HEADS = 12
HEAD_DIM = 64
FF = 3072
L = 512
SEGS = 4
MOST = 256
ROWS = 16
TOKENS = 8192


def raised(array, own_key, source, target, blocks, factor):
    owner, partner = [(jnp.arange(array.shape[axis_at]) // (array.shape[axis_at] // blocks)).reshape([-1 if axis == axis_at else 1 for axis in range(array.ndim)]) for axis_at in (source, target)]
    chosen = jax.random.permutation(own_key, blocks)[partner]
    strong = (owner == chosen) | (owner == (partner + blocks // 2) % blocks)
    return jnp.where(strong, factor * array, array)


def shard_levels(own_key, dims, split, least, high):
    factor_of = 1.0
    for position, blocks in split:
        steps = jax.random.uniform(jax.random.fold_in(jax.random.fold_in(own_key, 6), position), (blocks,), jnp.float32, least / len(split), high / len(split))
        factor_of = factor_of * jnp.repeat(jnp.exp(steps), dims[position] // blocks).reshape((-1,) + (1,) * (len(dims) - 1 - position))
    return factor_of


def split_up(amount, total, limit, slope):
    weights = [(1 << 20) // math.isqrt(rank ** slope) + 1 for rank in range(2, amount + 1)]
    surplus, given = total - limit - (amount - 1), [1] * (amount - 1)
    while surplus > 0:
        candidates = [i for i in range(amount - 1) if given[i] < limit]
        whole, left = sum([weights[i] for i in candidates]), surplus
        for i in candidates:
            extra = min(limit - given[i], max(1, left * weights[i] // whole), surplus)
            given[i] = given[i] + extra
            surplus = surplus - extra
    return np.array([limit] + given)


def uneven_parts(own_key, amount, total, bound, lean):
    if amount == 2:
        one = jax.random.randint(own_key, (), max(1, total - bound), min(bound, total - 1) + 1)
        return jnp.stack([one, total - one])
    sizes = jnp.asarray(split_up(amount, total, bound, lean), jnp.int32)
    twos = (amount - 1) // 2
    giver, sink = sizes[1:1 + 2 * twos:2], sizes[2:2 + 2 * twos:2]
    room = jnp.minimum(giver - 1, bound - sink)
    moved = jax.random.randint(jax.random.fold_in(own_key, 1), (twos,), 0, 1 << 20) % (room + 1)
    sizes = sizes.at[1:1 + 2 * twos:2].set(giver - moved).at[2:2 + 2 * twos:2].set(sink + moved)
    return sizes[jax.random.permutation(jax.random.fold_in(own_key, 2), amount)]


def scatter_about(stream_key, shape, deviation, reach, shards=(), held_as=jnp.bfloat16):
    loudness = shard_levels(stream_key, shape, shards, -0.22, 0.18) if shards else 1.0
    array = jax.random.normal(stream_key, shape, jnp.float32) * deviation * loudness
    return jnp.minimum(jnp.maximum(array, -reach), reach).astype(held_as)


def bell_draw_with(key, dims, width, limit, split, heavy, kind=jnp.bfloat16):
    entries = width * jax.random.normal(key, dims, jnp.float32)
    if split:
        entries = entries * shard_levels(key, dims, split, -0.22, 0.18)
    return jnp.clip(raised(entries, jax.random.fold_in(key, 3), *heavy), -limit, limit).astype(kind)


def setup_inputs(seed: int = 0) -> dict:
    streams_of = jax.random.split(jax.random.key(seed), 11)
    return {
        "tokens": bell_draw_with(streams_of[0], (TOKENS, D), 1.0, 6.0, ((0, 16),), (0, 1, 16, 2.0)),
        "segment_ids": jax.vmap(lambda own: jnp.searchsorted(jnp.cumsum(uneven_parts(own, SEGS, L, MOST, 0)), jnp.arange(L), side="right"))(jax.random.split(streams_of[1], ROWS)).reshape((ROWS, L)).astype(jnp.int32),
        "gain_attn": jnp.clip(1.0 + 0.18 * jax.random.normal(streams_of[2], (D,), jnp.float32), 0.1, 1.9),
        "gain_ffn": jnp.clip(1.0 + 0.18 * jax.random.normal(streams_of[3], (D,), jnp.float32), 0.1, 1.9),
        "random_scores": scatter_about(streams_of[4], (HEADS, L, L), 1.5, 6.0, ((0, 2), (1, 16)), jnp.float32),
        "w_value": scatter_about(streams_of[5], (D, D), D ** -0.5, 0.21875, ((0, 16), (1, 2)), jnp.float32),
        "w_output": scatter_about(streams_of[6], (D, D), (D // 16) ** -0.5, 0.875, ((0, 2), (1, 16)), jnp.float32),
        "w_up": scatter_about(streams_of[7], (D, FF), D ** -0.5, 0.21875, ((0, 16), (1, 2)), jnp.float32),
        "w_down": scatter_about(streams_of[8], (FF, D), FF ** -0.5, 0.109375, ((0, 2), (1, 16)), jnp.float32),
        "cotangent": bell_draw_with(streams_of[9], (TOKENS, D), 1.0, 6.0, ((0, 16),), (0, 1, 16, 2.0)),
    }


EPSILON = 1e-06
NEGATIVE = -1e+30

@jax.custom_vjp
def low(v):
    return lax.optimization_barrier(v.astype(jnp.bfloat16)).astype(jnp.float32)

@jax.custom_vjp
def low_back(v):
    return v

def low_keep(v):
    return (low(v), None)

def low_pass(kept, grad):
    return (grad,)

def back_keep(v):
    return (v, None)

def back_low(kept, grad):
    return (low(grad),)
low.defvjp(low_keep, low_pass)
low_back.defvjp(back_keep, back_low)

def rms_norm(values, gain):
    return values * lax.rsqrt(lax.optimization_barrier(jnp.mean(values * values, axis=-1, keepdims=True)) + EPSILON) * gain

def forward(segment_ids, tokens, gain_attn, gain_ffn, random_scores, w_value, w_output, w_up, w_down):
    highest = lax.Precision.HIGHEST
    normed = low(rms_norm(tokens, low(gain_attn)))
    values = low(low_back(jnp.dot(normed, low(w_value), precision=highest)))
    scores_low = low(random_scores)
    row_count = segment_ids.shape[0]
    value_rows = values.reshape(row_count, L, HEADS, HEAD_DIM)

    def one_row(pair):
        seg_row, value_row = pair
        same = seg_row[:, None] == seg_row[None, :]
        masked = jnp.where(same[None], scores_low, NEGATIVE)
        probs = jax.nn.softmax(masked, axis=-1)
        mixed_row = jnp.einsum('hij,jhc->ihc', low(probs), value_row, precision=highest)
        return mixed_row.reshape(L, HEADS * HEAD_DIM)
    mixed = lax.map(jax.checkpoint(one_row), (segment_ids, value_rows)).reshape(-1, D)
    mixed = low(low_back(mixed))
    attn = low_back(jnp.dot(mixed, low(w_output), precision=highest))
    resid = tokens + attn
    normed_two = low(rms_norm(resid, low(gain_ffn)))
    pre_act = low_back(jnp.dot(normed_two, low(w_up), precision=highest))
    act = low(jax.nn.gelu(pre_act))
    return resid + jnp.dot(act, low(w_down), precision=highest)

def reference(tokens, segment_ids, gain_attn, gain_ffn, random_scores, w_value, w_output, w_up, w_down, cotangent):
    tokens_full = tokens.astype(jnp.float32)

    def wrapped(tok, g_one, g_two, scores, wval, wout, wup, wdown):
        return forward(segment_ids, tok, g_one, g_two, scores, wval, wout, wup, wdown)
    result, pullback = jax.vjp(wrapped, tokens_full, gain_attn, gain_ffn, random_scores, w_value, w_output, w_up, w_down)
    grads = pullback(cotangent.astype(jnp.float32))
    return (result.astype(jnp.bfloat16), grads[0].astype(jnp.bfloat16), grads[1], grads[2], grads[3], grads[4], grads[5], grads[6], grads[7])
```

```python
import jax
import jax.numpy as jnp
from jax import lax
from jax.experimental import pallas as pl
from jax.experimental.pallas import tpu as pltpu
from jax.sharding import PartitionSpec as P

EPSILON = 1e-06
NEGATIVE = -1e30
BF = jnp.bfloat16
F32 = jnp.float32
UNITS = 16
LANES = 128
RING_CHIPS = 8
VMEM_BYTES = 56 * 1024 * 1024
NT = (((1,), (1,)), ((), ()))
TN = (((0,), (0,)), ((), ()))
NN = (((1,), (0,)), ((), ()))


def mm(a, b, dims=NN):
    return lax.dot_general(a, b, dims, preferred_element_type=F32)


def params():
    return pltpu.CompilerParams(vmem_limit_bytes=VMEM_BYTES)


def vmem(count):
    return [pl.BlockSpec(memory_space=pltpu.VMEM)] * count


def smem():
    return pl.BlockSpec(memory_space=pltpu.SMEM)


def hbm(count):
    return [pl.BlockSpec(memory_space=pl.ANY)] * count


def sds(shape, dtype):
    return jax.ShapeDtypeStruct(shape, dtype)


def gelu_pair(x):
    c = 0.7978845608028654
    a = 0.044715
    square = x * x
    t = jnp.tanh(c * x * (1.0 + a * square))
    half = 0.5 * (1.0 + t)
    return x * half, half + 0.5 * x * (1.0 - t * t) * (c * (1.0 + 3.0 * a * square))


def multiple(value, of):
    return pl.multiple_of(value, of)


def pack_first(scores, wv, gain_one, gain_two):
    heads, rows, length = scores.shape
    krows, width = wv.shape

    def kernel(s_ref, wv_ref, ga_ref, gf_ref, out, scr):
        out[: heads * rows, :] = s_ref[...].reshape(heads * rows, length).astype(BF)
        out[heads * rows :, :width] = wv_ref[...].astype(BF)
        scr[...] = jnp.zeros_like(scr)
        scr[0:1, :krows] = ga_ref[...]
        scr[1:2, :krows] = gf_ref[...]
        out[heads * rows :, width:] = scr[...].astype(BF)

    return pl.pallas_call(
        kernel,
        out_shape=sds((heads * rows + krows, length), BF),
        in_specs=vmem(4),
        out_specs=vmem(1)[0],
        scratch_shapes=[pltpu.VMEM((krows, length - width), F32)],
        compiler_params=params(),
        name="pack_first",
    )(scores, wv, gain_one.reshape(1, -1), gain_two.reshape(1, -1))


def pack_second(w_up, w_down, wo_first, wo_second):
    krows, hidden = w_up.shape
    half = wo_first.shape[0]

    def kernel(up_ref, down_ref, one_ref, two_ref, out):
        eye = (
            lax.broadcasted_iota(jnp.int32, (krows, krows), 0)
            == lax.broadcasted_iota(jnp.int32, (krows, krows), 1)
        ).astype(BF)
        out[:, :hidden] = up_ref[...].astype(BF)
        out[:, hidden : 2 * hidden] = mm(eye, down_ref[...].astype(BF), NT).astype(BF)
        out[:, 2 * hidden : 2 * hidden + half] = mm(eye, one_ref[...], NT).astype(BF)
        out[:, 2 * hidden + half :] = mm(eye, two_ref[...], NT).astype(BF)

    return pl.pallas_call(
        kernel,
        out_shape=sds((krows, 2 * hidden + 2 * half), BF),
        in_specs=vmem(4),
        out_specs=vmem(1)[0],
        compiler_params=params(),
        name="pack_second",
    )(w_up, w_down, wo_first, wo_second)


def mixer_forward(where, tokens, seg_row, seg_col, units, heads, width):
    length, model = tokens.shape
    size = width // heads
    rows = length // UNITS
    krows = model // UNITS
    wide = heads * LANES

    def kernel(where_ref, tok_ref, sr_ref, sc_ref, *rest):
        unit = rest[:UNITS]
        e_ref, va_ref, mixed_ref, mixf_ref, rb_ref, n1_ref, gains_ref, wv_ref, pieces = rest[UNITS:]
        for u in range(UNITS):
            d = where_ref[u]
            wv_ref[pl.ds(multiple(d * krows, 16), krows), :] = unit[u][heads * rows :, :width]
            some = unit[u][heads * rows : heads * rows + 16, width:].astype(F32)
            pieces[0, pl.ds(d, 1), :] = some[0:1, :]
            pieces[1, pl.ds(d, 1), :] = some[1:2, :]
        spread = (
            lax.broadcasted_iota(jnp.int32, (LANES, model), 1) % krows
            == lax.broadcasted_iota(jnp.int32, (LANES, model), 0)
        ).astype(BF)
        own = (
            lax.broadcasted_iota(jnp.int32, (UNITS, model), 1) // krows
            == lax.broadcasted_iota(jnp.int32, (UNITS, model), 0)
        )
        gains = []
        for t in range(2):
            full = jnp.where(own, mm(pieces[t].astype(BF), spread), 0.0)
            gains.append(jnp.sum(full, axis=0, keepdims=True))
            gains_ref[t : t + 1, :] = gains[t]
        x = tok_ref[...].astype(F32)
        inv = lax.rsqrt(jnp.mean(x * x, axis=-1, keepdims=True) + EPSILON)
        n1_ref[...] = (x * inv * gains[0]).astype(BF)
        values = mm(n1_ref[...], wv_ref[...]).astype(BF)
        tail = (lax.broadcasted_iota(jnp.int32, (length, LANES - size), 1) < 2).astype(BF)
        for h in range(heads):
            va_ref[:, h * LANES : h * LANES + size] = values[:, h * size : (h + 1) * size]
            va_ref[:, h * LANES + size : (h + 1) * LANES] = tail

        def one_head(h, carry):
            for u in range(UNITS):
                d = where_ref[u]
                at = pl.ds(multiple(d * rows, rows), rows)
                s = unit[u][pl.ds(multiple(h * rows, rows), rows), :].astype(F32)
                same = sc_ref[at, :] == sr_ref[...]
                e_ref[h, at, :] = jnp.where(same, jnp.exp(s), 0.0).astype(BF)
            return carry

        lax.fori_loop(0, heads, one_head, 0)
        for h in range(heads):
            lanes = slice(h * LANES, (h + 1) * LANES)
            sums = mm(e_ref[h], va_ref[:, lanes])
            inverse = 1.0 / sums[:, size : size + 1]
            mixed = sums * inverse
            rb_ref[:, lanes] = jnp.broadcast_to(inverse, (length, LANES))
            mixf_ref[:, lanes] = jnp.where(
                lax.broadcasted_iota(jnp.int32, (length, LANES), 1) < size, mixed, 0.0
            )
            mixed_ref[:, h * size : (h + 1) * size] = mixed[:, :size].astype(BF)

    return pl.pallas_call(
        kernel,
        out_shape=(
            sds((heads, length, length), BF),
            sds((length, wide), BF),
            sds((length, width), BF),
            sds((length, wide), F32),
            sds((length, wide), F32),
            sds((length, model), BF),
            sds((2, model), F32),
            sds((model, width), BF),
        ),
        in_specs=[smem()] + vmem(3 + UNITS),
        out_specs=tuple(vmem(8)),
        scratch_shapes=[pltpu.VMEM((2, UNITS, LANES), F32)],
        compiler_params=params(),
        name="mixer_forward",
    )(where, tokens, seg_row, seg_col, *units)


def ffn_main(place, tokens, mixed_own, mixed_other, cotangent, gains, units, heads):
    length, model = tokens.shape
    width = mixed_own.shape[1]
    krows = model // UNITS
    columns = units[0].shape[1]
    hidden = (columns - 2 * width) // 2
    size = width // heads
    wide = heads * LANES
    chunk = length // 2
    piece = hidden // 3

    def kernel(place_ref, tok_ref, own_ref, other_ref, cot_ref, gains_ref, *rest):
        unit = rest[:UNITS]
        (back_ref, resid_ref, n2_ref, act_ref, gpre_ref, wo_out, w, mixed, acc, sem) = rest[UNITS:]
        copies = []
        for u in range(UNITS):
            to = pl.ds(multiple(place_ref[u] * krows, 16), krows)
            copies.append(pltpu.make_async_copy(unit[u], w.at[to, :], sem.at[u]))
            copies[-1].start()
        first = place_ref[UNITS]
        mixed[:, pl.ds(multiple(first * width, LANES), width)] = own_ref[...]
        mixed[:, pl.ds(multiple((1 - first) * width, LANES), width)] = other_ref[...]
        for copy in copies:
            copy.wait()
        start = multiple(2 * hidden + first * width, LANES)
        wo_own = w[:, pl.ds(start, width)]
        zeros = jnp.zeros((model, LANES - size), BF)
        for h in range(heads):
            wo_out[:, h * LANES : h * LANES + size] = wo_own[:, h * size : (h + 1) * size]
            wo_out[:, h * LANES + size : (h + 1) * LANES] = zeros

        def some_tokens(r, carry):
            at = pl.ds(multiple(r * chunk, chunk), chunk)
            attn = mm(mixed[at, :], w[:, 2 * hidden :], NT)
            resid = tok_ref[at, :].astype(F32) + attn
            resid_ref[at, :] = resid
            inv = lax.rsqrt(jnp.mean(resid * resid, axis=-1, keepdims=True) + EPSILON)
            n2_ref[at, :] = (resid * inv * gains_ref[1:2, :]).astype(BF)
            for j in range(hidden // piece):
                cols = slice(j * piece, (j + 1) * piece)
                down = slice(hidden + j * piece, hidden + (j + 1) * piece)
                pre = mm(n2_ref[at, :], w[:, cols])
                act, slope = gelu_pair(pre)
                act_ref[at, cols] = act.astype(BF)
                gpre_ref[at, cols] = (mm(cot_ref[at, :], w[:, down]) * slope).astype(BF)
                part = mm(gpre_ref[at, cols], w[:, cols], NT)
                if j == 0:
                    acc[...] = part
                else:
                    acc[...] += part
            back_ref[at, :] = acc[...].astype(BF)
            return carry

        lax.fori_loop(0, length // chunk, some_tokens, 0)

    return pl.pallas_call(
        kernel,
        out_shape=(
            sds((length, model), BF),
            sds((length, model), F32),
            sds((length, model), BF),
            sds((length, hidden), BF),
            sds((length, hidden), BF),
            sds((model, wide), BF),
        ),
        in_specs=[smem()] + vmem(5) + hbm(UNITS),
        out_specs=tuple(vmem(6)),
        scratch_shapes=[
            pltpu.VMEM((model, columns), BF),
            pltpu.VMEM((length, 2 * width), BF),
            pltpu.VMEM((chunk, model), F32),
            pltpu.SemaphoreType.DMA((UNITS,)),
        ],
        compiler_params=params(),
        name="ffn_main",
    )(place, tokens, mixed_own, mixed_other, cotangent, gains, *units)


def ffn_grads(where, n2, gpre, act, cotangent):
    length, model = n2.shape
    hidden = act.shape[1]
    krows = model // UNITS
    half = UNITS // 2

    def kernel(where_ref, n2_ref, gpre_ref, act_ref, cot_ref, keep, give, scr, sem):
        piece = hidden // 3
        for j in range(3):
            cols = slice(j * piece, (j + 1) * piece)
            scr[:, cols] = mm(n2_ref[...], gpre_ref[:, cols], TN).astype(BF)
            down = slice(hidden + j * piece, hidden + (j + 1) * piece)
            scr[:, down] = mm(cot_ref[...], act_ref[:, cols], TN).astype(BF)
        copies = []
        for u in range(UNITS):
            at = pl.ds(multiple(where_ref[u] * krows, 16), krows)
            to = keep.at[u] if u < half else give.at[u - half]
            copies.append(pltpu.make_async_copy(scr.at[at, :], to, sem.at[u]))
            copies[-1].start()
        for copy in copies:
            copy.wait()

    shape = sds((half, krows, 2 * hidden), BF)
    return pl.pallas_call(
        kernel,
        out_shape=(shape, shape),
        in_specs=[smem()] + vmem(4),
        out_specs=tuple(hbm(2)),
        scratch_shapes=[pltpu.VMEM((model, 2 * hidden), BF), pltpu.SemaphoreType.DMA((UNITS,))],
        compiler_params=params(),
        name="ffn_grads",
    )(where, n2, gpre, act, cotangent)


def ffn_out(where, act, units, width):
    length, hidden = act.shape
    krows, columns = units[0].shape
    model = krows * UNITS

    def kernel(where_ref, act_ref, *rest):
        unit = rest[:UNITS]
        out, w, sem = rest[UNITS:]
        copies = []
        for u in range(UNITS):
            to = pl.ds(multiple(where_ref[u] * krows, 16), krows)
            source = unit[u].at[:, pl.ds(hidden, hidden)]
            copies.append(pltpu.make_async_copy(source, w.at[to, :], sem.at[u]))
            copies[-1].start()
        for copy in copies:
            copy.wait()
        chunk = length // 2
        for r in range(2):
            at = slice(r * chunk, (r + 1) * chunk)
            out[at, :] = mm(act_ref[at, :], w[...], NT).astype(BF)

    return pl.pallas_call(
        kernel,
        out_shape=sds((length, model), BF),
        in_specs=[smem()] + vmem(1) + hbm(UNITS),
        out_specs=vmem(1)[0],
        scratch_shapes=[pltpu.VMEM((model, hidden), BF), pltpu.SemaphoreType.DMA((UNITS,))],
        compiler_params=params(),
        name="ffn_out",
    )(where, act, *units)


def mixer_back(back_own, back_other, resid, cotangent, gains, wo, mixf, rb, e, n1, wv, tokens):
    length, model = resid.shape
    width = wv.shape[1]
    heads = e.shape[0]
    size = width // heads
    wide = heads * LANES
    chunk = length // 4
    krows = model // UNITS

    def kernel(a_ref, b_ref, res_ref, cot_ref, gains_ref, wo_ref, mixf_ref, rb_ref, e_ref, wv_ref, tok_ref,
               gres_ref, gat_ref, xh_ref, gv_ref, part_ref, ga_ref, gf_ref, gm, acc):
        acc[...] = jnp.zeros_like(acc)

        def some_tokens(r, carry):
            at = pl.ds(multiple(r * chunk, chunk), chunk)
            g2 = a_ref[at, :].astype(F32) + b_ref[at, :].astype(F32)
            res = res_ref[at, :]
            inv = lax.rsqrt(jnp.mean(res * res, axis=-1, keepdims=True) + EPSILON)
            hat = res * inv
            acc[0] += jnp.sum((g2 * hat).reshape(chunk // 8, 8, model), axis=0)
            z = gains_ref[1:2, :] * g2
            corr = jnp.mean(z * hat, axis=-1, keepdims=True)
            gres = cot_ref[at, :].astype(F32) + inv * (z - hat * corr)
            gres_ref[at, :] = gres
            gat_ref[at, :] = gres.astype(BF)
            return carry

        lax.fori_loop(0, length // chunk, some_tokens, 0)
        gm[...] = mm(gat_ref[...], wo_ref[...]).astype(BF)
        lane = lax.broadcasted_iota(jnp.int32, (length, LANES), 1)
        for h in range(heads):
            lanes = slice(h * LANES, (h + 1) * LANES)
            here = gm[:, lanes].astype(F32)
            inner = -jnp.sum(here * mixf_ref[:, lanes], axis=-1, keepdims=True)
            high = inner.astype(BF).astype(F32)
            xh_ref[:, lanes] = jnp.where(
                lane == size, high, jnp.where(lane == size + 1, inner - high, here)
            ).astype(BF)
            scaled = (here * rb_ref[:, lanes]).astype(BF)
            gv_ref[:, h * size : (h + 1) * size] = mm(e_ref[h], scaled, TN)[:, :size].astype(BF)

        def some_back(r, carry):
            at = pl.ds(multiple(r * chunk, chunk), chunk)
            part = mm(gv_ref[at, :], wv_ref[...], NT)
            part_ref[at, :] = part.astype(BF)
            x = tok_ref[at, :].astype(F32)
            inv = lax.rsqrt(jnp.mean(x * x, axis=-1, keepdims=True) + EPSILON)
            acc[1] += jnp.sum((part * (x * inv)).reshape(chunk // 8, 8, model), axis=0)
            return carry

        lax.fori_loop(0, length // chunk, some_back, 0)
        take = (
            lax.broadcasted_iota(jnp.int32, (model, LANES), 0) % krows
            == lax.broadcasted_iota(jnp.int32, (model, LANES), 1)
        ).astype(BF)
        own = (
            lax.broadcasted_iota(jnp.int32, (UNITS, model), 1) // krows
            == lax.broadcasted_iota(jnp.int32, (UNITS, model), 0)
        )
        for t, to in ((0, gf_ref), (1, ga_ref)):
            row = jnp.sum(acc[t], axis=0, keepdims=True)
            high = row.astype(BF).astype(F32)
            pieces = mm(jnp.where(own, high, 0.0).astype(BF), take)
            to[...] = pieces + mm(jnp.where(own, row - high, 0.0).astype(BF), take)

    return pl.pallas_call(
        kernel,
        out_shape=(
            sds((length, model), F32),
            sds((length, model), BF),
            sds((length, wide), BF),
            sds((length, width), BF),
            sds((length, model), BF),
            sds((UNITS, LANES), F32),
            sds((UNITS, LANES), F32),
        ),
        in_specs=vmem(11),
        out_specs=tuple(vmem(7)),
        scratch_shapes=[pltpu.VMEM((length, wide), BF), pltpu.VMEM((2, 8, model), F32)],
        compiler_params=params(),
        name="mixer_back",
    )(back_own, back_other, resid, cotangent, gains, wo, mixf, rb, e, wv, tokens)


def mixer_grads(where, xh, va, e, rb, n1, gv, gat, mixed, ga, ga_other, gf):
    length, model = n1.shape
    heads = e.shape[0]
    width = gv.shape[1]
    rows = length // UNITS
    krows = model // UNITS
    half = UNITS // 2
    deep = heads * rows + 2 * krows

    def kernel(where_ref, xh_ref, va_ref, e_ref, rb_ref, n1_ref, gv_ref, gat_ref, mixed_ref, ga_ref, gb_ref, gf_ref,
               keep, give, ds, wide_v, wide_o, pieces):
        def slot(u):
            return (keep, u) if u < half else (give, u - half)

        def one_head(h, carry):
            lanes = pl.ds(multiple(h * LANES, LANES), LANES)
            d = mm(xh_ref[:, lanes], va_ref[:, lanes], NT)
            for q in range(length // LANES):
                cols = slice(q * LANES, (q + 1) * LANES)
                ds[:, cols] = (e_ref[h, :, cols].astype(F32) * rb_ref[:, lanes] * d[:, cols]).astype(BF)
            for u in range(UNITS):
                ref, k = slot(u)
                at = pl.ds(multiple(where_ref[u] * rows, rows), rows)
                ref[k, pl.ds(multiple(h * rows, rows), rows), :] = ds[at, :]
            return carry

        lax.fori_loop(0, heads, one_head, 0)
        wide_v[...] = mm(n1_ref[...], gv_ref[...], TN).astype(BF)
        wide_o[...] = mm(gat_ref[...], mixed_ref[...], TN).astype(BF)
        pieces[0] = ga_ref[...] + gb_ref[...]
        pieces[1] = gf_ref[...]
        sub = lax.broadcasted_iota(jnp.int32, (krows, LANES), 0)
        top = heads * rows
        for u in range(UNITS):
            ref, k = slot(u)
            d = where_ref[u]
            at = pl.ds(multiple(d * krows, 16), krows)
            ref[k, top : top + krows, :width] = wide_v[at, :]
            ref[k, top + krows :, :width] = wide_o[at, :]
            both = jnp.where(
                sub == 0, pieces[0, pl.ds(d, 1), :], jnp.where(sub == 1, pieces[1, pl.ds(d, 1), :], 0.0)
            )
            ref[k, top : top + krows, width:] = both.astype(BF)
            ref[k, top + krows :, width:] = jnp.zeros((krows, length - width), BF)

    shape = sds((half, deep, length), BF)
    return pl.pallas_call(
        kernel,
        out_shape=(shape, shape),
        in_specs=[smem()] + vmem(11),
        out_specs=tuple(vmem(2)),
        scratch_shapes=[
            pltpu.VMEM((length, length), BF),
            pltpu.VMEM((model, width), BF),
            pltpu.VMEM((model, width), BF),
            pltpu.VMEM((2, UNITS, LANES), F32),
        ],
        compiler_params=params(),
        name="mixer_grads",
    )(where, xh, va, e, rb, n1, gv, gat, mixed, ga, ga_other, gf)


class Ring:
    def __init__(self, size):
        self.size = size
        self.chips = size // 2
        n = self.chips
        self.order = list(range(0, n, 2)) + list(range(n - 1, 0, -2))
        me = lax.axis_index("dp")
        self.core = me % 2
        chip = me // 2
        self.at = jnp.where(chip % 2 == 0, chip // 2, n - 1 - chip // 2)
        self.up = self.pairs(1)
        self.down = self.pairs(-1)
        self.swap = [(d, d ^ 1) for d in range(size)]

    def pairs(self, step):
        n = self.chips
        return [
            (self.order[p] * 2 + c, self.order[(p + step) % n] * 2 + c) for p in range(n) for c in range(2)
        ]

    def device(self, offset, core):
        n = self.chips
        p = (self.at + jnp.asarray(offset, jnp.int32) + n) % n
        chip = jnp.where(p < (n + 1) // 2, 2 * p, 2 * (n - 1 - p) + 1)
        return chip * 2 + core

    def gather(self, unit):
        n = self.chips
        ups, downs = [unit], [unit]
        for step in range(n // 2):
            ups.append(lax.ppermute(ups[-1], "dp", self.up))
            if step < n // 2 - 1:
                downs.append(lax.ppermute(downs[-1], "dp", self.down))
        mine = ups + downs[1:]
        theirs = [lax.ppermute(one, "dp", self.swap) for one in mine]
        return mine + theirs

    def gathered(self):
        n = self.chips
        offsets = [-s for s in range(n // 2 + 1)] + [s for s in range(1, n // 2)]
        return jnp.concatenate([self.device(offsets, self.core), self.device(offsets, 1 - self.core)])

    def scattered(self):
        offsets = list(range(self.chips))
        return jnp.concatenate([self.device(offsets, self.core), self.device(offsets, 1 - self.core)])

    def scatter(self, keep, give):
        n = self.chips
        got = lax.ppermute(give, "dp", self.swap)

        def add(k, *more):
            total = keep[k].astype(F32) + got[k].astype(F32)
            for one in more:
                total = total + one.astype(F32)
            return total

        far = n // 2
        up = lax.ppermute(add(far).astype(BF), "dp", self.up)
        down = lax.ppermute(add(far + 1).astype(BF), "dp", self.down)
        for step in range(1, far):
            up = lax.ppermute(add(far - step, up).astype(BF), "dp", self.up)
            if step < far - 1:
                down = lax.ppermute(add(far + 1 + step, down).astype(BF), "dp", self.down)
        return add(0, up, down)


def shards(
    tokens,
    segment_ids,
    gain_attn,
    gain_ffn,
    random_scores,
    w_value,
    w_output,
    w_up,
    w_down,
    cotangent,
):
    devices = lax.axis_size("dp")
    second = lax.axis_index("mp")
    length = segment_ids.shape[1]
    heads = random_scores.shape[0]
    model = tokens.shape[1]
    width = w_value.shape[1]
    rows = length // UNITS
    krows = model // UNITS
    ring = devices == UNITS and devices // 2 <= RING_CHIPS
    flip = [(0, 1), (1, 0)]

    wo_own = w_output.astype(BF)
    wo_other = lax.ppermute(wo_own, "mp", flip)
    wo_first = jnp.where(second == 0, wo_own, wo_other)
    wo_second = jnp.where(second == 0, wo_other, wo_own)
    if ring:
        net = Ring(devices)
        where_in = net.gathered().astype(jnp.int32)
        where_out = net.scattered().astype(jnp.int32)
        units_one = net.gather(pack_first(random_scores, w_value, gain_attn, gain_ffn))
        units_two = net.gather(pack_second(w_up, w_down, wo_first, wo_second))
    else:
        where_in = jnp.arange(UNITS, dtype=jnp.int32)
        where_out = where_in

        def gather(one, axis=0):
            return lax.all_gather(one.astype(BF), "dp", axis=axis, tiled=True)

        scores = gather(random_scores, 1).reshape(heads, UNITS, rows, length).transpose(1, 0, 2, 3)
        value = gather(w_value).reshape(UNITS, krows, width)
        gains = jnp.stack([gather(gain_attn), gather(gain_ffn)]).reshape(2, UNITS, krows).transpose(1, 0, 2)
        gains = jnp.pad(gains, ((0, 0), (0, krows - 2), (0, length - width - krows)))
        low = jnp.concatenate([value, gains], axis=2)
        both = jnp.concatenate([scores.reshape(UNITS, heads * rows, length), low], axis=1)
        units_one = [both[u] for u in range(UNITS)]
        packed = jnp.concatenate([gather(w_up), gather(w_down.T), gather(wo_first.T), gather(wo_second.T)], axis=1)
        packed = packed.reshape(UNITS, krows, packed.shape[1])
        units_two = [packed[u] for u in range(UNITS)]
    place = jnp.concatenate([where_in, jnp.reshape(second, (1,)).astype(jnp.int32)])

    e, va, mixed, mixf, rb, n1, gains, wv = mixer_forward(
        where_in, tokens, segment_ids, segment_ids.reshape(length, 1), units_one, heads, width
    )
    mixed_other = lax.ppermute(mixed, "mp", flip)
    back, resid, n2, act, gpre, wo = ffn_main(
        place, tokens, mixed, mixed_other, cotangent, gains, units_two, heads
    )
    back_other = lax.ppermute(back, "mp", flip)
    keep_two, give_two = ffn_grads(where_out, n2, gpre, act, cotangent)
    ffn = ffn_out(where_in, act, units_two, width)
    ffn_other = lax.ppermute(ffn, "mp", flip)
    gres, gat, xh, gv, part, ga, gf = mixer_back(
        back, back_other, resid, cotangent, gains, wo, mixf, rb, e, n1, wv, tokens
    )
    ga_other = lax.ppermute(ga, "mp", flip)
    part_other = lax.ppermute(part, "mp", flip)
    keep_one, give_one = mixer_grads(where_out, xh, va, e, rb, n1, gv, gat, mixed, ga, ga_other, gf)

    output = (resid + (ffn.astype(F32) + ffn_other.astype(F32))).astype(BF)
    grad_n1 = part.astype(F32) + part_other.astype(F32)
    x = tokens.astype(F32)
    inv = lax.rsqrt(jnp.mean(x * x, axis=-1, keepdims=True) + EPSILON)
    z = gains[0:1, :] * grad_n1
    hat = x * inv
    grad_tokens = (gres + inv * (z - hat * jnp.mean(z * hat, axis=-1, keepdims=True))).astype(BF)

    top = heads * rows
    if ring:
        two = net.scatter(keep_two, give_two)
        one = net.scatter(keep_one, give_one)
        out_up = two[:, : two.shape[1] // 2]
        out_down = two[:, two.shape[1] // 2 :].T
        out_scores = one[:top].reshape(heads, rows, length)
        out_value = one[top : top + krows, :width]
        out_output = one[top + krows :, :width].T
        out_gain_one = one[top, width : width + krows]
        out_gain_two = one[top + 1, width : width + krows]
    else:

        def scatter(one, axis=0):
            return lax.psum_scatter(one, "dp", scatter_dimension=axis, tiled=True)

        two = jnp.concatenate([keep_two, give_two]).astype(F32).reshape(model, -1)
        one = jnp.concatenate([keep_one, give_one]).astype(F32)
        out_up = scatter(two[:, : two.shape[1] // 2])
        out_down = scatter(two[:, two.shape[1] // 2 :]).T
        scores = one[:, :top].reshape(UNITS, heads, rows, length).transpose(1, 0, 2, 3)
        out_scores = scatter(scores.reshape(heads, length, length), 1)
        out_value = scatter(one[:, top : top + krows, :width].reshape(model, width))
        out_output = scatter(one[:, top + krows :, :width].reshape(model, width)).T
        out_gain_one = scatter(one[:, top, width : width + krows].reshape(model))
        out_gain_two = scatter(one[:, top + 1, width : width + krows].reshape(model))
    return (
        output,
        grad_tokens,
        out_gain_one,
        out_gain_two,
        out_scores,
        out_value,
        out_output,
        out_up,
        out_down,
    )


def solution(mesh):
    in_specs = (
        P("dp", None),
        P("dp", None),
        P("dp"),
        P("dp"),
        P("mp", "dp", None),
        P("dp", "mp"),
        P("mp", "dp"),
        P("dp", "mp"),
        P("mp", "dp"),
        P("dp", None),
    )
    out_specs = (
        P("dp", None),
        P("dp", None),
        P("dp"),
        P("dp"),
        P("mp", "dp", None),
        P("dp", "mp"),
        P("mp", "dp"),
        P("dp", "mp"),
        P("mp", "dp"),
    )
    return jax.shard_map(shards, mesh=mesh, in_specs=in_specs, out_specs=out_specs, check_vma=False)
```

```python
import jax
import jax.numpy as jnp
from jax import lax
from jax.experimental import pallas as pl
from jax.experimental.pallas import tpu as pltpu
from jax.sharding import PartitionSpec as P

EPSILON = 1e-06
NEGATIVE = -1e30
BF = jnp.bfloat16
F32 = jnp.float32
UNITS = 16
LANES = 128
PARTS = 2
RING_CHIPS = 8
VMEM_BYTES = 20 * 1024 * 1024
NT = (((1,), (1,)), ((), ()))
TN = (((0,), (0,)), ((), ()))
NN = (((1,), (0,)), ((), ()))


def mm(a, b, dims=NN):
    return lax.dot_general(a, b, dims, preferred_element_type=F32)


def run(kernel, name, scalars, arrays, outs, scratch=(), loose=(), loose_outs=(), micros=0):
    held = [pltpu.with_memory_space_constraint(one, pltpu.VMEM) for one in arrays]
    results = [pltpu.VMEM(*one) for one in outs] + [jax.ShapeDtypeStruct(*one) for one in loose_outs]
    specs = [pl.BlockSpec(memory_space=pltpu.SMEM)] * len(scalars)
    specs += [pl.BlockSpec(memory_space=pltpu.VMEM)] * len(arrays)
    specs += [pl.BlockSpec(memory_space=pltpu.HBM)] * len(loose)
    loose = [pltpu.with_memory_space_constraint(one, pltpu.HBM) for one in loose]
    out_specs = [pl.BlockSpec(memory_space=pltpu.VMEM)] * len(outs)
    out_specs += [pl.BlockSpec(memory_space=pl.ANY)] * len(loose_outs)
    return pl.pallas_call(
        kernel,
        out_shape=tuple(results),
        in_specs=specs,
        out_specs=tuple(out_specs),
        scratch_shapes=list(scratch),
        compiler_params=pltpu.CompilerParams(vmem_limit_bytes=VMEM_BYTES),
        cost_estimate=pl.CostEstimate(flops=1 + micros * 1_000_000_000, bytes_accessed=1, transcendentals=0),
        name=name,
    )(*scalars, *held, *loose)


def gelu_pair(x):
    c = 0.7978845608028654
    a = 0.044715
    square = x * x
    t = jnp.tanh(c * x * (1.0 + a * square))
    half = 0.5 * (1.0 + t)
    return x * half, half + 0.5 * x * (1.0 - t * t) * (c * (1.0 + 3.0 * a * square))


def multiple(value, of):
    return pl.multiple_of(value, of)


def fetch(refs, held, sem):
    copies = [pltpu.make_async_copy(ref, to, sem.at[n]) for n, (ref, to) in enumerate(zip(refs, held))]
    for copy in copies:
        copy.start()
    for copy in copies:
        copy.wait()


def pack_first(scores, wv, gain_one, gain_two, wo):
    heads, rows, length = scores.shape
    krows, width = wv.shape
    inputs = (scores, wv, gain_one.reshape(1, -1), gain_two.reshape(1, -1), wo)

    def kernel(*refs):
        out, wo_out, scr = refs[5:8]
        s_ref, wv_ref, ga_ref, gf_ref, wo_ref = refs[8:13]
        fetch(refs[:5], refs[8:13], refs[13])
        out[: heads * rows, :] = s_ref[...].reshape(heads * rows, length).astype(BF)
        out[heads * rows :, :width] = wv_ref[...].astype(BF)
        scr[...] = jnp.zeros_like(scr)
        scr[0:1, :krows] = ga_ref[...]
        scr[1:2, :krows] = gf_ref[...]
        out[heads * rows :, width:] = scr[...].astype(BF)
        wo_out[...] = wo_ref[...].astype(BF)

    return run(
        kernel,
        "pack_first",
        (),
        (),
        (((heads * rows + krows, length), BF), ((krows, width), BF)),
        (
            pltpu.VMEM((krows, length - width), F32),
            *[pltpu.VMEM(one.shape, one.dtype) for one in inputs],
            pltpu.SemaphoreType.DMA((5,)),
        ),
        loose=inputs,
    )


def pack_up(second, w_up, wo_own, wo_other):
    krows, hidden = w_up.shape
    half = wo_own.shape[1]

    def kernel(second_ref, own_ref, other_ref, up_ref, out, held, sem):
        fetch([up_ref], [held], sem)
        first = second_ref[0]
        out[:, :hidden] = held[...].astype(BF)
        out[:, pl.ds(multiple(hidden + first * half, LANES), half)] = own_ref[...]
        out[:, pl.ds(multiple(hidden + (1 - first) * half, LANES), half)] = other_ref[...]

    return run(
        kernel,
        "pack_up",
        (second,),
        (wo_own, wo_other),
        (((krows, hidden + 2 * half), BF),),
        (pltpu.VMEM(w_up.shape, F32), pltpu.SemaphoreType.DMA((1,))),
        loose=(w_up,),
    )[0]


def pack_down(w_down):
    krows, hidden = w_down.shape

    def kernel(down_ref, out, held, sem):
        fetch([down_ref], [held], sem)
        out[...] = held[...].astype(BF)

    return run(
        kernel,
        "pack_down",
        (),
        (),
        (((krows, hidden), BF),),
        (pltpu.VMEM(w_down.shape, F32), pltpu.SemaphoreType.DMA((1,))),
        loose=(w_down,),
    )[0]


def bring(units, where_ref, to, sem):
    rows = to.shape[0] // UNITS
    copies = []
    for u in range(UNITS):
        at = pl.ds(multiple(where_ref[u] * rows, 16), rows)
        copies.append(pltpu.make_async_copy(units[u], to.at[at, :], sem.at[u]))
        copies[-1].start()
    return copies


def mixer_forward(where, tokens, segments, units, heads, width):
    length, model = tokens.shape
    size = width // heads
    rows = length // UNITS
    krows = model // UNITS
    wide = heads * LANES

    deep = heads * rows + krows

    def kernel(where_ref, tok_ref, seg_ref, *rest):
        e_ref, va_ref, mixed_ref, mixf_ref, rb_ref, n1_ref, gains_ref, wv_ref, pieces, unit, same, sem = rest[UNITS:]
        copies = [
            pltpu.make_async_copy(rest[u], unit.at[where_ref[u]], sem.at[u]) for u in range(UNITS)
        ]
        for copy in copies:
            copy.start()
        documents = (seg_ref[...] == lax.broadcasted_iota(jnp.int32, (LANES, length), 0)).astype(BF)
        same[...] = mm(documents, documents, TN)
        for copy in copies:
            copy.wait()
        for d in range(UNITS):
            wv_ref[d * krows : (d + 1) * krows, :] = unit[d, heads * rows :, :width]
            some = unit[d, heads * rows : heads * rows + 16, width:].astype(F32)
            pieces[0, d : d + 1, :] = some[0:1, :]
            pieces[1, d : d + 1, :] = some[1:2, :]
        spread = (
            lax.broadcasted_iota(jnp.int32, (LANES, model), 1) % krows
            == lax.broadcasted_iota(jnp.int32, (LANES, model), 0)
        ).astype(BF)
        own = (
            lax.broadcasted_iota(jnp.int32, (UNITS, model), 1) // krows
            == lax.broadcasted_iota(jnp.int32, (UNITS, model), 0)
        )
        gains = []
        for t in range(2):
            full = jnp.where(own, mm(pieces[t].astype(BF), spread), 0.0)
            gains.append(jnp.sum(full, axis=0, keepdims=True))
            gains_ref[t : t + 1, :] = gains[t]
        x = tok_ref[...].astype(F32)
        inv = lax.rsqrt(jnp.mean(x * x, axis=-1, keepdims=True) + EPSILON)
        n1_ref[...] = (x * inv * gains[0]).astype(BF)
        values = mm(n1_ref[...], wv_ref[...]).astype(BF)
        tail = (lax.broadcasted_iota(jnp.int32, (length, LANES - size), 1) < 2).astype(BF)
        for h in range(heads):
            va_ref[:, h * LANES : h * LANES + size] = values[:, h * size : (h + 1) * size]
            va_ref[:, h * LANES + size : (h + 1) * LANES] = tail

        def one_head(h, carry):
            for d in range(UNITS):
                at = slice(d * rows, (d + 1) * rows)
                s = unit[d, pl.ds(multiple(h * rows, rows), rows), :].astype(F32)
                e_ref[h, at, :] = (jnp.exp(s) * same[at, :]).astype(BF)
            return carry

        lax.fori_loop(0, heads, one_head, 0)
        for h in range(heads):
            lanes = slice(h * LANES, (h + 1) * LANES)
            sums = mm(e_ref[h], va_ref[:, lanes])
            inverse = 1.0 / sums[:, size : size + 1]
            mixed = sums * inverse
            rb_ref[:, lanes] = jnp.broadcast_to(inverse, (length, LANES))
            mixf_ref[:, lanes] = jnp.where(
                lax.broadcasted_iota(jnp.int32, (length, LANES), 1) < size, mixed, 0.0
            )
            mixed_ref[:, h * size : (h + 1) * size] = mixed[:, :size].astype(BF)

    return run(
        kernel,
        "mixer_forward",
        (where,),
        (tokens, segments),
        (
            ((heads, length, length), BF),
            ((length, wide), BF),
            ((length, width), BF),
            ((length, wide), F32),
            ((length, wide), F32),
            ((length, model), BF),
            ((2, model), F32),
            ((model, width), BF),
        ),
        (
            pltpu.VMEM((2, UNITS, LANES), F32),
            pltpu.VMEM((UNITS, deep, length), BF),
            pltpu.VMEM((length, length), F32),
            pltpu.SemaphoreType.DMA((UNITS,)),
        ),
        loose=units,
        micros=6,
    )


def down_weights(where, cotangent, downs):
    length, model = cotangent.shape
    hidden = downs[0].shape[1]
    piece = hidden // 3

    def kernel(where_ref, cot_ref, *rest):
        out, gact, sem = rest[UNITS:]
        for copy in bring(rest[:UNITS], where_ref, out, sem):
            copy.wait()
        for j in range(3):
            cols = slice(j * piece, (j + 1) * piece)
            gact[:, cols] = mm(cot_ref[...], out[:, cols])

    return run(
        kernel,
        "down_weights",
        (where,),
        (cotangent,),
        (((model, hidden), BF), ((length, hidden), F32)),
        (pltpu.SemaphoreType.DMA((UNITS,)),),
        loose=downs,
        micros=4,
    )


def up_weights(where, ups):
    krows, columns = ups[0].shape

    def kernel(where_ref, *rest):
        out, sem = rest[UNITS:]
        for copy in bring(rest[:UNITS], where_ref, out, sem):
            copy.wait()

    return run(
        kernel,
        "up_weights",
        (where,),
        (),
        (((krows * UNITS, columns), BF),),
        (pltpu.SemaphoreType.DMA((UNITS,)),),
        loose=ups,
    )[0]


def ffn_main(second, tokens, mixed_own, mixed_other, gact, gains, w, part, parts):
    length, model = tokens.shape
    width = mixed_own.shape[1]
    hidden = gact.shape[1]
    chunk = length // parts
    piece = hidden // 3
    half = chunk // 2
    at = slice(part * chunk, (part + 1) * chunk)

    def kernel(second_ref, tok_ref, own_ref, other_ref, gact_ref, gains_ref, w_ref,
               back_one, back_two, resid_ref, n2_ref, act_ref, gpre_ref, mixed, acc):
        first = second_ref[0]
        mixed[:, pl.ds(multiple(first * width, LANES), width)] = own_ref[at, :]
        mixed[:, pl.ds(multiple((1 - first) * width, LANES), width)] = other_ref[at, :]
        attn = mm(mixed[...], w_ref[:, hidden:], NT)
        resid = tok_ref[at, :].astype(F32) + attn
        resid_ref[...] = resid
        inv = lax.rsqrt(jnp.mean(resid * resid, axis=-1, keepdims=True) + EPSILON)
        n2_ref[...] = (resid * inv * gains_ref[1:2, :]).astype(BF)
        for j in range(hidden // piece):
            cols = slice(j * piece, (j + 1) * piece)
            act, slope = gelu_pair(mm(n2_ref[...], w_ref[:, cols]))
            act_ref[:, cols] = act.astype(BF)
            gpre_ref[:, cols] = (gact_ref[at, cols] * slope).astype(BF)
            term = mm(gpre_ref[:, cols], w_ref[:, cols], NT)
            if j == 0:
                acc[...] = term
            else:
                acc[...] += term
        back_one[...] = acc[:half, :].astype(BF)
        back_two[...] = acc[half:, :].astype(BF)

    return run(
        kernel,
        "ffn_main",
        (second,),
        (tokens, mixed_own, mixed_other, gact, gains, w),
        (
            ((half, model), BF),
            ((half, model), BF),
            ((chunk, model), F32),
            ((chunk, model), BF),
            ((chunk, hidden), BF),
            ((chunk, hidden), BF),
        ),
        (
            pltpu.VMEM((chunk, 2 * width), BF),
            pltpu.VMEM((chunk, model), F32),
        ),
    )


def slots(keep, first, rest):
    half = UNITS // 2
    far = half // 2
    late = [k for k in range(half) if k not in (far, far + 1)]

    def slot(u):
        if u < half:
            return keep, u
        k = u - half
        return (rest, late.index(k)) if k in late else (first, k - far)

    return slot


def slot_shapes(rows, columns):
    half = UNITS // 2
    return tuple(((count, rows, columns), BF) for count in (half, 2, half - 2))


def ffn_grads(where, n2s, gpres, acts, cotangent):
    parts = len(n2s)
    chunk, model = n2s[0].shape
    hidden = acts[0].shape[1]
    krows = model // UNITS

    def kernel(where_ref, cot_ref, *rest):
        n2, gpre, act = rest[:parts], rest[parts : 2 * parts], rest[2 * parts : 3 * parts]
        slot = slots(*rest[3 * parts : 3 * parts + 3])
        scr, sem = rest[3 * parts + 3 :]
        piece = hidden // 3
        for j in range(3):
            cols = slice(j * piece, (j + 1) * piece)
            down = slice(hidden + j * piece, hidden + (j + 1) * piece)
            one = [mm(n2[r][...], gpre[r][:, cols], TN) for r in range(parts)]
            scr[:, cols] = sum(one).astype(BF)
            two = [mm(cot_ref[r * chunk : (r + 1) * chunk, :], act[r][:, cols], TN) for r in range(parts)]
            scr[:, down] = sum(two).astype(BF)
        copies = []
        for u in range(UNITS):
            at = pl.ds(multiple(where_ref[u] * krows, 16), krows)
            ref, k = slot(u)
            copies.append(pltpu.make_async_copy(scr.at[at, :], ref.at[k], sem.at[u]))
            copies[-1].start()
        for copy in copies:
            copy.wait()

    return run(
        kernel,
        "ffn_grads",
        (where,),
        (cotangent, *n2s, *gpres, *acts),
        (),
        (pltpu.VMEM((model, 2 * hidden), BF), pltpu.SemaphoreType.DMA((UNITS,))),
        loose_outs=slot_shapes(krows, 2 * hidden),
    )


def ffn_out(acts, wd):
    chunk, hidden = acts[0].shape
    model = wd.shape[0]

    def kernel(*refs):
        w_ref, out = refs[-2:]
        for r, act in enumerate(refs[:-2]):
            out[r * chunk : (r + 1) * chunk, :] = mm(act[...], w_ref[...], NT).astype(BF)

    return run(kernel, "ffn_out", (), (*acts, wd), (((chunk * len(acts), model), BF),))[0]


def cut_gain(row, krows):
    model = row.shape[1]
    take = (
        lax.broadcasted_iota(jnp.int32, (model, LANES), 0) % krows
        == lax.broadcasted_iota(jnp.int32, (model, LANES), 1)
    ).astype(BF)
    own = (
        lax.broadcasted_iota(jnp.int32, (UNITS, model), 1) // krows
        == lax.broadcasted_iota(jnp.int32, (UNITS, model), 0)
    )
    high = row.astype(BF).astype(F32)
    pieces = mm(jnp.where(own, high, 0.0).astype(BF), take)
    return pieces + mm(jnp.where(own, row - high, 0.0).astype(BF), take)


def resid_back(second, backs, others, resids, cotangent, gains, w, mixf, heads, size):
    length, model = cotangent.shape
    wide = heads * LANES
    count = len(backs)
    chunk = length // count
    krows = model // UNITS
    parts = len(resids)

    hidden = w.shape[1] - 2 * heads * size

    def kernel(second_ref, cot_ref, gains_ref, w_ref, mixf_ref, *rest):
        mine, other, res_refs = rest[:count], rest[count : 2 * count], rest[2 * count : 2 * count + parts]
        gres_ref, gat_ref, xh_ref, gf_ref, gm = rest[2 * count + parts :]
        total = jnp.zeros((8, model), F32)
        for r in range(count):
            at = slice(r * chunk, (r + 1) * chunk)
            g2 = mine[r][...].astype(F32) + other[r][...].astype(F32)
            per = count // parts
            res = res_refs[r // per][(r % per) * chunk : (r % per + 1) * chunk, :]
            inv = lax.rsqrt(jnp.mean(res * res, axis=-1, keepdims=True) + EPSILON)
            hat = res * inv
            total = total + jnp.sum((g2 * hat).reshape(chunk // 8, 8, model), axis=0)
            z = gains_ref[1:2, :] * g2
            corr = jnp.mean(z * hat, axis=-1, keepdims=True)
            gres = cot_ref[at, :].astype(F32) + inv * (z - hat * corr)
            gres_ref[at, :] = gres
            gat_ref[at, :] = gres.astype(BF)
        own = pl.ds(multiple(hidden + second_ref[0] * heads * size, LANES), heads * size)
        compact = mm(gat_ref[...], w_ref[:, own]).astype(BF)
        gm[...] = jnp.zeros_like(gm)
        for h in range(heads):
            gm[:, h * LANES : h * LANES + size] = compact[:, h * size : (h + 1) * size]
        lane = lax.broadcasted_iota(jnp.int32, (length, LANES), 1)
        for h in range(heads):
            lanes = slice(h * LANES, (h + 1) * LANES)
            here = gm[:, lanes].astype(F32)
            inner = -jnp.sum(here * mixf_ref[:, lanes], axis=-1, keepdims=True)
            high = inner.astype(BF).astype(F32)
            xh_ref[:, lanes] = jnp.where(
                lane == size, high, jnp.where(lane == size + 1, inner - high, here)
            ).astype(BF)
        gf_ref[...] = cut_gain(jnp.sum(total, axis=0, keepdims=True), krows)

    return run(
        kernel,
        "resid_back",
        (second,),
        (cotangent, gains, w, mixf, *backs, *others, *resids),
        (
            ((length, model), F32),
            ((length, model), BF),
            ((length, wide), BF),
            ((UNITS, LANES), F32),
        ),
        (pltpu.VMEM((length, wide), BF),),
    )


def score_grads(where_ref, xh_ref, va_ref, e_ref, rb_ref, ds, slot, first, count, rows):
    length = ds.shape[0]

    def one_head(h, carry):
        lanes = pl.ds(multiple((first + h) * LANES, LANES), LANES)
        d = mm(xh_ref[:, lanes], va_ref[:, lanes], NT)
        for q in range(length // LANES):
            cols = slice(q * LANES, (q + 1) * LANES)
            ds[:, cols] = (e_ref[first + h, :, cols].astype(F32) * rb_ref[:, lanes] * d[:, cols]).astype(BF)
        for u in range(UNITS):
            ref, k = slot(u)
            at = pl.ds(multiple(where_ref[u] * rows, rows), rows)
            ref[k, pl.ds(multiple(h * rows, rows), rows), :] = ds[at, :]
        return carry

    lax.fori_loop(0, count, one_head, 0)


def value_back(xh, rb, e, wv, tokens, size):
    length, model = tokens.shape
    heads = e.shape[0]
    width = heads * size
    chunk = length // 4
    krows = model // UNITS

    def kernel(xh_ref, rb_ref, e_ref, wv_ref, tok_ref, gv_ref, part_ref, ga_ref, acc):
        acc[...] = jnp.zeros_like(acc)
        for h in range(heads):
            lanes = slice(h * LANES, (h + 1) * LANES)
            scaled = (xh_ref[:, lanes].astype(F32) * rb_ref[:, lanes]).astype(BF)
            gv_ref[:, h * size : (h + 1) * size] = mm(e_ref[h], scaled, TN)[:, :size].astype(BF)

        def some_back(r, carry):
            at = pl.ds(multiple(r * chunk, chunk), chunk)
            part = mm(gv_ref[at, :], wv_ref[...], NT)
            part_ref[at, :] = part.astype(BF)
            x = tok_ref[at, :].astype(F32)
            inv = lax.rsqrt(jnp.mean(x * x, axis=-1, keepdims=True) + EPSILON)
            acc[...] += jnp.sum((part * (x * inv)).reshape(chunk // 8, 8, model), axis=0)
            return carry

        lax.fori_loop(0, length // chunk, some_back, 0)
        ga_ref[...] = cut_gain(jnp.sum(acc[...], axis=0, keepdims=True), krows)

    return run(
        kernel,
        "value_back",
        (),
        (xh, rb, e, wv, tokens),
        (
            ((length, width), BF),
            ((length, model), BF),
            ((UNITS, LANES), F32),
        ),
        (pltpu.VMEM((8, model), F32),),
    )


def mixer_grads(where, xh, va, e, rb, n1, gv, gat, mixed, ga, ga_other, gf, first, count):
    length, model = n1.shape
    width = gv.shape[1]
    rows = length // UNITS
    krows = model // UNITS
    top = count * rows
    deep = top + 2 * krows

    def kernel(where_ref, xh_ref, va_ref, e_ref, rb_ref, n1_ref, gv_ref, gat_ref, mixed_ref, ga_ref, gb_ref, gf_ref,
               keep, give, later, ds, wide_v, wide_o, pieces):
        slot = slots(keep, give, later)
        score_grads(where_ref, xh_ref, va_ref, e_ref, rb_ref, ds, slot, first, count, rows)
        wide_v[...] = mm(n1_ref[...], gv_ref[...], TN).astype(BF)
        wide_o[...] = mm(gat_ref[...], mixed_ref[...], TN).astype(BF)
        pieces[0] = ga_ref[...] + gb_ref[...]
        pieces[1] = gf_ref[...]
        sub = lax.broadcasted_iota(jnp.int32, (krows, LANES), 0)
        for u in range(UNITS):
            ref, k = slot(u)
            d = where_ref[u]
            at = pl.ds(multiple(d * krows, 16), krows)
            ref[k, top : top + krows, :width] = wide_v[at, :]
            ref[k, top + krows :, :width] = wide_o[at, :]
            both = jnp.where(
                sub == 0, pieces[0, pl.ds(d, 1), :], jnp.where(sub == 1, pieces[1, pl.ds(d, 1), :], 0.0)
            )
            ref[k, top : top + krows, width:] = both.astype(BF)
            ref[k, top + krows :, width:] = jnp.zeros((krows, length - width), BF)

    return run(
        kernel,
        "mixer_grads",
        (where,),
        (xh, va, e, rb, n1, gv, gat, mixed, ga, ga_other, gf),
        slot_shapes(deep, length),
        (
            pltpu.VMEM((length, length), BF),
            pltpu.VMEM((model, width), BF),
            pltpu.VMEM((model, width), BF),
            pltpu.VMEM((2, UNITS, LANES), F32),
        ),
    )


class Ring:
    def __init__(self, size):
        self.size = size
        self.chips = size // 2
        n = self.chips
        self.order = list(range(0, n, 2)) + list(range(n - 1, 0, -2))
        me = lax.axis_index("dp")
        self.core = me % 2
        chip = me // 2
        self.at = jnp.where(chip % 2 == 0, chip // 2, n - 1 - chip // 2)
        self.up = self.pairs(1)
        self.down = self.pairs(-1)
        self.swap = [(d, d ^ 1) for d in range(size)]

    def pairs(self, step):
        n = self.chips
        return [
            (self.order[p] * 2 + c, self.order[(p + step) % n] * 2 + c) for p in range(n) for c in range(2)
        ]

    def device(self, offset, core):
        n = self.chips
        p = (self.at + jnp.asarray(offset, jnp.int32) + n) % n
        chip = jnp.where(p < (n + 1) // 2, 2 * p, 2 * (n - 1 - p) + 1)
        return chip * 2 + core

    def gathered(self):
        n = self.chips
        offsets = [0]
        for s in range(1, n // 2 + 1):
            offsets.append(-s)
            if s < n // 2:
                offsets.append(s)
        return jnp.concatenate([self.device(offsets, self.core), self.device(offsets, 1 - self.core)])

    def scattered(self):
        offsets = list(range(self.chips))
        return jnp.concatenate([self.device(offsets, self.core), self.device(offsets, 1 - self.core)])


class Gather:
    def __init__(self, ring, unit):
        self.ring = ring
        self.last = [unit, unit]
        self.hops = 0
        self.mine = []
        self.theirs = []
        self.here = [unit]

    def values(self):
        return self.last

    def take(self, values):
        self.last = list(values)

    def hop(self):
        ring = self.ring
        self.hops += 1
        up = lax.ppermute(self.last[0], "dp", ring.up)
        new = [up]
        if self.hops < ring.chips // 2:
            new.append(lax.ppermute(self.last[1], "dp", ring.down))
        self.last = [up, new[-1]]
        self.swap()
        self.here = new

    def swap(self):
        self.theirs += [lax.ppermute(one, "dp", self.ring.swap) for one in self.here]
        self.mine += self.here
        self.here = []

    def finish(self):
        self.swap()
        return self.mine + self.theirs


class Scatter:
    def __init__(self, ring, keep, give, later):
        self.ring = ring
        self.keep = keep
        self.early = lax.ppermute(give, "dp", ring.swap)
        self.later = later
        self.last = []
        self.hops = 0

    def values(self):
        return self.last if self.hops else [self.early]

    def take(self, values):
        if self.hops:
            self.last = list(values)
        else:
            self.early = values[0]

    def total(self, k, *more):
        far = self.ring.chips // 2
        got = self.early[k - far] if k in (far, far + 1) else self.later[k if k < far else k - 2]
        value = self.keep[k].astype(F32) + got.astype(F32)
        for one in more:
            value = value + one.astype(F32)
        return value

    def hop(self):
        ring = self.ring
        far = ring.chips // 2
        self.hops += 1
        if self.hops == 1:
            self.later = lax.ppermute(self.later, "dp", ring.swap)
        up = self.total(far + 1 - self.hops, *self.last[:1]).astype(BF)
        new = [lax.ppermute(up, "dp", ring.up)]
        if self.hops < far:
            down = self.total(far + self.hops, *self.last[1:]).astype(BF)
            new.append(lax.ppermute(down, "dp", ring.down))
        else:
            new.append(self.last[1])
        self.last = new

    def result(self):
        return self.total(0, *self.last)


def together(chains, *more):
    values = [one for chain in chains for one in chain.values()]
    tied = lax.optimization_barrier(tuple(values) + more)
    at = 0
    for chain in chains:
        count = len(chain.values())
        chain.take(tied[at : at + count])
        at += count
    return tied[at:]


def tie(value, *after):
    return lax.optimization_barrier((value,) + after)[0] if after else value


def shards(
    tokens,
    segment_ids,
    gain_attn,
    gain_ffn,
    random_scores,
    w_value,
    w_output,
    w_up,
    w_down,
    cotangent,
):
    devices = lax.axis_size("dp")
    second = lax.axis_index("mp")
    length = segment_ids.shape[1]
    heads = random_scores.shape[0]
    model = tokens.shape[1]
    width = w_value.shape[1]
    size = width // heads
    rows = length // UNITS
    krows = model // UNITS
    ring = devices == UNITS and devices // 2 <= RING_CHIPS
    flip = [(0, 1), (1, 0)]
    second_at = jnp.reshape(second, (1,)).astype(jnp.int32)

    if ring:
        net = Ring(devices)
        far = net.chips // 2
        where_in = net.gathered().astype(jnp.int32)
        where_out = net.scattered().astype(jnp.int32)
        first_unit, wo_own = pack_first(random_scores, w_value, gain_attn, gain_ffn, w_output.T)
        wo_other = lax.ppermute(wo_own, "mp", flip)
        one = Gather(net, first_unit)
        one.hop()
        where_in, where_out, wo_other, up_from = together([one], where_in, where_out, wo_other, w_down.T)
        two = Gather(net, pack_down(up_from))
        one.hop()
        two.hop()
        (up_from,) = together([one, two], w_up)
        three = Gather(net, pack_up(second_at, up_from, wo_own, wo_other))
        for chain in (one, two, three):
            chain.hop()
        together([one, two, three])
        for chain in (one, two, three):
            chain.hop()
        together([one, two, three])
        first = one.finish()
    else:
        where_in = jnp.arange(UNITS, dtype=jnp.int32)
        where_out = where_in

        def gather(one, axis=0):
            return lax.all_gather(one.astype(BF), "dp", axis=axis, tiled=True)

        wo_own = w_output.astype(BF)
        wo_other = lax.ppermute(wo_own, "mp", flip)
        wo_first = jnp.where(second == 0, wo_own, wo_other)
        wo_second = jnp.where(second == 0, wo_other, wo_own)
        scores = gather(random_scores, 1).reshape(heads, UNITS, rows, length).transpose(1, 0, 2, 3)
        value = gather(w_value).reshape(UNITS, krows, width)
        gains = jnp.stack([gather(gain_attn), gather(gain_ffn)]).reshape(2, UNITS, krows).transpose(1, 0, 2)
        gains = jnp.pad(gains, ((0, 0), (0, krows - 2), (0, length - width - krows)))
        low = jnp.concatenate([value, gains], axis=2)
        both = jnp.concatenate([scores.reshape(UNITS, heads * rows, length), low], axis=1)
        up = jnp.concatenate([gather(w_up), gather(wo_first.T), gather(wo_second.T)], axis=1)
        up = up.reshape(UNITS, krows, up.shape[1])
        down = gather(w_down.T).reshape(UNITS, krows, w_down.shape[0])
        first, ups, downs = [[stack[u] for u in range(UNITS)] for stack in (both, up, down)]

    e, va, mixed, mixf, rb, n1, gains, wv = mixer_forward(
        where_in, tokens, segment_ids, first, heads, width
    )
    mixed_other = lax.ppermute(mixed, "mp", flip)
    if ring:
        two.hop()
        three.hop()
        (mixed,) = together([two, three], mixed)
        three.hop()
        downs, ups = two.finish(), three.finish()
    wd, gact = down_weights(where_in, cotangent, downs)
    w = up_weights(where_in, ups)
    backs, others, resids, n2s, acts, gpres = [], [], [], [], [], []
    for part in range(PARTS):
        one, two, resid, n2, act, gpre = ffn_main(
            second_at, tokens, mixed, mixed_other, gact, gains, w, part, PARTS
        )
        for new in (one, two):
            behind = others[-2:-1] if len(others) > 1 else []
            backs.append(new)
            others.append(lax.ppermute(tie(new, *behind), "mp", flip))
        resids.append(resid)
        n2s.append(n2)
        acts.append(act)
        gpres.append(gpre)
    parts_two = ffn_grads(where_out, n2s, gpres, acts, cotangent)
    ffn = ffn_out(acts, wd)
    ffn_other = lax.ppermute(tie(ffn, others[-1]), "mp", flip)
    if ring:
        ffn_sum = Scatter(net, *parts_two)
        together([ffn_sum])
        ffn_sum.hop()
        cotangent, ffn, *others = together([ffn_sum], cotangent, ffn, *others)
        ffn_sum.hop()
    gres, gat, xh, gf = resid_back(
        second_at, backs, others, resids, cotangent, gains, w, mixf, heads, size
    )
    gv, part, ga = value_back(xh, rb, e, wv, tokens, size)
    ga_other = lax.ppermute(ga, "mp", flip)
    part_other = lax.ppermute(part, "mp", flip)
    if ring:
        together([ffn_sum])
        ffn_sum.hop()
    parts_one = mixer_grads(
        where_out, xh, va, e, rb, n1, gv, gat, mixed, ga, ga_other, gf, 0, heads
    )

    top = heads * rows
    if ring:
        score_sum = Scatter(net, *parts_one)
        together([ffn_sum, score_sum])
        ffn_sum.hop()
        score_sum.hop()
        together([ffn_sum, score_sum])
        score_sum.hop()
        two = ffn_sum.result()
        (ffn_other,) = together([score_sum], ffn_other)
        score_sum.hop()
        (part_other,) = together([score_sum], part_other)
        score_sum.hop()
        one = score_sum.result()
        out_up = two[:, : two.shape[1] // 2]
        out_down = two[:, two.shape[1] // 2 :].T
        out_scores = one[:top].reshape(heads, rows, length)
        out_value = one[top : top + krows, :width]
        out_output = one[top + krows :, :width].T
        out_gain_one = one[top, width : width + krows]
        out_gain_two = one[top + 1, width : width + krows]
    else:

        def scatter(one, axis=0):
            return lax.psum_scatter(one, "dp", scatter_dimension=axis, tiled=True)

        def whole(keep, early, late):
            far = UNITS // 4
            return jnp.concatenate([keep, late[:far], early, late[far:]]).astype(F32)

        two = whole(*parts_two).reshape(model, -1)
        one = whole(*parts_one)
        out_up = scatter(two[:, : two.shape[1] // 2])
        out_down = scatter(two[:, two.shape[1] // 2 :]).T
        scores = one[:, :top].reshape(UNITS, heads, rows, length).transpose(1, 0, 2, 3)
        out_scores = scatter(scores.reshape(heads, length, length), 1)
        out_value = scatter(one[:, top : top + krows, :width].reshape(model, width))
        out_output = scatter(one[:, top + krows :, :width].reshape(model, width)).T
        out_gain_one = scatter(one[:, top, width : width + krows].reshape(model))
        out_gain_two = scatter(one[:, top + 1, width : width + krows].reshape(model))
    resid = jnp.concatenate(resids)
    output = (resid + (ffn.astype(F32) + ffn_other.astype(F32))).astype(BF)
    grad_n1 = part.astype(F32) + part_other.astype(F32)
    x = tokens.astype(F32)
    inv = lax.rsqrt(jnp.mean(x * x, axis=-1, keepdims=True) + EPSILON)
    z = gains[0:1, :] * grad_n1
    hat = x * inv
    grad_tokens = (gres + inv * (z - hat * jnp.mean(z * hat, axis=-1, keepdims=True))).astype(BF)

    return (
        output,
        grad_tokens,
        out_gain_one,
        out_gain_two,
        out_scores,
        out_value,
        out_output,
        out_up,
        out_down,
    )


def solution(mesh):
    in_specs = (
        P("dp", None),
        P("dp", None),
        P("dp"),
        P("dp"),
        P("mp", "dp", None),
        P("dp", "mp"),
        P("mp", "dp"),
        P("dp", "mp"),
        P("mp", "dp"),
        P("dp", None),
    )
    out_specs = (
        P("dp", None),
        P("dp", None),
        P("dp"),
        P("dp"),
        P("mp", "dp", None),
        P("dp", "mp"),
        P("mp", "dp"),
        P("dp", "mp"),
        P("mp", "dp"),
    )
    return jax.shard_map(shards, mesh=mesh, in_specs=in_specs, out_specs=out_specs, check_vma=False)
```

```python
import jax
import jax.numpy as jnp
from jax import lax
from jax.experimental import pallas as pl
from jax.experimental.pallas import tpu as pltpu
from jax.sharding import PartitionSpec as P

EPSILON = 1e-06
NEGATIVE = -1e30
BF = jnp.bfloat16
F32 = jnp.float32
UNITS = 16
LANES = 128
PARTS = 2
RING_CHIPS = 8
VMEM_BYTES = 20 * 1024 * 1024
NT = (((1,), (1,)), ((), ()))
TN = (((0,), (0,)), ((), ()))
NN = (((1,), (0,)), ((), ()))


def mm(a, b, dims=NN):
    return lax.dot_general(a, b, dims, preferred_element_type=F32)


def run(kernel, name, scalars, arrays, outs, scratch=(), loose=(), loose_outs=(), micros=0, aliases=None):
    held = [pltpu.with_memory_space_constraint(one, pltpu.VMEM) for one in arrays]
    results = [pltpu.VMEM(*one) for one in outs] + [jax.ShapeDtypeStruct(*one) for one in loose_outs]
    specs = [pl.BlockSpec(memory_space=pltpu.SMEM)] * len(scalars)
    specs += [pl.BlockSpec(memory_space=pltpu.VMEM)] * len(arrays)
    specs += [pl.BlockSpec(memory_space=pltpu.HBM)] * len(loose)
    loose = [pltpu.with_memory_space_constraint(one, pltpu.HBM) for one in loose]
    out_specs = [pl.BlockSpec(memory_space=pltpu.VMEM)] * len(outs)
    out_specs += [pl.BlockSpec(memory_space=pl.ANY)] * len(loose_outs)
    return pl.pallas_call(
        kernel,
        out_shape=tuple(results),
        in_specs=specs,
        out_specs=tuple(out_specs),
        scratch_shapes=list(scratch),
        compiler_params=pltpu.CompilerParams(vmem_limit_bytes=VMEM_BYTES),
        cost_estimate=pl.CostEstimate(flops=1 + micros * 1_000_000_000, bytes_accessed=1, transcendentals=0),
        input_output_aliases=aliases or {},
        name=name,
    )(*scalars, *held, *loose)


def gelu_pair(x):
    c = 0.7978845608028654
    a = 0.044715
    square = x * x
    t = jnp.tanh(c * x * (1.0 + a * square))
    half = 0.5 * (1.0 + t)
    return x * half, half + 0.5 * x * (1.0 - t * t) * (c * (1.0 + 3.0 * a * square))


def multiple(value, of):
    return pl.multiple_of(value, of)


class Unit:
    def __init__(self, heads, rows, krows, length, model, width, hidden):
        self.scores = heads * rows
        self.krows = krows
        self.length = length
        self.width = width
        self.hidden = hidden
        self.wide = width + model
        self.blocks = [("ffn", n * length) for n in range(2 * hidden // length)]
        self.blocks += [("proj", n * length) for n in range(self.wide // length)]
        self.tail = self.wide % length
        self.last = self.scores + krows * len(self.blocks)
        self.fold = krows // 3
        self.deep = self.last + self.fold
        self.cut = self.scores + krows * (2 * hidden // length // 3)
        self.gain_lane = 3 * self.tail

    def ffn_parts(self):
        parts = []
        for n, (kind, first) in enumerate(self.blocks):
            at = self.scores + n * self.krows
            if kind == "ffn":
                parts.append((at, 0, 0, first, self.krows, self.length))
            else:
                skip = max(self.width - first, 0)
                column = 2 * self.hidden + first + skip - self.width
                parts.append((at, skip, 0, column, self.krows, self.length - skip))
        for n in range(3):
            column = 2 * self.hidden + self.wide - self.tail - self.width
            parts.append((self.last, n * self.tail, n * self.fold, column, self.fold, self.tail))
        return parts

    def value_row(self):
        return self.scores + [kind for kind, _ in self.blocks].index("proj") * self.krows


def pack_unit(plan, scores, w_up, w_down):
    inputs = (scores, w_up, w_down)
    krows, length = plan.krows, plan.length
    per = plan.hidden // length

    def kernel(*refs):
        out, held, sem = refs[3], refs[4:7], refs[7]
        fetch(refs[:3], held, sem)
        s_ref, up_ref, down_ref = held
        out[: plan.scores, :] = s_ref[...].reshape(plan.scores, length).astype(BF)
        for n, (kind, column) in enumerate(plan.blocks):
            if kind == "ffn":
                at = slice(plan.scores + n * krows, plan.scores + (n + 1) * krows)
                ref, first = (up_ref, column) if n < per else (down_ref, column - plan.hidden)
                out[at, :] = ref[:, first : first + length].astype(BF)

    return run(
        kernel,
        "pack_unit",
        (),
        (),
        (((plan.deep, length), BF),),
        (*[pltpu.VMEM(one.shape, one.dtype) for one in inputs], pltpu.SemaphoreType.DMA((3,))),
        loose=inputs,
    )[0]


def pack_rest(plan, second, unit, wv, gain_one, gain_two, wo_own, wo_other):
    inputs = (wv, gain_one.reshape(1, -1), gain_two.reshape(1, -1), wo_own)
    krows, length, width = plan.krows, plan.length, plan.width

    def kernel(second_ref, other_ref, old, *rest):
        out, wide, gains = rest[4:7]
        held, sem = rest[7:11], rest[11]
        fetch(rest[:4], held, sem)
        wv_ref, ga_ref, gf_ref, own_ref = held
        first = second_ref[0]
        wide[:, :width] = wv_ref[...].astype(BF)
        wide[:, pl.ds(multiple(width + first * width, LANES), width)] = own_ref[...].astype(BF)
        wide[:, pl.ds(multiple(width + (1 - first) * width, LANES), width)] = other_ref[...].astype(BF)
        for n, (kind, column) in enumerate(plan.blocks):
            if kind == "proj":
                at = slice(plan.scores + n * krows, plan.scores + (n + 1) * krows)
                out[at, :] = wide[:, column : column + length]
        for n in range(3):
            lanes = slice(n * plan.tail, (n + 1) * plan.tail)
            out[plan.last :, lanes] = wide[n * plan.fold : (n + 1) * plan.fold, plan.wide - plan.tail :]
        gains[...] = jnp.zeros_like(gains)
        gains[0:1, :krows] = ga_ref[...]
        gains[1:2, :krows] = gf_ref[...]
        out[plan.last :, plan.gain_lane :] = gains[...].astype(BF)

    return run(
        kernel,
        "pack_rest",
        (second,),
        (wo_other, unit),
        (((plan.deep, length), BF),),
        (
            pltpu.VMEM((krows, plan.wide), BF),
            pltpu.VMEM((plan.fold, length - plan.gain_lane), F32),
            *[pltpu.VMEM(one.shape, one.dtype) for one in inputs],
            pltpu.SemaphoreType.DMA((4,)),
        ),
        loose=inputs,
        aliases={2: 0},
    )[0]


def fetch(refs, held, sem):
    copies = [pltpu.make_async_copy(ref, to, sem.at[n]) for n, (ref, to) in enumerate(zip(refs, held))]
    for copy in copies:
        copy.start()
    for copy in copies:
        copy.wait()


def pick(units, shares, where_ref, parts, target, sem):
    copies = []
    for n, (u, first, rows) in enumerate(shares):
        owner = where_ref[u]
        for m, part in enumerate(parts):
            row, column, count, columns = part[0], part[1], part[-2], part[-1]
            if first <= row and row + count <= first + rows:
                source = units[n].at[pl.ds(row - first, count), pl.ds(column, columns)]
                copies.append(pltpu.make_async_copy(source, target(m, owner), sem.at[u, m]))
                copies[-1].start()
    return copies


def mixer_rows(plan, units, shares, where_ref, seg_ref, e_ref, unit, same, sem):
    heads, length, _ = e_ref.shape
    rows = length // UNITS
    top = heads * rows
    mine = [n for n, (_, first, _) in enumerate(shares) if first == 0]

    def target(m, owner):
        return unit.at[pl.ds(multiple(owner * top, top), top), :]

    copies = pick([units[n] for n in mine], [shares[n] for n in mine], where_ref, [(0, 0, top, length)], target, sem)

    def write():
        documents = (seg_ref[...] == lax.broadcasted_iota(jnp.int32, (LANES, length), 0)).astype(BF)
        same[...] = mm(documents, documents, TN)
        for copy in copies:
            copy.wait()

        def one_head(h, carry):
            for n in mine:
                owner = where_ref[shares[n][0]]
                at = pl.ds(multiple(owner * rows, rows), rows)
                s = unit[pl.ds(multiple(owner * top + h * rows, rows), rows), :].astype(F32)
                e_ref[h, at, :] = (jnp.exp(s) * same[at, :]).astype(BF)
            return carry

        lax.fori_loop(0, heads, one_head, 0)

    return write


def mixer_first(plan, where, segments, units, shares, heads):
    length = segments.shape[1]
    rows = length // UNITS

    def kernel(where_ref, seg_ref, *rest):
        e_ref, unit, same, sem = rest[len(units) :]
        mixer_rows(plan, rest[: len(units)], shares, where_ref, seg_ref, e_ref, unit, same, sem)()

    return run(
        kernel,
        "mixer_first",
        (where,),
        (segments,),
        (((heads, length, length), BF),),
        (
            pltpu.VMEM((heads * length, length), BF),
            pltpu.VMEM((length, length), F32),
            pltpu.SemaphoreType.DMA((UNITS, 1)),
        ),
        loose=units,
    )[0]


def mixer_forward(plan, where, tokens, segments, e, units, shares, late, heads, width):
    length, model = tokens.shape
    size = width // heads
    krows = model // UNITS
    wide = heads * LANES
    parts = [
        (plan.value_row(), 0, krows, width),
        (plan.last, plan.gain_lane, plan.fold, LANES),
    ]
    count = len(units)

    def kernel(where_ref, tok_ref, seg_ref, e_old, *rest):
        unit_refs = rest[:count]
        e_ref, va_ref, mixed_ref, mixf_ref, rb_ref, n1_ref, gains_ref, wv_ref, pieces, unit, low, same, sem, more = rest[count:]

        def target(m, owner):
            if m == 0:
                return wv_ref.at[pl.ds(multiple(owner * krows, 16), krows), :]
            return low.at[owner]

        copies = pick(unit_refs, shares, where_ref, parts, target, sem)
        now = [n for n in range(count) if n in late]
        write = mixer_rows(
            plan, [unit_refs[n] for n in now], [shares[n] for n in now], where_ref, seg_ref, e_ref, unit, same, more
        )
        for copy in copies:
            copy.wait()
        for d in range(UNITS):
            some = low[d].astype(F32)
            pieces[0, d : d + 1, :] = some[0:1, :]
            pieces[1, d : d + 1, :] = some[1:2, :]
        spread = (
            lax.broadcasted_iota(jnp.int32, (LANES, model), 1) % krows
            == lax.broadcasted_iota(jnp.int32, (LANES, model), 0)
        ).astype(BF)
        own = (
            lax.broadcasted_iota(jnp.int32, (UNITS, model), 1) // krows
            == lax.broadcasted_iota(jnp.int32, (UNITS, model), 0)
        )
        gains = []
        for t in range(2):
            full = jnp.where(own, mm(pieces[t].astype(BF), spread), 0.0)
            gains.append(jnp.sum(full, axis=0, keepdims=True))
            gains_ref[t : t + 1, :] = gains[t]
        x = tok_ref[...].astype(F32)
        inv = lax.rsqrt(jnp.mean(x * x, axis=-1, keepdims=True) + EPSILON)
        n1_ref[...] = (x * inv * gains[0]).astype(BF)
        values = mm(n1_ref[...], wv_ref[...]).astype(BF)
        tail = (lax.broadcasted_iota(jnp.int32, (length, LANES - size), 1) < 2).astype(BF)
        for h in range(heads):
            va_ref[:, h * LANES : h * LANES + size] = values[:, h * size : (h + 1) * size]
            va_ref[:, h * LANES + size : (h + 1) * LANES] = tail

        write()
        for h in range(heads):
            lanes = slice(h * LANES, (h + 1) * LANES)
            sums = mm(e_ref[h], va_ref[:, lanes])
            inverse = 1.0 / sums[:, size : size + 1]
            mixed = sums * inverse
            rb_ref[:, lanes] = jnp.broadcast_to(inverse, (length, LANES))
            mixf_ref[:, lanes] = jnp.where(
                lax.broadcasted_iota(jnp.int32, (length, LANES), 1) < size, mixed, 0.0
            )
            mixed_ref[:, h * size : (h + 1) * size] = mixed[:, :size].astype(BF)

    return run(
        kernel,
        "mixer_forward",
        (where,),
        (tokens, segments, e),
        (
            ((heads, length, length), BF),
            ((length, wide), BF),
            ((length, width), BF),
            ((length, wide), F32),
            ((length, wide), F32),
            ((length, model), BF),
            ((2, model), F32),
            ((model, width), BF),
        ),
        (
            pltpu.VMEM((2, UNITS, LANES), F32),
            pltpu.VMEM((heads * length, length), BF),
            pltpu.VMEM((UNITS, plan.fold, LANES), BF),
            pltpu.VMEM((length, length), F32),
            pltpu.SemaphoreType.DMA((UNITS, len(parts))),
            pltpu.SemaphoreType.DMA((UNITS, 1)),
        ),
        loose=units,
        aliases={3: 0},
    )


def second_weights(plan, where, cotangent, units, shares):
    length, model = cotangent.shape
    hidden, krows = plan.hidden, plan.krows
    piece = hidden // 3
    parts = plan.ffn_parts()

    def kernel(where_ref, cot_ref, *rest):
        out, gact, sem = rest[len(units) :]

        def target(m, owner):
            _, _, row, column, rows, columns = parts[m]
            return out.at[pl.ds(multiple(owner * krows + row, 16), rows), pl.ds(column, columns)]

        for copy in pick(rest[: len(units)], shares, where_ref, parts, target, sem):
            copy.wait()
        for j in range(3):
            cols = slice(j * piece, (j + 1) * piece)
            gact[:, cols] = mm(cot_ref[...], out[:, hidden + j * piece : hidden + (j + 1) * piece])

    return run(
        kernel,
        "second_weights",
        (where,),
        (cotangent,),
        (((model, 2 * hidden + model), BF), ((length, hidden), F32)),
        (pltpu.SemaphoreType.DMA((UNITS, len(parts))),),
        loose=units,
    )


def ffn_main(second, tokens, mixed_own, mixed_other, gact, gains, w, part, parts, pieces):
    length, model = tokens.shape
    width = mixed_own.shape[1]
    hidden = gact.shape[1]
    chunk = length // parts
    piece = hidden // 3
    at = slice(part * chunk, (part + 1) * chunk)

    def kernel(second_ref, tok_ref, own_ref, other_ref, gact_ref, gains_ref, w_ref,
               *rest):
        backs = rest[:pieces]
        resid_ref, n2_ref, act_ref, gpre_ref, mixed, acc = rest[pieces:]
        first = second_ref[0]
        mixed[:, pl.ds(multiple(first * width, LANES), width)] = own_ref[at, :]
        mixed[:, pl.ds(multiple((1 - first) * width, LANES), width)] = other_ref[at, :]
        attn = mm(mixed[...], w_ref[:, 2 * hidden :], NT)
        resid = tok_ref[at, :].astype(F32) + attn
        resid_ref[...] = resid
        inv = lax.rsqrt(jnp.mean(resid * resid, axis=-1, keepdims=True) + EPSILON)
        n2_ref[...] = (resid * inv * gains_ref[1:2, :]).astype(BF)
        for j in range(hidden // piece):
            cols = slice(j * piece, (j + 1) * piece)
            act, slope = gelu_pair(mm(n2_ref[...], w_ref[:, cols]))
            act_ref[:, cols] = act.astype(BF)
            gpre_ref[:, cols] = (gact_ref[at, cols] * slope).astype(BF)
            term = mm(gpre_ref[:, cols], w_ref[:, cols], NT)
            if j == 0:
                acc[...] = term
            else:
                acc[...] += term
        for n, back_ref in enumerate(backs):
            back_ref[...] = acc[n * (chunk // pieces) : (n + 1) * (chunk // pieces), :].astype(BF)

    return run(
        kernel,
        "ffn_main",
        (second,),
        (tokens, mixed_own, mixed_other, gact, gains, w),
        (
            *[((chunk // pieces, model), BF)] * pieces,
            ((chunk, model), F32),
            ((chunk, model), BF),
            ((chunk, hidden), BF),
            ((chunk, hidden), BF),
        ),
        (
            pltpu.VMEM((chunk, 2 * width), BF),
            pltpu.VMEM((chunk, model), F32),
        ),
    )


def late_groups():
    half = UNITS // 2
    far = half // 2
    groups = [[far + 1 - hop, far - 1 + hop] for hop in range(2, far + 1)]
    return groups + [[0]]


def late_place(k):
    return next((g, group.index(k)) for g, group in enumerate(late_groups()) if k in group)


def slots(refs):
    half = UNITS // 2
    keep, one, two, *later = refs
    columns = keep.shape[2]

    def slot(u):
        if u < half:
            return [(keep.at[u], 0, columns)]
        k = u - half
        if k == half // 2:
            return [(one, 0, columns // 2), (two, columns // 2, columns // 2)]
        group, place = late_place(k)
        return [(later[group].at[place], 0, columns)]

    return slot


def slot_shapes(rows, columns):
    early = ((rows, columns // 2), BF)
    later = [((len(group), rows, columns), BF) for group in late_groups()]
    return [((UNITS // 2, rows, columns), BF), early, early, *later]


SLOTS = 3 + len(late_groups())


def far_sum(far, keep, early, second):
    _, rows, columns = keep.shape
    half = columns // 2

    def kernel(keep_ref, early_ref, second_ref, up, down):
        for out, one, at in ((up, early_ref, slice(0, half)), (down, second_ref, slice(half, columns))):
            out[...] = (keep_ref[far, :, at].astype(F32) + one[...].astype(F32)).astype(BF)

    return run(kernel, "far_sum", (), (keep, early, second), [((rows, half), BF)] * 2)


def next_sums(far, keep, later, up, down):
    _, rows, columns = keep.shape
    half = columns // 2

    def kernel(keep_ref, later_ref, up_ref, down_ref, up_out, down_out):
        for out, one, k, mine in ((up_out, up_ref, far - 1, 0), (down_out, down_ref, far + 1, 1)):
            for n in range(2):
                at = slice(n * half, (n + 1) * half)
                total = keep_ref[k, :, at].astype(F32) + later_ref[late_place(k)[1], :, at].astype(F32)
                if n == mine:
                    total = total + one[...].astype(F32)
                out[:, at] = total.astype(BF)

    return run(kernel, "next_sums", (), (keep, later, up, down), [((rows, columns), BF)] * 2)


def result_kernel(name, keep, later, up, down, shapes, cut):
    def kernel(keep_ref, later_ref, up_ref, down_ref, *rest):
        outs, held, sem = rest[: len(shapes)], rest[len(shapes) : -1], rest[-1]

        def total(rows, columns):
            value = keep_ref[0, rows, columns].astype(F32) + later_ref[late_place(0)[1], rows, columns].astype(F32)
            return value + up_ref[rows, columns].astype(F32) + down_ref[rows, columns].astype(F32)

        copies = []
        for n, (out, to) in enumerate(zip(outs, held)):
            cut(n, to, total)
            copies.append(pltpu.make_async_copy(to, out, sem.at[n]))
            copies[-1].start()
        for copy in copies:
            copy.wait()

    return run(
        kernel,
        name,
        (),
        (keep, later, up, down),
        (),
        (*[pltpu.VMEM(shape, F32) for shape in shapes], pltpu.SemaphoreType.DMA((len(shapes),))),
        loose_outs=[(shape, F32) for shape in shapes],
    )


def ffn_result(keep, later, up, down):
    _, rows, columns = keep.shape
    half = columns // 2

    def cut(n, to, total):
        to[...] = total(slice(None), slice(n * half, (n + 1) * half))

    return result_kernel("ffn_result", keep, later, up, down, [(rows, half)] * 2, cut)


def mixer_result(keep, later, up, down, heads, krows, width):
    _, deep, length = keep.shape
    top = deep - 2 * krows
    rows = top // heads
    shapes = [(heads, rows, length), (krows, width), (krows, width), (1, krows), (1, krows)]

    def cut(n, to, total):
        if n == 0:
            for h in range(heads):
                to[h] = total(slice(h * rows, (h + 1) * rows), slice(None))
        elif n < 3:
            to[...] = total(slice(top + (n - 1) * krows, top + n * krows), slice(0, width))
        else:
            to[...] = total(slice(top, top + 16), slice(width, length))[n - 3 : n - 2, :krows]

    return result_kernel("mixer_result", keep, later, up, down, shapes, cut)


def ffn_grads(where, n2s, gpres, acts, cotangent):
    parts = len(n2s)
    chunk, model = n2s[0].shape
    hidden = acts[0].shape[1]
    krows = model // UNITS

    def kernel(where_ref, cot_ref, *rest):
        n2, gpre, act = rest[:parts], rest[parts : 2 * parts], rest[2 * parts : 3 * parts]
        slot = slots(rest[3 * parts : 3 * parts + SLOTS])
        scr, sem = rest[3 * parts + SLOTS :]
        piece = hidden // 3
        for j in range(3):
            cols = slice(j * piece, (j + 1) * piece)
            down = slice(hidden + j * piece, hidden + (j + 1) * piece)
            one = [mm(n2[r][...], gpre[r][:, cols], TN) for r in range(parts)]
            scr[:, cols] = sum(one).astype(BF)
            two = [mm(cot_ref[r * chunk : (r + 1) * chunk, :], act[r][:, cols], TN) for r in range(parts)]
            scr[:, down] = sum(two).astype(BF)
        copies = []
        for u in range(UNITS):
            at = pl.ds(multiple(where_ref[u] * krows, 16), krows)
            for n, (to, first, many) in enumerate(slot(u)):
                copies.append(pltpu.make_async_copy(scr.at[at, pl.ds(first, many)], to, sem.at[u, n]))
                copies[-1].start()
        for copy in copies:
            copy.wait()

    return run(
        kernel,
        "ffn_grads",
        (where,),
        (cotangent, *n2s, *gpres, *acts),
        (),
        (pltpu.VMEM((model, 2 * hidden), BF), pltpu.SemaphoreType.DMA((UNITS, 2))),
        loose_outs=slot_shapes(krows, 2 * hidden),
    )


def ffn_out(acts, w):
    chunk, hidden = acts[0].shape
    model = w.shape[0]

    def kernel(*refs):
        parts = len(refs) // 2
        for act, out in zip(refs[:parts], refs[parts + 1 :]):
            out[...] = mm(act[...], refs[parts][:, hidden : 2 * hidden], NT).astype(BF)

    return run(kernel, "ffn_out", (), (*acts, w), [((chunk, model), BF)] * len(acts))


def cut_gain(row, krows):
    model = row.shape[1]
    take = (
        lax.broadcasted_iota(jnp.int32, (model, LANES), 0) % krows
        == lax.broadcasted_iota(jnp.int32, (model, LANES), 1)
    ).astype(BF)
    own = (
        lax.broadcasted_iota(jnp.int32, (UNITS, model), 1) // krows
        == lax.broadcasted_iota(jnp.int32, (UNITS, model), 0)
    )
    high = row.astype(BF).astype(F32)
    pieces = mm(jnp.where(own, high, 0.0).astype(BF), take)
    return pieces + mm(jnp.where(own, row - high, 0.0).astype(BF), take)


def resid_back(second, backs, others, resids, cotangent, gains, w, mixf, heads, size):
    length, model = cotangent.shape
    wide = heads * LANES
    count = len(backs)
    krows = model // UNITS
    parts = len(resids)

    hidden = w.shape[1] - 2 * heads * size

    def kernel(second_ref, cot_ref, gains_ref, w_ref, mixf_ref, *rest):
        mine, other, res_refs = rest[:count], rest[count : 2 * count], rest[2 * count : 2 * count + parts]
        gres_ref, gat_ref, xh_ref, gf_ref, gm = rest[2 * count + parts :]
        total = jnp.zeros((8, model), F32)
        begin = 0
        for r in range(count):
            chunk = mine[r].shape[0]
            at = slice(begin, begin + chunk)
            g2 = mine[r][...].astype(F32) + other[r][...].astype(F32)
            whole = length // parts
            res = res_refs[begin // whole][begin % whole : begin % whole + chunk, :]
            begin += chunk
            inv = lax.rsqrt(jnp.mean(res * res, axis=-1, keepdims=True) + EPSILON)
            hat = res * inv
            total = total + jnp.sum((g2 * hat).reshape(chunk // 8, 8, model), axis=0)
            z = gains_ref[1:2, :] * g2
            corr = jnp.mean(z * hat, axis=-1, keepdims=True)
            gres = cot_ref[at, :].astype(F32) + inv * (z - hat * corr)
            gres_ref[at, :] = gres
            gat_ref[at, :] = gres.astype(BF)
        own = pl.ds(multiple(hidden + second_ref[0] * heads * size, LANES), heads * size)
        compact = mm(gat_ref[...], w_ref[:, own]).astype(BF)
        gm[...] = jnp.zeros_like(gm)
        for h in range(heads):
            gm[:, h * LANES : h * LANES + size] = compact[:, h * size : (h + 1) * size]
        lane = lax.broadcasted_iota(jnp.int32, (length, LANES), 1)
        for h in range(heads):
            lanes = slice(h * LANES, (h + 1) * LANES)
            here = gm[:, lanes].astype(F32)
            inner = -jnp.sum(here * mixf_ref[:, lanes], axis=-1, keepdims=True)
            high = inner.astype(BF).astype(F32)
            xh_ref[:, lanes] = jnp.where(
                lane == size, high, jnp.where(lane == size + 1, inner - high, here)
            ).astype(BF)
        gf_ref[...] = cut_gain(jnp.sum(total, axis=0, keepdims=True), krows)

    return run(
        kernel,
        "resid_back",
        (second,),
        (cotangent, gains, w, mixf, *backs, *others, *resids),
        (
            ((length, model), F32),
            ((length, model), BF),
            ((length, wide), BF),
            ((UNITS, LANES), F32),
        ),
        (pltpu.VMEM((length, wide), BF),),
    )


def score_grads(where_ref, xh_ref, va_ref, e_ref, rb_ref, ds, slot, begin, count, rows):
    length = ds.shape[0]

    def one_head(h, carry):
        lanes = pl.ds(multiple((begin + h) * LANES, LANES), LANES)
        d = mm(xh_ref[:, lanes], va_ref[:, lanes], NT)
        for q in range(length // LANES):
            cols = slice(q * LANES, (q + 1) * LANES)
            ds[:, cols] = (e_ref[begin + h, :, cols].astype(F32) * rb_ref[:, lanes] * d[:, cols]).astype(BF)
        for u in range(UNITS):
            at = pl.ds(multiple(where_ref[u] * rows, rows), rows)
            for to, first, many in slot(u):
                to[pl.ds(multiple(h * rows, rows), rows), :] = ds[at, first : first + many]
        return carry

    lax.fori_loop(0, count, one_head, 0)


def value_back(xh, rb, e, wv, tokens, size):
    length, model = tokens.shape
    heads = e.shape[0]
    width = heads * size
    chunk = length // 2
    krows = model // UNITS

    def kernel(xh_ref, rb_ref, e_ref, wv_ref, tok_ref, gv_ref, part_one, part_two, ga_ref, acc):
        acc[...] = jnp.zeros_like(acc)
        for h in range(heads):
            lanes = slice(h * LANES, (h + 1) * LANES)
            scaled = (xh_ref[:, lanes].astype(F32) * rb_ref[:, lanes]).astype(BF)
            gv_ref[:, h * size : (h + 1) * size] = mm(e_ref[h], scaled, TN)[:, :size].astype(BF)

        for r, part_ref in enumerate((part_one, part_two)):
            at = slice(r * chunk, (r + 1) * chunk)
            part = mm(gv_ref[at, :], wv_ref[...], NT)
            part_ref[...] = part.astype(BF)
            x = tok_ref[at, :].astype(F32)
            inv = lax.rsqrt(jnp.mean(x * x, axis=-1, keepdims=True) + EPSILON)
            acc[...] += jnp.sum((part * (x * inv)).reshape(chunk // 8, 8, model), axis=0)
        ga_ref[...] = cut_gain(jnp.sum(acc[...], axis=0, keepdims=True), krows)

    return run(
        kernel,
        "value_back",
        (),
        (xh, rb, e, wv, tokens),
        (
            ((length, width), BF),
            ((chunk, model), BF),
            ((chunk, model), BF),
            ((UNITS, LANES), F32),
        ),
        (pltpu.VMEM((8, model), F32),),
    )


def mixer_grads(where, xh, va, e, rb, krows):
    heads, length, _ = e.shape
    rows = length // UNITS
    deep = heads * rows + 2 * krows

    def kernel(where_ref, xh_ref, va_ref, e_ref, rb_ref, *rest):
        outs, ds = rest[:-1], rest[-1]
        score_grads(where_ref, xh_ref, va_ref, e_ref, rb_ref, ds, slots(outs), 0, heads, rows)
        for u in range(UNITS):
            for to, _, many in slots(outs)(u):
                to[heads * rows :, :] = jnp.zeros((2 * krows, many), BF)

    return run(
        kernel,
        "mixer_grads",
        (where,),
        (xh, va, e, rb),
        slot_shapes(deep, length),
        (pltpu.VMEM((length, length), BF),),
    )


def weight_grads(where, parts, n1, gv, gat, mixed, ga, ga_other, gf):
    model = n1.shape[1]
    width = gv.shape[1]
    krows = model // UNITS
    deep, length = parts[0].shape[1:]
    top = deep - 2 * krows

    def kernel(where_ref, n1_ref, gv_ref, gat_ref, mixed_ref, ga_ref, gb_ref, gf_ref, *rest):
        slot = slots(rest[SLOTS : 2 * SLOTS])
        wide_v, wide_o, pieces = rest[2 * SLOTS :]
        wide_v[:, :width] = mm(n1_ref[...], gv_ref[...], TN).astype(BF)
        wide_o[:, :width] = mm(gat_ref[...], mixed_ref[...], TN).astype(BF)
        wide_o[:, width:] = jnp.zeros((model, length - width), BF)
        pieces[0] = ga_ref[...] + gb_ref[...]
        pieces[1] = gf_ref[...]
        sub = lax.broadcasted_iota(jnp.int32, (krows, LANES), 0)
        for d in range(UNITS):
            both = jnp.where(
                sub == 0, pieces[0, d : d + 1, :], jnp.where(sub == 1, pieces[1, d : d + 1, :], 0.0)
            )
            wide_v[d * krows : (d + 1) * krows, width:] = both.astype(BF)
        for u in range(UNITS):
            at = pl.ds(multiple(where_ref[u] * krows, 16), krows)
            for to, first, many in slot(u):
                to[top : top + krows, :] = wide_v[at, first : first + many]
                to[top + krows :, :] = wide_o[at, first : first + many]

    return run(
        kernel,
        "weight_grads",
        (where,),
        (n1, gv, gat, mixed, ga, ga_other, gf, *parts),
        slot_shapes(deep, length),
        (
            pltpu.VMEM((model, length), BF),
            pltpu.VMEM((model, length), BF),
            pltpu.VMEM((2, UNITS, LANES), F32),
        ),
        aliases={8 + n: n for n in range(SLOTS)},
    )


class Ring:
    def __init__(self, size):
        self.size = size
        self.chips = size // 2
        n = self.chips
        self.order = list(range(0, n, 2)) + list(range(n - 1, 0, -2))
        me = lax.axis_index("dp")
        self.core = me % 2
        chip = me // 2
        self.at = jnp.where(chip % 2 == 0, chip // 2, n - 1 - chip // 2)
        self.up = self.pairs(1)
        self.down = self.pairs(-1)
        self.swap = [(d, d ^ 1) for d in range(size)]

    def pairs(self, step):
        n = self.chips
        return [
            (self.order[p] * 2 + c, self.order[(p + step) % n] * 2 + c) for p in range(n) for c in range(2)
        ]

    def device(self, offset, core):
        n = self.chips
        p = (self.at + jnp.asarray(offset, jnp.int32) + n) % n
        chip = jnp.where(p < (n + 1) // 2, 2 * p, 2 * (n - 1 - p) + 1)
        return chip * 2 + core

    def gathered(self):
        n = self.chips
        offsets = [0]
        for s in range(1, n // 2):
            offsets += [-s, s]
        offsets.append(n // 2)
        return jnp.concatenate([self.device(offsets, self.core), self.device(offsets, 1 - self.core)])

    def scattered(self):
        offsets = list(range(self.chips))
        return jnp.concatenate([self.device(offsets, self.core), self.device(offsets, 1 - self.core)])


class Gather:
    def __init__(self, ring, unit, cut):
        self.ring = ring
        self.rows = unit.shape[0]
        self.cut = cut
        self.last = [unit, unit]
        self.hops = 0
        self.mine = []
        self.theirs = []
        self.here = [unit]

    def values(self):
        return self.last

    def take(self, values):
        self.last = list(values)

    def hop(self):
        ring = self.ring
        self.hops += 1
        up, down = self.last
        if self.hops == ring.chips // 2:
            up, down = up[: self.cut], down[self.cut :]
        self.last = [lax.ppermute(up, "dp", ring.up), lax.ppermute(down, "dp", ring.down)]
        self.swap()
        self.here = self.last

    def swap(self):
        self.theirs += [lax.ppermute(one, "dp", self.ring.swap) for one in self.here]
        self.mine += self.here
        self.here = []

    def finish(self):
        self.swap()
        return self.mine + self.theirs

    def shares(self):
        n = self.ring.chips
        own = [(u, 0, self.rows) for u in range(n - 1)]
        own += [(n - 1, 0, self.cut), (n - 1, self.cut, self.rows - self.cut)]
        return own + [(u + n, first, rows) for u, first, rows in own]


class Scatter:
    def __init__(self, ring, keep, *give):
        self.ring = ring
        self.keep = keep
        early, self.later = give[:2], list(give[2:])
        self.early = [lax.ppermute(one, "dp", ring.swap) for one in early]
        self.last = []
        self.hops = 0

    def values(self):
        return self.last if self.hops else self.early

    def take(self, values):
        if self.hops:
            self.last = list(values)
        else:
            self.early = list(values)

    def total(self, k, one):
        group, place = late_place(k)
        got = self.later[group][place]
        return (self.keep[k].astype(F32) + got.astype(F32) + one.astype(F32)).astype(BF)

    def hop(self):
        ring = self.ring
        far = ring.chips // 2
        self.hops += 1
        if self.hops == 1:
            up, down = far_sum(far, self.keep, *self.early)
            self.later = [lax.ppermute(tie(one, up), "dp", ring.swap) for one in self.later]
        elif self.hops == 2:
            up, down = next_sums(far, self.keep, self.later[0], *self.last)
        else:
            up = self.total(far + 1 - self.hops, self.last[0])
            down = self.total(far - 1 + self.hops, self.last[1])
        self.last = [lax.ppermute(up, "dp", ring.up), lax.ppermute(down, "dp", ring.down)]

    def result(self):
        return self.keep, self.later[-1], *self.last


def together(chains, *more):
    values = [one for chain in chains for one in chain.values()]
    tied = lax.optimization_barrier(tuple(values) + more)
    at = 0
    for chain in chains:
        count = len(chain.values())
        chain.take(tied[at : at + count])
        at += count
    return tied[at:]


def tie(value, *after):
    return lax.optimization_barrier((value,) + after)[0] if after else value


def shards(
    tokens,
    segment_ids,
    gain_attn,
    gain_ffn,
    random_scores,
    w_value,
    w_output,
    w_up,
    w_down,
    cotangent,
):
    devices = lax.axis_size("dp")
    second = lax.axis_index("mp")
    length = segment_ids.shape[1]
    heads = random_scores.shape[0]
    model = tokens.shape[1]
    width = w_value.shape[1]
    size = width // heads
    rows = length // UNITS
    krows = model // UNITS
    ring = devices == UNITS and devices // 2 <= RING_CHIPS
    flip = [(0, 1), (1, 0)]
    second_at = jnp.reshape(second, (1,)).astype(jnp.int32)
    plan = Unit(heads, rows, krows, length, model, width, w_up.shape[1])

    if ring:
        net = Ring(devices)
        far = net.chips // 2
        where_in = net.gathered().astype(jnp.int32)
        where_out = net.scattered().astype(jnp.int32)
        wo_other = lax.ppermute(w_output.T, "mp", flip)
        unit = pack_unit(plan, random_scores, w_up, w_down.T)
        unit = pack_rest(plan, second_at, unit, w_value, gain_attn, gain_ffn, w_output.T, wo_other)
        one = Gather(net, unit, plan.cut)
        one.hop()
        where_in, where_out = together([one], where_in, where_out)
        for step in range(1, far - 1):
            one.hop()
            together([one])
        there = one.mine + one.theirs
        shares = one.shares()
        half = len(shares) // 2
        early = [n for n in range(len(one.mine))] + [half + n for n in range(len(one.theirs))]
        one.hop()
        e = mixer_first(plan, where_in, segment_ids, there, [shares[n] for n in early], heads)
        (e,) = together([one], e)
        units = one.finish()
        late = [n for n in range(len(shares)) if n not in early]
    else:
        where_in = jnp.arange(UNITS, dtype=jnp.int32)
        where_out = where_in

        def gather(one, axis=0):
            return lax.all_gather(one.astype(BF), "dp", axis=axis, tiled=True)

        wo_own = w_output.T.astype(BF)
        wo_other = lax.ppermute(wo_own, "mp", flip)
        halves = [jnp.where(second == n, wo_own, wo_other) for n in range(2)]
        scores = gather(random_scores, 1).reshape(heads, UNITS, rows, length).transpose(1, 0, 2, 3)
        wide = [gather(one) for one in (w_value, *halves)]
        wide = jnp.concatenate(wide, axis=1).reshape(UNITS, krows, plan.wide)
        ffn = jnp.concatenate([gather(w_up), gather(w_down.T)], axis=1).reshape(UNITS, krows, -1)
        stack = [scores.reshape(UNITS, heads * rows, length)]
        for kind, column in plan.blocks:
            stack.append((ffn if kind == "ffn" else wide)[:, :, column : column + length])
        gains = jnp.stack([gather(gain_attn), gather(gain_ffn)]).reshape(2, UNITS, krows).transpose(1, 0, 2)
        gains = jnp.pad(gains, ((0, 0), (0, plan.fold - 2), (0, length - plan.gain_lane - krows)))
        tail = wide[:, :, plan.wide - plan.tail :].reshape(UNITS, 3, plan.fold, plan.tail)
        stack.append(jnp.concatenate([tail[:, 0], tail[:, 1], tail[:, 2], gains], axis=2))
        whole = jnp.concatenate(stack, axis=1)
        units = [whole[u] for u in range(UNITS)]
        shares = [(u, 0, plan.deep) for u in range(UNITS)]
        early, late = list(range(UNITS // 2)), list(range(UNITS // 2, UNITS))
        e = mixer_first(plan, where_in, segment_ids, units[: UNITS // 2], shares[: UNITS // 2], heads)

    e, va, mixed, mixf, rb, n1, gains, wv = mixer_forward(
        plan, where_in, tokens, segment_ids, e, units, shares, late, heads, width
    )
    mixed_other = lax.ppermute(mixed, "mp", flip)
    w, gact = second_weights(plan, where_in, cotangent, units, shares)
    backs, others, resids, n2s, acts, gpres = [], [], [], [], [], []
    for part in range(PARTS):
        *new, resid, n2, act, gpre = ffn_main(
            second_at, tokens, mixed, mixed_other, gact, gains, w, part, PARTS, 1
        )
        for back in new:
            backs.append(back)
            others.append(lax.ppermute(tie(back, *others[-1:]), "mp", flip))
        resids.append(resid)
        n2s.append(n2)
        acts.append(act)
        gpres.append(gpre)
    parts_two = ffn_grads(where_out, n2s, gpres, acts, cotangent)
    ffn = list(ffn_out(acts, w))
    ffn_other = []
    if ring:
        ffn_sum = Scatter(net, *parts_two)
        ffn_sum.hop()
        ffn_sum.hop()
        cotangent, *both = lax.optimization_barrier((cotangent, *ffn, *others))
        ffn, others = both[:PARTS], both[PARTS:]
        ffn_other.append(lax.ppermute(ffn[0], "mp", flip))
    gres, gat, xh, gf = resid_back(
        second_at, backs, others, resids, cotangent, gains, w, mixf, heads, size
    )
    gv, part_one, part_two, ga = value_back(xh, rb, e, wv, tokens, size)
    ga_other = lax.ppermute(ga, "mp", flip)
    if ring:
        ffn_other[0], ffn[1] = together([ffn_sum], ffn_other[0], ffn[1])
        ffn_sum.hop()
        ffn_other.append(lax.ppermute(ffn[1], "mp", flip))
    parts_one = mixer_grads(where_out, xh, va, e, rb, krows)
    parts_one = weight_grads(where_out, parts_one, n1, gv, gat, mixed, ga, ga_other, gf)

    top = heads * rows
    if ring:
        score_sum = Scatter(net, *parts_one)
        ffn_other[1], part_one = together([ffn_sum, score_sum], ffn_other[1], part_one)
        ffn_sum.hop()
        score_sum.hop()
        part_other = [lax.ppermute(part_one, "mp", flip)]
        part_other[0], part_two = together([ffn_sum, score_sum], part_other[0], part_two)
        score_sum.hop()
        part_other.append(lax.ppermute(part_two, "mp", flip))
        together([score_sum])
        score_sum.hop()
        out_up, out_down = ffn_result(*ffn_sum.result())
        (part_other[1],) = together([score_sum], part_other[1])
        score_sum.hop()
        out_scores, out_value, out_output, *out_gains = mixer_result(*score_sum.result(), heads, krows, width)
        out_down, out_output = out_down.T, out_output.T
        out_gain_one, out_gain_two = [one.reshape(krows) for one in out_gains]
    else:
        ffn_other = [lax.ppermute(one, "mp", flip) for one in ffn]
        part_other = [lax.ppermute(one, "mp", flip) for one in (part_one, part_two)]

        def scatter(one, axis=0):
            return lax.psum_scatter(one, "dp", scatter_dimension=axis, tiled=True)

        def whole(keep, early, second, *later):
            far = UNITS // 4
            given = []
            for k in range(UNITS // 2):
                group, place = late_place(k) if k != far else (0, 0)
                one = later[group][place] if k != far else jnp.concatenate([early, second], axis=1)
                given.append(one)
            return jnp.concatenate([keep, jnp.stack(given)]).astype(F32)

        two = whole(*parts_two).reshape(model, -1)
        one = whole(*parts_one)
        out_up = scatter(two[:, : two.shape[1] // 2])
        out_down = scatter(two[:, two.shape[1] // 2 :]).T
        scores = one[:, :top].reshape(UNITS, heads, rows, length).transpose(1, 0, 2, 3)
        out_scores = scatter(scores.reshape(heads, length, length), 1)
        out_value = scatter(one[:, top : top + krows, :width].reshape(model, width))
        out_output = scatter(one[:, top + krows :, :width].reshape(model, width)).T
        out_gain_one = scatter(one[:, top, width : width + krows].reshape(model))
        out_gain_two = scatter(one[:, top + 1, width : width + krows].reshape(model))
    outputs = [
        (resid + (mine.astype(F32) + other.astype(F32))).astype(BF)
        for resid, mine, other in zip(resids, ffn, ffn_other)
    ]
    output = jnp.concatenate(outputs)
    backs = []
    for r, (mine, other) in enumerate(zip((part_one, part_two), part_other)):
        grad_n1 = mine.astype(F32) + other.astype(F32)
        at = slice(r * mine.shape[0], (r + 1) * mine.shape[0])
        x = tokens[at].astype(F32)
        inv = lax.rsqrt(jnp.mean(x * x, axis=-1, keepdims=True) + EPSILON)
        z = gains[0:1, :] * grad_n1
        hat = x * inv
        backs.append((gres[at] + inv * (z - hat * jnp.mean(z * hat, axis=-1, keepdims=True))).astype(BF))
    grad_tokens = jnp.concatenate(backs)
    return (
        output,
        grad_tokens,
        out_gain_one,
        out_gain_two,
        out_scores,
        out_value,
        out_output,
        out_up,
        out_down,
    )


def solution(mesh):
    in_specs = (
        P("dp", None),
        P("dp", None),
        P("dp"),
        P("dp"),
        P("mp", "dp", None),
        P("dp", "mp"),
        P("mp", "dp"),
        P("dp", "mp"),
        P("mp", "dp"),
        P("dp", None),
    )
    out_specs = (
        P("dp", None),
        P("dp", None),
        P("dp"),
        P("dp"),
        P("mp", "dp", None),
        P("dp", "mp"),
        P("mp", "dp"),
        P("dp", "mp"),
        P("mp", "dp"),
    )
    return jax.shard_map(shards, mesh=mesh, in_specs=in_specs, out_specs=out_specs, check_vma=False)
```

```python
import jax
import jax.numpy as jnp
from jax import lax
from jax.experimental import pallas as pl
from jax.experimental.pallas import tpu as pltpu
from jax.sharding import PartitionSpec as P

EPSILON = 1e-06
NEGATIVE = -1e30
BF = jnp.bfloat16
F32 = jnp.float32
UNITS = 16
LANES = 128
PARTS = 2
RING_CHIPS = 8
VMEM_BYTES = 20 * 1024 * 1024
NT = (((1,), (1,)), ((), ()))
TN = (((0,), (0,)), ((), ()))
NN = (((1,), (0,)), ((), ()))


def mm(a, b, dims=NN):
    return lax.dot_general(a, b, dims, preferred_element_type=F32)


def run(kernel, name, scalars, arrays, outs, scratch=(), loose=(), loose_outs=(), aliases=None, near=0):
    held = [pltpu.with_memory_space_constraint(one, pltpu.VMEM) for one in arrays]
    results = [pltpu.VMEM(*one) for one in outs] + [jax.ShapeDtypeStruct(*one) for one in loose_outs]
    specs = [pl.BlockSpec(memory_space=pltpu.SMEM)] * len(scalars)
    specs += [pl.BlockSpec(memory_space=pltpu.VMEM)] * len(arrays)
    far = len(loose) - near
    specs += [pl.BlockSpec(memory_space=pltpu.HBM)] * far + [pl.BlockSpec(memory_space=pl.ANY)] * near
    loose = [pltpu.with_memory_space_constraint(one, pltpu.HBM) for one in loose[:far]] + list(loose[far:])
    out_specs = [pl.BlockSpec(memory_space=pltpu.VMEM)] * len(outs)
    out_specs += [pl.BlockSpec(memory_space=pl.ANY)] * len(loose_outs)
    return pl.pallas_call(
        kernel,
        out_shape=tuple(results),
        in_specs=specs,
        out_specs=tuple(out_specs),
        scratch_shapes=list(scratch),
        compiler_params=pltpu.CompilerParams(vmem_limit_bytes=VMEM_BYTES),
        cost_estimate=pl.CostEstimate(flops=1, bytes_accessed=1, transcendentals=0),
        input_output_aliases=aliases or {},
        name=name,
    )(*scalars, *held, *loose)


def gelu_pair(x):
    c = 0.7978845608028654
    a = 0.044715
    square = x * x
    t = jnp.tanh(c * x * (1.0 + a * square))
    half = 0.5 * (1.0 + t)
    return x * half, half + 0.5 * x * (1.0 - t * t) * (c * (1.0 + 3.0 * a * square))


def multiple(value, of):
    return pl.multiple_of(value, of)


class Unit:
    def __init__(self, heads, rows, krows, length, model, width, hidden):
        self.scores = heads * rows
        self.krows = krows
        self.length = length
        self.width = width
        self.hidden = hidden
        self.wide = width + model
        self.blocks = [("ffn", n * length) for n in range(2 * hidden // length)]
        self.blocks += [("proj", n * length) for n in range(self.wide // length)]
        self.tail = self.wide % length
        self.last = self.scores + krows * len(self.blocks)
        self.fold = krows // 3
        self.deep = self.last + self.fold
        self.cut = self.scores + krows * (2 * hidden // length // 3)
        self.gain_lane = 3 * self.tail

    def ffn_parts(self):
        parts = []
        for n, (kind, first) in enumerate(self.blocks):
            at = self.scores + n * self.krows
            if kind == "ffn":
                parts.append((at, 0, 0, first, self.krows, self.length))
            else:
                skip = max(self.width - first, 0)
                column = 2 * self.hidden + first + skip - self.width
                parts.append((at, skip, 0, column, self.krows, self.length - skip))
        for n in range(3):
            column = 2 * self.hidden + self.wide - self.tail - self.width
            parts.append((self.last, n * self.tail, n * self.fold, column, self.fold, self.tail))
        return parts

    def value_row(self):
        return self.scores + [kind for kind, _ in self.blocks].index("proj") * self.krows


def other_parts(plan, first):
    begin = plan.width + first * plan.width
    parts = []
    for n, (kind, column) in enumerate(plan.blocks):
        low, high = max(begin, column), min(begin + plan.width, column + plan.length)
        if kind == "proj" and low < high:
            parts.append((plan.scores + n * plan.krows, low - column, 0, low - begin, plan.krows, high - low))
    low = max(begin, plan.wide - plan.tail)
    if low < begin + plan.width:
        for n in range(3):
            lanes = n * plan.tail + low - (plan.wide - plan.tail)
            parts.append((plan.last, lanes, n * plan.fold, low - begin, plan.fold, begin + plan.width - low))
    return parts


def put_half(plan, out, half_ref, first):
    for row, lane, at, column, rows, lanes in other_parts(plan, first):
        out[row : row + rows, lane : lane + lanes] = half_ref[at : at + rows, column : column + lanes]


def pack_unit(plan, second, scores, wv, gain_one, gain_two, w_up, w_down, wo):
    inputs = (scores, wv, gain_one.reshape(1, -1), gain_two.reshape(1, -1), w_up, w_down, wo)
    count = len(inputs)
    krows, length, width = plan.krows, plan.length, plan.width
    per = plan.hidden // length
    assert plan.tail <= width

    def kernel(second_ref, *rest):
        out, wo_out, gains = rest[count : count + 3]
        held, sem = rest[count + 3 : -1], rest[-1]
        fetch(rest[:count], held, sem)
        s_ref, wv_ref, ga_ref, gf_ref, up_ref, down_ref, own_ref = held
        out[: plan.scores, :] = s_ref[...].reshape(plan.scores, length).astype(BF)
        for n, (kind, column) in enumerate(plan.blocks):
            at = slice(plan.scores + n * krows, plan.scores + (n + 1) * krows)
            if kind == "ffn":
                ref, first = (up_ref, column) if n < per else (down_ref, column - plan.hidden)
                out[at, :] = ref[:, first : first + length].astype(BF)
            else:
                out[at, :] = jnp.zeros((krows, length), BF)
        out[plan.last :, : plan.gain_lane] = jnp.zeros((plan.fold, plan.gain_lane), BF)
        out[plan.value_row() : plan.value_row() + krows, :width] = wv_ref[...].astype(BF)
        wo_out[...] = own_ref[...].astype(BF)
        for place in range(2):

            @pl.when(second_ref[0] == place)
            def _():
                put_half(plan, out, wo_out, place)

        gains[...] = jnp.zeros_like(gains)
        gains[0:1, :krows] = ga_ref[...]
        gains[1:2, :krows] = gf_ref[...]
        out[plan.last :, plan.gain_lane :] = gains[...].astype(BF)

    return run(
        kernel,
        "pack_unit",
        (second,),
        (),
        (((plan.deep, length), BF), ((krows, width), BF)),
        (
            pltpu.VMEM((plan.fold, length - plan.gain_lane), F32),
            *[pltpu.VMEM(one.shape, one.dtype) for one in inputs],
            pltpu.SemaphoreType.DMA((count,)),
        ),
        loose=inputs,
    )


def fill_units(plan, second, units, others):
    count = len(units)

    def kernel(second_ref, *rest):
        for place in range(2):

            @pl.when(second_ref[0] == 1 - place)
            def _():
                for n in range(count):
                    put_half(plan, rest[2 * count + n], rest[count + n], place)

    return run(
        kernel,
        "fill_units",
        (second,),
        (*units, *others),
        [(one.shape, BF) for one in units],
        aliases={1 + n: n for n in range(count)},
    )


def fetch(refs, held, sem):
    copies = [pltpu.make_async_copy(ref, to, sem.at[n]) for n, (ref, to) in enumerate(zip(refs, held))]
    for copy in copies:
        copy.start()
    for copy in copies:
        copy.wait()


def pick(units, shares, where_ref, parts, target, sem):
    copies = []
    for n, (u, first, rows) in enumerate(shares):
        owner = where_ref[u]
        for m, part in enumerate(parts):
            row, column, count, columns = part[0], part[1], part[-2], part[-1]
            if first <= row and row + count <= first + rows:
                source = units[n].at[pl.ds(row - first, count), pl.ds(column, columns)]
                copies.append(pltpu.make_async_copy(source, target(m, owner), sem.at[u, m]))
                copies[-1].start()
    return copies


def mixer_rows(plan, units, shares, where_ref, seg_ref, e_ref, unit, same, sem):
    heads, length, _ = e_ref.shape
    rows = length // UNITS
    top = heads * rows
    mine = [n for n, (_, first, _) in enumerate(shares) if first == 0]

    def target(m, owner):
        return unit.at[pl.ds(multiple(owner * top, top), top), :]

    copies = pick([units[n] for n in mine], [shares[n] for n in mine], where_ref, [(0, 0, top, length)], target, sem)

    def write():
        documents = (seg_ref[...] == lax.broadcasted_iota(jnp.int32, (LANES, length), 0)).astype(BF)
        same[...] = mm(documents, documents, TN)
        for copy in copies:
            copy.wait()

        def one_head(h, carry):
            for n in mine:
                owner = where_ref[shares[n][0]]
                at = pl.ds(multiple(owner * rows, rows), rows)
                s = unit[pl.ds(multiple(owner * top + h * rows, rows), rows), :].astype(F32)
                e_ref[h, at, :] = (jnp.exp(s) * same[at, :]).astype(BF)
            return carry

        lax.fori_loop(0, heads, one_head, 0)

    return write


def low_parts(plan):
    return [
        (plan.value_row(), 0, plan.krows, plan.width),
        (plan.last, plan.gain_lane, plan.fold, LANES),
    ]


def bring_low(plan, units, shares, where_ref, wv_ref, low_ref, sem):
    krows = plan.krows

    def target(m, owner):
        if m == 0:
            return wv_ref.at[pl.ds(multiple(owner * krows, 16), krows), :]
        return low_ref.at[owner]

    return pick(units, shares, where_ref, low_parts(plan), target, sem)


def mixer_first(plan, where, tokens, segments, units, shares, heads):
    length, model = tokens.shape
    rows = length // UNITS

    def kernel(where_ref, tok_ref, seg_ref, *rest):
        e_ref, wv_ref, low_ref, hat_ref, unit, same, sem, more = rest[len(units) :]
        write = mixer_rows(plan, rest[: len(units)], shares, where_ref, seg_ref, e_ref, unit, same, sem)
        copies = bring_low(plan, rest[: len(units)], shares, where_ref, wv_ref, low_ref, more)
        x = tok_ref[...].astype(F32)
        hat_ref[...] = x * lax.rsqrt(jnp.mean(x * x, axis=-1, keepdims=True) + EPSILON)
        write()
        for copy in copies:
            copy.wait()

    return run(
        kernel,
        "mixer_first",
        (where,),
        (tokens, segments),
        (
            ((heads, length, length), BF),
            ((model, plan.width), BF),
            ((UNITS, plan.fold, LANES), BF),
            ((length, model), F32),
        ),
        (
            pltpu.VMEM((heads * length, length), BF),
            pltpu.VMEM((length, length), F32),
            pltpu.SemaphoreType.DMA((UNITS, 1)),
            pltpu.SemaphoreType.DMA((UNITS, 2)),
        ),
        loose=units,
    )


def mixer_forward(plan, where, segments, early, units, shares, heads, width):
    length, model = early[3].shape
    size = width // heads
    krows = model // UNITS
    wide = heads * LANES
    count = len(units)

    def kernel(where_ref, seg_ref, e_old, wv_old, low_old, hat_ref, *rest):
        e_ref, wv_ref, low, va_ref, mixed_ref, sums_ref, n1_ref, gains_ref, pieces, unit, same, sem, more = rest[count:]
        copies = bring_low(plan, rest[:count], shares, where_ref, wv_ref, low, sem)
        write = mixer_rows(plan, rest[:count], shares, where_ref, seg_ref, e_ref, unit, same, more)
        for copy in copies:
            copy.wait()
        for d in range(UNITS):
            some = low[d].astype(F32)
            pieces[0, d : d + 1, :] = some[0:1, :]
            pieces[1, d : d + 1, :] = some[1:2, :]
        spread = (
            lax.broadcasted_iota(jnp.int32, (LANES, model), 1) % krows
            == lax.broadcasted_iota(jnp.int32, (LANES, model), 0)
        ).astype(BF)
        own = (
            lax.broadcasted_iota(jnp.int32, (UNITS, model), 1) // krows
            == lax.broadcasted_iota(jnp.int32, (UNITS, model), 0)
        )
        gains = []
        for t in range(2):
            full = jnp.where(own, mm(pieces[t].astype(BF), spread), 0.0)
            gains.append(jnp.sum(full, axis=0, keepdims=True))
            gains_ref[t : t + 1, :] = gains[t]
        n1_ref[...] = (hat_ref[...] * gains[0]).astype(BF)
        values = mm(n1_ref[...], wv_ref[...]).astype(BF)
        tail = (lax.broadcasted_iota(jnp.int32, (length, LANES - size), 1) < 2).astype(BF)
        for h in range(heads):
            va_ref[:, h * LANES : h * LANES + size] = values[:, h * size : (h + 1) * size]
            va_ref[:, h * LANES + size : (h + 1) * LANES] = tail

        write()
        for h in range(heads):
            lanes = slice(h * LANES, (h + 1) * LANES)
            sums = mm(e_ref[h], va_ref[:, lanes])
            sums_ref[:, lanes] = sums
            mixed_ref[:, h * size : (h + 1) * size] = (sums * (1.0 / sums[:, size : size + 1]))[:, :size].astype(BF)

    return run(
        kernel,
        "mixer_forward",
        (where,),
        (segments, *early),
        (
            ((heads, length, length), BF),
            ((model, width), BF),
            ((UNITS, plan.fold, LANES), BF),
            ((length, wide), BF),
            ((length, width), BF),
            ((length, wide), F32),
            ((length, model), BF),
            ((2, model), F32),
        ),
        (
            pltpu.VMEM((2, UNITS, LANES), F32),
            pltpu.VMEM((heads * length, length), BF),
            pltpu.VMEM((length, length), F32),
            pltpu.SemaphoreType.DMA((UNITS, 2)),
            pltpu.SemaphoreType.DMA((UNITS, 1)),
        ),
        loose=units,
        aliases={2: 0, 3: 1, 4: 2},
        near=len(units),
    )


def second_weights(plan, where, cotangent, sums, units, shares, near, size):
    length, model = cotangent.shape
    hidden, krows = plan.hidden, plan.krows
    piece = hidden // 3
    parts = plan.ffn_parts()

    def kernel(where_ref, cot_ref, sums_ref, *rest):
        out, gact, mixf_ref, rb_ref, sem = rest[len(units) :]

        def target(m, owner):
            _, _, row, column, rows, columns = parts[m]
            return out.at[pl.ds(multiple(owner * krows + row, 16), rows), pl.ds(column, columns)]

        copies = pick(rest[: len(units)], shares, where_ref, parts, target, sem)
        inside = lax.broadcasted_iota(jnp.int32, (length, LANES), 1) < size
        for h in range(sums.shape[1] // LANES):
            lanes = slice(h * LANES, (h + 1) * LANES)
            inverse = jnp.broadcast_to(1.0 / sums_ref[:, h * LANES + size : h * LANES + size + 1], (length, LANES))
            rb_ref[:, lanes] = inverse
            mixf_ref[:, lanes] = jnp.where(inside, sums_ref[:, lanes] * inverse, 0.0)
        for copy in copies:
            copy.wait()
        for j in range(3):
            cols = slice(j * piece, (j + 1) * piece)
            gact[:, cols] = mm(cot_ref[...], out[:, hidden + j * piece : hidden + (j + 1) * piece])

    return run(
        kernel,
        "second_weights",
        (where,),
        (cotangent, sums),
        (((model, 2 * hidden + model), BF), ((length, hidden), F32), (sums.shape, F32), (sums.shape, F32)),
        (pltpu.SemaphoreType.DMA((UNITS, len(parts))),),
        loose=units,
        near=near,
    )


def ffn_main(second, tokens, mixed_own, mixed_other, gact, gains, w, part, parts, pieces):
    length, model = tokens.shape
    width = mixed_own.shape[1]
    hidden = gact.shape[1]
    chunk = length // parts
    piece = hidden // 3
    at = slice(part * chunk, (part + 1) * chunk)

    def kernel(second_ref, tok_ref, own_ref, other_ref, gact_ref, gains_ref, w_ref,
               *rest):
        backs = rest[:pieces]
        resid_ref, n2_ref, act_ref, gpre_ref, mixed, acc = rest[pieces:]
        first = second_ref[0]
        mixed[:, pl.ds(multiple(first * width, LANES), width)] = own_ref[at, :]
        mixed[:, pl.ds(multiple((1 - first) * width, LANES), width)] = other_ref[at, :]
        attn = mm(mixed[...], w_ref[:, 2 * hidden :], NT)
        resid = tok_ref[at, :].astype(F32) + attn
        resid_ref[...] = resid
        inv = lax.rsqrt(jnp.mean(resid * resid, axis=-1, keepdims=True) + EPSILON)
        n2_ref[...] = (resid * inv * gains_ref[1:2, :]).astype(BF)
        for j in range(hidden // piece):
            cols = slice(j * piece, (j + 1) * piece)
            act, slope = gelu_pair(mm(n2_ref[...], w_ref[:, cols]))
            act_ref[:, cols] = act.astype(BF)
            gpre_ref[:, cols] = (gact_ref[at, cols] * slope).astype(BF)
            term = mm(gpre_ref[:, cols], w_ref[:, cols], NT)
            if j == 0:
                acc[...] = term
            else:
                acc[...] += term
        for n, back_ref in enumerate(backs):
            back_ref[...] = acc[n * (chunk // pieces) : (n + 1) * (chunk // pieces), :].astype(BF)

    return run(
        kernel,
        "ffn_main",
        (second,),
        (tokens, mixed_own, mixed_other, gact, gains, w),
        (
            *[((chunk // pieces, model), BF)] * pieces,
            ((chunk, model), F32),
            ((chunk, model), BF),
            ((chunk, hidden), BF),
            ((chunk, hidden), BF),
        ),
        (
            pltpu.VMEM((chunk, 2 * width), BF),
            pltpu.VMEM((chunk, model), F32),
        ),
    )


def late_units(first):
    return [k for k in range(UNITS // 2) if k not in first]


def slots(refs, first, pieces):
    half = UNITS // 2
    count = len(first) * pieces
    keep, early, later = refs[0], refs[1 : 1 + count], refs[1 + count :]
    late = late_units(first)

    def slot(u):
        if u < half:
            return [keep.at[u]]
        k = u - half
        if k in first:
            at = first.index(k) * pieces
            return early[at : at + pieces]
        n = late.index(k)
        return [later[0].at[n] if len(later) == 1 else later[n]]

    return slot


def slot_shapes(rows, columns, first, pieces, apart):
    half = UNITS // 2
    cuts = [(rows, columns)] if pieces == 1 else [(rows - SMALL, columns), (SMALL, columns)]
    early = [(cut, BF) for _ in first for cut in cuts]
    count = half - len(first)
    later = [((rows, columns), BF)] * count if apart else [((count, rows, columns), BF)]
    return [((half, rows, columns), BF), *early, *later]


SMALL = 16
FFN_FIRST = [UNITS // 4, UNITS // 4 - 1]
MIXER_FIRST = [UNITS // 4]


def pieces_sum(k, keep, pieces):
    _, rows, columns = keep.shape

    def kernel(keep_ref, *refs):
        begin = 0
        for one in refs[:-1]:
            at = slice(begin, begin + one.shape[0])
            begin = at.stop
            refs[-1][at, :] = (keep_ref[k, at, :].astype(F32) + one[...].astype(F32)).astype(BF)

    return run(kernel, "pieces_sum", (), (keep, *pieces), [((rows, columns), BF)])[0]


def result_kernel(name, keep, own, up, down, shapes, cut):
    def kernel(keep_ref, own_ref, up_ref, down_ref, *rest):
        outs, held, sem = rest[: len(shapes)], rest[len(shapes) : -1], rest[-1]

        def total(rows, columns):
            value = keep_ref[0, rows, columns].astype(F32) + own_ref[rows, columns].astype(F32)
            return value + up_ref[rows, columns].astype(F32) + down_ref[rows, columns].astype(F32)

        copies = []
        for n, (out, to) in enumerate(zip(outs, held)):
            cut(n, to, total)
            copies.append(pltpu.make_async_copy(to, out, sem.at[n]))
            copies[-1].start()
        for copy in copies:
            copy.wait()

    return run(
        kernel,
        name,
        (),
        (keep, own, up, down),
        (),
        (*[pltpu.VMEM(shape, F32) for shape in shapes], pltpu.SemaphoreType.DMA((len(shapes),))),
        loose_outs=[(shape, F32) for shape in shapes],
    )


def ffn_result(keep, own, up, down):
    _, rows, columns = keep.shape
    half = columns // 2

    def cut(n, to, total):
        to[...] = total(slice(None), slice(n * half, (n + 1) * half))

    return result_kernel("ffn_result", keep, own, up, down, [(rows, half)] * 2, cut)


def mixer_result(keep, own, up, down, heads, krows, width):
    _, deep, length = keep.shape
    top = deep - 2 * krows
    rows = top // heads
    shapes = [(heads, rows, length), (krows, width), (krows, width), (1, krows), (1, krows)]

    def cut(n, to, total):
        if n == 0:
            for h in range(heads):
                to[h] = total(slice(h * rows, (h + 1) * rows), slice(None))
        elif n < 3:
            to[...] = total(slice(top + (n - 1) * krows, top + n * krows), slice(0, width))
        else:
            to[...] = total(slice(top, top + 16), slice(width, length))[n - 3 : n - 2, :krows]

    return result_kernel("mixer_result", keep, own, up, down, shapes, cut)


def ffn_grads(where, n2s, gpres, acts, cotangent, w):
    parts = len(n2s)
    chunk, model = n2s[0].shape
    hidden = acts[0].shape[1]
    krows = model // UNITS

    def kernel(where_ref, cot_ref, w_ref, *rest):
        n2, gpre, act = rest[:parts], rest[parts : 2 * parts], rest[2 * parts : 3 * parts]
        out_ref = rest[3 * parts]
        slot = slots(rest[3 * parts + 1 : -2], FFN_FIRST, 1)
        scr, sem = rest[-2:]
        piece = hidden // 3
        for j in range(3):
            cols = slice(j * piece, (j + 1) * piece)
            down = slice(hidden + j * piece, hidden + (j + 1) * piece)
            one = [mm(n2[r][...], gpre[r][:, cols], TN) for r in range(parts)]
            scr[:, cols] = sum(one).astype(BF)
            two = [mm(cot_ref[r * chunk : (r + 1) * chunk, :], act[r][:, cols], TN) for r in range(parts)]
            scr[:, down] = sum(two).astype(BF)
        copies = []
        for u in range(UNITS):
            at = pl.ds(multiple(where_ref[u] * krows, 16), krows)
            (to,) = slot(u)
            copies.append(pltpu.make_async_copy(scr.at[at, :], to, sem.at[u]))
            copies[-1].start()
        for r in range(parts):
            out_ref[r * chunk : (r + 1) * chunk, :] = mm(act[r][...], w_ref[:, hidden : 2 * hidden], NT).astype(BF)
        for copy in copies:
            copy.wait()

    return run(
        kernel,
        "ffn_grads",
        (where,),
        (cotangent, w, *n2s, *gpres, *acts),
        (((chunk * parts, model), BF),),
        (pltpu.VMEM((model, 2 * hidden), BF), pltpu.SemaphoreType.DMA((UNITS,))),
        loose_outs=slot_shapes(krows, 2 * hidden, FFN_FIRST, 1, False),
    )


def cut_gain(row, krows):
    model = row.shape[1]
    take = (
        lax.broadcasted_iota(jnp.int32, (model, LANES), 0) % krows
        == lax.broadcasted_iota(jnp.int32, (model, LANES), 1)
    ).astype(BF)
    own = (
        lax.broadcasted_iota(jnp.int32, (UNITS, model), 1) // krows
        == lax.broadcasted_iota(jnp.int32, (UNITS, model), 0)
    )
    high = row.astype(BF).astype(F32)
    pieces = mm(jnp.where(own, high, 0.0).astype(BF), take)
    return pieces + mm(jnp.where(own, row - high, 0.0).astype(BF), take)


def resid_back(second, backs, others, resids, cotangent, gains, w, mixf, heads, size):
    length, model = cotangent.shape
    wide = heads * LANES
    count = len(backs)
    krows = model // UNITS
    parts = len(resids)

    hidden = w.shape[1] - 2 * heads * size

    def kernel(second_ref, cot_ref, gains_ref, w_ref, mixf_ref, *rest):
        mine, other, res_refs = rest[:count], rest[count : 2 * count], rest[2 * count : 2 * count + parts]
        gres_ref, gat_ref, xh_ref, gf_ref, gm = rest[2 * count + parts :]
        total = jnp.zeros((8, model), F32)
        begin = 0
        for r in range(count):
            chunk = mine[r].shape[0]
            at = slice(begin, begin + chunk)
            g2 = mine[r][...].astype(F32) + other[r][...].astype(F32)
            whole = length // parts
            res = res_refs[begin // whole][begin % whole : begin % whole + chunk, :]
            begin += chunk
            inv = lax.rsqrt(jnp.mean(res * res, axis=-1, keepdims=True) + EPSILON)
            hat = res * inv
            total = total + jnp.sum((g2 * hat).reshape(chunk // 8, 8, model), axis=0)
            z = gains_ref[1:2, :] * g2
            corr = jnp.mean(z * hat, axis=-1, keepdims=True)
            gres = cot_ref[at, :].astype(F32) + inv * (z - hat * corr)
            gres_ref[at, :] = gres
            gat_ref[at, :] = gres.astype(BF)
        own = pl.ds(multiple(hidden + second_ref[0] * heads * size, LANES), heads * size)
        compact = mm(gat_ref[...], w_ref[:, own]).astype(BF)
        gm[...] = jnp.zeros_like(gm)
        for h in range(heads):
            gm[:, h * LANES : h * LANES + size] = compact[:, h * size : (h + 1) * size]
        lane = lax.broadcasted_iota(jnp.int32, (length, LANES), 1)
        for h in range(heads):
            lanes = slice(h * LANES, (h + 1) * LANES)
            here = gm[:, lanes].astype(F32)
            inner = -jnp.sum(here * mixf_ref[:, lanes], axis=-1, keepdims=True)
            high = inner.astype(BF).astype(F32)
            xh_ref[:, lanes] = jnp.where(
                lane == size, high, jnp.where(lane == size + 1, inner - high, here)
            ).astype(BF)
        gf_ref[...] = cut_gain(jnp.sum(total, axis=0, keepdims=True), krows)

    return run(
        kernel,
        "resid_back",
        (second,),
        (cotangent, gains, w, mixf, *backs, *others, *resids),
        (
            ((length, model), F32),
            ((length, model), BF),
            ((length, wide), BF),
            ((UNITS, LANES), F32),
        ),
        (pltpu.VMEM((length, wide), BF),),
    )


def score_grads(where_ref, xh_ref, va_ref, e_ref, rb_ref, ds, slot, begin, count, rows):
    length = ds.shape[0]

    def one_head(h, carry):
        lanes = pl.ds(multiple((begin + h) * LANES, LANES), LANES)
        d = mm(xh_ref[:, lanes], va_ref[:, lanes], NT)
        inverse = rb_ref[:, lanes]
        for q in range(length // LANES):
            cols = slice(q * LANES, (q + 1) * LANES)
            ds[:, cols] = (e_ref[begin + h, :, cols].astype(F32) * inverse * d[:, cols]).astype(BF)
        for u in range(UNITS):
            at = pl.ds(multiple(where_ref[u] * rows, rows), rows)
            slot(u)[0][pl.ds(multiple(h * rows, rows), rows), :] = ds[at, :]
        return carry

    lax.fori_loop(0, count, one_head, 0)


def value_back(xh, rb, e, wv, tokens, size, cut):
    length, model = tokens.shape
    heads = e.shape[0]
    width = heads * size
    krows = model // UNITS

    def kernel(xh_ref, rb_ref, e_ref, wv_ref, tok_ref, gv_ref, part_one, part_two, ga_ref, acc):
        acc[...] = jnp.zeros_like(acc)
        for h in range(heads):
            lanes = slice(h * LANES, (h + 1) * LANES)
            scaled = (xh_ref[:, lanes].astype(F32) * rb_ref[:, lanes]).astype(BF)
            gv_ref[:, h * size : (h + 1) * size] = mm(e_ref[h], scaled, TN)[:, :size].astype(BF)

        for at, part_ref in ((slice(0, cut), part_one), (slice(cut, length), part_two)):
            part = mm(gv_ref[at, :], wv_ref[...], NT)
            part_ref[...] = part.astype(BF)
            x = tok_ref[at, :].astype(F32)
            inv = lax.rsqrt(jnp.mean(x * x, axis=-1, keepdims=True) + EPSILON)
            acc[...] += jnp.sum((part * (x * inv)).reshape((at.stop - at.start) // 8, 8, model), axis=0)

        ga_ref[...] = jnp.zeros_like(ga_ref)
        ga_ref[:UNITS, :] = cut_gain(jnp.sum(acc[...], axis=0, keepdims=True), krows)

    return run(
        kernel,
        "value_back",
        (),
        (xh, rb, e, wv, tokens),
        (
            ((length, width), BF),
            ((cut, model), BF),
            ((length - cut, model), BF),
            ((4 * UNITS, LANES), F32),
        ),
        (pltpu.VMEM((8, model), F32),),
    )


def mixer_grads(where, xh, va, e, rb, krows):
    heads, length, _ = e.shape
    rows = length // UNITS
    deep = heads * rows + 2 * krows

    def kernel(where_ref, xh_ref, va_ref, e_ref, rb_ref, *rest):
        outs, ds = rest[:-1], rest[-1]
        score_grads(where_ref, xh_ref, va_ref, e_ref, rb_ref, ds, slots(outs, MIXER_FIRST, 2), 0, heads, rows)
        for u in range(UNITS):
            for n, to in enumerate(slots(outs, MIXER_FIRST, 2)(u)):
                begin = 0 if n else heads * rows
                to[begin:, :] = jnp.zeros((to.shape[0] - begin, length), BF)

    return run(
        kernel,
        "mixer_grads",
        (where,),
        (xh, va, e, rb),
        slot_shapes(deep, length, MIXER_FIRST, 2, False),
        (pltpu.VMEM((length, length), BF),),
    )


def weight_grads(where, parts, n1, gv, gat, mixed, ga, ga_other, gf):
    model = n1.shape[1]
    width = gv.shape[1]
    krows = model // UNITS
    deep, length = parts[0].shape[1:]
    top = deep - 2 * krows

    def kernel(where_ref, n1_ref, gv_ref, gat_ref, mixed_ref, ga_ref, gb_ref, gf_ref, *rest):
        slot = slots(rest[len(parts) : 2 * len(parts)], MIXER_FIRST, 2)
        wide_v, wide_o, pieces = rest[2 * len(parts) :]
        wide_v[:, :width] = mm(n1_ref[...], gv_ref[...], TN).astype(BF)
        wide_o[:, :width] = mm(gat_ref[...], mixed_ref[...], TN).astype(BF)
        wide_o[:, width:] = jnp.zeros((model, length - width), BF)
        pieces[0] = ga_ref[:UNITS, :] + gb_ref[:UNITS, :]
        pieces[1] = gf_ref[...]
        sub = lax.broadcasted_iota(jnp.int32, (krows, LANES), 0)
        for d in range(UNITS):
            both = jnp.where(
                sub == 0, pieces[0, d : d + 1, :], jnp.where(sub == 1, pieces[1, d : d + 1, :], 0.0)
            )
            wide_v[d * krows : (d + 1) * krows, width:] = both.astype(BF)
        for u in range(UNITS):
            at = pl.ds(multiple(where_ref[u] * krows, 16), krows)
            to, *small = slot(u)
            to[top : top + krows, :] = wide_v[at, :]
            if small:
                to[top + krows :, :] = wide_o[pl.ds(multiple(where_ref[u] * krows, 16), krows - SMALL), :]
                small[0][...] = wide_o[pl.ds(multiple(where_ref[u] * krows + krows - SMALL, 16), SMALL), :]
            else:
                to[top + krows :, :] = wide_o[at, :]

    return run(
        kernel,
        "weight_grads",
        (where,),
        (n1, gv, gat, mixed, ga, ga_other, gf, *parts),
        slot_shapes(deep, length, MIXER_FIRST, 2, False),
        (
            pltpu.VMEM((model, length), BF),
            pltpu.VMEM((model, length), BF),
            pltpu.VMEM((2, UNITS, LANES), F32),
        ),
        aliases={8 + n: n for n in range(len(parts))},
    )


class Ring:
    def __init__(self, size):
        self.size = size
        self.chips = size // 2
        n = self.chips
        self.order = list(range(0, n, 2)) + list(range(n - 1, 0, -2))
        me = lax.axis_index("dp")
        self.core = me % 2
        chip = me // 2
        self.at = jnp.where(chip % 2 == 0, chip // 2, n - 1 - chip // 2)
        self.up = self.pairs(1)
        self.down = self.pairs(-1)
        self.swap = [(d, d ^ 1) for d in range(size)]

    def pairs(self, step):
        n = self.chips
        return [
            (self.order[p] * 2 + c, self.order[(p + step) % n] * 2 + c) for p in range(n) for c in range(2)
        ]

    def device(self, offset, core):
        n = self.chips
        p = (self.at + jnp.asarray(offset, jnp.int32) + n) % n
        chip = jnp.where(p < (n + 1) // 2, 2 * p, 2 * (n - 1 - p) + 1)
        return chip * 2 + core

    def gathered(self):
        n = self.chips
        offsets = [0]
        for s in range(1, n // 2):
            offsets += [-s, s]
        offsets.append(n // 2)
        return jnp.concatenate([self.device(offsets, self.core), self.device(offsets, 1 - self.core)])

    def scattered(self):
        offsets = list(range(self.chips))
        return jnp.concatenate([self.device(offsets, self.core), self.device(offsets, 1 - self.core)])


class Gather:
    def __init__(self, ring, unit, cut):
        self.ring = ring
        self.rows = unit.shape[0]
        self.cut = cut
        self.last = [unit, unit]
        self.hops = 0
        self.mine = []
        self.theirs = []
        self.here = [unit]

    def values(self):
        return self.last

    def take(self, values):
        self.last = list(values)

    def hop(self, swap=True):
        ring = self.ring
        self.hops += 1
        up, down = self.last
        if self.hops == ring.chips // 2:
            up, down = up[: self.cut], down[self.cut :]
        self.last = [lax.ppermute(up, "dp", ring.up), lax.ppermute(down, "dp", ring.down)]
        if swap:
            self.swap()
        self.here = self.last

    def swap(self):
        self.theirs += [lax.ppermute(one, "dp", self.ring.swap) for one in self.here]
        self.mine += self.here
        self.here = []

    def finish(self):
        self.swap()
        return self.mine + self.theirs

    def shares(self):
        n = self.ring.chips
        own = [(u, 0, self.rows) for u in range(n - 1)]
        own += [(n - 1, 0, self.cut), (n - 1, self.cut, self.rows - self.cut)]
        return own + [(u + n, first, rows) for u, first, rows in own]


class Scatter:
    def __init__(self, ring, first, pieces, keep, *give):
        self.ring = ring
        self.keep = keep
        count = len(first) * pieces
        swapped = [lax.ppermute(one, "dp", ring.swap) for one in give[:count]]
        self.early = {k: swapped[n * pieces : (n + 1) * pieces] for n, k in enumerate(first)}
        self.first = first
        self.late = late_units(first)
        self.later = give[count:]
        self.got = {}
        self.last = {}

    def values(self):
        return list(self.last.values()) if self.last else [one for k in self.first for one in self.early[k]]

    def take(self, values):
        if self.last:
            self.last = dict(zip(self.last, values))
        else:
            pieces = len(values) // len(self.first)
            self.early = {k: values[n * pieces : (n + 1) * pieces] for n, k in enumerate(self.first)}

    def swap_all(self, *after):
        stack = lax.ppermute(tie(self.later[0], *after), "dp", self.ring.swap)
        self.got = {k: stack[n] for n, k in enumerate(self.late)}

    def hop(self, way, k):
        if k in self.early and len(self.early[k]) > 1:
            value = pieces_sum(k, self.keep, self.early[k]).astype(F32)
        else:
            got = self.early[k][0] if k in self.early else self.got[k]
            value = self.keep[k].astype(F32) + got.astype(F32)
        if way in self.last:
            value = value + self.last[way].astype(F32)
        value = value.astype(BF)
        self.last[way] = lax.ppermute(value, "dp", self.ring.up if way == "up" else self.ring.down)
        return value

    def result(self):
        return self.keep, self.got[0], self.last["up"], self.last["down"]


def together(chains, *more):
    values = [one for chain in chains for one in chain.values()]
    tied = lax.optimization_barrier(tuple(values) + more)
    at = 0
    for chain in chains:
        count = len(chain.values())
        chain.take(tied[at : at + count])
        at += count
    return tied[at:]


def tie(value, *after):
    return lax.optimization_barrier((value,) + after)[0] if after else value


def shards(
    tokens,
    segment_ids,
    gain_attn,
    gain_ffn,
    random_scores,
    w_value,
    w_output,
    w_up,
    w_down,
    cotangent,
):
    devices = lax.axis_size("dp")
    second = lax.axis_index("mp")
    length = segment_ids.shape[1]
    heads = random_scores.shape[0]
    model = tokens.shape[1]
    width = w_value.shape[1]
    size = width // heads
    rows = length // UNITS
    krows = model // UNITS
    ring = devices == UNITS and devices // 2 <= RING_CHIPS
    flip = [(0, 1), (1, 0)]
    second_at = jnp.reshape(second, (1,)).astype(jnp.int32)
    plan = Unit(heads, rows, krows, length, model, width, w_up.shape[1])

    if ring:
        net = Ring(devices)
        far = net.chips // 2
        where_in = net.gathered().astype(jnp.int32)
        where_out = net.scattered().astype(jnp.int32)
        unit, wo_own = pack_unit(
            plan, second_at, random_scores, w_value, gain_attn, gain_ffn, w_up, w_down.T, w_output.T
        )
        one = Gather(net, unit, plan.cut)
        one.hop(False)
        wo_other = lax.ppermute(tie(wo_own, where_in, where_out), "mp", flip)
        wo_next = [lax.ppermute(wo_other, "dp", way) for way in (net.up, net.down)]
        one.here = list(fill_units(plan, second_at, [unit], [wo_other]))
        one.swap()
        wo_next = together([one], *wo_next)
        one.last = list(fill_units(plan, second_at, one.last, wo_next))
        one.here = one.last
        for step in range(1, far - 1):
            one.hop()
            together([one])
            one.here = one.last
        there = one.mine + one.theirs
        shares = one.shares()
        half = len(shares) // 2
        early = [n for n in range(len(one.mine))] + [half + n for n in range(len(one.theirs))]
        one.hop()
        begun = mixer_first(plan, where_in, tokens, segment_ids, there, [shares[n] for n in early], heads)
        begun = together([one], *begun)
        one.here = one.last
        units = one.finish()
        late = [n for n in range(len(shares)) if n not in early]
        near = late
        order = [n for n in range(len(shares)) if n not in near] + near
        units, shares = [units[n] for n in order], [shares[n] for n in order]
        late = [n for n, old in enumerate(order) if old in late]
    else:
        where_in = jnp.arange(UNITS, dtype=jnp.int32)
        where_out = where_in

        def gather(one, axis=0):
            return lax.all_gather(one.astype(BF), "dp", axis=axis, tiled=True)

        wo_own = w_output.T.astype(BF)
        wo_other = lax.ppermute(wo_own, "mp", flip)
        halves = [jnp.where(second == n, wo_own, wo_other) for n in range(2)]
        scores = gather(random_scores, 1).reshape(heads, UNITS, rows, length).transpose(1, 0, 2, 3)
        wide = [gather(one) for one in (w_value, *halves)]
        wide = jnp.concatenate(wide, axis=1).reshape(UNITS, krows, plan.wide)
        ffn = jnp.concatenate([gather(w_up), gather(w_down.T)], axis=1).reshape(UNITS, krows, -1)
        stack = [scores.reshape(UNITS, heads * rows, length)]
        for kind, column in plan.blocks:
            stack.append((ffn if kind == "ffn" else wide)[:, :, column : column + length])
        gains = jnp.stack([gather(gain_attn), gather(gain_ffn)]).reshape(2, UNITS, krows).transpose(1, 0, 2)
        gains = jnp.pad(gains, ((0, 0), (0, plan.fold - 2), (0, length - plan.gain_lane - krows)))
        tail = wide[:, :, plan.wide - plan.tail :].reshape(UNITS, 3, plan.fold, plan.tail)
        stack.append(jnp.concatenate([tail[:, 0], tail[:, 1], tail[:, 2], gains], axis=2))
        whole = jnp.concatenate(stack, axis=1)
        units = [whole[u] for u in range(UNITS)]
        shares = [(u, 0, plan.deep) for u in range(UNITS)]
        early, late, near = list(range(UNITS // 2)), list(range(UNITS // 2, UNITS)), []
        begun = mixer_first(plan, where_in, tokens, segment_ids, units[: UNITS // 2], shares[: UNITS // 2], heads)

    e, wv, _, va, mixed, sums, n1, gains = mixer_forward(
        plan, where_in, segment_ids, begun, [units[n] for n in late], [shares[n] for n in late], heads, width
    )
    mixed_other = lax.ppermute(mixed, "mp", flip)
    w, gact, mixf, rb = second_weights(plan, where_in, cotangent, sums, units, shares, len(near), size)
    backs, others, resids, n2s, acts, gpres = [], [], [], [], [], []
    for part in range(PARTS):
        *new, resid, n2, act, gpre = ffn_main(
            second_at, tokens, mixed, mixed_other, gact, gains, w, part, PARTS, 1
        )
        for back in new:
            backs.append(back)
            others.append(lax.ppermute(tie(back, *others[-1:]), "mp", flip))
        resids.append(resid)
        n2s.append(n2)
        acts.append(act)
        gpres.append(gpre)
    ffn, *parts_two = ffn_grads(where_out, n2s, gpres, acts, cotangent, w)
    if ring:
        ffn_sum = Scatter(net, FFN_FIRST, 1, *parts_two)
        ffn_sum.swap_all(others[0], *ffn_sum.values())
        for step in range(2):
            ffn_sum.hop("down", far + step)
            ffn_sum.hop("up", far - 1 - step)
            together([ffn_sum])
    gres, gat, xh, gf = resid_back(
        second_at, backs, others, resids, cotangent, gains, w, mixf, heads, size
    )
    ffn_cut = 7 * length // 16
    ffn_one, ffn_two = ffn[:ffn_cut], ffn[ffn_cut:]
    one_other = lax.ppermute(tie(ffn_one, xh), "mp", flip)
    gv, part_one, part_two, ga = value_back(xh, rb, e, wv, tokens, size, length // 2)
    ga_other = lax.ppermute(ga, "mp", flip)
    if ring:
        for step in range(2, far - 1):
            ffn_sum.hop("down", far + step)
            ffn_sum.hop("up", far - 1 - step)
    parts_one = mixer_grads(where_out, xh, va, e, rb, krows)
    parts_one = weight_grads(where_out, parts_one, n1, gv, gat, mixed, ga, ga_other, gf)

    top = heads * rows
    if ring:
        score_sum = Scatter(net, MIXER_FIRST, 2, *parts_one)
        one_other, ffn_two = together([ffn_sum, score_sum], one_other, ffn_two)
        value = score_sum.hop("up", far)
        ffn_sum.hop("down", 2 * far - 1)
        score_sum.swap_all(value)
        two_other = lax.ppermute(ffn_two, "mp", flip)
        part_one, part_two = together([ffn_sum, score_sum], part_one, part_two)
        for step in range(1, far):
            score_sum.hop("up", far - step)
            score_sum.hop("down", far + step)
            if step == 1:
                part_other = [lax.ppermute(part_one, "mp", flip)]
                two_other, part_two = together([score_sum], two_other, part_two)
            elif step < far - 1:
                part_other.append(lax.ppermute(part_two, "mp", flip))
                (part_other[0],) = together([score_sum], part_other[0])
        out_up, out_down = ffn_result(*ffn_sum.result())
        out_scores, out_value, out_output, *out_gains = mixer_result(*score_sum.result(), heads, krows, width)
        out_down, out_output = out_down.T, out_output.T
        out_gain_one, out_gain_two = [one.reshape(krows) for one in out_gains]
    else:
        two_other = lax.ppermute(ffn_two, "mp", flip)
        part_other = [lax.ppermute(one, "mp", flip) for one in (part_one, part_two)]

        def scatter(one, axis=0):
            return lax.psum_scatter(one, "dp", scatter_dimension=axis, tiled=True)

        def whole(first, pieces, keep, *give):
            late = late_units(first)
            early, later = give[: len(first) * pieces], give[len(first) * pieces :]
            given = []
            for k in range(UNITS // 2):
                if k in first:
                    at = first.index(k) * pieces
                    given.append(jnp.concatenate(early[at : at + pieces]))
                else:
                    given.append(later[0][late.index(k)] if len(later) == 1 else later[late.index(k)])
            return jnp.concatenate([keep, jnp.stack(given)]).astype(F32)

        two = whole(FFN_FIRST, 1, *parts_two).reshape(model, -1)
        one = whole(MIXER_FIRST, 2, *parts_one)
        out_up = scatter(two[:, : two.shape[1] // 2])
        out_down = scatter(two[:, two.shape[1] // 2 :]).T
        scores = one[:, :top].reshape(UNITS, heads, rows, length).transpose(1, 0, 2, 3)
        out_scores = scatter(scores.reshape(heads, length, length), 1)
        out_value = scatter(one[:, top : top + krows, :width].reshape(model, width))
        out_output = scatter(one[:, top + krows :, :width].reshape(model, width)).T
        out_gain_one = scatter(one[:, top, width : width + krows].reshape(model))
        out_gain_two = scatter(one[:, top + 1, width : width + krows].reshape(model))
    ffn_other = jnp.concatenate([one_other, two_other])
    output = (jnp.concatenate(resids) + (ffn.astype(F32) + ffn_other.astype(F32))).astype(BF)
    backs = []
    begin = 0
    for mine, other in zip((part_one, part_two), part_other):
        grad_n1 = mine.astype(F32) + other.astype(F32)
        at = slice(begin, begin + mine.shape[0])
        begin = at.stop
        x = tokens[at].astype(F32)
        inv = lax.rsqrt(jnp.mean(x * x, axis=-1, keepdims=True) + EPSILON)
        z = gains[0:1, :] * grad_n1
        hat = x * inv
        backs.append((gres[at] + inv * (z - hat * jnp.mean(z * hat, axis=-1, keepdims=True))).astype(BF))
    grad_tokens = jnp.concatenate(backs)
    return (
        output,
        grad_tokens,
        out_gain_one,
        out_gain_two,
        out_scores,
        out_value,
        out_output,
        out_up,
        out_down,
    )


def solution(mesh):
    in_specs = (
        P("dp", None),
        P("dp", None),
        P("dp"),
        P("dp"),
        P("mp", "dp", None),
        P("dp", "mp"),
        P("mp", "dp"),
        P("dp", "mp"),
        P("mp", "dp"),
        P("dp", None),
    )
    out_specs = (
        P("dp", None),
        P("dp", None),
        P("dp"),
        P("dp"),
        P("mp", "dp", None),
        P("dp", "mp"),
        P("mp", "dp"),
        P("dp", "mp"),
        P("mp", "dp"),
    )
    return jax.shard_map(shards, mesh=mesh, in_specs=in_specs, out_specs=out_specs, check_vma=False)
```

```python
import jax
import jax.numpy as jnp
from jax import lax
from jax.experimental import pallas as pl
from jax.experimental.pallas import tpu as pltpu
from jax.sharding import PartitionSpec as P

EPSILON = 1e-06
NEGATIVE = -1e30
BF = jnp.bfloat16
F32 = jnp.float32
UNITS = 16
LANES = 128
PARTS = 2
RING_CHIPS = 8
VMEM_BYTES = 20 * 1024 * 1024
NT = (((1,), (1,)), ((), ()))
TN = (((0,), (0,)), ((), ()))
NN = (((1,), (0,)), ((), ()))


def mm(a, b, dims=NN):
    return lax.dot_general(a, b, dims, preferred_element_type=F32)


def run(kernel, name, scalars, arrays, outs, scratch=(), loose=(), loose_outs=(), aliases=None, near=0):
    held = [pltpu.with_memory_space_constraint(one, pltpu.VMEM) for one in arrays]
    results = [pltpu.VMEM(*one) for one in outs] + [jax.ShapeDtypeStruct(*one) for one in loose_outs]
    specs = [pl.BlockSpec(memory_space=pltpu.SMEM)] * len(scalars)
    specs += [pl.BlockSpec(memory_space=pltpu.VMEM)] * len(arrays)
    far = len(loose) - near
    specs += [pl.BlockSpec(memory_space=pltpu.HBM)] * far + [pl.BlockSpec(memory_space=pl.ANY)] * near
    loose = [pltpu.with_memory_space_constraint(one, pltpu.HBM) for one in loose[:far]] + list(loose[far:])
    out_specs = [pl.BlockSpec(memory_space=pltpu.VMEM)] * len(outs)
    out_specs += [pl.BlockSpec(memory_space=pl.ANY)] * len(loose_outs)
    return pl.pallas_call(
        kernel,
        out_shape=tuple(results),
        in_specs=specs,
        out_specs=tuple(out_specs),
        scratch_shapes=list(scratch),
        compiler_params=pltpu.CompilerParams(vmem_limit_bytes=VMEM_BYTES),
        cost_estimate=pl.CostEstimate(flops=1, bytes_accessed=1, transcendentals=0),
        input_output_aliases=aliases or {},
        name=name,
    )(*scalars, *held, *loose)


def gelu_pair(x):
    c = 0.7978845608028654
    a = 0.044715
    square = x * x
    t = jnp.tanh(c * x * (1.0 + a * square))
    half = 0.5 * (1.0 + t)
    return x * half, half + 0.5 * x * (1.0 - t * t) * (c * (1.0 + 3.0 * a * square))


def multiple(value, of):
    return pl.multiple_of(value, of)


class Unit:
    def __init__(self, heads, rows, krows, length, model, width, hidden):
        self.scores = heads * rows
        self.krows = krows
        self.length = length
        self.width = width
        self.hidden = hidden
        self.wide = width + model
        self.blocks = [("ffn", n * length) for n in range(2 * hidden // length)]
        self.blocks += [("proj", n * length) for n in range(self.wide // length)]
        self.tail = self.wide % length
        self.last = self.scores + krows * len(self.blocks)
        self.fold = krows // 3
        self.deep = self.last + self.fold
        self.cut = self.scores + krows * (2 * hidden // length // 3)
        self.gain_lane = 3 * self.tail

    def ffn_parts(self):
        parts = []
        for n, (kind, first) in enumerate(self.blocks):
            at = self.scores + n * self.krows
            if kind == "ffn":
                parts.append((at, 0, 0, first, self.krows, self.length))
            else:
                skip = max(self.width - first, 0)
                column = 2 * self.hidden + first + skip - self.width
                parts.append((at, skip, 0, column, self.krows, self.length - skip))
        for n in range(3):
            column = 2 * self.hidden + self.wide - self.tail - self.width
            parts.append((self.last, n * self.tail, n * self.fold, column, self.fold, self.tail))
        return parts

    def value_row(self):
        return self.scores + [kind for kind, _ in self.blocks].index("proj") * self.krows


def other_parts(plan, first):
    begin = plan.width + first * plan.width
    parts = []
    for n, (kind, column) in enumerate(plan.blocks):
        low, high = max(begin, column), min(begin + plan.width, column + plan.length)
        if kind == "proj" and low < high:
            parts.append((plan.scores + n * plan.krows, low - column, 0, low - begin, plan.krows, high - low))
    low = max(begin, plan.wide - plan.tail)
    if low < begin + plan.width:
        for n in range(3):
            lanes = n * plan.tail + low - (plan.wide - plan.tail)
            parts.append((plan.last, lanes, n * plan.fold, low - begin, plan.fold, begin + plan.width - low))
    return parts


def put_half(plan, out, half_ref, first):
    for row, lane, at, column, rows, lanes in other_parts(plan, first):
        out[row : row + rows, lane : lane + lanes] = half_ref[at : at + rows, column : column + lanes]


def pack_unit(plan, second, scores, wv, gain_one, gain_two, w_up, w_down, wo):
    inputs = (scores, wv, gain_one.reshape(1, -1), gain_two.reshape(1, -1), w_up, w_down, wo)
    count = len(inputs)
    krows, length, width = plan.krows, plan.length, plan.width
    per = plan.hidden // length
    assert plan.tail <= width

    def kernel(second_ref, *rest):
        out, wo_out, gains = rest[count : count + 3]
        held, sem = rest[count + 3 : -1], rest[-1]
        fetch(rest[:count], held, sem)
        s_ref, wv_ref, ga_ref, gf_ref, up_ref, down_ref, own_ref = held
        out[: plan.scores, :] = s_ref[...].reshape(plan.scores, length).astype(BF)
        for n, (kind, column) in enumerate(plan.blocks):
            at = slice(plan.scores + n * krows, plan.scores + (n + 1) * krows)
            if kind == "ffn":
                ref, first = (up_ref, column) if n < per else (down_ref, column - plan.hidden)
                out[at, :] = ref[:, first : first + length].astype(BF)
            else:
                out[at, :] = jnp.zeros((krows, length), BF)
        out[plan.last :, : plan.gain_lane] = jnp.zeros((plan.fold, plan.gain_lane), BF)
        out[plan.value_row() : plan.value_row() + krows, :width] = wv_ref[...].astype(BF)
        wo_out[...] = own_ref[...].astype(BF)
        for place in range(2):

            @pl.when(second_ref[0] == place)
            def _():
                put_half(plan, out, wo_out, place)

        gains[...] = jnp.zeros_like(gains)
        gains[0:1, :krows] = ga_ref[...]
        gains[1:2, :krows] = gf_ref[...]
        out[plan.last :, plan.gain_lane :] = gains[...].astype(BF)

    return run(
        kernel,
        "pack_unit",
        (second,),
        (),
        (((plan.deep, length), BF), ((krows, width), BF)),
        (
            pltpu.VMEM((plan.fold, length - plan.gain_lane), F32),
            *[pltpu.VMEM(one.shape, one.dtype) for one in inputs],
            pltpu.SemaphoreType.DMA((count,)),
        ),
        loose=inputs,
    )


def fill_units(plan, second, units, others):
    count = len(units)

    def kernel(second_ref, *rest):
        for place in range(2):

            @pl.when(second_ref[0] == 1 - place)
            def _():
                for n in range(count):
                    put_half(plan, rest[2 * count + n], rest[count + n], place)

    return run(
        kernel,
        "fill_units",
        (second,),
        (*units, *others),
        [(one.shape, BF) for one in units],
        aliases={1 + n: n for n in range(count)},
    )


def fetch(refs, held, sem):
    copies = [pltpu.make_async_copy(ref, to, sem.at[n]) for n, (ref, to) in enumerate(zip(refs, held))]
    for copy in copies:
        copy.start()
    for copy in copies:
        copy.wait()


def pick(units, shares, where_ref, parts, target, sem):
    copies = []
    for n, (u, first, rows) in enumerate(shares):
        owner = where_ref[u]
        for m, part in enumerate(parts):
            row, column, count, columns = part[0], part[1], part[-2], part[-1]
            if first <= row and row + count <= first + rows:
                source = units[n].at[pl.ds(row - first, count), pl.ds(column, columns)]
                copies.append(pltpu.make_async_copy(source, target(m, owner), sem.at[u, m]))
                copies[-1].start()
    return copies


def document_mask(seg_ref, same):
    length = same.shape[0]
    documents = (seg_ref[...] == lax.broadcasted_iota(jnp.int32, (LANES, length), 0)).astype(BF)
    same[...] = mm(documents, documents, TN)


def exponentials(where_ref, shares, sources, e_ref, same):
    heads, length, _ = e_ref.shape
    rows = length // UNITS

    def one_head(h, carry):
        for (u, _, _), (ref, first) in zip(shares, sources):
            at = pl.ds(multiple(where_ref[u] * rows, rows), rows)
            s = ref[pl.ds(multiple(first + h * rows, rows), rows), :].astype(F32)
            e_ref[h, at, :] = (jnp.exp(s) * same[at, :]).astype(BF)
        return carry

    lax.fori_loop(0, heads, one_head, 0)


def low_parts(plan):
    return [
        (plan.value_row(), 0, plan.krows, plan.width),
        (plan.last, plan.gain_lane, plan.fold, LANES),
    ]


def bring_low(plan, units, shares, where_ref, wv_ref, low_ref, sem):
    krows = plan.krows

    def target(m, owner):
        if m == 0:
            return wv_ref.at[pl.ds(multiple(owner * krows, 16), krows), :]
        return low_ref.at[owner]

    return pick(units, shares, where_ref, low_parts(plan), target, sem)


def mixer_first(plan, where, tokens, segments, units, shares, heads):
    length, model = tokens.shape
    rows = length // UNITS

    def kernel(where_ref, tok_ref, seg_ref, *rest):
        e_ref, wv_ref, low_ref, hat_ref, unit, same, sem, more = rest[len(units) :]
        top = heads * rows

        def target(m, owner):
            return unit.at[pl.ds(multiple(owner * top, top), top), :]

        came = pick(rest[: len(units)], shares, where_ref, [(0, 0, top, length)], target, sem)
        copies = bring_low(plan, rest[: len(units)], shares, where_ref, wv_ref, low_ref, more)
        document_mask(seg_ref, same)
        x = tok_ref[...].astype(F32)
        hat_ref[...] = x * lax.rsqrt(jnp.mean(x * x, axis=-1, keepdims=True) + EPSILON)
        for copy in came:
            copy.wait()
        sources = [(unit, where_ref[u] * top) for u, _, _ in shares]
        exponentials(where_ref, shares, sources, e_ref, same)
        for copy in copies:
            copy.wait()

    return run(
        kernel,
        "mixer_first",
        (where,),
        (tokens, segments),
        (
            ((heads, length, length), BF),
            ((model, plan.width), BF),
            ((UNITS, plan.fold, LANES), BF),
            ((length, model), F32),
        ),
        (
            pltpu.VMEM((heads * length, length), BF),
            pltpu.VMEM((length, length), F32),
            pltpu.SemaphoreType.DMA((UNITS, 1)),
            pltpu.SemaphoreType.DMA((UNITS, 2)),
        ),
        loose=units,
    )


def mixer_forward(plan, where, segments, early, units, shares, heads, width):
    length, model = early[3].shape
    size = width // heads
    krows = model // UNITS
    wide = heads * LANES
    count = len(units)

    def kernel(where_ref, seg_ref, e_old, wv_old, low_old, hat_ref, *rest):
        e_ref, wv_ref, low, va_ref, sums_ref, n1_ref, gains_ref, *mixed, pieces, same = rest[count:]
        for (u, first, rows), ref in zip(shares, rest[:count]):
            for m, (row, lane, deep, lanes) in enumerate(low_parts(plan)):
                if first <= row < first + rows:
                    part = ref[row - first : row - first + deep, lane : lane + lanes]
                    if m == 0:
                        wv_ref[pl.ds(multiple(where_ref[u] * krows, 16), krows), :] = part
                    else:
                        low[where_ref[u]] = part
        document_mask(seg_ref, same)
        scored = [n for n in range(count) if shares[n][1] == 0]
        exponentials(where_ref, [shares[n] for n in scored], [(rest[n], 0) for n in scored], e_ref, same)
        for d in range(UNITS):
            some = low[d].astype(F32)
            pieces[0, d : d + 1, :] = some[0:1, :]
            pieces[1, d : d + 1, :] = some[1:2, :]
        spread = (
            lax.broadcasted_iota(jnp.int32, (LANES, model), 1) % krows
            == lax.broadcasted_iota(jnp.int32, (LANES, model), 0)
        ).astype(BF)
        own = (
            lax.broadcasted_iota(jnp.int32, (UNITS, model), 1) // krows
            == lax.broadcasted_iota(jnp.int32, (UNITS, model), 0)
        )
        gains = []
        for t in range(2):
            full = jnp.where(own, mm(pieces[t].astype(BF), spread), 0.0)
            gains.append(jnp.sum(full, axis=0, keepdims=True))
            gains_ref[t : t + 1, :] = gains[t]
        n1_ref[...] = (hat_ref[...] * gains[0]).astype(BF)
        values = mm(n1_ref[...], wv_ref[...]).astype(BF)
        tail = (lax.broadcasted_iota(jnp.int32, (length, LANES - size), 1) < 2).astype(BF)
        for h in range(heads):
            va_ref[:, h * LANES : h * LANES + size] = values[:, h * size : (h + 1) * size]
            va_ref[:, h * LANES + size : (h + 1) * LANES] = tail

        for h in range(heads):
            lanes = slice(h * LANES, (h + 1) * LANES)
            sums = mm(e_ref[h], va_ref[:, lanes])
            sums_ref[:, lanes] = sums
            values = (sums * (1.0 / sums[:, size : size + 1]))[:, :size].astype(BF)
            for part, mixed_ref in enumerate(mixed):
                some = slice(part * (length // PARTS), (part + 1) * (length // PARTS))
                mixed_ref[:, h * size : (h + 1) * size] = values[some, :]

    return run(
        kernel,
        "mixer_forward",
        (where,),
        (segments, *early, *units),
        (
            ((heads, length, length), BF),
            ((model, width), BF),
            ((UNITS, plan.fold, LANES), BF),
            ((length, wide), BF),
            ((length, wide), F32),
            ((length, model), BF),
            ((2, model), F32),
            *[((length // PARTS, width), BF)] * PARTS,
        ),
        (
            pltpu.VMEM((2, UNITS, LANES), F32),
            pltpu.VMEM((length, length), F32),
        ),
        aliases={2: 0, 3: 1, 4: 2},
    )


def second_weights(plan, where, second, cotangent, sums, units, shares, near, size):
    length, model = cotangent.shape
    hidden, krows, width = plan.hidden, plan.krows, plan.width
    piece = hidden // 3
    parts = plan.ffn_parts()

    def kernel(where_ref, second_ref, cot_ref, sums_ref, *rest):
        out, gact, mixf_ref, rb_ref, own_ref, sem = rest[len(units) :]

        def target(m, owner):
            _, _, row, column, rows, columns = parts[m]
            return out.at[pl.ds(multiple(owner * krows + row, 16), rows), pl.ds(column, columns)]

        copies = pick(rest[: len(units)], shares, where_ref, parts, target, sem)
        inside = lax.broadcasted_iota(jnp.int32, (length, LANES), 1) < size
        for h in range(sums.shape[1] // LANES):
            lanes = slice(h * LANES, (h + 1) * LANES)
            inverse = jnp.broadcast_to(1.0 / sums_ref[:, h * LANES + size : h * LANES + size + 1], (length, LANES))
            rb_ref[:, lanes] = inverse
            mixf_ref[:, lanes] = jnp.where(inside, sums_ref[:, lanes] * inverse, 0.0)
        for copy in copies:
            copy.wait()
        for j in range(3):
            cols = slice(j * piece, (j + 1) * piece)
            gact[:, cols] = mm(cot_ref[...], out[:, hidden + j * piece : hidden + (j + 1) * piece])
        own = out[:, pl.ds(multiple(2 * hidden + second_ref[0] * width, LANES), width)]
        own_ref[...] = jnp.zeros_like(own_ref)
        for h in range(width // size):
            own_ref[:, h * LANES : h * LANES + size] = own[:, h * size : (h + 1) * size]

    return run(
        kernel,
        "second_weights",
        (where, second),
        (cotangent, sums),
        (
            ((model, 2 * hidden + model), BF),
            ((length, hidden), F32),
            (sums.shape, F32),
            (sums.shape, F32),
            ((model, sums.shape[1]), BF),
        ),
        (pltpu.SemaphoreType.DMA((UNITS, len(parts))),),
        loose=units,
        near=near,
    )


def ffn_main(second, tokens, mixed_own, mixed_other, gact, gains, w, part, parts, pieces):
    length, model = tokens.shape
    width = mixed_own.shape[1]
    hidden = gact.shape[1]
    chunk = length // parts
    piece = hidden // 3
    at = slice(part * chunk, (part + 1) * chunk)

    def kernel(second_ref, tok_ref, own_ref, other_ref, gact_ref, gains_ref, w_ref,
               *rest):
        backs = rest[:pieces]
        resid_ref, n2_ref, act_ref, gpre_ref, mixed, acc = rest[pieces:]
        first = second_ref[0]
        mixed[:, pl.ds(multiple(first * width, LANES), width)] = own_ref[...]
        mixed[:, pl.ds(multiple((1 - first) * width, LANES), width)] = other_ref[...]
        attn = mm(mixed[...], w_ref[:, 2 * hidden :], NT)
        resid = tok_ref[at, :].astype(F32) + attn
        resid_ref[...] = resid
        inv = lax.rsqrt(jnp.mean(resid * resid, axis=-1, keepdims=True) + EPSILON)
        n2_ref[...] = (resid * inv * gains_ref[1:2, :]).astype(BF)
        for j in range(hidden // piece):
            cols = slice(j * piece, (j + 1) * piece)
            act, slope = gelu_pair(mm(n2_ref[...], w_ref[:, cols]))
            act_ref[:, cols] = act.astype(BF)
            gpre_ref[:, cols] = (gact_ref[at, cols] * slope).astype(BF)
            term = mm(gpre_ref[:, cols], w_ref[:, cols], NT)
            if j == 0:
                acc[...] = term
            else:
                acc[...] += term
        for n, back_ref in enumerate(backs):
            back_ref[...] = acc[n * (chunk // pieces) : (n + 1) * (chunk // pieces), :].astype(BF)

    return run(
        kernel,
        "ffn_main",
        (second,),
        (tokens, mixed_own, mixed_other, gact, gains, w),
        (
            *[((chunk // pieces, model), BF)] * pieces,
            ((chunk, model), F32),
            ((chunk, model), BF),
            ((chunk, hidden), BF),
            ((chunk, hidden), BF),
        ),
        (
            pltpu.VMEM((chunk, 2 * width), BF),
            pltpu.VMEM((chunk, model), F32),
        ),
    )


def late_units(first):
    return [k for k in range(UNITS // 2) if k not in first]


def slots(refs, first, pieces):
    half = UNITS // 2
    count = len(first) * pieces
    keep, early, later = refs[0], refs[1 : 1 + count], refs[1 + count :]
    late = late_units(first)

    def slot(u):
        if u < half:
            return [keep.at[u]]
        k = u - half
        if k in first:
            at = first.index(k) * pieces
            return early[at : at + pieces]
        n = late.index(k)
        return [later[0].at[n] if len(later) == 1 else later[n]]

    return slot


def slot_shapes(rows, columns, first, pieces, apart):
    half = UNITS // 2
    early = [((rows, columns), BF)] * (len(first) * pieces)
    count = half - len(first)
    later = [((rows, columns), BF)] * count if apart else [((count, rows, columns), BF)]
    return [((half, rows, columns), BF), *early, *later]


FFN_FIRST = [UNITS // 4, UNITS // 4 - 1]
MIXER_FIRST = [UNITS // 4]


def result_kernel(name, keep, own, up, down, shapes, cut):
    def kernel(keep_ref, own_ref, up_ref, down_ref, *rest):
        outs, held, sem = rest[: len(shapes)], rest[len(shapes) : -1], rest[-1]

        def total(rows, columns):
            value = keep_ref[0, rows, columns].astype(F32) + own_ref[rows, columns].astype(F32)
            return value + up_ref[rows, columns].astype(F32) + down_ref[rows, columns].astype(F32)

        copies = []
        for n, (out, to) in enumerate(zip(outs, held)):
            cut(n, to, total)
            copies.append(pltpu.make_async_copy(to, out, sem.at[n]))
            copies[-1].start()
        for copy in copies:
            copy.wait()

    return run(
        kernel,
        name,
        (),
        (keep, own, up, down),
        (),
        (*[pltpu.VMEM(shape, F32) for shape in shapes], pltpu.SemaphoreType.DMA((len(shapes),))),
        loose_outs=[(shape, F32) for shape in shapes],
    )


def ffn_result(keep, own, up, down):
    _, rows, columns = keep.shape
    half = columns // 2

    def cut(n, to, total):
        to[...] = total(slice(None), slice(n * half, (n + 1) * half))

    return result_kernel("ffn_result", keep, own, up, down, [(rows, half)] * 2, cut)


def mixer_result(keep, own, up, down, heads, krows, width):
    _, deep, length = keep.shape
    top = deep - low_rows(krows)
    rows = top // heads
    lead, half, fold = length - width, length // 2, krows // 3
    shapes = [(heads, rows, length), (krows, width), (krows, width), (1, krows), (1, krows)]

    def cut(n, to, total):
        low = top + krows
        if n == 0:
            for h in range(heads):
                to[h] = total(slice(h * rows, (h + 1) * rows), slice(None))
        elif n == 1:
            to[...] = total(slice(top, low), slice(0, width))
        elif n == 2:
            to[:, :lead] = total(slice(top, low), slice(width, length))
            for m in range(3):
                some = slice(low + m // 2 * fold, low + (m // 2 + 1) * fold)
                to[m * fold : (m + 1) * fold, lead:] = total(some, slice(m % 2 * half, (m % 2 + 1) * half))
        else:
            to[...] = total(slice(low + fold, low + 2 * fold), slice(half, half + LANES))[n - 3 : n - 2, :krows]

    return result_kernel("mixer_result", keep, own, up, down, shapes, cut)


def ffn_out(acts, w, cut):
    chunk, hidden = acts[0].shape
    model = w.shape[0]
    length = chunk * len(acts)

    def kernel(*refs):
        w_ref, out = refs[-4:-3][0], refs[-1]
        for r, act in enumerate(refs[:-4]):
            out[r * chunk : (r + 1) * chunk, :] = mm(act[...], w_ref[:, hidden : 2 * hidden], NT).astype(BF)
        refs[-3][...] = out[:cut, :]
        refs[-2][...] = out[cut:, :]

    return run(
        kernel,
        "ffn_out",
        (),
        (*acts, w),
        (((cut, model), BF), ((length - cut, model), BF)),
        (pltpu.VMEM((length, model), BF),),
    )


def ffn_grads(where, n2s, gpres, acts, cotangent):
    parts = len(n2s)
    chunk, model = n2s[0].shape
    hidden = acts[0].shape[1]
    krows = model // UNITS

    def kernel(where_ref, cot_ref, *rest):
        n2, gpre, act = rest[:parts], rest[parts : 2 * parts], rest[2 * parts : 3 * parts]
        slot = slots(rest[3 * parts : -2], FFN_FIRST, 1)
        scr, sem = rest[-2:]
        piece = hidden // 3
        for j in range(3):
            cols = slice(j * piece, (j + 1) * piece)
            down = slice(hidden + j * piece, hidden + (j + 1) * piece)
            one = [mm(n2[r][...], gpre[r][:, cols], TN) for r in range(parts)]
            scr[:, cols] = sum(one).astype(BF)
            two = [mm(cot_ref[r * chunk : (r + 1) * chunk, :], act[r][:, cols], TN) for r in range(parts)]
            scr[:, down] = sum(two).astype(BF)
        copies = []
        for u in range(UNITS):
            at = pl.ds(multiple(where_ref[u] * krows, 16), krows)
            (to,) = slot(u)
            copies.append(pltpu.make_async_copy(scr.at[at, :], to, sem.at[u]))
            copies[-1].start()
        for copy in copies:
            copy.wait()

    return run(
        kernel,
        "ffn_grads",
        (where,),
        (cotangent, *n2s, *gpres, *acts),
        (),
        (pltpu.VMEM((model, 2 * hidden), BF), pltpu.SemaphoreType.DMA((UNITS,))),
        loose_outs=slot_shapes(krows, 2 * hidden, FFN_FIRST, 1, False),
    )


def cut_gain(row, krows):
    model = row.shape[1]
    take = (
        lax.broadcasted_iota(jnp.int32, (model, LANES), 0) % krows
        == lax.broadcasted_iota(jnp.int32, (model, LANES), 1)
    ).astype(BF)
    own = (
        lax.broadcasted_iota(jnp.int32, (UNITS, model), 1) // krows
        == lax.broadcasted_iota(jnp.int32, (UNITS, model), 0)
    )
    high = row.astype(BF).astype(F32)
    pieces = mm(jnp.where(own, high, 0.0).astype(BF), take)
    return pieces + mm(jnp.where(own, row - high, 0.0).astype(BF), take)


def resid_back(backs, others, resids, cotangent, gains, wo, mixf, heads, size):
    length, model = cotangent.shape
    wide = heads * LANES
    count = len(backs)
    krows = model // UNITS
    parts = len(resids)


    def kernel(cot_ref, gains_ref, wo_ref, mixf_ref, *rest):
        mine, other, res_refs = rest[:count], rest[count : 2 * count], rest[2 * count : 2 * count + parts]
        gres_ref, gat_ref, xh_ref, gf_ref, gm = rest[2 * count + parts :]
        total = jnp.zeros((8, model), F32)
        begin = 0
        for r in range(count):
            chunk = mine[r].shape[0]
            at = slice(begin, begin + chunk)
            g2 = mine[r][...].astype(F32) + other[r][...].astype(F32)
            whole = length // parts
            res = res_refs[begin // whole][begin % whole : begin % whole + chunk, :]
            begin += chunk
            inv = lax.rsqrt(jnp.mean(res * res, axis=-1, keepdims=True) + EPSILON)
            hat = res * inv
            total = total + jnp.sum((g2 * hat).reshape(chunk // 8, 8, model), axis=0)
            z = gains_ref[1:2, :] * g2
            corr = jnp.mean(z * hat, axis=-1, keepdims=True)
            gres = cot_ref[at, :].astype(F32) + inv * (z - hat * corr)
            gres_ref[at, :] = gres
            gat_ref[at, :] = gres.astype(BF)
        gm[...] = mm(gat_ref[...], wo_ref[...]).astype(BF)
        lane = lax.broadcasted_iota(jnp.int32, (length, LANES), 1)
        for h in range(heads):
            lanes = slice(h * LANES, (h + 1) * LANES)
            here = gm[:, lanes].astype(F32)
            inner = -jnp.sum(here * mixf_ref[:, lanes], axis=-1, keepdims=True)
            high = inner.astype(BF).astype(F32)
            xh_ref[:, lanes] = jnp.where(
                lane == size, high, jnp.where(lane == size + 1, inner - high, here)
            ).astype(BF)
        gf_ref[...] = cut_gain(jnp.sum(total, axis=0, keepdims=True), krows)

    return run(
        kernel,
        "resid_back",
        (),
        (cotangent, gains, wo, mixf, *backs, *others, *resids),
        (
            ((length, model), F32),
            ((length, model), BF),
            ((length, wide), BF),
            ((UNITS, LANES), F32),
        ),
        (pltpu.VMEM((length, wide), BF),),
    )


def score_grads(where_ref, xh_ref, va_ref, e_ref, rb_ref, ds, slot, begin, count, rows):
    length = ds.shape[0]

    def one_head(h, carry):
        lanes = pl.ds(multiple((begin + h) * LANES, LANES), LANES)
        d = mm(xh_ref[:, lanes], va_ref[:, lanes], NT)
        inverse = rb_ref[:, lanes]
        for q in range(length // LANES):
            cols = slice(q * LANES, (q + 1) * LANES)
            ds[:, cols] = (e_ref[begin + h, :, cols].astype(F32) * inverse * d[:, cols]).astype(BF)
        for u in range(UNITS):
            at = pl.ds(multiple(where_ref[u] * rows, rows), rows)
            slot(u)[0][pl.ds(multiple(h * rows, rows), rows), :] = ds[at, :]
        return carry

    lax.fori_loop(0, count, one_head, 0)


def value_back(xh, rb, e, wv, tokens, size, cut):
    length, model = tokens.shape
    heads = e.shape[0]
    width = heads * size
    krows = model // UNITS

    def kernel(xh_ref, rb_ref, e_ref, wv_ref, tok_ref, gv_ref, part_one, part_two, ga_ref, acc):
        acc[...] = jnp.zeros_like(acc)
        for h in range(heads):
            lanes = slice(h * LANES, (h + 1) * LANES)
            scaled = (xh_ref[:, lanes].astype(F32) * rb_ref[:, lanes]).astype(BF)
            gv_ref[:, h * size : (h + 1) * size] = mm(e_ref[h], scaled, TN)[:, :size].astype(BF)

        for at, part_ref in ((slice(0, cut), part_one), (slice(cut, length), part_two)):
            part = mm(gv_ref[at, :], wv_ref[...], NT)
            part_ref[...] = part.astype(BF)
            x = tok_ref[at, :].astype(F32)
            inv = lax.rsqrt(jnp.mean(x * x, axis=-1, keepdims=True) + EPSILON)
            acc[...] += jnp.sum((part * (x * inv)).reshape((at.stop - at.start) // 8, 8, model), axis=0)

        ga_ref[...] = jnp.zeros_like(ga_ref)
        ga_ref[:UNITS, :] = cut_gain(jnp.sum(acc[...], axis=0, keepdims=True), krows)

    return run(
        kernel,
        "value_back",
        (),
        (xh, rb, e, wv, tokens),
        (
            ((length, width), BF),
            ((cut, model), BF),
            ((length - cut, model), BF),
            ((4 * UNITS, LANES), F32),
        ),
        (pltpu.VMEM((8, model), F32),),
    )


def low_rows(krows):
    return krows + 2 * (krows // 3)


def mixer_grads(where, xh, va, e, rb, krows):
    heads, length, _ = e.shape
    rows = length // UNITS
    deep = heads * rows + low_rows(krows)

    def kernel(where_ref, xh_ref, va_ref, e_ref, rb_ref, *rest):
        outs, ds = rest[:-1], rest[-1]
        score_grads(where_ref, xh_ref, va_ref, e_ref, rb_ref, ds, slots(outs, MIXER_FIRST, 1), 0, heads, rows)
        for u in range(UNITS):
            for to in slots(outs, MIXER_FIRST, 1)(u):
                to[heads * rows :, :] = jnp.zeros((low_rows(krows), length), BF)

    return run(
        kernel,
        "mixer_grads",
        (where,),
        (xh, va, e, rb),
        slot_shapes(deep, length, MIXER_FIRST, 1, False),
        (pltpu.VMEM((length, length), BF),),
    )


def weight_grads(where, parts, n1, gv, gat, mixed, ga, ga_other, gf):
    length = n1.shape[0]
    chunk = mixed[0].shape[0]
    model = n1.shape[1]
    width = gv.shape[1]
    krows = model // UNITS
    deep, length = parts[0].shape[1:]
    top = deep - low_rows(krows)
    lead, half, fold = length - width, length // 2, krows // 3
    assert width - lead == half

    def kernel(where_ref, n1_ref, gv_ref, gat_ref, ga_ref, gb_ref, gf_ref, *rest):
        mixed_refs, rest = rest[: len(mixed)], rest[len(mixed) :]
        slot = slots(rest[len(parts) : 2 * len(parts)], MIXER_FIRST, 1)
        wide, other, folded, pieces = rest[2 * len(parts) :]
        wide[:, :width] = mm(n1_ref[...], gv_ref[...], TN).astype(BF)
        some = [mm(gat_ref[n * chunk : (n + 1) * chunk, :], one[...], TN) for n, one in enumerate(mixed_refs)]
        other[...] = sum(some).astype(BF)
        wide[:, width:] = other[:, :lead]
        pieces[0] = ga_ref[:UNITS, :] + gb_ref[:UNITS, :]
        pieces[1] = gf_ref[...]
        sub = lax.broadcasted_iota(jnp.int32, (fold, LANES), 0)
        for d in range(UNITS):
            for n in range(3):
                at = slice(d * krows + n * fold, d * krows + (n + 1) * fold)
                to = slice((2 * d + n // 2) * fold, (2 * d + n // 2 + 1) * fold)
                folded[to, (n % 2) * half : (n % 2 + 1) * half] = other[at, lead:]
            both = jnp.where(
                sub == 0, pieces[0, d : d + 1, :], jnp.where(sub == 1, pieces[1, d : d + 1, :], 0.0)
            )
            at = slice((2 * d + 1) * fold, (2 * d + 2) * fold)
            folded[at, half : half + LANES] = both.astype(BF)
            folded[at, half + LANES :] = jnp.zeros((fold, half - LANES), BF)
        for u in range(UNITS):
            (to,) = slot(u)
            to[top : top + krows, :] = wide[pl.ds(multiple(where_ref[u] * krows, 16), krows), :]
            to[top + krows :, :] = folded[pl.ds(multiple(where_ref[u] * 2 * fold, 16), 2 * fold), :]

    return run(
        kernel,
        "weight_grads",
        (where,),
        (n1, gv, gat, ga, ga_other, gf, *mixed, *parts),
        slot_shapes(deep, length, MIXER_FIRST, 1, False),
        (
            pltpu.VMEM((model, length), BF),
            pltpu.VMEM((model, width), BF),
            pltpu.VMEM((UNITS * 2 * fold, length), BF),
            pltpu.VMEM((2, UNITS, LANES), F32),
        ),
        aliases={7 + len(mixed) + n: n for n in range(len(parts))},
    )


class Ring:
    def __init__(self, size):
        self.size = size
        self.chips = size // 2
        n = self.chips
        self.order = list(range(0, n, 2)) + list(range(n - 1, 0, -2))
        me = lax.axis_index("dp")
        self.core = me % 2
        chip = me // 2
        self.at = jnp.where(chip % 2 == 0, chip // 2, n - 1 - chip // 2)
        self.up = self.pairs(1)
        self.down = self.pairs(-1)
        self.swap = [(d, d ^ 1) for d in range(size)]

    def pairs(self, step):
        n = self.chips
        return [
            (self.order[p] * 2 + c, self.order[(p + step) % n] * 2 + c) for p in range(n) for c in range(2)
        ]

    def device(self, offset, core):
        n = self.chips
        p = (self.at + jnp.asarray(offset, jnp.int32) + n) % n
        chip = jnp.where(p < (n + 1) // 2, 2 * p, 2 * (n - 1 - p) + 1)
        return chip * 2 + core

    def gathered(self):
        n = self.chips
        offsets = [0]
        for s in range(1, n // 2):
            offsets += [-s, s]
        offsets.append(n // 2)
        return jnp.concatenate([self.device(offsets, self.core), self.device(offsets, 1 - self.core)])

    def scattered(self):
        offsets = list(range(self.chips))
        return jnp.concatenate([self.device(offsets, self.core), self.device(offsets, 1 - self.core)])


class Gather:
    def __init__(self, ring, unit, cut):
        self.ring = ring
        self.rows = unit.shape[0]
        self.cut = cut
        self.last = [unit, unit]
        self.hops = 0
        self.mine = []
        self.theirs = []
        self.here = [unit]

    def values(self):
        return self.last

    def take(self, values):
        self.last = list(values)

    def hop(self, swap=True):
        ring = self.ring
        self.hops += 1
        up, down = self.last
        if self.hops == ring.chips // 2:
            up, down = up[: self.cut], down[self.cut :]
        self.last = [lax.ppermute(up, "dp", ring.up), lax.ppermute(down, "dp", ring.down)]
        if swap:
            self.swap()
        self.here = self.last

    def swap(self):
        self.theirs += [lax.ppermute(one, "dp", self.ring.swap) for one in self.here]
        self.mine += self.here
        self.here = []

    def finish(self):
        self.swap()
        return self.mine + self.theirs

    def shares(self):
        n = self.ring.chips
        own = [(u, 0, self.rows) for u in range(n - 1)]
        own += [(n - 1, 0, self.cut), (n - 1, self.cut, self.rows - self.cut)]
        return own + [(u + n, first, rows) for u, first, rows in own]


class Scatter:
    def __init__(self, ring, first, pieces, keep, *give):
        self.ring = ring
        self.keep = keep
        count = len(first) * pieces
        swapped = [lax.ppermute(one, "dp", ring.swap) for one in give[:count]]
        self.early = {k: swapped[n * pieces : (n + 1) * pieces] for n, k in enumerate(first)}
        self.first = first
        self.late = late_units(first)
        self.later = give[count:]
        self.got = {}
        self.last = {}

    def values(self):
        return list(self.last.values()) if self.last else [one for k in self.first for one in self.early[k]]

    def take(self, values):
        if self.last:
            self.last = dict(zip(self.last, values))
        else:
            pieces = len(values) // len(self.first)
            self.early = {k: values[n * pieces : (n + 1) * pieces] for n, k in enumerate(self.first)}

    def swap_all(self, *after):
        stack = lax.ppermute(tie(self.later[0], *after), "dp", self.ring.swap)
        self.got = {k: stack[n] for n, k in enumerate(self.late)}

    def hop(self, way, k):
        got = self.early[k][0] if k in self.early else self.got[k]
        value = self.keep[k].astype(F32) + got.astype(F32)
        if way in self.last:
            value = value + self.last[way].astype(F32)
        value = value.astype(BF)
        self.last[way] = lax.ppermute(value, "dp", self.ring.up if way == "up" else self.ring.down)
        return value

    def result(self):
        return self.keep, self.got[0], self.last["up"], self.last["down"]


def together(chains, *more):
    values = [one for chain in chains for one in chain.values()]
    tied = lax.optimization_barrier(tuple(values) + more)
    at = 0
    for chain in chains:
        count = len(chain.values())
        chain.take(tied[at : at + count])
        at += count
    return tied[at:]


def tie(value, *after):
    return lax.optimization_barrier((value,) + after)[0] if after else value


def shards(
    tokens,
    segment_ids,
    gain_attn,
    gain_ffn,
    random_scores,
    w_value,
    w_output,
    w_up,
    w_down,
    cotangent,
):
    devices = lax.axis_size("dp")
    second = lax.axis_index("mp")
    length = segment_ids.shape[1]
    heads = random_scores.shape[0]
    model = tokens.shape[1]
    width = w_value.shape[1]
    size = width // heads
    rows = length // UNITS
    krows = model // UNITS
    ring = devices == UNITS and devices // 2 <= RING_CHIPS
    flip = [(0, 1), (1, 0)]
    second_at = jnp.reshape(second, (1,)).astype(jnp.int32)
    plan = Unit(heads, rows, krows, length, model, width, w_up.shape[1])

    if ring:
        net = Ring(devices)
        far = net.chips // 2
        where_in = net.gathered().astype(jnp.int32)
        where_out = net.scattered().astype(jnp.int32)
        unit, wo_own = pack_unit(
            plan, second_at, random_scores, w_value, gain_attn, gain_ffn, w_up, w_down.T, w_output.T
        )
        one = Gather(net, unit, plan.cut)
        one.hop(False)
        wo_other = lax.ppermute(tie(wo_own, where_in, where_out), "mp", flip)
        wo_next = [lax.ppermute(wo_other, "dp", way) for way in (net.up, net.down)]
        one.here = list(fill_units(plan, second_at, [unit], [wo_other]))
        one.swap()
        wo_next = together([one], *wo_next)
        one.last = list(fill_units(plan, second_at, one.last, wo_next))
        one.here = one.last
        for step in range(1, far - 1):
            one.hop()
            together([one])
            one.here = one.last
        there = one.mine + one.theirs
        shares = one.shares()
        half = len(shares) // 2
        early = [n for n in range(len(one.mine))] + [half + n for n in range(len(one.theirs))]
        one.hop()
        begun = mixer_first(plan, where_in, tokens, segment_ids, there, [shares[n] for n in early], heads)
        begun = together([one], *begun)
        one.here = one.last
        units = one.finish()
        late = [n for n in range(len(shares)) if n not in early]
        near = late
        order = [n for n in range(len(shares)) if n not in near] + near
        units, shares = [units[n] for n in order], [shares[n] for n in order]
        late = [n for n, old in enumerate(order) if old in late]
    else:
        where_in = jnp.arange(UNITS, dtype=jnp.int32)
        where_out = where_in

        def gather(one, axis=0):
            return lax.all_gather(one.astype(BF), "dp", axis=axis, tiled=True)

        wo_own = w_output.T.astype(BF)
        wo_other = lax.ppermute(wo_own, "mp", flip)
        halves = [jnp.where(second == n, wo_own, wo_other) for n in range(2)]
        scores = gather(random_scores, 1).reshape(heads, UNITS, rows, length).transpose(1, 0, 2, 3)
        wide = [gather(one) for one in (w_value, *halves)]
        wide = jnp.concatenate(wide, axis=1).reshape(UNITS, krows, plan.wide)
        ffn = jnp.concatenate([gather(w_up), gather(w_down.T)], axis=1).reshape(UNITS, krows, -1)
        stack = [scores.reshape(UNITS, heads * rows, length)]
        for kind, column in plan.blocks:
            stack.append((ffn if kind == "ffn" else wide)[:, :, column : column + length])
        gains = jnp.stack([gather(gain_attn), gather(gain_ffn)]).reshape(2, UNITS, krows).transpose(1, 0, 2)
        gains = jnp.pad(gains, ((0, 0), (0, plan.fold - 2), (0, length - plan.gain_lane - krows)))
        tail = wide[:, :, plan.wide - plan.tail :].reshape(UNITS, 3, plan.fold, plan.tail)
        stack.append(jnp.concatenate([tail[:, 0], tail[:, 1], tail[:, 2], gains], axis=2))
        whole = jnp.concatenate(stack, axis=1)
        units = [whole[u] for u in range(UNITS)]
        shares = [(u, 0, plan.deep) for u in range(UNITS)]
        early, late, near = list(range(UNITS // 2)), list(range(UNITS // 2, UNITS)), []
        begun = mixer_first(plan, where_in, tokens, segment_ids, units[: UNITS // 2], shares[: UNITS // 2], heads)

    e, wv, _, va, sums, n1, gains, *mixed = mixer_forward(
        plan, where_in, segment_ids, begun, [units[n] for n in late], [shares[n] for n in late], heads, width
    )
    mixed_other = [lax.ppermute(one, "mp", flip) for one in mixed]
    w, gact, mixf, rb, wo = second_weights(plan, where_in, second_at, cotangent, sums, units, shares, len(near), size)
    backs, others, resids, n2s, acts, gpres = [], [], [], [], [], []
    for part in range(PARTS):
        *new, resid, n2, act, gpre = ffn_main(
            second_at, tokens, mixed[part], mixed_other[part], gact, gains, w, part, PARTS, 1
        )
        for back in new:
            backs.append(back)
            others.append(lax.ppermute(tie(back, *others[-1:]), "mp", flip))
        resids.append(resid)
        n2s.append(n2)
        acts.append(act)
        gpres.append(gpre)
    parts_two = ffn_grads(where_out, n2s, gpres, acts, cotangent)
    ffn_one, ffn_two = ffn_out(acts, w, 7 * length // 16)
    if ring:
        ffn_sum = Scatter(net, FFN_FIRST, 1, *parts_two)
        ffn_sum.swap_all(others[0], *ffn_sum.values())
        for step in range(2):
            ffn_sum.hop("down", far + step)
            ffn_sum.hop("up", far - 1 - step)
            ffn_one, ffn_two = together([ffn_sum], ffn_one, ffn_two)
    gres, gat, xh, gf = resid_back(
        backs, others, resids, cotangent, gains, wo, mixf, heads, size
    )
    one_other = lax.ppermute(tie(ffn_one, xh), "mp", flip)
    gv, part_one, part_two, ga = value_back(xh, rb, e, wv, tokens, size, length // 2)
    ga_other = lax.ppermute(ga, "mp", flip)
    if ring:
        for step in range(2, far - 1):
            ffn_sum.hop("down", far + step)
            ffn_sum.hop("up", far - 1 - step)
    parts_one = mixer_grads(where_out, xh, va, e, rb, krows)
    parts_one = weight_grads(where_out, parts_one, n1, gv, gat, mixed, ga, ga_other, gf)

    top = heads * rows
    if ring:
        score_sum = Scatter(net, MIXER_FIRST, 1, *parts_one)
        one_other, ffn_two = together([ffn_sum, score_sum], one_other, ffn_two)
        value = score_sum.hop("up", far)
        ffn_sum.hop("down", 2 * far - 1)
        score_sum.swap_all(value)
        two_other = lax.ppermute(ffn_two, "mp", flip)
        part_one, part_two = together([ffn_sum, score_sum], part_one, part_two)
        for step in range(1, far):
            score_sum.hop("up", far - step)
            score_sum.hop("down", far + step)
            if step == 1:
                part_other = [lax.ppermute(part_one, "mp", flip)]
                two_other, part_two = together([score_sum], two_other, part_two)
            elif step < far - 1:
                part_other.append(lax.ppermute(part_two, "mp", flip))
                (part_other[0],) = together([score_sum], part_other[0])
        out_up, out_down = ffn_result(*ffn_sum.result())
        out_scores, out_value, out_output, *out_gains = mixer_result(*score_sum.result(), heads, krows, width)
        out_down, out_output = out_down.T, out_output.T
        out_gain_one, out_gain_two = [one.reshape(krows) for one in out_gains]
    else:
        two_other = lax.ppermute(ffn_two, "mp", flip)
        part_other = [lax.ppermute(one, "mp", flip) for one in (part_one, part_two)]

        def scatter(one, axis=0):
            return lax.psum_scatter(one, "dp", scatter_dimension=axis, tiled=True)

        def whole(first, pieces, keep, *give):
            late = late_units(first)
            early, later = give[: len(first) * pieces], give[len(first) * pieces :]
            given = []
            for k in range(UNITS // 2):
                if k in first:
                    at = first.index(k) * pieces
                    given.append(jnp.concatenate(early[at : at + pieces]))
                else:
                    given.append(later[0][late.index(k)] if len(later) == 1 else later[late.index(k)])
            return jnp.concatenate([keep, jnp.stack(given)]).astype(F32)

        two = whole(FFN_FIRST, 1, *parts_two).reshape(model, -1)
        one = whole(MIXER_FIRST, 1, *parts_one)
        out_up = scatter(two[:, : two.shape[1] // 2])
        out_down = scatter(two[:, two.shape[1] // 2 :]).T
        scores = one[:, :top].reshape(UNITS, heads, rows, length).transpose(1, 0, 2, 3)
        out_scores = scatter(scores.reshape(heads, length, length), 1)
        out_value = scatter(one[:, top : top + krows, :width].reshape(model, width))
        low, fold, half = top + krows, krows // 3, length // 2
        folded = [one[:, low + n // 2 * fold : low + (n // 2 + 1) * fold, n % 2 * half :][:, :, :half] for n in range(3)]
        other = jnp.concatenate([one[:, top:low, width:], jnp.concatenate(folded, axis=1)], axis=2)
        out_output = scatter(other.reshape(model, width)).T
        out_gain_one = scatter(one[:, low + fold, half : half + krows].reshape(model))
        out_gain_two = scatter(one[:, low + fold + 1, half : half + krows].reshape(model))
    ffn = jnp.concatenate([ffn_one, ffn_two])
    ffn_other = jnp.concatenate([one_other, two_other])
    output = (jnp.concatenate(resids) + (ffn.astype(F32) + ffn_other.astype(F32))).astype(BF)
    backs = []
    begin = 0
    for mine, other in zip((part_one, part_two), part_other):
        grad_n1 = mine.astype(F32) + other.astype(F32)
        at = slice(begin, begin + mine.shape[0])
        begin = at.stop
        x = tokens[at].astype(F32)
        inv = lax.rsqrt(jnp.mean(x * x, axis=-1, keepdims=True) + EPSILON)
        z = gains[0:1, :] * grad_n1
        hat = x * inv
        backs.append((gres[at] + inv * (z - hat * jnp.mean(z * hat, axis=-1, keepdims=True))).astype(BF))
    grad_tokens = jnp.concatenate(backs)
    return (
        output,
        grad_tokens,
        out_gain_one,
        out_gain_two,
        out_scores,
        out_value,
        out_output,
        out_up,
        out_down,
    )


def solution(mesh):
    in_specs = (
        P("dp", None),
        P("dp", None),
        P("dp"),
        P("dp"),
        P("mp", "dp", None),
        P("dp", "mp"),
        P("mp", "dp"),
        P("dp", "mp"),
        P("mp", "dp"),
        P("dp", None),
    )
    out_specs = (
        P("dp", None),
        P("dp", None),
        P("dp"),
        P("dp"),
        P("mp", "dp", None),
        P("dp", "mp"),
        P("mp", "dp"),
        P("dp", "mp"),
        P("mp", "dp"),
    )
    return jax.shard_map(shards, mesh=mesh, in_specs=in_specs, out_specs=out_specs, check_vma=False)
```

```python
import jax
import jax.numpy as jnp
from jax import lax
from jax.experimental import pallas as pl
from jax.experimental.pallas import tpu as pltpu
from jax.sharding import PartitionSpec as P

EPSILON = 1e-06
NEGATIVE = -1e30
BF = jnp.bfloat16
F32 = jnp.float32
UNITS = 16
LANES = 128
PARTS = 2
RING_CHIPS = 8
VMEM_BYTES = 20 * 1024 * 1024
NT = (((1,), (1,)), ((), ()))
TN = (((0,), (0,)), ((), ()))
NN = (((1,), (0,)), ((), ()))


def mm(a, b, dims=NN):
    return lax.dot_general(a, b, dims, preferred_element_type=F32)


def run(kernel, name, scalars, arrays, outs, scratch=(), loose=(), loose_outs=(), aliases=None, near=0):
    held = [pltpu.with_memory_space_constraint(one, pltpu.VMEM) for one in arrays]
    results = [pltpu.VMEM(*one) for one in outs] + [jax.ShapeDtypeStruct(*one) for one in loose_outs]
    specs = [pl.BlockSpec(memory_space=pltpu.SMEM)] * len(scalars)
    specs += [pl.BlockSpec(memory_space=pltpu.VMEM)] * len(arrays)
    far = len(loose) - near
    specs += [pl.BlockSpec(memory_space=pltpu.HBM)] * far + [pl.BlockSpec(memory_space=pl.ANY)] * near
    loose = [pltpu.with_memory_space_constraint(one, pltpu.HBM) for one in loose[:far]] + list(loose[far:])
    out_specs = [pl.BlockSpec(memory_space=pltpu.VMEM)] * len(outs)
    out_specs += [pl.BlockSpec(memory_space=pl.ANY)] * len(loose_outs)
    return pl.pallas_call(
        kernel,
        out_shape=tuple(results),
        in_specs=specs,
        out_specs=tuple(out_specs),
        scratch_shapes=list(scratch),
        compiler_params=pltpu.CompilerParams(vmem_limit_bytes=VMEM_BYTES),
        cost_estimate=pl.CostEstimate(flops=1, bytes_accessed=1, transcendentals=0),
        input_output_aliases=aliases or {},
        name=name,
    )(*scalars, *held, *loose)


def gelu_pair(x):
    c = 0.7978845608028654
    a = 0.044715
    square = x * x
    t = jnp.tanh(c * x * (1.0 + a * square))
    half = 0.5 * (1.0 + t)
    return x * half, half + 0.5 * x * (1.0 - t * t) * (c * (1.0 + 3.0 * a * square))


def multiple(value, of):
    return pl.multiple_of(value, of)


class Unit:
    def __init__(self, heads, rows, krows, length, model, width, hidden):
        self.scores = heads * rows
        self.krows = krows
        self.length = length
        self.width = width
        self.hidden = hidden
        self.wide = width + model
        self.blocks = [("ffn", n * length) for n in range(2 * hidden // length)]
        self.blocks += [("proj", n * length) for n in range(self.wide // length)]
        self.tail = self.wide % length
        self.last = self.scores + krows * len(self.blocks)
        self.fold = krows // 3
        self.deep = self.last + self.fold
        self.cut = self.scores + krows * (2 * hidden // length // 3)
        self.gain_lane = 3 * self.tail

    def ffn_parts(self):
        parts = []
        for n, (kind, first) in enumerate(self.blocks):
            at = self.scores + n * self.krows
            if kind == "ffn":
                parts.append((at, 0, 0, first, self.krows, self.length))
            else:
                skip = max(self.width - first, 0)
                column = 2 * self.hidden + first + skip - self.width
                parts.append((at, skip, 0, column, self.krows, self.length - skip))
        for n in range(3):
            column = 2 * self.hidden + self.wide - self.tail - self.width
            parts.append((self.last, n * self.tail, n * self.fold, column, self.fold, self.tail))
        return parts

    def value_row(self):
        return self.scores + [kind for kind, _ in self.blocks].index("proj") * self.krows


def other_parts(plan, first):
    begin = plan.width + first * plan.width
    parts = []
    for n, (kind, column) in enumerate(plan.blocks):
        low, high = max(begin, column), min(begin + plan.width, column + plan.length)
        if kind == "proj" and low < high:
            parts.append((plan.scores + n * plan.krows, low - column, 0, low - begin, plan.krows, high - low))
    low = max(begin, plan.wide - plan.tail)
    if low < begin + plan.width:
        for n in range(3):
            lanes = n * plan.tail + low - (plan.wide - plan.tail)
            parts.append((plan.last, lanes, n * plan.fold, low - begin, plan.fold, begin + plan.width - low))
    return parts


def put_half(plan, out, half_ref, first):
    for row, lane, at, column, rows, lanes in other_parts(plan, first):
        out[row : row + rows, lane : lane + lanes] = half_ref[at : at + rows, column : column + lanes]


def pack_unit(plan, second, scores, wv, gain_one, gain_two, w_up, w_down, wo):
    inputs = (scores, wv, gain_one.reshape(1, -1), gain_two.reshape(1, -1), w_up, w_down, wo)
    count = len(inputs)
    krows, length, width = plan.krows, plan.length, plan.width
    per = plan.hidden // length
    assert plan.tail <= width

    def kernel(second_ref, *rest):
        out, wo_out, gains = rest[count : count + 3]
        held, sem = rest[count + 3 : -1], rest[-1]
        fetch(rest[:count], held, sem)
        s_ref, wv_ref, ga_ref, gf_ref, up_ref, down_ref, own_ref = held
        out[: plan.scores, :] = s_ref[...].reshape(plan.scores, length).astype(BF)
        for n, (kind, column) in enumerate(plan.blocks):
            at = slice(plan.scores + n * krows, plan.scores + (n + 1) * krows)
            if kind == "ffn":
                ref, first = (up_ref, column) if n < per else (down_ref, column - plan.hidden)
                out[at, :] = ref[:, first : first + length].astype(BF)
            else:
                out[at, :] = jnp.zeros((krows, length), BF)
        out[plan.last :, : plan.gain_lane] = jnp.zeros((plan.fold, plan.gain_lane), BF)
        out[plan.value_row() : plan.value_row() + krows, :width] = wv_ref[...].astype(BF)
        wo_out[...] = own_ref[...].astype(BF)
        for place in range(2):

            @pl.when(second_ref[0] == place)
            def _():
                put_half(plan, out, wo_out, place)

        gains[...] = jnp.zeros_like(gains)
        gains[0:1, :krows] = ga_ref[...]
        gains[1:2, :krows] = gf_ref[...]
        out[plan.last :, plan.gain_lane :] = gains[...].astype(BF)

    return run(
        kernel,
        "pack_unit",
        (second,),
        (),
        (((plan.deep, length), BF), ((krows, width), BF)),
        (
            pltpu.VMEM((plan.fold, length - plan.gain_lane), F32),
            *[pltpu.VMEM(one.shape, one.dtype) for one in inputs],
            pltpu.SemaphoreType.DMA((count,)),
        ),
        loose=inputs,
    )


def fill_units(plan, second, units, others):
    count = len(units)

    def kernel(second_ref, *rest):
        for place in range(2):

            @pl.when(second_ref[0] == 1 - place)
            def _():
                for n in range(count):
                    put_half(plan, rest[2 * count + n], rest[count + n], place)

    return run(
        kernel,
        "fill_units",
        (second,),
        (*units, *others),
        [(one.shape, BF) for one in units],
        aliases={1 + n: n for n in range(count)},
    )


def fetch(refs, held, sem):
    copies = [pltpu.make_async_copy(ref, to, sem.at[n]) for n, (ref, to) in enumerate(zip(refs, held))]
    for copy in copies:
        copy.start()
    for copy in copies:
        copy.wait()


def pick(units, shares, where_ref, parts, target, sem):
    copies = []
    for n, (u, first, rows) in enumerate(shares):
        owner = where_ref[u]
        for m, part in enumerate(parts):
            row, column, count, columns = part[0], part[1], part[-2], part[-1]
            if first <= row and row + count <= first + rows:
                source = units[n].at[pl.ds(row - first, count), pl.ds(column, columns)]
                copies.append(pltpu.make_async_copy(source, target(m, owner), sem.at[u, m]))
                copies[-1].start()
    return copies


def document_mask(seg_ref, same):
    length = same.shape[0]
    documents = (seg_ref[...] == lax.broadcasted_iota(jnp.int32, (LANES, length), 0)).astype(BF)
    same[...] = mm(documents, documents, TN)


def exponentials(where_ref, shares, sources, e_ref, same):
    heads, length, _ = e_ref.shape
    rows = length // UNITS

    def one_head(h, carry):
        for (u, _, _), (ref, first) in zip(shares, sources):
            at = pl.ds(multiple(where_ref[u] * rows, rows), rows)
            s = ref[pl.ds(multiple(first + h * rows, rows), rows), :].astype(F32)
            e_ref[h, at, :] = (jnp.exp(s) * same[at, :]).astype(BF)
        return carry

    lax.fori_loop(0, heads, one_head, 0)


def low_parts(plan):
    return [
        (plan.value_row(), 0, plan.krows, plan.width),
        (plan.last, plan.gain_lane, plan.fold, LANES),
    ]


def bring_low(plan, units, shares, where_ref, wv_ref, low_ref, sem):
    krows = plan.krows

    def target(m, owner):
        if m == 0:
            return wv_ref.at[pl.ds(multiple(owner * krows, 16), krows), :]
        return low_ref.at[owner]

    return pick(units, shares, where_ref, low_parts(plan), target, sem)


def mixer_first(plan, where, tokens, segments, units, shares, heads):
    length, model = tokens.shape
    rows = length // UNITS

    def kernel(where_ref, tok_ref, seg_ref, *rest):
        e_ref, wv_ref, low_ref, hat_ref, unit, same, sem, more = rest[len(units) :]
        top = heads * rows

        def target(m, owner):
            return unit.at[pl.ds(multiple(owner * top, top), top), :]

        came = pick(rest[: len(units)], shares, where_ref, [(0, 0, top, length)], target, sem)
        copies = bring_low(plan, rest[: len(units)], shares, where_ref, wv_ref, low_ref, more)
        document_mask(seg_ref, same)
        x = tok_ref[...].astype(F32)
        hat_ref[...] = x * lax.rsqrt(jnp.mean(x * x, axis=-1, keepdims=True) + EPSILON)
        for copy in came:
            copy.wait()
        sources = [(unit, where_ref[u] * top) for u, _, _ in shares]
        exponentials(where_ref, shares, sources, e_ref, same)
        for copy in copies:
            copy.wait()

    return run(
        kernel,
        "mixer_first",
        (where,),
        (tokens, segments),
        (
            ((heads, length, length), BF),
            ((model, plan.width), BF),
            ((UNITS, plan.fold, LANES), BF),
            ((length, model), F32),
        ),
        (
            pltpu.VMEM((heads * length, length), BF),
            pltpu.VMEM((length, length), F32),
            pltpu.SemaphoreType.DMA((UNITS, 1)),
            pltpu.SemaphoreType.DMA((UNITS, 2)),
        ),
        loose=units,
    )


def mixer_forward(plan, where, segments, early, units, shares, heads, width):
    length, model = early[3].shape
    size = width // heads
    krows = model // UNITS
    wide = heads * LANES
    count = len(units)

    def kernel(where_ref, seg_ref, e_old, wv_old, low_old, hat_ref, *rest):
        e_ref, wv_ref, low, va_ref, sums_ref, n1_ref, gains_ref, *mixed, pieces, same = rest[count:]
        for (u, first, rows), ref in zip(shares, rest[:count]):
            for m, (row, lane, deep, lanes) in enumerate(low_parts(plan)):
                if first <= row < first + rows:
                    part = ref[row - first : row - first + deep, lane : lane + lanes]
                    if m == 0:
                        wv_ref[pl.ds(multiple(where_ref[u] * krows, 16), krows), :] = part
                    else:
                        low[where_ref[u]] = part
        document_mask(seg_ref, same)
        scored = [n for n in range(count) if shares[n][1] == 0]
        exponentials(where_ref, [shares[n] for n in scored], [(rest[n], 0) for n in scored], e_ref, same)
        for d in range(UNITS):
            some = low[d].astype(F32)
            pieces[0, d : d + 1, :] = some[0:1, :]
            pieces[1, d : d + 1, :] = some[1:2, :]
        spread = (
            lax.broadcasted_iota(jnp.int32, (LANES, model), 1) % krows
            == lax.broadcasted_iota(jnp.int32, (LANES, model), 0)
        ).astype(BF)
        own = (
            lax.broadcasted_iota(jnp.int32, (UNITS, model), 1) // krows
            == lax.broadcasted_iota(jnp.int32, (UNITS, model), 0)
        )
        gains = []
        for t in range(2):
            full = jnp.where(own, mm(pieces[t].astype(BF), spread), 0.0)
            gains.append(jnp.sum(full, axis=0, keepdims=True))
            gains_ref[t : t + 1, :] = gains[t]
        n1_ref[...] = (hat_ref[...] * gains[0]).astype(BF)
        values = mm(n1_ref[...], wv_ref[...]).astype(BF)
        tail = (lax.broadcasted_iota(jnp.int32, (length, LANES - size), 1) < 2).astype(BF)
        for h in range(heads):
            va_ref[:, h * LANES : h * LANES + size] = values[:, h * size : (h + 1) * size]
            va_ref[:, h * LANES + size : (h + 1) * LANES] = tail

        for h in range(heads):
            lanes = slice(h * LANES, (h + 1) * LANES)
            sums = mm(e_ref[h], va_ref[:, lanes])
            sums_ref[:, lanes] = sums
            values = (sums * (1.0 / sums[:, size : size + 1]))[:, :size].astype(BF)
            for part, mixed_ref in enumerate(mixed):
                some = slice(part * (length // PARTS), (part + 1) * (length // PARTS))
                mixed_ref[:, h * size : (h + 1) * size] = values[some, :]

    return run(
        kernel,
        "mixer_forward",
        (where,),
        (segments, *early, *units),
        (
            ((heads, length, length), BF),
            ((model, width), BF),
            ((UNITS, plan.fold, LANES), BF),
            ((length, wide), BF),
            ((length, wide), F32),
            ((length, model), BF),
            ((2, model), F32),
            *[((length // PARTS, width), BF)] * PARTS,
        ),
        (
            pltpu.VMEM((2, UNITS, LANES), F32),
            pltpu.VMEM((length, length), F32),
        ),
        aliases={2: 0, 3: 1, 4: 2},
    )


def second_weights(plan, where, second, cotangent, sums, units, shares, near, size):
    length, model = cotangent.shape
    wide = sums.shape[1]
    hidden, krows, width = plan.hidden, plan.krows, plan.width
    piece = hidden // 3
    parts = plan.ffn_parts()

    def kernel(where_ref, second_ref, cot_ref, sums_ref, *rest):
        out, gact, mixf_ref, rb_ref, own_ref, sem = rest[len(units) :]

        def target(m, owner):
            _, _, row, column, rows, columns = parts[m]
            return out.at[pl.ds(multiple(owner * krows + row, 16), rows), pl.ds(column, columns)]

        copies = pick(rest[: len(units)], shares, where_ref, parts, target, sem)
        inside = lax.broadcasted_iota(jnp.int32, (length, LANES), 1) < size
        for h in range(wide // LANES):
            lanes = slice(h * LANES, (h + 1) * LANES)
            inverse = jnp.broadcast_to(1.0 / sums_ref[:, h * LANES + size : h * LANES + size + 1], (length, LANES))
            rb_ref[:, lanes] = inverse
            mixf_ref[:, lanes] = jnp.where(inside, sums_ref[:, lanes] * inverse, 0.0)
        for copy in copies:
            copy.wait()
        for j in range(3):
            cols = slice(j * piece, (j + 1) * piece)
            gact[:, cols] = mm(cot_ref[...], out[:, hidden + j * piece : hidden + (j + 1) * piece])
        own = out[:, pl.ds(multiple(2 * hidden + second_ref[0] * width, LANES), width)]
        own_ref[...] = jnp.zeros_like(own_ref)
        for h in range(width // size):
            own_ref[:, h * LANES : h * LANES + size] = own[:, h * size : (h + 1) * size]

    return run(
        kernel,
        "second_weights",
        (where, second),
        (cotangent, sums),
        (
            ((model, 2 * hidden + model), BF),
            ((length, hidden), F32),
            (sums.shape, F32),
            (sums.shape, F32),
            ((model, wide), BF),
        ),
        (pltpu.SemaphoreType.DMA((UNITS, len(parts))),),
        loose=units,
        near=near,
    )


def ffn_main(second, tokens, mixed_own, mixed_other, gact, gains, w, part, parts, before):
    length, model = tokens.shape
    width = mixed_own.shape[1]
    hidden = gact.shape[1]
    chunk = length // parts
    piece = hidden // 3
    at = slice(part * chunk, (part + 1) * chunk)

    def kernel(second_ref, tok_ref, own_ref, other_ref, gact_ref, gains_ref, w_ref, *rest):
        back_ref, resid_ref, n2_ref, act_ref, gpre_ref, mixed, acc = rest[len(before) :]
        first = second_ref[0]
        mixed[:, pl.ds(multiple(first * width, LANES), width)] = own_ref[...]
        mixed[:, pl.ds(multiple((1 - first) * width, LANES), width)] = other_ref[...]
        attn = mm(mixed[...], w_ref[:, 2 * hidden :], NT)
        resid = tok_ref[at, :].astype(F32) + attn
        resid_ref[...] = resid
        inv = lax.rsqrt(jnp.mean(resid * resid, axis=-1, keepdims=True) + EPSILON)
        n2_ref[at, :] = (resid * inv * gains_ref[1:2, :]).astype(BF)
        for j in range(hidden // piece):
            cols = slice(j * piece, (j + 1) * piece)
            act, slope = gelu_pair(mm(n2_ref[at, :], w_ref[:, cols]))
            act_ref[at, cols] = act.astype(BF)
            gpre_ref[at, cols] = (gact_ref[at, cols] * slope).astype(BF)
            term = mm(gpre_ref[at, cols], w_ref[:, cols], NT)
            if j == 0:
                acc[...] = term
            else:
                acc[...] += term
        back_ref[...] = acc[...].astype(BF)

    return run(
        kernel,
        "ffn_main",
        (second,),
        (tokens, mixed_own, mixed_other, gact, gains, w, *before),
        (
            ((chunk, model), BF),
            ((chunk, model), F32),
            ((length, model), BF),
            ((length, hidden), BF),
            ((length, hidden), BF),
        ),
        (
            pltpu.VMEM((chunk, 2 * width), BF),
            pltpu.VMEM((chunk, model), F32),
        ),
        aliases={7 + n: 2 + n for n in range(len(before))},
    )


def late_units(first):
    return [k for k in range(UNITS // 2) if k not in first]


def slots(refs, first, pieces):
    half = UNITS // 2
    count = len(first) * pieces
    keep, early, later = refs[0], refs[1 : 1 + count], refs[1 + count :]
    late = late_units(first)

    def slot(u):
        if u < half:
            return [keep.at[u]]
        k = u - half
        if k in first:
            at = first.index(k) * pieces
            return early[at : at + pieces]
        n = late.index(k)
        return [later[0].at[n] if len(later) == 1 else later[n]]

    return slot


def slot_shapes(rows, columns, first, pieces, apart):
    half = UNITS // 2
    early = [((rows, columns), BF)] * (len(first) * pieces)
    count = half - len(first)
    later = [((rows, columns), BF)] * count if apart else [((count, rows, columns), BF)]
    return [((half, rows, columns), BF), *early, *later]


FFN_FIRST = [UNITS // 4, UNITS // 4 - 1]
MIXER_FIRST = [UNITS // 4]


def result_kernel(name, keep, own, up, down, shapes, cut):
    def kernel(keep_ref, own_ref, up_ref, down_ref, *rest):
        outs, held, sem = rest[: len(shapes)], rest[len(shapes) : -1], rest[-1]

        def total(rows, columns):
            value = keep_ref[0, rows, columns].astype(F32) + own_ref[rows, columns].astype(F32)
            return value + up_ref[rows, columns].astype(F32) + down_ref[rows, columns].astype(F32)

        copies = []
        for n, (out, to) in enumerate(zip(outs, held)):
            cut(n, to, total)
            copies.append(pltpu.make_async_copy(to, out, sem.at[n]))
            copies[-1].start()
        for copy in copies:
            copy.wait()

    return run(
        kernel,
        name,
        (),
        (keep, own, up, down),
        (),
        (*[pltpu.VMEM(shape, F32) for shape in shapes], pltpu.SemaphoreType.DMA((len(shapes),))),
        loose_outs=[(shape, F32) for shape in shapes],
    )


def ffn_result(keep, own, up, down):
    _, rows, columns = keep.shape
    half = columns // 2

    def cut(n, to, total):
        to[...] = total(slice(None), slice(n * half, (n + 1) * half))

    return result_kernel("ffn_result", keep, own, up, down, [(rows, half)] * 2, cut)


def mixer_result(keep, own, up, down, heads, krows, width):
    _, deep, length = keep.shape
    top = deep - low_rows(krows)
    rows = top // heads
    lead, half, fold = length - width, length // 2, krows // 3
    shapes = [(heads, rows, length), (krows, width), (krows, width), (1, krows), (1, krows)]

    def cut(n, to, total):
        low = top + krows
        if n == 0:
            for h in range(heads):
                to[h] = total(slice(h * rows, (h + 1) * rows), slice(None))
        elif n == 1:
            to[...] = total(slice(top, low), slice(0, width))
        elif n == 2:
            to[:, :lead] = total(slice(top, low), slice(width, length))
            for m in range(3):
                some = slice(low + m // 2 * fold, low + (m // 2 + 1) * fold)
                to[m * fold : (m + 1) * fold, lead:] = total(some, slice(m % 2 * half, (m % 2 + 1) * half))
        else:
            to[...] = total(slice(low + fold, low + 2 * fold), slice(half, half + LANES))[n - 3 : n - 2, :krows]

    return result_kernel("mixer_result", keep, own, up, down, shapes, cut)


def ffn_out(act, w, cut):
    length, hidden = act.shape
    model = w.shape[0]

    def kernel(act_ref, w_ref, one, two):
        one[...] = mm(act_ref[:cut, :], w_ref[:, hidden : 2 * hidden], NT).astype(BF)
        two[...] = mm(act_ref[cut:, :], w_ref[:, hidden : 2 * hidden], NT).astype(BF)

    return run(kernel, "ffn_out", (), (act, w), (((cut, model), BF), ((length - cut, model), BF)))


def ffn_grads(where, n2, gpre, act, cotangent):
    model, hidden = n2.shape[1], act.shape[1]
    krows = model // UNITS

    def kernel(where_ref, cot_ref, n2_ref, gpre_ref, act_ref, *rest):
        slot = slots(rest[:-2], FFN_FIRST, 1)
        scr, sem = rest[-2:]
        piece = hidden // 3
        for j in range(3):
            cols = slice(j * piece, (j + 1) * piece)
            down = slice(hidden + j * piece, hidden + (j + 1) * piece)
            scr[:, cols] = mm(n2_ref[...], gpre_ref[:, cols], TN).astype(BF)
            scr[:, down] = mm(cot_ref[...], act_ref[:, cols], TN).astype(BF)
        copies = []
        for u in range(UNITS):
            at = pl.ds(multiple(where_ref[u] * krows, 16), krows)
            (to,) = slot(u)
            copies.append(pltpu.make_async_copy(scr.at[at, :], to, sem.at[u]))
            copies[-1].start()
        for copy in copies:
            copy.wait()

    return run(
        kernel,
        "ffn_grads",
        (where,),
        (cotangent, n2, gpre, act),
        (),
        (pltpu.VMEM((model, 2 * hidden), BF), pltpu.SemaphoreType.DMA((UNITS,))),
        loose_outs=slot_shapes(krows, 2 * hidden, FFN_FIRST, 1, False),
    )


def cut_gain(row, krows):
    model = row.shape[1]
    take = (
        lax.broadcasted_iota(jnp.int32, (model, LANES), 0) % krows
        == lax.broadcasted_iota(jnp.int32, (model, LANES), 1)
    ).astype(BF)
    own = (
        lax.broadcasted_iota(jnp.int32, (UNITS, model), 1) // krows
        == lax.broadcasted_iota(jnp.int32, (UNITS, model), 0)
    )
    high = row.astype(BF).astype(F32)
    pieces = mm(jnp.where(own, high, 0.0).astype(BF), take)
    return pieces + mm(jnp.where(own, row - high, 0.0).astype(BF), take)


def resid_back(back, other, resid, cotangent, gains, wo, mixf, part, heads, size, before):
    chunk, model = resid.shape
    wide = heads * LANES
    at = slice(part * chunk, (part + 1) * chunk)

    def kernel(cot_ref, gains_ref, wo_ref, mixf_ref, back_ref, other_ref, res_ref, *rest):
        gres_ref, gat_ref, xh_ref, gain_ref, gm = rest[len(before) :]
        g2 = back_ref[...].astype(F32) + other_ref[...].astype(F32)
        res = res_ref[...]
        inv = lax.rsqrt(jnp.mean(res * res, axis=-1, keepdims=True) + EPSILON)
        hat = res * inv
        total = jnp.sum((g2 * hat).reshape(chunk // 8, 8, model), axis=0)
        gain_ref[...] = total + rest[0][...] if before else total
        z = gains_ref[1:2, :] * g2
        corr = jnp.mean(z * hat, axis=-1, keepdims=True)
        gres = cot_ref[at, :].astype(F32) + inv * (z - hat * corr)
        gres_ref[...] = gres
        gat_ref[...] = gres.astype(BF)
        gm[...] = mm(gat_ref[...], wo_ref[...]).astype(BF)
        lane = lax.broadcasted_iota(jnp.int32, (chunk, LANES), 1)
        for h in range(heads):
            lanes = slice(h * LANES, (h + 1) * LANES)
            here = gm[:, lanes].astype(F32)
            inner = -jnp.sum(here * mixf_ref[at, lanes], axis=-1, keepdims=True)
            high = inner.astype(BF).astype(F32)
            xh_ref[:, lanes] = jnp.where(
                lane == size, high, jnp.where(lane == size + 1, inner - high, here)
            ).astype(BF)

    return run(
        kernel,
        "resid_back",
        (),
        (cotangent, gains, wo, mixf, back, other, resid, *before),
        (
            ((chunk, model), F32),
            ((chunk, model), BF),
            ((chunk, wide), BF),
            ((8, model), F32),
        ),
        (pltpu.VMEM((chunk, wide), BF),),
    )


def value_terms(xh_ref, rb_ref, e_ref, at, h):
    lanes = slice(h * LANES, (h + 1) * LANES)
    scaled = (xh_ref[:, lanes].astype(F32) * rb_ref[at, lanes]).astype(BF)
    return mm(e_ref[h, at, :], scaled, TN)


def value_first(xh, rb, e, size):
    heads, length, _ = e.shape
    at = slice(0, xh.shape[0])

    def kernel(xh_ref, rb_ref, e_ref, out):
        for h in range(heads):
            out[:, h * size : (h + 1) * size] = value_terms(xh_ref, rb_ref, e_ref, at, h)[:, :size]

    return run(kernel, "value_first", (), (xh, rb, e), (((length, heads * size), F32),))[0]


def value_back(xh, first, rb, e, wv, tokens, size, cut):
    length, model = tokens.shape
    heads = e.shape[0]
    width = heads * size
    krows = model // UNITS
    last = slice(length - xh.shape[0], length)

    def kernel(xh_ref, first_ref, rb_ref, e_ref, wv_ref, tok_ref, gv_ref, part_one, part_two, ga_ref, acc):
        acc[...] = jnp.zeros_like(acc)
        for h in range(heads):
            cols = slice(h * size, (h + 1) * size)
            term = value_terms(xh_ref, rb_ref, e_ref, last, h)[:, :size]
            gv_ref[:, cols] = (first_ref[:, cols] + term).astype(BF)

        for at, part_ref in ((slice(0, cut), part_one), (slice(cut, length), part_two)):
            part = mm(gv_ref[at, :], wv_ref[...], NT)
            part_ref[...] = part.astype(BF)
            x = tok_ref[at, :].astype(F32)
            inv = lax.rsqrt(jnp.mean(x * x, axis=-1, keepdims=True) + EPSILON)
            acc[...] += jnp.sum((part * (x * inv)).reshape((at.stop - at.start) // 8, 8, model), axis=0)

        ga_ref[...] = jnp.zeros_like(ga_ref)
        ga_ref[:UNITS, :] = cut_gain(jnp.sum(acc[...], axis=0, keepdims=True), krows)

    return run(
        kernel,
        "value_back",
        (),
        (xh, first, rb, e, wv, tokens),
        (
            ((length, width), BF),
            ((cut, model), BF),
            ((length - cut, model), BF),
            ((4 * UNITS, LANES), F32),
        ),
        (pltpu.VMEM((8, model), F32),),
    )


def low_rows(krows):
    return krows + 2 * (krows // 3)


def mixer_grads(where, xh, va, e, rb, krows, part, before):
    heads, length, _ = e.shape
    rows = length // UNITS
    chunk = xh.shape[0]
    owners = chunk // rows
    at = slice(part * chunk, (part + 1) * chunk)
    deep = heads * rows + low_rows(krows)

    def kernel(where_ref, xh_ref, va_ref, e_ref, rb_ref, *rest):
        outs, ds = rest[len(before) : -1], rest[-1]
        slot = slots(outs, MIXER_FIRST, 1)

        for h in range(heads):
            lanes = slice(h * LANES, (h + 1) * LANES)
            d = mm(xh_ref[:, lanes], va_ref[:, lanes], NT)
            inverse = rb_ref[at, lanes]
            for q in range(length // LANES):
                cols = slice(q * LANES, (q + 1) * LANES)
                ds[h, :, cols] = (e_ref[h, at, cols].astype(F32) * inverse * d[:, cols]).astype(BF)
        for u in range(UNITS):
            owner = where_ref[u] - part * owners

            @pl.when((owner >= 0) & (owner < owners))
            def _(u=u, owner=owner):
                some = pl.ds(multiple(owner * rows, rows), rows)
                for h in range(heads):
                    slot(u)[0][h * rows : (h + 1) * rows, :] = ds[h, some, :]

    return run(
        kernel,
        "mixer_grads",
        (where,),
        (xh, va, e, rb, *before),
        slot_shapes(deep, length, MIXER_FIRST, 1, False),
        (pltpu.VMEM((heads, chunk, length), BF),),
        aliases={5 + n: n for n in range(len(before))},
    )


def weight_grads(where, parts, n1, gv, gats, mixed, ga, ga_other, gain):
    length = n1.shape[0]
    model = n1.shape[1]
    width = gv.shape[1]
    krows = model // UNITS
    deep, length = parts[0].shape[1:]
    top = deep - low_rows(krows)
    lead, half, fold = length - width, length // 2, krows // 3
    assert width - lead == half

    def kernel(where_ref, n1_ref, gv_ref, ga_ref, gb_ref, gain_ref, *rest):
        gat_refs, mixed_refs, rest = rest[: len(mixed)], rest[len(mixed) : 2 * len(mixed)], rest[2 * len(mixed) :]
        slot = slots(rest[len(parts) : 2 * len(parts)], MIXER_FIRST, 1)
        wide, other, folded, pieces = rest[2 * len(parts) :]
        wide[:, :width] = mm(n1_ref[...], gv_ref[...], TN).astype(BF)
        some = [mm(gat_ref[...], one[...], TN) for gat_ref, one in zip(gat_refs, mixed_refs)]
        other[...] = sum(some).astype(BF)
        wide[:, width:] = other[:, :lead]
        pieces[0] = ga_ref[:UNITS, :] + gb_ref[:UNITS, :]
        pieces[1] = cut_gain(jnp.sum(gain_ref[...], axis=0, keepdims=True), krows)
        sub = lax.broadcasted_iota(jnp.int32, (fold, LANES), 0)
        for d in range(UNITS):
            for n in range(3):
                at = slice(d * krows + n * fold, d * krows + (n + 1) * fold)
                to = slice((2 * d + n // 2) * fold, (2 * d + n // 2 + 1) * fold)
                folded[to, (n % 2) * half : (n % 2 + 1) * half] = other[at, lead:]
            both = jnp.where(
                sub == 0, pieces[0, d : d + 1, :], jnp.where(sub == 1, pieces[1, d : d + 1, :], 0.0)
            )
            at = slice((2 * d + 1) * fold, (2 * d + 2) * fold)
            folded[at, half : half + LANES] = both.astype(BF)
            folded[at, half + LANES :] = jnp.zeros((fold, half - LANES), BF)
        for u in range(UNITS):
            (to,) = slot(u)
            to[top : top + krows, :] = wide[pl.ds(multiple(where_ref[u] * krows, 16), krows), :]
            to[top + krows :, :] = folded[pl.ds(multiple(where_ref[u] * 2 * fold, 16), 2 * fold), :]

    return run(
        kernel,
        "weight_grads",
        (where,),
        (n1, gv, ga, ga_other, gain, *gats, *mixed, *parts),
        slot_shapes(deep, length, MIXER_FIRST, 1, False),
        (
            pltpu.VMEM((model, length), BF),
            pltpu.VMEM((model, width), BF),
            pltpu.VMEM((UNITS * 2 * fold, length), BF),
            pltpu.VMEM((2, UNITS, LANES), F32),
        ),
        aliases={6 + 2 * len(mixed) + n: n for n in range(len(parts))},
    )


class Ring:
    def __init__(self, size):
        self.size = size
        self.chips = size // 2
        n = self.chips
        self.order = list(range(0, n, 2)) + list(range(n - 1, 0, -2))
        me = lax.axis_index("dp")
        self.core = me % 2
        chip = me // 2
        self.at = jnp.where(chip % 2 == 0, chip // 2, n - 1 - chip // 2)
        self.up = self.pairs(1)
        self.down = self.pairs(-1)
        self.swap = [(d, d ^ 1) for d in range(size)]

    def pairs(self, step):
        n = self.chips
        return [
            (self.order[p] * 2 + c, self.order[(p + step) % n] * 2 + c) for p in range(n) for c in range(2)
        ]

    def device(self, offset, core):
        n = self.chips
        p = (self.at + jnp.asarray(offset, jnp.int32) + n) % n
        chip = jnp.where(p < (n + 1) // 2, 2 * p, 2 * (n - 1 - p) + 1)
        return chip * 2 + core

    def gathered(self):
        n = self.chips
        offsets = [0]
        for s in range(1, n // 2):
            offsets += [-s, s]
        offsets.append(n // 2)
        return jnp.concatenate([self.device(offsets, self.core), self.device(offsets, 1 - self.core)])

    def scattered(self):
        offsets = list(range(self.chips))
        return jnp.concatenate([self.device(offsets, self.core), self.device(offsets, 1 - self.core)])


class Gather:
    def __init__(self, ring, unit, cut):
        self.ring = ring
        self.rows = unit.shape[0]
        self.cut = cut
        self.last = [unit, unit]
        self.hops = 0
        self.mine = []
        self.theirs = []
        self.here = [unit]

    def values(self):
        return self.last

    def take(self, values):
        self.last = list(values)

    def hop(self, swap=True):
        ring = self.ring
        self.hops += 1
        up, down = self.last
        if self.hops == ring.chips // 2:
            up, down = up[: self.cut], down[self.cut :]
        self.last = [lax.ppermute(up, "dp", ring.up), lax.ppermute(down, "dp", ring.down)]
        if swap:
            self.swap()
        self.here = self.last

    def swap(self):
        self.theirs += [lax.ppermute(one, "dp", self.ring.swap) for one in self.here]
        self.mine += self.here
        self.here = []

    def finish(self):
        self.swap()
        return self.mine + self.theirs

    def shares(self):
        n = self.ring.chips
        own = [(u, 0, self.rows) for u in range(n - 1)]
        own += [(n - 1, 0, self.cut), (n - 1, self.cut, self.rows - self.cut)]
        return own + [(u + n, first, rows) for u, first, rows in own]


class Scatter:
    def __init__(self, ring, first, pieces, keep, *give):
        self.ring = ring
        self.keep = keep
        count = len(first) * pieces
        swapped = [lax.ppermute(one, "dp", ring.swap) for one in give[:count]]
        self.early = {k: swapped[n * pieces : (n + 1) * pieces] for n, k in enumerate(first)}
        self.first = first
        self.late = late_units(first)
        self.later = give[count:]
        self.got = {}
        self.last = {}

    def values(self):
        return list(self.last.values()) if self.last else [one for k in self.first for one in self.early[k]]

    def take(self, values):
        if self.last:
            self.last = dict(zip(self.last, values))
        else:
            pieces = len(values) // len(self.first)
            self.early = {k: values[n * pieces : (n + 1) * pieces] for n, k in enumerate(self.first)}

    def swap_all(self, *after):
        stack = lax.ppermute(tie(self.later[0], *after), "dp", self.ring.swap)
        self.got = {k: stack[n] for n, k in enumerate(self.late)}

    def hop(self, way, k):
        got = self.early[k][0] if k in self.early else self.got[k]
        value = self.keep[k].astype(F32) + got.astype(F32)
        if way in self.last:
            value = value + self.last[way].astype(F32)
        value = value.astype(BF)
        self.last[way] = lax.ppermute(value, "dp", self.ring.up if way == "up" else self.ring.down)
        return value

    def result(self):
        return self.keep, self.got[0], self.last["up"], self.last["down"]


def together(chains, *more):
    values = [one for chain in chains for one in chain.values()]
    tied = lax.optimization_barrier(tuple(values) + more)
    at = 0
    for chain in chains:
        count = len(chain.values())
        chain.take(tied[at : at + count])
        at += count
    return tied[at:]


def tie(value, *after):
    return lax.optimization_barrier((value,) + after)[0] if after else value


def shards(
    tokens,
    segment_ids,
    gain_attn,
    gain_ffn,
    random_scores,
    w_value,
    w_output,
    w_up,
    w_down,
    cotangent,
):
    devices = lax.axis_size("dp")
    second = lax.axis_index("mp")
    length = segment_ids.shape[1]
    heads = random_scores.shape[0]
    model = tokens.shape[1]
    width = w_value.shape[1]
    size = width // heads
    rows = length // UNITS
    krows = model // UNITS
    ring = devices == UNITS and devices // 2 <= RING_CHIPS
    flip = [(0, 1), (1, 0)]
    second_at = jnp.reshape(second, (1,)).astype(jnp.int32)
    plan = Unit(heads, rows, krows, length, model, width, w_up.shape[1])

    if ring:
        net = Ring(devices)
        far = net.chips // 2
        where_in = net.gathered().astype(jnp.int32)
        where_out = net.scattered().astype(jnp.int32)
        unit, wo_own = pack_unit(
            plan, second_at, random_scores, w_value, gain_attn, gain_ffn, w_up, w_down.T, w_output.T
        )
        one = Gather(net, unit, plan.cut)
        one.hop(False)
        wo_other = lax.ppermute(tie(wo_own, where_in, where_out), "mp", flip)
        wo_next = [lax.ppermute(wo_other, "dp", way) for way in (net.up, net.down)]
        one.here = list(fill_units(plan, second_at, [unit], [wo_other]))
        one.swap()
        wo_next = together([one], *wo_next)
        one.last = list(fill_units(plan, second_at, one.last, wo_next))
        one.here = one.last
        for step in range(1, far - 1):
            one.hop()
            together([one])
            one.here = one.last
        there = one.mine + one.theirs
        shares = one.shares()
        half = len(shares) // 2
        early = [n for n in range(len(one.mine))] + [half + n for n in range(len(one.theirs))]
        one.hop()
        begun = mixer_first(plan, where_in, tokens, segment_ids, there, [shares[n] for n in early], heads)
        begun = together([one], *begun)
        one.here = one.last
        units = one.finish()
        late = [n for n in range(len(shares)) if n not in early]
        near = late
        order = [n for n in range(len(shares)) if n not in near] + near
        units, shares = [units[n] for n in order], [shares[n] for n in order]
        late = [n for n, old in enumerate(order) if old in late]
    else:
        where_in = jnp.arange(UNITS, dtype=jnp.int32)
        where_out = where_in

        def gather(one, axis=0):
            return lax.all_gather(one.astype(BF), "dp", axis=axis, tiled=True)

        wo_own = w_output.T.astype(BF)
        wo_other = lax.ppermute(wo_own, "mp", flip)
        halves = [jnp.where(second == n, wo_own, wo_other) for n in range(2)]
        scores = gather(random_scores, 1).reshape(heads, UNITS, rows, length).transpose(1, 0, 2, 3)
        wide = [gather(one) for one in (w_value, *halves)]
        wide = jnp.concatenate(wide, axis=1).reshape(UNITS, krows, plan.wide)
        ffn = jnp.concatenate([gather(w_up), gather(w_down.T)], axis=1).reshape(UNITS, krows, -1)
        stack = [scores.reshape(UNITS, heads * rows, length)]
        for kind, column in plan.blocks:
            stack.append((ffn if kind == "ffn" else wide)[:, :, column : column + length])
        gains = jnp.stack([gather(gain_attn), gather(gain_ffn)]).reshape(2, UNITS, krows).transpose(1, 0, 2)
        gains = jnp.pad(gains, ((0, 0), (0, plan.fold - 2), (0, length - plan.gain_lane - krows)))
        tail = wide[:, :, plan.wide - plan.tail :].reshape(UNITS, 3, plan.fold, plan.tail)
        stack.append(jnp.concatenate([tail[:, 0], tail[:, 1], tail[:, 2], gains], axis=2))
        whole = jnp.concatenate(stack, axis=1)
        units = [whole[u] for u in range(UNITS)]
        shares = [(u, 0, plan.deep) for u in range(UNITS)]
        early, late, near = list(range(UNITS // 2)), list(range(UNITS // 2, UNITS)), []
        begun = mixer_first(plan, where_in, tokens, segment_ids, units[: UNITS // 2], shares[: UNITS // 2], heads)

    e, wv, _, va, sums, n1, gains, *mixed = mixer_forward(
        plan, where_in, segment_ids, begun, [units[n] for n in late], [shares[n] for n in late], heads, width
    )
    mixed_other = [lax.ppermute(one, "mp", flip) for one in mixed]
    w, gact, mixf, rb, wo = second_weights(plan, where_in, second_at, cotangent, sums, units, shares, len(near), size)
    backs, others, resids, kept = [], [], [], []
    for part in range(PARTS):
        back, resid, *kept = ffn_main(
            second_at, tokens, mixed[part], mixed_other[part], gact, gains, w, part, PARTS, kept
        )
        backs.append(back)
        others.append(lax.ppermute(tie(back, *others[-1:]), "mp", flip))
        resids.append(resid)
    n2, act, gpre = kept
    parts_two = ffn_grads(where_out, n2, gpre, act, cotangent)
    early = resid_back(backs[0], others[0], resids[0], cotangent, gains, wo, mixf, 0, heads, size, [])
    ffn_one, ffn_two = ffn_out(tie(act, *early), w, 3 * length // 8)
    if ring:
        ffn_sum = Scatter(net, FFN_FIRST, 1, *parts_two)
        ffn_sum.swap_all(others[0], *ffn_sum.values())
        for step in range(2):
            ffn_sum.hop("down", far + step)
            ffn_sum.hop("up", far - 1 - step)
            if step == 0:
                ffn_one, ffn_two, *early = together([ffn_sum], ffn_one, ffn_two, *early)
    first_values = value_first(early[2], rb, e, size)
    parts_one = mixer_grads(where_out, early[2], va, e, rb, krows, 0, [])
    cot_late = tie(cotangent, first_values, *parts_one)
    final = resid_back(backs[1], others[1], resids[1], cot_late, gains, wo, mixf, 1, heads, size, early[3:])
    gres, gats = (early[0], final[0]), (early[1], final[1])
    xh = final[2]
    one_other = lax.ppermute(tie(ffn_one, xh), "mp", flip)
    gv, part_one, part_two, ga = value_back(xh, first_values, rb, e, wv, tokens, size, length // 2)
    ga_other = lax.ppermute(ga, "mp", flip)
    if ring:
        together([ffn_sum])
        for step in range(2, far - 1):
            ffn_sum.hop("down", far + step)
            ffn_sum.hop("up", far - 1 - step)
    parts_one = mixer_grads(where_out, xh, va, e, rb, krows, 1, parts_one)
    parts_one = weight_grads(where_out, parts_one, n1, gv, gats, mixed, ga, ga_other, final[3])

    top = heads * rows
    if ring:
        score_sum = Scatter(net, MIXER_FIRST, 1, *parts_one)
        one_other, ffn_two = together([ffn_sum, score_sum], one_other, ffn_two)
        value = score_sum.hop("up", far)
        ffn_sum.hop("down", 2 * far - 1)
        score_sum.swap_all(value)
        two_other = lax.ppermute(ffn_two, "mp", flip)
        part_one, part_two = together([score_sum], part_one, part_two)
        for step in range(1, far):
            score_sum.hop("up", far - step)
            score_sum.hop("down", far + step)
            if step == 1:
                part_other = [lax.ppermute(part_one, "mp", flip)]
                two_other, part_two = together([ffn_sum, score_sum], two_other, part_two)
            elif step < far - 1:
                part_other.append(lax.ppermute(part_two, "mp", flip))
                (part_other[0],) = together([score_sum], part_other[0])
        out_up, out_down = ffn_result(*ffn_sum.result())
        out_scores, out_value, out_output, *out_gains = mixer_result(*score_sum.result(), heads, krows, width)
        out_down, out_output = out_down.T, out_output.T
        out_gain_one, out_gain_two = [one.reshape(krows) for one in out_gains]
    else:
        two_other = lax.ppermute(ffn_two, "mp", flip)
        part_other = [lax.ppermute(one, "mp", flip) for one in (part_one, part_two)]

        def scatter(one, axis=0):
            return lax.psum_scatter(one, "dp", scatter_dimension=axis, tiled=True)

        def whole(first, pieces, keep, *give):
            late = late_units(first)
            early, later = give[: len(first) * pieces], give[len(first) * pieces :]
            given = []
            for k in range(UNITS // 2):
                if k in first:
                    at = first.index(k) * pieces
                    given.append(jnp.concatenate(early[at : at + pieces]))
                else:
                    given.append(later[0][late.index(k)] if len(later) == 1 else later[late.index(k)])
            return jnp.concatenate([keep, jnp.stack(given)]).astype(F32)

        two = whole(FFN_FIRST, 1, *parts_two).reshape(model, -1)
        one = whole(MIXER_FIRST, 1, *parts_one)
        out_up = scatter(two[:, : two.shape[1] // 2])
        out_down = scatter(two[:, two.shape[1] // 2 :]).T
        scores = one[:, :top].reshape(UNITS, heads, rows, length).transpose(1, 0, 2, 3)
        out_scores = scatter(scores.reshape(heads, length, length), 1)
        out_value = scatter(one[:, top : top + krows, :width].reshape(model, width))
        low, fold, half = top + krows, krows // 3, length // 2
        folded = [one[:, low + n // 2 * fold : low + (n // 2 + 1) * fold, n % 2 * half :][:, :, :half] for n in range(3)]
        other = jnp.concatenate([one[:, top:low, width:], jnp.concatenate(folded, axis=1)], axis=2)
        out_output = scatter(other.reshape(model, width)).T
        out_gain_one = scatter(one[:, low + fold, half : half + krows].reshape(model))
        out_gain_two = scatter(one[:, low + fold + 1, half : half + krows].reshape(model))
    ffn = jnp.concatenate([ffn_one, ffn_two])
    ffn_other = jnp.concatenate([one_other, two_other])
    output = (jnp.concatenate(resids) + (ffn.astype(F32) + ffn_other.astype(F32))).astype(BF)
    backs = []
    begin = 0
    for mine, other in zip((part_one, part_two), part_other):
        grad_n1 = mine.astype(F32) + other.astype(F32)
        at = slice(begin, begin + mine.shape[0])
        begin = at.stop
        x = tokens[at].astype(F32)
        inv = lax.rsqrt(jnp.mean(x * x, axis=-1, keepdims=True) + EPSILON)
        z = gains[0:1, :] * grad_n1
        hat = x * inv
        backs.append((gres[len(backs)] + inv * (z - hat * jnp.mean(z * hat, axis=-1, keepdims=True))).astype(BF))
    grad_tokens = jnp.concatenate(backs)
    return (
        output,
        grad_tokens,
        out_gain_one,
        out_gain_two,
        out_scores,
        out_value,
        out_output,
        out_up,
        out_down,
    )


def solution(mesh):
    in_specs = (
        P("dp", None),
        P("dp", None),
        P("dp"),
        P("dp"),
        P("mp", "dp", None),
        P("dp", "mp"),
        P("mp", "dp"),
        P("dp", "mp"),
        P("mp", "dp"),
        P("dp", None),
    )
    out_specs = (
        P("dp", None),
        P("dp", None),
        P("dp"),
        P("dp"),
        P("mp", "dp", None),
        P("dp", "mp"),
        P("mp", "dp"),
        P("dp", "mp"),
        P("mp", "dp"),
    )
    return jax.shard_map(shards, mesh=mesh, in_specs=in_specs, out_specs=out_specs, check_vma=False)
```

```python
import jax
import jax.numpy as jnp
from jax import lax
from jax.experimental import pallas as pl
from jax.experimental.pallas import tpu as pltpu
from jax.sharding import PartitionSpec as P

EPSILON = 1e-06
NEGATIVE = -1e30
BF = jnp.bfloat16
F32 = jnp.float32
UNITS = 16
LANES = 128
PARTS = 2
RING_CHIPS = 8
VMEM_BYTES = 20 * 1024 * 1024
NT = (((1,), (1,)), ((), ()))
TN = (((0,), (0,)), ((), ()))
NN = (((1,), (0,)), ((), ()))


def mm(a, b, dims=NN):
    return lax.dot_general(a, b, dims, preferred_element_type=F32)


def run(kernel, name, scalars, arrays, outs, scratch=(), loose=(), loose_outs=(), aliases=None, near=0):
    held = [pltpu.with_memory_space_constraint(one, pltpu.VMEM) for one in arrays]
    results = [pltpu.VMEM(*one) for one in outs] + [jax.ShapeDtypeStruct(*one) for one in loose_outs]
    specs = [pl.BlockSpec(memory_space=pltpu.SMEM)] * len(scalars)
    specs += [pl.BlockSpec(memory_space=pltpu.VMEM)] * len(arrays)
    far = len(loose) - near
    specs += [pl.BlockSpec(memory_space=pltpu.HBM)] * far + [pl.BlockSpec(memory_space=pl.ANY)] * near
    loose = [pltpu.with_memory_space_constraint(one, pltpu.HBM) for one in loose[:far]] + list(loose[far:])
    out_specs = [pl.BlockSpec(memory_space=pltpu.VMEM)] * len(outs)
    out_specs += [pl.BlockSpec(memory_space=pl.ANY)] * len(loose_outs)
    return pl.pallas_call(
        kernel,
        out_shape=tuple(results),
        in_specs=specs,
        out_specs=tuple(out_specs),
        scratch_shapes=list(scratch),
        compiler_params=pltpu.CompilerParams(vmem_limit_bytes=VMEM_BYTES),
        cost_estimate=pl.CostEstimate(flops=1, bytes_accessed=1, transcendentals=0),
        input_output_aliases=aliases or {},
        name=name,
    )(*scalars, *held, *loose)


def gelu_pair(x):
    c = 0.7978845608028654
    a = 0.044715
    square = x * x
    t = jnp.tanh(c * x * (1.0 + a * square))
    half = 0.5 * (1.0 + t)
    return x * half, half + 0.5 * x * (1.0 - t * t) * (c * (1.0 + 3.0 * a * square))


def multiple(value, of):
    return pl.multiple_of(value, of)


class Unit:
    def __init__(self, heads, rows, krows, length, model, width, hidden):
        self.scores = heads * rows
        self.krows = krows
        self.length = length
        self.width = width
        self.hidden = hidden
        self.wide = width + model
        self.blocks = [("ffn", n * length) for n in range(2 * hidden // length)]
        self.blocks += [("proj", n * length) for n in range(self.wide // length)]
        self.tail = self.wide % length
        self.last = self.scores + krows * len(self.blocks)
        self.fold = krows // 3
        self.deep = self.last + self.fold
        self.cut = self.scores + krows * (2 * hidden // length // 3)
        self.gain_lane = 3 * self.tail
        self.head = self.value_row()

    def projection_parts(self):
        parts = []
        for n, (kind, first) in enumerate(self.blocks):
            at = self.scores + n * self.krows
            if kind == "proj":
                skip = max(self.width - first, 0)
                parts.append((at, skip, 0, first + skip - self.width, self.krows, self.length - skip))
        for n in range(3):
            column = self.wide - self.tail - self.width
            parts.append((self.last, n * self.tail, n * self.fold, column, self.fold, self.tail))
        return parts

    def ffn_blocks(self, first, rows):
        inside = [
            n
            for n, (kind, _) in enumerate(self.blocks)
            if kind == "ffn" and first <= self.scores + n * self.krows < first + rows
        ]
        return (inside[0], len(inside)) if inside else (0, 0)

    def value_row(self):
        return self.scores + [kind for kind, _ in self.blocks].index("proj") * self.krows


def other_parts(plan, first):
    begin = plan.width + first * plan.width
    parts = []
    for n, (kind, column) in enumerate(plan.blocks):
        low, high = max(begin, column), min(begin + plan.width, column + plan.length)
        if kind == "proj" and low < high:
            parts.append((plan.scores + n * plan.krows, low - column, 0, low - begin, plan.krows, high - low))
    low = max(begin, plan.wide - plan.tail)
    if low < begin + plan.width:
        for n in range(3):
            lanes = n * plan.tail + low - (plan.wide - plan.tail)
            parts.append((plan.last, lanes, n * plan.fold, low - begin, plan.fold, begin + plan.width - low))
    return parts


def put_half(plan, low, half_ref, first):
    for row, lane, at, column, rows, lanes in other_parts(plan, first):
        row = row - plan.head
        low[row : row + rows, lane : lane + lanes] = half_ref[at : at + rows, column : column + lanes]


def pack_unit(plan, second, scores, wv, gain_one, gain_two, w_up, w_down, wo):
    inputs = (scores, wv, gain_one.reshape(1, -1), gain_two.reshape(1, -1), w_up, w_down, wo)
    count = len(inputs)
    krows, length, width = plan.krows, plan.length, plan.width
    per = plan.hidden // length
    assert plan.tail <= width

    def kernel(second_ref, *rest):
        out, low, wo_out, gains = rest[count : count + 4]
        held, sem = rest[count + 4 : -1], rest[-1]
        fetch(rest[:count], held, sem)
        s_ref, wv_ref, ga_ref, gf_ref, up_ref, down_ref, own_ref = held
        out[: plan.scores, :] = s_ref[...].reshape(plan.scores, length).astype(BF)
        for n, (kind, column) in enumerate(plan.blocks):
            at = slice(plan.scores + n * krows, plan.scores + (n + 1) * krows)
            if kind == "ffn":
                ref, first = (up_ref, column) if n < per else (down_ref, column - plan.hidden)
                out[at, :] = ref[:, first : first + length].astype(BF)
        low[...] = jnp.zeros_like(low)
        low[:krows, :width] = wv_ref[...].astype(BF)
        wo_out[...] = own_ref[...].astype(BF)
        for place in range(2):

            @pl.when(second_ref[0] == place)
            def _():
                put_half(plan, low, wo_out, place)

        gains[...] = jnp.zeros_like(gains)
        gains[0:1, :krows] = ga_ref[...]
        gains[1:2, :krows] = gf_ref[...]
        low[plan.last - plan.head :, plan.gain_lane :] = gains[...].astype(BF)

    return run(
        kernel,
        "pack_unit",
        (second,),
        (),
        (((plan.head, length), BF), ((plan.deep - plan.head, length), BF), ((krows, width), BF)),
        (
            pltpu.VMEM((plan.fold, length - plan.gain_lane), F32),
            *[pltpu.VMEM(one.shape, one.dtype) for one in inputs],
            pltpu.SemaphoreType.DMA((count,)),
        ),
        loose=inputs,
    )


def fill_low(plan, second, low, other):
    def kernel(second_ref, old, other_ref, out):
        for place in range(2):

            @pl.when(second_ref[0] == 1 - place)
            def _():
                put_half(plan, out, other_ref, place)

    return run(kernel, "fill_low", (second,), (low, other), ((low.shape, BF),), aliases={1: 0})[0]


def join_units(plan, uppers, lowers):
    count = len(uppers)

    def kernel(*refs):
        for n in range(count):
            out = refs[2 * count + n]
            out[: plan.head, :] = refs[n][...]
            out[plan.head :, :] = refs[count + n][...]

    return run(kernel, "join_units", (), (*uppers, *lowers), [((plan.deep, plan.length), BF)] * count)


def fetch(refs, held, sem):
    copies = [pltpu.make_async_copy(ref, to, sem.at[n]) for n, (ref, to) in enumerate(zip(refs, held))]
    for copy in copies:
        copy.start()
    for copy in copies:
        copy.wait()


def pick(units, shares, where_ref, parts, target, sem):
    copies = []
    for n, (u, first, rows) in enumerate(shares):
        owner = where_ref[u]
        for m, part in enumerate(parts):
            row, column, count, columns = part[0], part[1], part[-2], part[-1]
            if first <= row and row + count <= first + rows:
                source = units[n].at[pl.ds(row - first, count), pl.ds(column, columns)]
                copies.append(pltpu.make_async_copy(source, target(m, owner), sem.at[u, m]))
                copies[-1].start()
    return copies


def document_mask(seg_ref, same):
    length = same.shape[0]
    documents = (seg_ref[...] == lax.broadcasted_iota(jnp.int32, (LANES, length), 0)).astype(BF)
    same[...] = mm(documents, documents, TN)


def exponentials(where_ref, shares, sources, e_ref, same):
    heads, length, _ = e_ref.shape
    rows = length // UNITS

    def one_head(h, carry):
        for (u, _, _), (ref, first) in zip(shares, sources):
            at = pl.ds(multiple(where_ref[u] * rows, rows), rows)
            s = ref[pl.ds(multiple(first + h * rows, rows), rows), :].astype(F32)
            e_ref[h, at, :] = (jnp.exp(s) * same[at, :]).astype(BF)
        return carry

    lax.fori_loop(0, heads, one_head, 0)


def low_parts(plan):
    return [
        (plan.value_row(), 0, plan.krows, plan.width),
        (plan.last, plan.gain_lane, plan.fold, LANES),
    ]


def bring_low(plan, units, shares, where_ref, wv_ref, low_ref, sem):
    krows = plan.krows

    def target(m, owner):
        if m == 0:
            return wv_ref.at[pl.ds(multiple(owner * krows, 16), krows), :]
        return low_ref.at[owner]

    return pick(units, shares, where_ref, low_parts(plan), target, sem)


def mixer_first(plan, where, tokens, segments, units, shares, heads):
    length, model = tokens.shape
    rows = length // UNITS

    def kernel(where_ref, tok_ref, seg_ref, *rest):
        e_ref, wv_ref, low_ref, hat_ref, unit, same, sem, more = rest[len(units) :]
        top = heads * rows

        def target(m, owner):
            return unit.at[pl.ds(multiple(owner * top, top), top), :]

        came = pick(rest[: len(units)], shares, where_ref, [(0, 0, top, length)], target, sem)
        copies = bring_low(plan, rest[: len(units)], shares, where_ref, wv_ref, low_ref, more)
        document_mask(seg_ref, same)
        x = tok_ref[...].astype(F32)
        hat_ref[...] = x * lax.rsqrt(jnp.mean(x * x, axis=-1, keepdims=True) + EPSILON)
        for copy in came:
            copy.wait()
        sources = [(unit, where_ref[u] * top) for u, _, _ in shares]
        exponentials(where_ref, shares, sources, e_ref, same)
        for copy in copies:
            copy.wait()

    return run(
        kernel,
        "mixer_first",
        (where,),
        (tokens, segments),
        (
            ((heads, length, length), BF),
            ((model, plan.width), BF),
            ((UNITS, plan.fold, LANES), BF),
            ((length, model), F32),
        ),
        (
            pltpu.VMEM((heads * length, length), BF),
            pltpu.VMEM((length, length), F32),
            pltpu.SemaphoreType.DMA((UNITS, 1)),
            pltpu.SemaphoreType.DMA((UNITS, 2)),
        ),
        loose=units,
    )


def mixer_forward(plan, where, segments, early, units, shares, heads, width):
    length, model = early[3].shape
    size = width // heads
    krows = model // UNITS
    wide = heads * LANES
    count = len(units)

    def kernel(where_ref, seg_ref, e_old, wv_old, low_old, hat_ref, *rest):
        e_ref, wv_ref, low, va_ref, sums_ref, n1_ref, gains_ref, *mixed, pieces, same = rest[count:]
        for (u, first, rows), ref in zip(shares, rest[:count]):
            for m, (row, lane, deep, lanes) in enumerate(low_parts(plan)):
                if first <= row < first + rows:
                    part = ref[row - first : row - first + deep, lane : lane + lanes]
                    if m == 0:
                        wv_ref[pl.ds(multiple(where_ref[u] * krows, 16), krows), :] = part
                    else:
                        low[where_ref[u]] = part
        document_mask(seg_ref, same)
        scored = [n for n in range(count) if shares[n][1] == 0]
        exponentials(where_ref, [shares[n] for n in scored], [(rest[n], 0) for n in scored], e_ref, same)
        for d in range(UNITS):
            some = low[d].astype(F32)
            pieces[0, d : d + 1, :] = some[0:1, :]
            pieces[1, d : d + 1, :] = some[1:2, :]
        spread = (
            lax.broadcasted_iota(jnp.int32, (LANES, model), 1) % krows
            == lax.broadcasted_iota(jnp.int32, (LANES, model), 0)
        ).astype(BF)
        own = (
            lax.broadcasted_iota(jnp.int32, (UNITS, model), 1) // krows
            == lax.broadcasted_iota(jnp.int32, (UNITS, model), 0)
        )
        gains = []
        for t in range(2):
            full = jnp.where(own, mm(pieces[t].astype(BF), spread), 0.0)
            gains.append(jnp.sum(full, axis=0, keepdims=True))
            gains_ref[t : t + 1, :] = gains[t]
        n1_ref[...] = (hat_ref[...] * gains[0]).astype(BF)
        values = mm(n1_ref[...], wv_ref[...]).astype(BF)
        tail = (lax.broadcasted_iota(jnp.int32, (length, LANES - size), 1) < 2).astype(BF)
        for h in range(heads):
            va_ref[:, h * LANES : h * LANES + size] = values[:, h * size : (h + 1) * size]
            va_ref[:, h * LANES + size : (h + 1) * LANES] = tail

        for h in range(heads):
            lanes = slice(h * LANES, (h + 1) * LANES)
            sums = mm(e_ref[h], va_ref[:, lanes])
            sums_ref[:, lanes] = sums
            values = (sums * (1.0 / sums[:, size : size + 1]))[:, :size].astype(BF)
            for part, mixed_ref in enumerate(mixed):
                some = slice(part * (length // PARTS), (part + 1) * (length // PARTS))
                mixed_ref[:, h * size : (h + 1) * size] = values[some, :]

    return run(
        kernel,
        "mixer_forward",
        (where,),
        (segments, *early, *units),
        (
            ((heads, length, length), BF),
            ((model, width), BF),
            ((UNITS, plan.fold, LANES), BF),
            ((length, wide), BF),
            ((length, wide), F32),
            ((length, model), BF),
            ((2, model), F32),
            *[((length // PARTS, width), BF)] * PARTS,
        ),
        (
            pltpu.VMEM((2, UNITS, LANES), F32),
            pltpu.VMEM((length, length), F32),
        ),
        aliases={2: 0, 3: 1, 4: 2},
    )


def second_weights(plan, where, second, cotangent, sums, units, shares, near, size):
    length, model = cotangent.shape
    wide = sums.shape[1]
    hidden, krows, width = plan.hidden, plan.krows, plan.width
    parts = plan.projection_parts()
    blocks = 2 * hidden // length

    def kernel(where_ref, second_ref, cot_ref, sums_ref, *rest):
        out, wo_ref, gact, mixf_ref, rb_ref, own_ref, sem, more = rest[len(units) :]

        def target(m, owner):
            _, _, row, column, rows, columns = parts[m]
            return wo_ref.at[pl.ds(multiple(owner * krows + row, 16), rows), pl.ds(column, columns)]

        copies = []
        for n, (u, first, rows) in enumerate(shares):
            begin, count = plan.ffn_blocks(first, rows)
            if count:
                source = rest[n].at[pl.ds(plan.scores + begin * krows - first, count * krows), :]
                to = out.at[pl.ds(begin, count), pl.ds(multiple(where_ref[u] * krows, 16), krows), :]
                copies.append(pltpu.make_async_copy(source.reshape(count, krows, length), to, more.at[n]))
                copies[-1].start()
        copies += pick(rest[: len(units)], shares, where_ref, parts, target, sem)
        inside = lax.broadcasted_iota(jnp.int32, (length, LANES), 1) < size
        for h in range(wide // LANES):
            lanes = slice(h * LANES, (h + 1) * LANES)
            inverse = jnp.broadcast_to(1.0 / sums_ref[:, h * LANES + size : h * LANES + size + 1], (length, LANES))
            rb_ref[:, lanes] = inverse
            mixf_ref[:, lanes] = jnp.where(inside, sums_ref[:, lanes] * inverse, 0.0)
        for copy in copies:
            copy.wait()
        for j in range(blocks // 2):
            gact[:, j * length : (j + 1) * length] = mm(cot_ref[...], out[blocks // 2 + j])
        own = wo_ref[:, pl.ds(multiple(second_ref[0] * width, LANES), width)]
        own_ref[...] = jnp.zeros_like(own_ref)
        for h in range(width // size):
            own_ref[:, h * LANES : h * LANES + size] = own[:, h * size : (h + 1) * size]

    return run(
        kernel,
        "second_weights",
        (where, second),
        (cotangent, sums),
        (
            ((blocks, model, length), BF),
            ((model, model), BF),
            ((length, hidden), F32),
            (sums.shape, F32),
            (sums.shape, F32),
            ((model, wide), BF),
        ),
        (pltpu.SemaphoreType.DMA((UNITS, len(parts))), pltpu.SemaphoreType.DMA((len(units),))),
        loose=units,
        near=near,
    )


def ffn_main(second, tokens, mixed_own, mixed_other, gact, gains, w, wo, part, parts, before):
    length, model = tokens.shape
    width = mixed_own.shape[1]
    hidden = gact.shape[1]
    chunk = length // parts
    piece = w.shape[2]
    at = slice(part * chunk, (part + 1) * chunk)

    def kernel(second_ref, tok_ref, own_ref, other_ref, gact_ref, gains_ref, w_ref, wo_ref, *rest):
        back_ref, resid_ref, n2_ref, act_ref, gpre_ref, mixed = rest[len(before) :]
        first = second_ref[0]
        mixed[:, pl.ds(multiple(first * width, LANES), width)] = own_ref[...]
        mixed[:, pl.ds(multiple((1 - first) * width, LANES), width)] = other_ref[...]
        attn = mm(mixed[...], wo_ref[...], NT)
        resid = tok_ref[at, :].astype(F32) + attn
        resid_ref[...] = resid
        inv = lax.rsqrt(jnp.mean(resid * resid, axis=-1, keepdims=True) + EPSILON)
        n2 = (resid * inv * gains_ref[1:2, :]).astype(BF)
        n2_ref[at, :] = n2
        terms = []
        pres = [mm(n2, w_ref[j]) for j in range(hidden // piece)]
        for j in range(hidden // piece):
            cols = slice(j * piece, (j + 1) * piece)
            act, slope = gelu_pair(pres[j])
            act_ref[at, cols] = act.astype(BF)
            gpre = (gact_ref[at, cols] * slope).astype(BF)
            gpre_ref[at, cols] = gpre
            terms.append(mm(gpre, w_ref[j], NT))
        back_ref[...] = sum(terms).astype(BF)

    return run(
        kernel,
        "ffn_main",
        (second,),
        (tokens, mixed_own, mixed_other, gact, gains, w, wo, *before),
        (
            ((chunk, model), BF),
            ((chunk, model), F32),
            ((length, model), BF),
            ((length, hidden), BF),
            ((length, hidden), BF),
        ),
        (
            pltpu.VMEM((chunk, 2 * width), BF),
        ),
        aliases={8 + n: 2 + n for n in range(len(before))},
    )


def late_units(first):
    return [k for k in range(UNITS // 2) if k not in first]


def slots(refs, first, pieces):
    half = UNITS // 2
    count = len(first) * pieces
    keep, early, later = refs[0], refs[1 : 1 + count], refs[1 + count :]
    late = late_units(first)

    def slot(u):
        if u < half:
            return [keep.at[u]]
        k = u - half
        if k in first:
            at = first.index(k) * pieces
            return early[at : at + pieces]
        n = late.index(k)
        return [later[0].at[n] if len(later) == 1 else later[n]]

    return slot


def slot_shapes(rows, columns, first, pieces, apart):
    half = UNITS // 2
    early = [((rows, columns), BF)] * (len(first) * pieces)
    count = half - len(first)
    later = [((rows, columns), BF)] * count if apart else [((count, rows, columns), BF)]
    return [((half, rows, columns), BF), *early, *later]


FFN_FIRST = [UNITS // 4, UNITS // 4 - 1]
MIXER_FIRST = [UNITS // 4]


def result_kernel(name, keep, own, up, down, shapes, cut):
    def kernel(keep_ref, own_ref, up_ref, down_ref, *rest):
        outs, held, sem = rest[: len(shapes)], rest[len(shapes) : -1], rest[-1]

        def total(rows, columns):
            value = keep_ref[0, rows, columns].astype(F32) + own_ref[rows, columns].astype(F32)
            return value + up_ref[rows, columns].astype(F32) + down_ref[rows, columns].astype(F32)

        copies = []
        for n, (out, to) in enumerate(zip(outs, held)):
            cut(n, to, total)
            copies.append(pltpu.make_async_copy(to, out, sem.at[n]))
            copies[-1].start()
        for copy in copies:
            copy.wait()

    return run(
        kernel,
        name,
        (),
        (keep, own, up, down),
        (),
        (*[pltpu.VMEM(shape, F32) for shape in shapes], pltpu.SemaphoreType.DMA((len(shapes),))),
        loose_outs=[(shape, F32) for shape in shapes],
    )


def ffn_result(keep, own, up, down):
    _, rows, columns = keep.shape
    half = columns // 2

    def cut(n, to, total):
        to[...] = total(slice(None), slice(n * half, (n + 1) * half))

    return result_kernel("ffn_result", keep, own, up, down, [(rows, half)] * 2, cut)


def mixer_result(keep, own, up, down, heads, krows, width):
    _, deep, length = keep.shape
    top = deep - low_rows(krows)
    rows = top // heads
    lead, half, fold = length - width, length // 2, krows // 3
    shapes = [(heads, rows, length), (krows, width), (krows, width), (1, krows), (1, krows)]

    def cut(n, to, total):
        low = top + krows
        if n == 0:
            for h in range(heads):
                to[h] = total(slice(h * rows, (h + 1) * rows), slice(None))
        elif n == 1:
            to[...] = total(slice(top, low), slice(0, width))
        elif n == 2:
            to[:, :lead] = total(slice(top, low), slice(width, length))
            for m in range(3):
                some = slice(low + m // 2 * fold, low + (m // 2 + 1) * fold)
                to[m * fold : (m + 1) * fold, lead:] = total(some, slice(m % 2 * half, (m % 2 + 1) * half))
        else:
            to[...] = total(slice(low + fold, low + 2 * fold), slice(half, half + LANES))[n - 3 : n - 2, :krows]

    return result_kernel("mixer_result", keep, own, up, down, shapes, cut)


def ffn_out(act, w, cut):
    length, hidden = act.shape
    blocks, model, piece = w.shape

    def kernel(act_ref, w_ref, one, two):
        for out, at in ((one, slice(0, cut)), (two, slice(cut, length))):
            terms = [
                mm(act_ref[at, j * piece : (j + 1) * piece], w_ref[blocks // 2 + j], NT) for j in range(blocks // 2)
            ]
            out[...] = sum(terms).astype(BF)

    return run(kernel, "ffn_out", (), (act, w), (((cut, model), BF), ((length - cut, model), BF)))


def ffn_grads(where, n2, gpre, act, cotangent):
    model, hidden = n2.shape[1], act.shape[1]
    krows = model // UNITS

    def kernel(where_ref, cot_ref, n2_ref, gpre_ref, act_ref, *rest):
        slot = slots(rest[:-2], FFN_FIRST, 1)
        scr, sem = rest[-2:]
        piece = hidden // 3
        for j in range(3):
            cols = slice(j * piece, (j + 1) * piece)
            down = slice(hidden + j * piece, hidden + (j + 1) * piece)
            scr[:, cols] = mm(n2_ref[...], gpre_ref[:, cols], TN).astype(BF)
            scr[:, down] = mm(cot_ref[...], act_ref[:, cols], TN).astype(BF)
        for u in range(UNITS):
            at = pl.ds(multiple(where_ref[u] * krows, 16), krows)
            (to,) = slot(u)
            to[...] = scr[at, :]

    return run(
        kernel,
        "ffn_grads",
        (where,),
        (cotangent, n2, gpre, act),
        slot_shapes(krows, 2 * hidden, FFN_FIRST, 1, False),
        (pltpu.VMEM((model, 2 * hidden), BF), pltpu.SemaphoreType.DMA((UNITS,))),
    )


def cut_gain(row, krows):
    model = row.shape[1]
    take = (
        lax.broadcasted_iota(jnp.int32, (model, LANES), 0) % krows
        == lax.broadcasted_iota(jnp.int32, (model, LANES), 1)
    ).astype(BF)
    own = (
        lax.broadcasted_iota(jnp.int32, (UNITS, model), 1) // krows
        == lax.broadcasted_iota(jnp.int32, (UNITS, model), 0)
    )
    high = row.astype(BF).astype(F32)
    pieces = mm(jnp.where(own, high, 0.0).astype(BF), take)
    return pieces + mm(jnp.where(own, row - high, 0.0).astype(BF), take)


def resid_back(back, other, resid, cotangent, gains, wo, mixf, part, heads, size, before):
    chunk, model = resid.shape
    wide = heads * LANES
    at = slice(part * chunk, (part + 1) * chunk)

    def kernel(cot_ref, gains_ref, wo_ref, mixf_ref, back_ref, other_ref, res_ref, *rest):
        gres_ref, gat_ref, xh_ref, gain_ref, gm = rest[len(before) :]
        g2 = back_ref[...].astype(F32) + other_ref[...].astype(F32)
        res = res_ref[...]
        inv = lax.rsqrt(jnp.mean(res * res, axis=-1, keepdims=True) + EPSILON)
        hat = res * inv
        total = jnp.sum((g2 * hat).reshape(chunk // 8, 8, model), axis=0)
        gain_ref[...] = total + rest[0][...] if before else total
        z = gains_ref[1:2, :] * g2
        corr = jnp.mean(z * hat, axis=-1, keepdims=True)
        gres = cot_ref[at, :].astype(F32) + inv * (z - hat * corr)
        gres_ref[...] = gres
        gat_ref[...] = gres.astype(BF)
        gm[...] = mm(gat_ref[...], wo_ref[...]).astype(BF)
        lane = lax.broadcasted_iota(jnp.int32, (chunk, LANES), 1)
        for h in range(heads):
            lanes = slice(h * LANES, (h + 1) * LANES)
            here = gm[:, lanes].astype(F32)
            inner = -jnp.sum(here * mixf_ref[at, lanes], axis=-1, keepdims=True)
            high = inner.astype(BF).astype(F32)
            xh_ref[:, lanes] = jnp.where(
                lane == size, high, jnp.where(lane == size + 1, inner - high, here)
            ).astype(BF)

    return run(
        kernel,
        "resid_back",
        (),
        (cotangent, gains, wo, mixf, back, other, resid, *before),
        (
            ((chunk, model), F32),
            ((chunk, model), BF),
            ((chunk, wide), BF),
            ((8, model), F32),
        ),
        (pltpu.VMEM((chunk, wide), BF),),
    )


def value_terms(xh_ref, rb_ref, e_ref, at, h):
    lanes = slice(h * LANES, (h + 1) * LANES)
    scaled = (xh_ref[:, lanes].astype(F32) * rb_ref[at, lanes]).astype(BF)
    return mm(e_ref[h, at, :], scaled, TN)


def value_first(xh, rb, e, size):
    heads, length, _ = e.shape
    at = slice(0, xh.shape[0])

    def kernel(xh_ref, rb_ref, e_ref, out):
        for h in range(heads):
            out[:, h * size : (h + 1) * size] = value_terms(xh_ref, rb_ref, e_ref, at, h)[:, :size]

    return run(kernel, "value_first", (), (xh, rb, e), (((length, heads * size), F32),))[0]


def value_back(xh, first, rb, e, wv, tokens, size, cut):
    length, model = tokens.shape
    heads = e.shape[0]
    width = heads * size
    krows = model // UNITS
    last = slice(length - xh.shape[0], length)

    def kernel(xh_ref, first_ref, rb_ref, e_ref, wv_ref, tok_ref, gv_ref, part_one, part_two, ga_ref, acc):
        acc[...] = jnp.zeros_like(acc)
        for h in range(heads):
            cols = slice(h * size, (h + 1) * size)
            term = value_terms(xh_ref, rb_ref, e_ref, last, h)[:, :size]
            gv_ref[:, cols] = (first_ref[:, cols] + term).astype(BF)

        for at, part_ref in ((slice(0, cut), part_one), (slice(cut, length), part_two)):
            part = mm(gv_ref[at, :], wv_ref[...], NT)
            part_ref[...] = part.astype(BF)
            x = tok_ref[at, :].astype(F32)
            inv = lax.rsqrt(jnp.mean(x * x, axis=-1, keepdims=True) + EPSILON)
            acc[...] += jnp.sum((part * (x * inv)).reshape((at.stop - at.start) // 8, 8, model), axis=0)

        ga_ref[...] = jnp.zeros_like(ga_ref)
        ga_ref[:UNITS, :] = cut_gain(jnp.sum(acc[...], axis=0, keepdims=True), krows)

    return run(
        kernel,
        "value_back",
        (),
        (xh, first, rb, e, wv, tokens),
        (
            ((length, width), BF),
            ((cut, model), BF),
            ((length - cut, model), BF),
            ((4 * UNITS, LANES), F32),
        ),
        (pltpu.VMEM((8, model), F32),),
    )


def low_rows(krows):
    return krows + 2 * (krows // 3)


def mixer_grads(where, xh, va, e, rb, krows, part, before):
    heads, length, _ = e.shape
    rows = length // UNITS
    chunk = xh.shape[0]
    owners = chunk // rows
    at = slice(part * chunk, (part + 1) * chunk)
    deep = heads * rows + low_rows(krows)

    def kernel(where_ref, xh_ref, va_ref, e_ref, rb_ref, *rest):
        outs, ds = rest[len(before) : -1], rest[-1]
        slot = slots(outs, MIXER_FIRST, 1)

        for h in range(heads):
            lanes = slice(h * LANES, (h + 1) * LANES)
            d = mm(xh_ref[:, lanes], va_ref[:, lanes], NT)
            inverse = rb_ref[at, lanes]
            for q in range(length // LANES):
                cols = slice(q * LANES, (q + 1) * LANES)
                ds[h, :, cols] = (e_ref[h, at, cols].astype(F32) * inverse * d[:, cols]).astype(BF)
        for u in range(UNITS):
            owner = where_ref[u] - part * owners

            @pl.when((owner >= 0) & (owner < owners))
            def _(u=u, owner=owner):
                some = pl.ds(multiple(owner * rows, rows), rows)
                for h in range(heads):
                    slot(u)[0][h * rows : (h + 1) * rows, :] = ds[h, some, :]

    return run(
        kernel,
        "mixer_grads",
        (where,),
        (xh, va, e, rb, *before),
        slot_shapes(deep, length, MIXER_FIRST, 1, False),
        (pltpu.VMEM((heads, chunk, length), BF),),
        aliases={5 + n: n for n in range(len(before))},
    )


def weight_grads(where, parts, n1, gv, gats, mixed, ga, ga_other, gain):
    length = n1.shape[0]
    model = n1.shape[1]
    width = gv.shape[1]
    krows = model // UNITS
    deep, length = parts[0].shape[1:]
    top = deep - low_rows(krows)
    lead, half, fold = length - width, length // 2, krows // 3
    assert width - lead == half

    def kernel(where_ref, n1_ref, gv_ref, ga_ref, gb_ref, gain_ref, *rest):
        gat_refs, mixed_refs, rest = rest[: len(mixed)], rest[len(mixed) : 2 * len(mixed)], rest[2 * len(mixed) :]
        slot = slots(rest[len(parts) : 2 * len(parts)], MIXER_FIRST, 1)
        wide, other, folded, pieces = rest[2 * len(parts) :]
        wide[:, :width] = mm(n1_ref[...], gv_ref[...], TN).astype(BF)
        some = [mm(gat_ref[...], one[...], TN) for gat_ref, one in zip(gat_refs, mixed_refs)]
        other[...] = sum(some).astype(BF)
        wide[:, width:] = other[:, :lead]
        pieces[0] = ga_ref[:UNITS, :] + gb_ref[:UNITS, :]
        pieces[1] = cut_gain(jnp.sum(gain_ref[...], axis=0, keepdims=True), krows)
        sub = lax.broadcasted_iota(jnp.int32, (fold, LANES), 0)
        for d in range(UNITS):
            for n in range(3):
                at = slice(d * krows + n * fold, d * krows + (n + 1) * fold)
                to = slice((2 * d + n // 2) * fold, (2 * d + n // 2 + 1) * fold)
                folded[to, (n % 2) * half : (n % 2 + 1) * half] = other[at, lead:]
            both = jnp.where(
                sub == 0, pieces[0, d : d + 1, :], jnp.where(sub == 1, pieces[1, d : d + 1, :], 0.0)
            )
            at = slice((2 * d + 1) * fold, (2 * d + 2) * fold)
            folded[at, half : half + LANES] = both.astype(BF)
            folded[at, half + LANES :] = jnp.zeros((fold, half - LANES), BF)
        for u in range(UNITS):
            (to,) = slot(u)
            to[top : top + krows, :] = wide[pl.ds(multiple(where_ref[u] * krows, 16), krows), :]
            to[top + krows :, :] = folded[pl.ds(multiple(where_ref[u] * 2 * fold, 16), 2 * fold), :]

    return run(
        kernel,
        "weight_grads",
        (where,),
        (n1, gv, ga, ga_other, gain, *gats, *mixed, *parts),
        slot_shapes(deep, length, MIXER_FIRST, 1, False),
        (
            pltpu.VMEM((model, length), BF),
            pltpu.VMEM((model, width), BF),
            pltpu.VMEM((UNITS * 2 * fold, length), BF),
            pltpu.VMEM((2, UNITS, LANES), F32),
        ),
        aliases={6 + 2 * len(mixed) + n: n for n in range(len(parts))},
    )


class Ring:
    def __init__(self, size):
        self.size = size
        self.chips = size // 2
        n = self.chips
        self.order = list(range(0, n, 2)) + list(range(n - 1, 0, -2))
        me = lax.axis_index("dp")
        self.core = me % 2
        chip = me // 2
        self.at = jnp.where(chip % 2 == 0, chip // 2, n - 1 - chip // 2)
        self.up = self.pairs(1)
        self.down = self.pairs(-1)
        self.swap = [(d, d ^ 1) for d in range(size)]

    def pairs(self, step):
        n = self.chips
        return [
            (self.order[p] * 2 + c, self.order[(p + step) % n] * 2 + c) for p in range(n) for c in range(2)
        ]

    def device(self, offset, core):
        n = self.chips
        p = (self.at + jnp.asarray(offset, jnp.int32) + n) % n
        chip = jnp.where(p < (n + 1) // 2, 2 * p, 2 * (n - 1 - p) + 1)
        return chip * 2 + core

    def gathered(self):
        n = self.chips
        offsets = [0]
        for s in range(1, n // 2):
            offsets += [-s, s]
        offsets.append(n // 2)
        return jnp.concatenate([self.device(offsets, self.core), self.device(offsets, 1 - self.core)])

    def scattered(self):
        offsets = list(range(self.chips))
        return jnp.concatenate([self.device(offsets, self.core), self.device(offsets, 1 - self.core)])


class Gather:
    def __init__(self, ring, unit, cut):
        self.ring = ring
        self.rows = unit.shape[0]
        self.cut = cut
        self.last = [unit, unit]
        self.hops = 0
        self.mine = []
        self.theirs = []
        self.here = [unit]

    def values(self):
        return self.last

    def take(self, values):
        self.last = list(values)

    def arrived(self, units):
        self.hops = 1
        self.last = self.here = list(units)

    def hop(self):
        ring = self.ring
        self.hops += 1
        up, down = self.last
        if self.hops == ring.chips // 2:
            up, down = up[: self.cut], down[self.cut :]
        self.last = [lax.ppermute(up, "dp", ring.up), lax.ppermute(down, "dp", ring.down)]
        self.swap()
        self.here = self.last

    def swap(self):
        self.theirs += [lax.ppermute(one, "dp", self.ring.swap) for one in self.here]
        self.mine += self.here
        self.here = []

    def finish(self):
        self.swap()
        return self.mine + self.theirs

    def shares(self):
        n = self.ring.chips
        own = [(u, 0, self.rows) for u in range(n - 1)]
        own += [(n - 1, 0, self.cut), (n - 1, self.cut, self.rows - self.cut)]
        return own + [(u + n, first, rows) for u, first, rows in own]


class Scatter:
    def __init__(self, ring, first, pieces, keep, *give):
        self.ring = ring
        self.keep = keep
        count = len(first) * pieces
        swapped = [lax.ppermute(one, "dp", ring.swap) for one in give[:count]]
        self.early = {k: swapped[n * pieces : (n + 1) * pieces] for n, k in enumerate(first)}
        self.first = first
        self.late = late_units(first)
        self.later = give[count:]
        self.got = {}
        self.last = {}

    def values(self):
        return list(self.last.values()) if self.last else [one for k in self.first for one in self.early[k]]

    def take(self, values):
        if self.last:
            self.last = dict(zip(self.last, values))
        else:
            pieces = len(values) // len(self.first)
            self.early = {k: values[n * pieces : (n + 1) * pieces] for n, k in enumerate(self.first)}

    def swap_all(self, *after):
        stack = lax.ppermute(tie(self.later[0], *after), "dp", self.ring.swap)
        self.got = {k: stack[n] for n, k in enumerate(self.late)}

    def hop(self, way, k):
        got = self.early[k][0] if k in self.early else self.got[k]
        value = self.keep[k].astype(F32) + got.astype(F32)
        if way in self.last:
            value = value + self.last[way].astype(F32)
        value = value.astype(BF)
        self.last[way] = lax.ppermute(value, "dp", self.ring.up if way == "up" else self.ring.down)
        return value

    def result(self):
        return self.keep, self.got[0], self.last["up"], self.last["down"]


def together(chains, *more):
    values = [one for chain in chains for one in chain.values()]
    tied = lax.optimization_barrier(tuple(values) + more)
    at = 0
    for chain in chains:
        count = len(chain.values())
        chain.take(tied[at : at + count])
        at += count
    return tied[at:]


def tie(value, *after):
    return lax.optimization_barrier((value,) + after)[0] if after else value


def shards(
    tokens,
    segment_ids,
    gain_attn,
    gain_ffn,
    random_scores,
    w_value,
    w_output,
    w_up,
    w_down,
    cotangent,
):
    devices = lax.axis_size("dp")
    second = lax.axis_index("mp")
    length = segment_ids.shape[1]
    heads = random_scores.shape[0]
    model = tokens.shape[1]
    width = w_value.shape[1]
    size = width // heads
    rows = length // UNITS
    krows = model // UNITS
    ring = devices == UNITS and devices // 2 <= RING_CHIPS
    flip = [(0, 1), (1, 0)]
    second_at = jnp.reshape(second, (1,)).astype(jnp.int32)
    plan = Unit(heads, rows, krows, length, model, width, w_up.shape[1])

    if ring:
        net = Ring(devices)
        far = net.chips // 2
        where_in = net.gathered().astype(jnp.int32)
        where_out = net.scattered().astype(jnp.int32)
        upper, lower, wo_own = pack_unit(
            plan, second_at, random_scores, w_value, gain_attn, gain_ffn, w_up, w_down.T, w_output.T
        )
        ways = (net.up, net.down)
        uppers = [lax.ppermute(upper, "dp", way) for way in ways]
        wo_other = lax.ppermute(tie(wo_own, where_in, where_out), "mp", flip)
        lower = fill_low(plan, second_at, lower, wo_other)
        lowers = [lax.ppermute(lower, "dp", way) for way in ways]
        (unit,) = join_units(plan, [upper], [lower])
        one = Gather(net, unit, plan.cut)
        one.swap()
        uppers[0], uppers[1], *lowers = lax.optimization_barrier((*uppers, *lowers))
        one.arrived(join_units(plan, uppers, lowers))
        for step in range(1, far - 1):
            one.hop()
            together([one])
            one.here = one.last
        there = one.mine + one.theirs
        shares = one.shares()
        half = len(shares) // 2
        early = [n for n in range(len(one.mine))] + [half + n for n in range(len(one.theirs))]
        one.hop()
        begun = mixer_first(plan, where_in, tokens, segment_ids, there, [shares[n] for n in early], heads)
        begun = together([one], *begun)
        one.here = one.last
        units = one.finish()
        late = [n for n in range(len(shares)) if n not in early]
        near = late
        order = [n for n in range(len(shares)) if n not in near] + near
        units, shares = [units[n] for n in order], [shares[n] for n in order]
        late = [n for n, old in enumerate(order) if old in late]
    else:
        where_in = jnp.arange(UNITS, dtype=jnp.int32)
        where_out = where_in

        def gather(one, axis=0):
            return lax.all_gather(one.astype(BF), "dp", axis=axis, tiled=True)

        wo_own = w_output.T.astype(BF)
        wo_other = lax.ppermute(wo_own, "mp", flip)
        halves = [jnp.where(second == n, wo_own, wo_other) for n in range(2)]
        scores = gather(random_scores, 1).reshape(heads, UNITS, rows, length).transpose(1, 0, 2, 3)
        wide = [gather(one) for one in (w_value, *halves)]
        wide = jnp.concatenate(wide, axis=1).reshape(UNITS, krows, plan.wide)
        ffn = jnp.concatenate([gather(w_up), gather(w_down.T)], axis=1).reshape(UNITS, krows, -1)
        stack = [scores.reshape(UNITS, heads * rows, length)]
        for kind, column in plan.blocks:
            stack.append((ffn if kind == "ffn" else wide)[:, :, column : column + length])
        gains = jnp.stack([gather(gain_attn), gather(gain_ffn)]).reshape(2, UNITS, krows).transpose(1, 0, 2)
        gains = jnp.pad(gains, ((0, 0), (0, plan.fold - 2), (0, length - plan.gain_lane - krows)))
        tail = wide[:, :, plan.wide - plan.tail :].reshape(UNITS, 3, plan.fold, plan.tail)
        stack.append(jnp.concatenate([tail[:, 0], tail[:, 1], tail[:, 2], gains], axis=2))
        whole = jnp.concatenate(stack, axis=1)
        units = [whole[u] for u in range(UNITS)]
        shares = [(u, 0, plan.deep) for u in range(UNITS)]
        early, late, near = list(range(UNITS // 2)), list(range(UNITS // 2, UNITS)), []
        begun = mixer_first(plan, where_in, tokens, segment_ids, units[: UNITS // 2], shares[: UNITS // 2], heads)

    e, wv, _, va, sums, n1, gains, *mixed = mixer_forward(
        plan, where_in, segment_ids, begun, [units[n] for n in late], [shares[n] for n in late], heads, width
    )
    mixed_other = [lax.ppermute(one, "mp", flip) for one in mixed]
    w, wo_whole, gact, mixf, rb, wo = second_weights(plan, where_in, second_at, cotangent, sums, units, shares, len(near), size)
    backs, others, resids, kept = [], [], [], []
    for part in range(PARTS):
        back, resid, *kept = ffn_main(
            second_at, tokens, mixed[part], mixed_other[part], gact, gains, w, wo_whole, part, PARTS, kept
        )
        backs.append(back)
        others.append(lax.ppermute(tie(back, *others[-1:]), "mp", flip))
        resids.append(resid)
    n2, act, gpre = kept
    parts_two = ffn_grads(where_out, n2, gpre, act, cotangent)
    early = resid_back(backs[0], others[0], resids[0], cotangent, gains, wo, mixf, 0, heads, size, [])
    ffn_one, ffn_two = ffn_out(tie(act, *early), w, 3 * length // 8)
    first_values = value_first(early[2], rb, e, size)
    parts_one = mixer_grads(where_out, early[2], va, e, rb, krows, 0, [])
    if ring:
        ffn_sum = Scatter(net, FFN_FIRST, 1, *parts_two)
        ffn_sum.swap_all(others[0], *ffn_sum.values())
        for step in range(2):
            ffn_sum.hop("down", far + step)
            ffn_sum.hop("up", far - 1 - step)
            if step == 0:
                ffn_one, ffn_two, first_values, *more = together(
                    [ffn_sum], ffn_one, ffn_two, first_values, *early, *parts_one
                )
                early, parts_one = more[: len(early)], more[len(early) :]
    cot_late = tie(cotangent, first_values, *parts_one)
    final = resid_back(backs[1], others[1], resids[1], cot_late, gains, wo, mixf, 1, heads, size, early[3:])
    gres, gats = (early[0], final[0]), (early[1], final[1])
    xh = final[2]
    gv, part_one, part_two, ga = value_back(xh, first_values, rb, e, wv, tokens, size, length // 2)
    ga_other = lax.ppermute(ga, "mp", flip)
    one_other = lax.ppermute(tie(ffn_one, ga), "mp", flip)
    if ring:
        together([ffn_sum])
        for step in range(2, far - 1):
            ffn_sum.hop("down", far + step)
            ffn_sum.hop("up", far - 1 - step)
    parts_one = mixer_grads(where_out, xh, va, e, rb, krows, 1, parts_one)
    parts_one = weight_grads(where_out, parts_one, n1, gv, gats, mixed, ga, ga_other, final[3])

    top = heads * rows
    if ring:
        score_sum = Scatter(net, MIXER_FIRST, 1, *parts_one)
        one_other, ffn_two = together([ffn_sum, score_sum], one_other, ffn_two)
        value = score_sum.hop("up", far)
        ffn_sum.hop("down", 2 * far - 1)
        score_sum.swap_all(value)
        two_other = lax.ppermute(ffn_two, "mp", flip)
        part_one, part_two = together([score_sum], part_one, part_two)
        for step in range(1, far):
            score_sum.hop("up", far - step)
            score_sum.hop("down", far + step)
            if step == 1:
                part_other = [lax.ppermute(part_one, "mp", flip)]
                two_other, part_two = together([ffn_sum, score_sum], two_other, part_two)
            elif step < far - 1:
                part_other.append(lax.ppermute(part_two, "mp", flip))
                (part_other[0],) = together([score_sum], part_other[0])
        out_up, out_down = ffn_result(*ffn_sum.result())
        out_scores, out_value, out_output, *out_gains = mixer_result(*score_sum.result(), heads, krows, width)
        out_down, out_output = out_down.T, out_output.T
        out_gain_one, out_gain_two = [one.reshape(krows) for one in out_gains]
    else:
        two_other = lax.ppermute(ffn_two, "mp", flip)
        part_other = [lax.ppermute(one, "mp", flip) for one in (part_one, part_two)]

        def scatter(one, axis=0):
            return lax.psum_scatter(one, "dp", scatter_dimension=axis, tiled=True)

        def whole(first, pieces, keep, *give):
            late = late_units(first)
            early, later = give[: len(first) * pieces], give[len(first) * pieces :]
            given = []
            for k in range(UNITS // 2):
                if k in first:
                    at = first.index(k) * pieces
                    given.append(jnp.concatenate(early[at : at + pieces]))
                else:
                    given.append(later[0][late.index(k)] if len(later) == 1 else later[late.index(k)])
            return jnp.concatenate([keep, jnp.stack(given)]).astype(F32)

        two = whole(FFN_FIRST, 1, *parts_two).reshape(model, -1)
        one = whole(MIXER_FIRST, 1, *parts_one)
        out_up = scatter(two[:, : two.shape[1] // 2])
        out_down = scatter(two[:, two.shape[1] // 2 :]).T
        scores = one[:, :top].reshape(UNITS, heads, rows, length).transpose(1, 0, 2, 3)
        out_scores = scatter(scores.reshape(heads, length, length), 1)
        out_value = scatter(one[:, top : top + krows, :width].reshape(model, width))
        low, fold, half = top + krows, krows // 3, length // 2
        folded = [one[:, low + n // 2 * fold : low + (n // 2 + 1) * fold, n % 2 * half :][:, :, :half] for n in range(3)]
        other = jnp.concatenate([one[:, top:low, width:], jnp.concatenate(folded, axis=1)], axis=2)
        out_output = scatter(other.reshape(model, width)).T
        out_gain_one = scatter(one[:, low + fold, half : half + krows].reshape(model))
        out_gain_two = scatter(one[:, low + fold + 1, half : half + krows].reshape(model))
    ffn = jnp.concatenate([ffn_one, ffn_two])
    ffn_other = jnp.concatenate([one_other, two_other])
    output = (jnp.concatenate(resids) + (ffn.astype(F32) + ffn_other.astype(F32))).astype(BF)
    backs = []
    begin = 0
    for mine, other in zip((part_one, part_two), part_other):
        grad_n1 = mine.astype(F32) + other.astype(F32)
        at = slice(begin, begin + mine.shape[0])
        begin = at.stop
        x = tokens[at].astype(F32)
        inv = lax.rsqrt(jnp.mean(x * x, axis=-1, keepdims=True) + EPSILON)
        z = gains[0:1, :] * grad_n1
        hat = x * inv
        backs.append((gres[len(backs)] + inv * (z - hat * jnp.mean(z * hat, axis=-1, keepdims=True))).astype(BF))
    grad_tokens = jnp.concatenate(backs)
    return (
        output,
        grad_tokens,
        out_gain_one,
        out_gain_two,
        out_scores,
        out_value,
        out_output,
        out_up,
        out_down,
    )


def solution(mesh):
    in_specs = (
        P("dp", None),
        P("dp", None),
        P("dp"),
        P("dp"),
        P("mp", "dp", None),
        P("dp", "mp"),
        P("mp", "dp"),
        P("dp", "mp"),
        P("mp", "dp"),
        P("dp", None),
    )
    out_specs = (
        P("dp", None),
        P("dp", None),
        P("dp"),
        P("dp"),
        P("mp", "dp", None),
        P("dp", "mp"),
        P("mp", "dp"),
        P("dp", "mp"),
        P("mp", "dp"),
    )
    return jax.shard_map(shards, mesh=mesh, in_specs=in_specs, out_specs=out_specs, check_vma=False)
```

```python
import jax
import jax.numpy as jnp
from jax import lax
from jax.experimental import pallas as pl
from jax.experimental.pallas import tpu as pltpu
from jax.sharding import PartitionSpec as P

EPSILON = 1e-06
NEGATIVE = -1e30
BF = jnp.bfloat16
F32 = jnp.float32
UNITS = 16
LANES = 128
PARTS = 2
RING_CHIPS = 8
VMEM_BYTES = 20 * 1024 * 1024
NT = (((1,), (1,)), ((), ()))
TN = (((0,), (0,)), ((), ()))
NN = (((1,), (0,)), ((), ()))


def mm(a, b, dims=NN):
    return lax.dot_general(a, b, dims, preferred_element_type=F32)


def run(kernel, name, scalars, arrays, outs, scratch=(), loose=(), loose_outs=(), aliases=None, near=0):
    held = [pltpu.with_memory_space_constraint(one, pltpu.VMEM) for one in arrays]
    results = [pltpu.VMEM(*one) for one in outs] + [jax.ShapeDtypeStruct(*one) for one in loose_outs]
    specs = [pl.BlockSpec(memory_space=pltpu.SMEM)] * len(scalars)
    specs += [pl.BlockSpec(memory_space=pltpu.VMEM)] * len(arrays)
    far = len(loose) - near
    specs += [pl.BlockSpec(memory_space=pltpu.HBM)] * far + [pl.BlockSpec(memory_space=pl.ANY)] * near
    loose = [pltpu.with_memory_space_constraint(one, pltpu.HBM) for one in loose[:far]] + list(loose[far:])
    out_specs = [pl.BlockSpec(memory_space=pltpu.VMEM)] * len(outs)
    out_specs += [pl.BlockSpec(memory_space=pl.ANY)] * len(loose_outs)
    return pl.pallas_call(
        kernel,
        out_shape=tuple(results),
        in_specs=specs,
        out_specs=tuple(out_specs),
        scratch_shapes=list(scratch),
        compiler_params=pltpu.CompilerParams(vmem_limit_bytes=VMEM_BYTES),
        cost_estimate=pl.CostEstimate(flops=1, bytes_accessed=1, transcendentals=0),
        input_output_aliases=aliases or {},
        name=name,
    )(*scalars, *held, *loose)


def gelu_pair(x):
    c = 0.7978845608028654
    a = 0.044715
    square = x * x
    t = jnp.tanh(c * x * (1.0 + a * square))
    half = 0.5 * (1.0 + t)
    return x * half, half + 0.5 * x * (1.0 - t * t) * (c * (1.0 + 3.0 * a * square))


def multiple(value, of):
    return pl.multiple_of(value, of)


class Unit:
    def __init__(self, heads, rows, krows, length, model, width, hidden):
        self.scores = heads * rows
        self.krows = krows
        self.length = length
        self.width = width
        self.hidden = hidden
        self.wide = width + model
        self.blocks = [("ffn", n * length) for n in range(2 * hidden // length)]
        self.blocks += [("proj", n * length) for n in range(self.wide // length)]
        self.tail = self.wide % length
        self.last = self.scores + krows * len(self.blocks)
        self.fold = krows // 3
        self.deep = self.last + self.fold
        self.cut = self.scores + krows * (2 * hidden // length // 3)
        self.gain_lane = 3 * self.tail
        self.head = self.value_row()

    def projection_parts(self):
        parts = []
        for n, (kind, first) in enumerate(self.blocks):
            at = self.scores + n * self.krows
            if kind == "proj":
                skip = max(self.width - first, 0)
                parts.append((at, skip, 0, first + skip - self.width, self.krows, self.length - skip))
        for n in range(3):
            column = self.wide - self.tail - self.width
            parts.append((self.last, n * self.tail, n * self.fold, column, self.fold, self.tail))
        return parts

    def ffn_blocks(self, first, rows):
        inside = [
            n
            for n, (kind, _) in enumerate(self.blocks)
            if kind == "ffn" and first <= self.scores + n * self.krows < first + rows
        ]
        return (inside[0], len(inside)) if inside else (0, 0)

    def value_row(self):
        return self.scores + [kind for kind, _ in self.blocks].index("proj") * self.krows


def other_parts(plan, first):
    begin = plan.width + first * plan.width
    parts = []
    for n, (kind, column) in enumerate(plan.blocks):
        low, high = max(begin, column), min(begin + plan.width, column + plan.length)
        if kind == "proj" and low < high:
            parts.append((plan.scores + n * plan.krows, low - column, 0, low - begin, plan.krows, high - low))
    low = max(begin, plan.wide - plan.tail)
    if low < begin + plan.width:
        for n in range(3):
            lanes = n * plan.tail + low - (plan.wide - plan.tail)
            parts.append((plan.last, lanes, n * plan.fold, low - begin, plan.fold, begin + plan.width - low))
    return parts


def put_half(plan, low, half_ref, first):
    for row, lane, at, column, rows, lanes in other_parts(plan, first):
        row = row - plan.head
        low[row : row + rows, lane : lane + lanes] = half_ref[at : at + rows, column : column + lanes]


def pack_unit(plan, second, scores, wv, gain_one, gain_two, w_up, w_down, wo):
    inputs = (scores, wv, gain_one.reshape(1, -1), gain_two.reshape(1, -1), w_up, w_down, wo)
    count = len(inputs)
    krows, length, width = plan.krows, plan.length, plan.width
    per = plan.hidden // length
    assert plan.tail <= width

    def kernel(second_ref, *rest):
        out, low, wo_out, gains = rest[count : count + 4]
        held, sem = rest[count + 4 : -1], rest[-1]
        fetch(rest[:count], held, sem)
        s_ref, wv_ref, ga_ref, gf_ref, up_ref, down_ref, own_ref = held
        out[: plan.scores, :] = s_ref[...].reshape(plan.scores, length).astype(BF)
        for n, (kind, column) in enumerate(plan.blocks):
            at = slice(plan.scores + n * krows, plan.scores + (n + 1) * krows)
            if kind == "ffn":
                ref, first = (up_ref, column) if n < per else (down_ref, column - plan.hidden)
                out[at, :] = ref[:, first : first + length].astype(BF)
        low[...] = jnp.zeros_like(low)
        low[:krows, :width] = wv_ref[...].astype(BF)
        wo_out[...] = own_ref[...].astype(BF)
        for place in range(2):

            @pl.when(second_ref[0] == place)
            def _():
                put_half(plan, low, wo_out, place)

        gains[...] = jnp.zeros_like(gains)
        gains[0:1, :krows] = ga_ref[...]
        gains[1:2, :krows] = gf_ref[...]
        low[plan.last - plan.head :, plan.gain_lane :] = gains[...].astype(BF)

    return run(
        kernel,
        "pack_unit",
        (second,),
        (),
        (((plan.head, length), BF), ((plan.deep - plan.head, length), BF), ((krows, width), BF)),
        (
            pltpu.VMEM((plan.fold, length - plan.gain_lane), F32),
            *[pltpu.VMEM(one.shape, one.dtype) for one in inputs],
            pltpu.SemaphoreType.DMA((count,)),
        ),
        loose=inputs,
    )


def fill_low(plan, second, low, other):
    def kernel(second_ref, old, other_ref, out):
        for place in range(2):

            @pl.when(second_ref[0] == 1 - place)
            def _():
                put_half(plan, out, other_ref, place)

    return run(kernel, "fill_low", (second,), (low, other), ((low.shape, BF),), aliases={1: 0})[0]


def join_units(plan, uppers, lowers):
    count = len(uppers)

    def kernel(*refs):
        for n in range(count):
            out = refs[2 * count + n]
            out[: plan.head, :] = refs[n][...]
            out[plan.head :, :] = refs[count + n][...]

    return run(kernel, "join_units", (), (*uppers, *lowers), [((plan.deep, plan.length), BF)] * count)


def fetch(refs, held, sem):
    copies = [pltpu.make_async_copy(ref, to, sem.at[n]) for n, (ref, to) in enumerate(zip(refs, held))]
    for copy in copies:
        copy.start()
    for copy in copies:
        copy.wait()


def pick(units, shares, where_ref, parts, target, sem):
    copies = []
    for n, (u, first, rows) in enumerate(shares):
        owner = where_ref[u]
        for m, part in enumerate(parts):
            row, column, count, columns = part[0], part[1], part[-2], part[-1]
            if first <= row and row + count <= first + rows:
                source = units[n].at[pl.ds(row - first, count), pl.ds(column, columns)]
                copies.append(pltpu.make_async_copy(source, target(m, owner), sem.at[u, m]))
                copies[-1].start()
    return copies


def document_mask(seg_ref, same):
    length = same.shape[0]
    documents = (seg_ref[...] == lax.broadcasted_iota(jnp.int32, (LANES, length), 0)).astype(BF)
    same[...] = mm(documents, documents, TN)


def exponentials(where_ref, shares, sources, e_ref, same):
    heads, length, _ = e_ref.shape
    rows = length // UNITS

    def one_head(h, carry):
        for (u, _, _), (ref, first) in zip(shares, sources):
            at = pl.ds(multiple(where_ref[u] * rows, rows), rows)
            s = ref[pl.ds(multiple(first + h * rows, rows), rows), :].astype(F32)
            e_ref[h, at, :] = (jnp.exp(s) * same[at, :]).astype(BF)
        return carry

    lax.fori_loop(0, heads, one_head, 0)


def low_parts(plan):
    return [
        (plan.value_row(), 0, plan.krows, plan.width),
        (plan.last, plan.gain_lane, plan.fold, LANES),
    ]


def bring_low(plan, units, shares, where_ref, wv_ref, low_ref, sem):
    krows = plan.krows

    def target(m, owner):
        if m == 0:
            return wv_ref.at[pl.ds(multiple(owner * krows, 16), krows), :]
        return low_ref.at[owner]

    return pick(units, shares, where_ref, low_parts(plan), target, sem)


def mixer_first(plan, where, tokens, segments, units, shares, heads):
    length, model = tokens.shape
    rows = length // UNITS

    def kernel(where_ref, tok_ref, seg_ref, *rest):
        e_ref, wv_ref, low_ref, hat_ref, unit, same, sem, more = rest[len(units) :]
        top = heads * rows

        def target(m, owner):
            return unit.at[pl.ds(multiple(owner * top, top), top), :]

        came = pick(rest[: len(units)], shares, where_ref, [(0, 0, top, length)], target, sem)
        copies = bring_low(plan, rest[: len(units)], shares, where_ref, wv_ref, low_ref, more)
        document_mask(seg_ref, same)
        x = tok_ref[...].astype(F32)
        hat_ref[...] = x * lax.rsqrt(jnp.mean(x * x, axis=-1, keepdims=True) + EPSILON)
        for copy in came:
            copy.wait()
        sources = [(unit, where_ref[u] * top) for u, _, _ in shares]
        exponentials(where_ref, shares, sources, e_ref, same)
        for copy in copies:
            copy.wait()

    return run(
        kernel,
        "mixer_first",
        (where,),
        (tokens, segments),
        (
            ((heads, length, length), BF),
            ((model, plan.width), BF),
            ((UNITS, plan.fold, LANES), BF),
            ((length, model), F32),
        ),
        (
            pltpu.VMEM((heads * length, length), BF),
            pltpu.VMEM((length, length), F32),
            pltpu.SemaphoreType.DMA((UNITS, 1)),
            pltpu.SemaphoreType.DMA((UNITS, 2)),
        ),
        loose=units,
    )


def mixer_forward(plan, where, segments, early, units, shares, heads, width):
    length, model = early[3].shape
    size = width // heads
    krows = model // UNITS
    wide = heads * LANES
    count = len(units)

    def kernel(where_ref, seg_ref, e_old, wv_old, low_old, hat_ref, *rest):
        e_ref, wv_ref, low, va_ref, sums_ref, n1_ref, gains_ref, *mixed, pieces, same = rest[count:]
        for (u, first, rows), ref in zip(shares, rest[:count]):
            for m, (row, lane, deep, lanes) in enumerate(low_parts(plan)):
                if first <= row < first + rows:
                    part = ref[row - first : row - first + deep, lane : lane + lanes]
                    if m == 0:
                        wv_ref[pl.ds(multiple(where_ref[u] * krows, 16), krows), :] = part
                    else:
                        low[where_ref[u]] = part
        document_mask(seg_ref, same)
        scored = [n for n in range(count) if shares[n][1] == 0]
        exponentials(where_ref, [shares[n] for n in scored], [(rest[n], 0) for n in scored], e_ref, same)
        for d in range(UNITS):
            some = low[d].astype(F32)
            pieces[0, d : d + 1, :] = some[0:1, :]
            pieces[1, d : d + 1, :] = some[1:2, :]
        spread = (
            lax.broadcasted_iota(jnp.int32, (LANES, model), 1) % krows
            == lax.broadcasted_iota(jnp.int32, (LANES, model), 0)
        ).astype(BF)
        own = (
            lax.broadcasted_iota(jnp.int32, (UNITS, model), 1) // krows
            == lax.broadcasted_iota(jnp.int32, (UNITS, model), 0)
        )
        gains = []
        for t in range(2):
            full = jnp.where(own, mm(pieces[t].astype(BF), spread), 0.0)
            gains.append(jnp.sum(full, axis=0, keepdims=True))
            gains_ref[t : t + 1, :] = gains[t]
        n1_ref[...] = (hat_ref[...] * gains[0]).astype(BF)
        values = mm(n1_ref[...], wv_ref[...]).astype(BF)
        tail = (lax.broadcasted_iota(jnp.int32, (length, LANES - size), 1) < 2).astype(BF)
        for h in range(heads):
            va_ref[:, h * LANES : h * LANES + size] = values[:, h * size : (h + 1) * size]
            va_ref[:, h * LANES + size : (h + 1) * LANES] = tail

        for h in range(heads):
            lanes = slice(h * LANES, (h + 1) * LANES)
            sums = mm(e_ref[h], va_ref[:, lanes])
            sums_ref[:, lanes] = sums
            values = (sums * (1.0 / sums[:, size : size + 1]))[:, :size].astype(BF)
            for part, mixed_ref in enumerate(mixed):
                some = slice(part * (length // PARTS), (part + 1) * (length // PARTS))
                mixed_ref[:, h * size : (h + 1) * size] = values[some, :]

    return run(
        kernel,
        "mixer_forward",
        (where,),
        (segments, *early, *units),
        (
            ((heads, length, length), BF),
            ((model, width), BF),
            ((UNITS, plan.fold, LANES), BF),
            ((length, wide), BF),
            ((length, wide), F32),
            ((length, model), BF),
            ((2, model), F32),
            *[((length // PARTS, width), BF)] * PARTS,
        ),
        (
            pltpu.VMEM((2, UNITS, LANES), F32),
            pltpu.VMEM((length, length), F32),
        ),
        aliases={2: 0, 3: 1, 4: 2},
    )


def second_weights(plan, where, second, cotangent, sums, units, shares, near, size):
    length, model = cotangent.shape
    wide = sums.shape[1]
    hidden, krows, width = plan.hidden, plan.krows, plan.width
    parts = plan.projection_parts()
    blocks = 2 * hidden // length

    def kernel(where_ref, second_ref, cot_ref, sums_ref, *rest):
        out, wo_ref, gact, mixf_ref, rb_ref, own_ref, sem, more = rest[len(units) :]

        def target(m, owner):
            _, _, row, column, rows, columns = parts[m]
            return wo_ref.at[pl.ds(multiple(owner * krows + row, 16), rows), pl.ds(column, columns)]

        copies = []
        for n, (u, first, rows) in enumerate(shares):
            begin, count = plan.ffn_blocks(first, rows)
            if count:
                source = rest[n].at[pl.ds(plan.scores + begin * krows - first, count * krows), :]
                to = out.at[pl.ds(begin, count), pl.ds(multiple(where_ref[u] * krows, 16), krows), :]
                copies.append(pltpu.make_async_copy(source.reshape(count, krows, length), to, more.at[n]))
                copies[-1].start()
        copies += pick(rest[: len(units)], shares, where_ref, parts, target, sem)
        inside = lax.broadcasted_iota(jnp.int32, (length, LANES), 1) < size
        for h in range(wide // LANES):
            lanes = slice(h * LANES, (h + 1) * LANES)
            inverse = jnp.broadcast_to(1.0 / sums_ref[:, h * LANES + size : h * LANES + size + 1], (length, LANES))
            rb_ref[:, lanes] = inverse
            mixf_ref[:, lanes] = jnp.where(inside, sums_ref[:, lanes] * inverse, 0.0)
        for copy in copies:
            copy.wait()
        for j in range(blocks // 2):
            gact[:, j * length : (j + 1) * length] = mm(cot_ref[...], out[blocks // 2 + j])
        own = wo_ref[:, pl.ds(multiple(second_ref[0] * width, LANES), width)]
        own_ref[...] = jnp.zeros_like(own_ref)
        for h in range(width // size):
            own_ref[:, h * LANES : h * LANES + size] = own[:, h * size : (h + 1) * size]

    return run(
        kernel,
        "second_weights",
        (where, second),
        (cotangent, sums),
        (
            ((blocks, model, length), BF),
            ((model, model), BF),
            ((length, hidden), F32),
            (sums.shape, F32),
            (sums.shape, F32),
            ((model, wide), BF),
        ),
        (pltpu.SemaphoreType.DMA((UNITS, len(parts))), pltpu.SemaphoreType.DMA((len(units),))),
        loose=units,
        near=near,
    )


def ffn_main(second, tokens, mixed_own, mixed_other, gact, gains, w, wo, part, parts, before):
    length, model = tokens.shape
    width = mixed_own.shape[1]
    hidden = gact.shape[1]
    chunk = length // parts
    piece = w.shape[2]
    at = slice(part * chunk, (part + 1) * chunk)

    def kernel(second_ref, tok_ref, own_ref, other_ref, gact_ref, gains_ref, w_ref, wo_ref, *rest):
        back_ref, resid_ref, n2_ref, act_ref, gpre_ref, mixed = rest[len(before) :]
        first = second_ref[0]
        mixed[:, pl.ds(multiple(first * width, LANES), width)] = own_ref[...]
        mixed[:, pl.ds(multiple((1 - first) * width, LANES), width)] = other_ref[...]
        attn = mm(mixed[...], wo_ref[...], NT)
        resid = tok_ref[at, :].astype(F32) + attn
        resid_ref[...] = resid
        inv = lax.rsqrt(jnp.mean(resid * resid, axis=-1, keepdims=True) + EPSILON)
        n2 = (resid * inv * gains_ref[1:2, :]).astype(BF)
        n2_ref[at, :] = n2
        terms = []
        pres = [mm(n2, w_ref[j]) for j in range(hidden // piece)]
        for j in range(hidden // piece):
            cols = slice(j * piece, (j + 1) * piece)
            act, slope = gelu_pair(pres[j])
            act_ref[at, cols] = act.astype(BF)
            gpre = (gact_ref[at, cols] * slope).astype(BF)
            gpre_ref[at, cols] = gpre
            terms.append(mm(gpre, w_ref[j], NT))
        back_ref[...] = sum(terms).astype(BF)

    return run(
        kernel,
        "ffn_main",
        (second,),
        (tokens, mixed_own, mixed_other, gact, gains, w, wo, *before),
        (
            ((chunk, model), BF),
            ((chunk, model), F32),
            ((length, model), BF),
            ((length, hidden), BF),
            ((length, hidden), BF),
        ),
        (
            pltpu.VMEM((chunk, 2 * width), BF),
        ),
        aliases={8 + n: 2 + n for n in range(len(before))},
    )


def late_units(first):
    return [k for k in range(UNITS // 2) if k not in first]


def slots(refs, first, pieces):
    half = UNITS // 2
    count = len(first) * pieces
    keep, early, later = refs[0], refs[1 : 1 + count], refs[1 + count :]
    late = late_units(first)

    def slot(u):
        if u < half:
            return [keep.at[u]]
        k = u - half
        if k in first:
            at = first.index(k) * pieces
            return early[at : at + pieces]
        n = late.index(k)
        return [later[0].at[n] if len(later) == 1 else later[n]]

    return slot


def slot_shapes(rows, columns, first, pieces, apart):
    half = UNITS // 2
    early = [((rows, columns), BF)] * (len(first) * pieces)
    count = half - len(first)
    later = [((rows, columns), BF)] * count if apart else [((count, rows, columns), BF)]
    return [((half, rows, columns), BF), *early, *later]


FFN_FIRST = [UNITS // 4, UNITS // 4 - 1]
MIXER_FIRST = [UNITS // 4]


def result_kernel(name, keep, own, up, down, shapes, cut):
    def kernel(keep_ref, own_ref, up_ref, down_ref, *rest):
        outs, held, sem = rest[: len(shapes)], rest[len(shapes) : -1], rest[-1]

        def total(rows, columns):
            value = keep_ref[0, rows, columns].astype(F32) + own_ref[rows, columns].astype(F32)
            return value + up_ref[rows, columns].astype(F32) + down_ref[rows, columns].astype(F32)

        copies = []
        for n, (out, to) in enumerate(zip(outs, held)):
            cut(n, to, total)
            copies.append(pltpu.make_async_copy(to, out, sem.at[n]))
            copies[-1].start()
        for copy in copies:
            copy.wait()

    return run(
        kernel,
        name,
        (),
        (keep, own, up, down),
        (),
        (*[pltpu.VMEM(shape, F32) for shape in shapes], pltpu.SemaphoreType.DMA((len(shapes),))),
        loose_outs=[(shape, F32) for shape in shapes],
    )


def ffn_result(keep, own, up, down):
    _, rows, columns = keep.shape
    half = columns // 2

    def cut(n, to, total):
        to[...] = total(slice(None), slice(n * half, (n + 1) * half))

    return result_kernel("ffn_result", keep, own, up, down, [(rows, half)] * 2, cut)


def mixer_result(keep, own, up, down, heads, krows, width):
    _, deep, length = keep.shape
    top = deep - low_rows(krows)
    rows = top // heads
    lead, half, fold = length - width, length // 2, krows // 3
    shapes = [(heads, rows, length), (krows, width), (krows, width), (1, krows), (1, krows)]

    def cut(n, to, total):
        low = top + krows
        if n == 0:
            for h in range(heads):
                to[h] = total(slice(h * rows, (h + 1) * rows), slice(None))
        elif n == 1:
            to[...] = total(slice(top, low), slice(0, width))
        elif n == 2:
            to[:, :lead] = total(slice(top, low), slice(width, length))
            for m in range(3):
                some = slice(low + m // 2 * fold, low + (m // 2 + 1) * fold)
                to[m * fold : (m + 1) * fold, lead:] = total(some, slice(m % 2 * half, (m % 2 + 1) * half))
        else:
            to[...] = total(slice(low + fold, low + 2 * fold), slice(half, half + LANES))[n - 3 : n - 2, :krows]

    return result_kernel("mixer_result", keep, own, up, down, shapes, cut)


def ffn_out(act, w, cut):
    length, hidden = act.shape
    blocks, model, piece = w.shape

    def kernel(act_ref, w_ref, one, two):
        for out, at in ((one, slice(0, cut)), (two, slice(cut, length))):
            terms = [
                mm(act_ref[at, j * piece : (j + 1) * piece], w_ref[blocks // 2 + j], NT) for j in range(blocks // 2)
            ]
            out[...] = sum(terms).astype(BF)

    return run(kernel, "ffn_out", (), (act, w), (((cut, model), BF), ((length - cut, model), BF)))


def ffn_grads(where, n2, gpre, act, cotangent):
    model, hidden = n2.shape[1], act.shape[1]
    krows = model // UNITS

    def kernel(where_ref, cot_ref, n2_ref, gpre_ref, act_ref, *rest):
        slot = slots(rest[:-2], FFN_FIRST, 1)
        scr, sem = rest[-2:]
        piece = hidden // 3
        for j in range(3):
            cols = slice(j * piece, (j + 1) * piece)
            down = slice(hidden + j * piece, hidden + (j + 1) * piece)
            scr[:, cols] = mm(n2_ref[...], gpre_ref[:, cols], TN).astype(BF)
            scr[:, down] = mm(cot_ref[...], act_ref[:, cols], TN).astype(BF)
        for u in range(UNITS):
            at = pl.ds(multiple(where_ref[u] * krows, 16), krows)
            (to,) = slot(u)
            to[...] = scr[at, :]

    return run(
        kernel,
        "ffn_grads",
        (where,),
        (cotangent, n2, gpre, act),
        slot_shapes(krows, 2 * hidden, FFN_FIRST, 1, False),
        (pltpu.VMEM((model, 2 * hidden), BF), pltpu.SemaphoreType.DMA((UNITS,))),
    )


def cut_gain(row, krows):
    model = row.shape[1]
    take = (
        lax.broadcasted_iota(jnp.int32, (model, LANES), 0) % krows
        == lax.broadcasted_iota(jnp.int32, (model, LANES), 1)
    ).astype(BF)
    own = (
        lax.broadcasted_iota(jnp.int32, (UNITS, model), 1) // krows
        == lax.broadcasted_iota(jnp.int32, (UNITS, model), 0)
    )
    high = row.astype(BF).astype(F32)
    pieces = mm(jnp.where(own, high, 0.0).astype(BF), take)
    return pieces + mm(jnp.where(own, row - high, 0.0).astype(BF), take)


def resid_back(back, other, resid, cotangent, gains, wo, mixf, part, heads, size, before):
    chunk, model = resid.shape
    wide = heads * LANES
    at = slice(part * chunk, (part + 1) * chunk)

    def kernel(cot_ref, gains_ref, wo_ref, mixf_ref, back_ref, other_ref, res_ref, *rest):
        gres_ref, gat_ref, xh_ref, gain_ref, gm = rest[len(before) :]
        g2 = back_ref[...].astype(F32) + other_ref[...].astype(F32)
        res = res_ref[...]
        inv = lax.rsqrt(jnp.mean(res * res, axis=-1, keepdims=True) + EPSILON)
        hat = res * inv
        total = jnp.sum((g2 * hat).reshape(chunk // 8, 8, model), axis=0)
        gain_ref[...] = total + rest[0][...] if before else total
        z = gains_ref[1:2, :] * g2
        corr = jnp.mean(z * hat, axis=-1, keepdims=True)
        gres = cot_ref[at, :].astype(F32) + inv * (z - hat * corr)
        gres_ref[...] = gres
        gat_ref[...] = gres.astype(BF)
        gm[...] = mm(gat_ref[...], wo_ref[...]).astype(BF)
        lane = lax.broadcasted_iota(jnp.int32, (chunk, LANES), 1)
        for h in range(heads):
            lanes = slice(h * LANES, (h + 1) * LANES)
            here = gm[:, lanes].astype(F32)
            inner = -jnp.sum(here * mixf_ref[at, lanes], axis=-1, keepdims=True)
            high = inner.astype(BF).astype(F32)
            xh_ref[:, lanes] = jnp.where(
                lane == size, high, jnp.where(lane == size + 1, inner - high, here)
            ).astype(BF)

    return run(
        kernel,
        "resid_back",
        (),
        (cotangent, gains, wo, mixf, back, other, resid, *before),
        (
            ((chunk, model), F32),
            ((chunk, model), BF),
            ((chunk, wide), BF),
            ((8, model), F32),
        ),
        (pltpu.VMEM((chunk, wide), BF),),
    )


def value_terms(xh_ref, rb_ref, e_ref, at, h):
    lanes = slice(h * LANES, (h + 1) * LANES)
    scaled = (xh_ref[:, lanes].astype(F32) * rb_ref[at, lanes]).astype(BF)
    return mm(e_ref[h, at, :], scaled, TN)


def value_first(xh, rb, e, size):
    heads, length, _ = e.shape
    at = slice(0, xh.shape[0])

    def kernel(xh_ref, rb_ref, e_ref, out):
        for h in range(heads):
            out[:, h * size : (h + 1) * size] = value_terms(xh_ref, rb_ref, e_ref, at, h)[:, :size]

    return run(kernel, "value_first", (), (xh, rb, e), (((length, heads * size), F32),))[0]


def value_back(xh, first, rb, e, wv, tokens, size, cut):
    length, model = tokens.shape
    heads = e.shape[0]
    width = heads * size
    krows = model // UNITS
    last = slice(length - xh.shape[0], length)

    def kernel(xh_ref, first_ref, rb_ref, e_ref, wv_ref, tok_ref, gv_ref, part_one, part_two, ga_ref, acc):
        acc[...] = jnp.zeros_like(acc)
        for h in range(heads):
            cols = slice(h * size, (h + 1) * size)
            term = value_terms(xh_ref, rb_ref, e_ref, last, h)[:, :size]
            gv_ref[:, cols] = (first_ref[:, cols] + term).astype(BF)

        for at, part_ref in ((slice(0, cut), part_one), (slice(cut, length), part_two)):
            part = mm(gv_ref[at, :], wv_ref[...], NT)
            part_ref[...] = part.astype(BF)
            x = tok_ref[at, :].astype(F32)
            inv = lax.rsqrt(jnp.mean(x * x, axis=-1, keepdims=True) + EPSILON)
            acc[...] += jnp.sum((part * (x * inv)).reshape((at.stop - at.start) // 8, 8, model), axis=0)

        ga_ref[...] = jnp.zeros_like(ga_ref)
        ga_ref[:UNITS, :] = cut_gain(jnp.sum(acc[...], axis=0, keepdims=True), krows)

    return run(
        kernel,
        "value_back",
        (),
        (xh, first, rb, e, wv, tokens),
        (
            ((length, width), BF),
            ((cut, model), BF),
            ((length - cut, model), BF),
            ((4 * UNITS, LANES), F32),
        ),
        (pltpu.VMEM((8, model), F32),),
    )


def token_grads(mine, other, gres, tokens, gains, part, before):
    chunk, model = mine.shape
    length = tokens.shape[0]
    at = slice(part * chunk, (part + 1) * chunk)

    def kernel(mine_ref, other_ref, gres_ref, tok_ref, gains_ref, *rest):
        out, held, sem = rest[len(before) :]
        x = tok_ref[at, :].astype(F32)
        inv = lax.rsqrt(jnp.mean(x * x, axis=-1, keepdims=True) + EPSILON)
        hat = x * inv
        z = gains_ref[0:1, :] * (mine_ref[...].astype(F32) + other_ref[...].astype(F32))
        held[...] = (gres_ref[...] + inv * (z - hat * jnp.mean(z * hat, axis=-1, keepdims=True))).astype(BF)
        copy = pltpu.make_async_copy(held, out.at[at, :], sem)
        copy.start()
        copy.wait()

    return run(
        kernel,
        "token_grads",
        (),
        (mine, other, gres, tokens, gains),
        (),
        (pltpu.VMEM((chunk, model), BF), pltpu.SemaphoreType.DMA),
        loose=before,
        loose_outs=(((length, model), BF),),
        aliases={5: 0} if before else None,
    )[0]


def low_rows(krows):
    return krows + 2 * (krows // 3)


def mixer_grads(where, xh, va, e, rb, krows, part, before):
    heads, length, _ = e.shape
    rows = length // UNITS
    chunk = xh.shape[0]
    owners = chunk // rows
    at = slice(part * chunk, (part + 1) * chunk)
    deep = heads * rows + low_rows(krows)

    def kernel(where_ref, xh_ref, va_ref, e_ref, rb_ref, *rest):
        outs, ds = rest[len(before) : -1], rest[-1]
        slot = slots(outs, MIXER_FIRST, 1)

        for h in range(heads):
            lanes = slice(h * LANES, (h + 1) * LANES)
            d = mm(xh_ref[:, lanes], va_ref[:, lanes], NT)
            inverse = rb_ref[at, lanes]
            for q in range(length // LANES):
                cols = slice(q * LANES, (q + 1) * LANES)
                ds[h, :, cols] = (e_ref[h, at, cols].astype(F32) * inverse * d[:, cols]).astype(BF)
        for u in range(UNITS):
            owner = where_ref[u] - part * owners

            @pl.when((owner >= 0) & (owner < owners))
            def _(u=u, owner=owner):
                some = pl.ds(multiple(owner * rows, rows), rows)
                for h in range(heads):
                    slot(u)[0][h * rows : (h + 1) * rows, :] = ds[h, some, :]

    return run(
        kernel,
        "mixer_grads",
        (where,),
        (xh, va, e, rb, *before),
        slot_shapes(deep, length, MIXER_FIRST, 1, False),
        (pltpu.VMEM((heads, chunk, length), BF),),
        aliases={5 + n: n for n in range(len(before))},
    )


def weight_grads(where, parts, n1, gv, gats, mixed, ga, ga_other, gain):
    length = n1.shape[0]
    model = n1.shape[1]
    width = gv.shape[1]
    krows = model // UNITS
    deep, length = parts[0].shape[1:]
    top = deep - low_rows(krows)
    lead, half, fold = length - width, length // 2, krows // 3
    assert width - lead == half

    def kernel(where_ref, n1_ref, gv_ref, ga_ref, gb_ref, gain_ref, *rest):
        gat_refs, mixed_refs, rest = rest[: len(mixed)], rest[len(mixed) : 2 * len(mixed)], rest[2 * len(mixed) :]
        slot = slots(rest[len(parts) : 2 * len(parts)], MIXER_FIRST, 1)
        wide, other, folded, pieces = rest[2 * len(parts) :]
        wide[:, :width] = mm(n1_ref[...], gv_ref[...], TN).astype(BF)
        some = [mm(gat_ref[...], one[...], TN) for gat_ref, one in zip(gat_refs, mixed_refs)]
        other[...] = sum(some).astype(BF)
        wide[:, width:] = other[:, :lead]
        pieces[0] = ga_ref[:UNITS, :] + gb_ref[:UNITS, :]
        pieces[1] = cut_gain(jnp.sum(gain_ref[...], axis=0, keepdims=True), krows)
        sub = lax.broadcasted_iota(jnp.int32, (fold, LANES), 0)
        for d in range(UNITS):
            for n in range(3):
                at = slice(d * krows + n * fold, d * krows + (n + 1) * fold)
                to = slice((2 * d + n // 2) * fold, (2 * d + n // 2 + 1) * fold)
                folded[to, (n % 2) * half : (n % 2 + 1) * half] = other[at, lead:]
            both = jnp.where(
                sub == 0, pieces[0, d : d + 1, :], jnp.where(sub == 1, pieces[1, d : d + 1, :], 0.0)
            )
            at = slice((2 * d + 1) * fold, (2 * d + 2) * fold)
            folded[at, half : half + LANES] = both.astype(BF)
            folded[at, half + LANES :] = jnp.zeros((fold, half - LANES), BF)
        for u in range(UNITS):
            (to,) = slot(u)
            to[top : top + krows, :] = wide[pl.ds(multiple(where_ref[u] * krows, 16), krows), :]
            to[top + krows :, :] = folded[pl.ds(multiple(where_ref[u] * 2 * fold, 16), 2 * fold), :]

    return run(
        kernel,
        "weight_grads",
        (where,),
        (n1, gv, ga, ga_other, gain, *gats, *mixed, *parts),
        slot_shapes(deep, length, MIXER_FIRST, 1, False),
        (
            pltpu.VMEM((model, length), BF),
            pltpu.VMEM((model, width), BF),
            pltpu.VMEM((UNITS * 2 * fold, length), BF),
            pltpu.VMEM((2, UNITS, LANES), F32),
        ),
        aliases={6 + 2 * len(mixed) + n: n for n in range(len(parts))},
    )


class Ring:
    def __init__(self, size):
        self.size = size
        self.chips = size // 2
        n = self.chips
        self.order = list(range(0, n, 2)) + list(range(n - 1, 0, -2))
        me = lax.axis_index("dp")
        self.core = me % 2
        chip = me // 2
        self.at = jnp.where(chip % 2 == 0, chip // 2, n - 1 - chip // 2)
        self.up = self.pairs(1)
        self.down = self.pairs(-1)
        self.swap = [(d, d ^ 1) for d in range(size)]

    def pairs(self, step):
        n = self.chips
        return [
            (self.order[p] * 2 + c, self.order[(p + step) % n] * 2 + c) for p in range(n) for c in range(2)
        ]

    def device(self, offset, core):
        n = self.chips
        p = (self.at + jnp.asarray(offset, jnp.int32) + n) % n
        chip = jnp.where(p < (n + 1) // 2, 2 * p, 2 * (n - 1 - p) + 1)
        return chip * 2 + core

    def gathered(self):
        n = self.chips
        offsets = [0]
        for s in range(1, n // 2):
            offsets += [-s, s]
        offsets.append(n // 2)
        return jnp.concatenate([self.device(offsets, self.core), self.device(offsets, 1 - self.core)])

    def scattered(self):
        offsets = list(range(self.chips))
        return jnp.concatenate([self.device(offsets, self.core), self.device(offsets, 1 - self.core)])


class Gather:
    def __init__(self, ring, unit, cut):
        self.ring = ring
        self.rows = unit.shape[0]
        self.cut = cut
        self.last = [unit, unit]
        self.hops = 0
        self.mine = []
        self.theirs = []
        self.here = [unit]

    def values(self):
        return self.last

    def take(self, values):
        self.last = list(values)

    def arrived(self, units):
        self.hops = 1
        self.last = self.here = list(units)

    def hop(self):
        ring = self.ring
        self.hops += 1
        up, down = self.last
        if self.hops == ring.chips // 2:
            up, down = up[: self.cut], down[self.cut :]
        self.last = [lax.ppermute(up, "dp", ring.up), lax.ppermute(down, "dp", ring.down)]
        self.swap()
        self.here = self.last

    def swap(self):
        self.theirs += [lax.ppermute(one, "dp", self.ring.swap) for one in self.here]
        self.mine += self.here
        self.here = []

    def finish(self):
        self.swap()
        return self.mine + self.theirs

    def shares(self):
        n = self.ring.chips
        own = [(u, 0, self.rows) for u in range(n - 1)]
        own += [(n - 1, 0, self.cut), (n - 1, self.cut, self.rows - self.cut)]
        return own + [(u + n, first, rows) for u, first, rows in own]


class Scatter:
    def __init__(self, ring, first, pieces, keep, *give):
        self.ring = ring
        self.keep = keep
        count = len(first) * pieces
        swapped = [lax.ppermute(one, "dp", ring.swap) for one in give[:count]]
        self.early = {k: swapped[n * pieces : (n + 1) * pieces] for n, k in enumerate(first)}
        self.first = first
        self.late = late_units(first)
        self.later = give[count:]
        self.got = {}
        self.last = {}

    def values(self):
        return list(self.last.values()) if self.last else [one for k in self.first for one in self.early[k]]

    def take(self, values):
        if self.last:
            self.last = dict(zip(self.last, values))
        else:
            pieces = len(values) // len(self.first)
            self.early = {k: values[n * pieces : (n + 1) * pieces] for n, k in enumerate(self.first)}

    def swap_all(self, *after):
        stack = lax.ppermute(tie(self.later[0], *after), "dp", self.ring.swap)
        self.got = {k: stack[n] for n, k in enumerate(self.late)}

    def hop(self, way, k):
        got = self.early[k][0] if k in self.early else self.got[k]
        value = self.keep[k].astype(F32) + got.astype(F32)
        if way in self.last:
            value = value + self.last[way].astype(F32)
        value = value.astype(BF)
        self.last[way] = lax.ppermute(value, "dp", self.ring.up if way == "up" else self.ring.down)
        return value

    def result(self):
        return self.keep, self.got[0], self.last["up"], self.last["down"]


def together(chains, *more):
    values = [one for chain in chains for one in chain.values()]
    tied = lax.optimization_barrier(tuple(values) + more)
    at = 0
    for chain in chains:
        count = len(chain.values())
        chain.take(tied[at : at + count])
        at += count
    return tied[at:]


def tie(value, *after):
    return lax.optimization_barrier((value,) + after)[0] if after else value


def shards(
    tokens,
    segment_ids,
    gain_attn,
    gain_ffn,
    random_scores,
    w_value,
    w_output,
    w_up,
    w_down,
    cotangent,
):
    devices = lax.axis_size("dp")
    second = lax.axis_index("mp")
    length = segment_ids.shape[1]
    heads = random_scores.shape[0]
    model = tokens.shape[1]
    width = w_value.shape[1]
    size = width // heads
    rows = length // UNITS
    krows = model // UNITS
    ring = devices == UNITS and devices // 2 <= RING_CHIPS
    flip = [(0, 1), (1, 0)]
    second_at = jnp.reshape(second, (1,)).astype(jnp.int32)
    plan = Unit(heads, rows, krows, length, model, width, w_up.shape[1])

    if ring:
        net = Ring(devices)
        far = net.chips // 2
        where_in = net.gathered().astype(jnp.int32)
        where_out = net.scattered().astype(jnp.int32)
        upper, lower, wo_own = pack_unit(
            plan, second_at, random_scores, w_value, gain_attn, gain_ffn, w_up, w_down.T, w_output.T
        )
        ways = (net.up, net.down)
        uppers = [lax.ppermute(upper, "dp", way) for way in ways]
        wo_other = lax.ppermute(tie(wo_own, where_in, where_out), "mp", flip)
        lower = fill_low(plan, second_at, lower, wo_other)
        lowers = [lax.ppermute(lower, "dp", way) for way in ways]
        (unit,) = join_units(plan, [upper], [lower])
        one = Gather(net, unit, plan.cut)
        one.swap()
        uppers[0], uppers[1], *lowers = lax.optimization_barrier((*uppers, *lowers))
        one.arrived(join_units(plan, uppers, lowers))
        for step in range(1, far - 1):
            one.hop()
            together([one])
            one.here = one.last
        there = one.mine + one.theirs
        shares = one.shares()
        half = len(shares) // 2
        early = [n for n in range(len(one.mine))] + [half + n for n in range(len(one.theirs))]
        one.hop()
        begun = mixer_first(plan, where_in, tokens, segment_ids, there, [shares[n] for n in early], heads)
        begun = together([one], *begun)
        one.here = one.last
        units = one.finish()
        late = [n for n in range(len(shares)) if n not in early]
        near = late
        order = [n for n in range(len(shares)) if n not in near] + near
        units, shares = [units[n] for n in order], [shares[n] for n in order]
        late = [n for n, old in enumerate(order) if old in late]
    else:
        where_in = jnp.arange(UNITS, dtype=jnp.int32)
        where_out = where_in

        def gather(one, axis=0):
            return lax.all_gather(one.astype(BF), "dp", axis=axis, tiled=True)

        wo_own = w_output.T.astype(BF)
        wo_other = lax.ppermute(wo_own, "mp", flip)
        halves = [jnp.where(second == n, wo_own, wo_other) for n in range(2)]
        scores = gather(random_scores, 1).reshape(heads, UNITS, rows, length).transpose(1, 0, 2, 3)
        wide = [gather(one) for one in (w_value, *halves)]
        wide = jnp.concatenate(wide, axis=1).reshape(UNITS, krows, plan.wide)
        ffn = jnp.concatenate([gather(w_up), gather(w_down.T)], axis=1).reshape(UNITS, krows, -1)
        stack = [scores.reshape(UNITS, heads * rows, length)]
        for kind, column in plan.blocks:
            stack.append((ffn if kind == "ffn" else wide)[:, :, column : column + length])
        gains = jnp.stack([gather(gain_attn), gather(gain_ffn)]).reshape(2, UNITS, krows).transpose(1, 0, 2)
        gains = jnp.pad(gains, ((0, 0), (0, plan.fold - 2), (0, length - plan.gain_lane - krows)))
        tail = wide[:, :, plan.wide - plan.tail :].reshape(UNITS, 3, plan.fold, plan.tail)
        stack.append(jnp.concatenate([tail[:, 0], tail[:, 1], tail[:, 2], gains], axis=2))
        whole = jnp.concatenate(stack, axis=1)
        units = [whole[u] for u in range(UNITS)]
        shares = [(u, 0, plan.deep) for u in range(UNITS)]
        early, late, near = list(range(UNITS // 2)), list(range(UNITS // 2, UNITS)), []
        begun = mixer_first(plan, where_in, tokens, segment_ids, units[: UNITS // 2], shares[: UNITS // 2], heads)

    e, wv, _, va, sums, n1, gains, *mixed = mixer_forward(
        plan, where_in, segment_ids, begun, [units[n] for n in late], [shares[n] for n in late], heads, width
    )
    mixed_other = [lax.ppermute(one, "mp", flip) for one in mixed]
    w, wo_whole, gact, mixf, rb, wo = second_weights(plan, where_in, second_at, cotangent, sums, units, shares, len(near), size)
    backs, others, resids, kept = [], [], [], []
    for part in range(PARTS):
        back, resid, *kept = ffn_main(
            second_at, tokens, mixed[part], mixed_other[part], gact, gains, w, wo_whole, part, PARTS, kept
        )
        backs.append(back)
        others.append(lax.ppermute(tie(back, *others[-1:]), "mp", flip))
        resids.append(resid)
    n2, act, gpre = kept
    parts_two = ffn_grads(where_out, n2, gpre, act, cotangent)
    early = resid_back(backs[0], others[0], resids[0], cotangent, gains, wo, mixf, 0, heads, size, [])
    ffn_one, ffn_two = ffn_out(tie(act, *early), w, 3 * length // 8)
    first_values = value_first(early[2], rb, e, size)
    parts_one = mixer_grads(where_out, early[2], va, e, rb, krows, 0, [])
    if ring:
        ffn_sum = Scatter(net, FFN_FIRST, 1, *parts_two)
        ffn_sum.swap_all(others[0], *ffn_sum.values())
        for step in range(2):
            ffn_sum.hop("down", far + step)
            ffn_sum.hop("up", far - 1 - step)
            if step == 0:
                ffn_one, ffn_two, first_values, *more = together(
                    [ffn_sum], ffn_one, ffn_two, first_values, *early, *parts_one
                )
                early, parts_one = more[: len(early)], more[len(early) :]
    cot_late = tie(cotangent, first_values, *parts_one)
    final = resid_back(backs[1], others[1], resids[1], cot_late, gains, wo, mixf, 1, heads, size, early[3:])
    gres, gats = (early[0], final[0]), (early[1], final[1])
    xh = final[2]
    gv, part_one, part_two, ga = value_back(xh, first_values, rb, e, wv, tokens, size, length // 2)
    ga_other = lax.ppermute(ga, "mp", flip)
    one_other = lax.ppermute(tie(ffn_one, ga), "mp", flip)
    if ring:
        together([ffn_sum])
        for step in range(2, far - 1):
            ffn_sum.hop("down", far + step)
            ffn_sum.hop("up", far - 1 - step)
    parts_one = mixer_grads(where_out, xh, va, e, rb, krows, 1, parts_one)
    parts_one = weight_grads(where_out, parts_one, n1, gv, gats, mixed, ga, ga_other, final[3])

    top = heads * rows
    if ring:
        score_sum = Scatter(net, MIXER_FIRST, 1, *parts_one)
        one_other, ffn_two = together([ffn_sum, score_sum], one_other, ffn_two)
        value = score_sum.hop("up", far)
        ffn_sum.hop("down", 2 * far - 1)
        score_sum.swap_all(value)
        two_other = lax.ppermute(ffn_two, "mp", flip)
        part_one, part_two = together([score_sum], part_one, part_two)
        for step in range(1, far):
            score_sum.hop("up", far - step)
            score_sum.hop("down", far + step)
            if step == 1:
                part_other = [lax.ppermute(part_one, "mp", flip)]
                two_other, part_two = together([ffn_sum, score_sum], two_other, part_two)
            elif step < far - 1:
                part_other.append(lax.ppermute(part_two, "mp", flip))
                (part_other[0],) = together([score_sum], part_other[0])
        out_up, out_down = ffn_result(*ffn_sum.result())
        out_scores, out_value, out_output, *out_gains = mixer_result(*score_sum.result(), heads, krows, width)
        out_down, out_output = out_down.T, out_output.T
        out_gain_one, out_gain_two = [one.reshape(krows) for one in out_gains]
    else:
        two_other = lax.ppermute(ffn_two, "mp", flip)
        part_other = [lax.ppermute(one, "mp", flip) for one in (part_one, part_two)]

        def scatter(one, axis=0):
            return lax.psum_scatter(one, "dp", scatter_dimension=axis, tiled=True)

        def whole(first, pieces, keep, *give):
            late = late_units(first)
            early, later = give[: len(first) * pieces], give[len(first) * pieces :]
            given = []
            for k in range(UNITS // 2):
                if k in first:
                    at = first.index(k) * pieces
                    given.append(jnp.concatenate(early[at : at + pieces]))
                else:
                    given.append(later[0][late.index(k)] if len(later) == 1 else later[late.index(k)])
            return jnp.concatenate([keep, jnp.stack(given)]).astype(F32)

        two = whole(FFN_FIRST, 1, *parts_two).reshape(model, -1)
        one = whole(MIXER_FIRST, 1, *parts_one)
        out_up = scatter(two[:, : two.shape[1] // 2])
        out_down = scatter(two[:, two.shape[1] // 2 :]).T
        scores = one[:, :top].reshape(UNITS, heads, rows, length).transpose(1, 0, 2, 3)
        out_scores = scatter(scores.reshape(heads, length, length), 1)
        out_value = scatter(one[:, top : top + krows, :width].reshape(model, width))
        low, fold, half = top + krows, krows // 3, length // 2
        folded = [one[:, low + n // 2 * fold : low + (n // 2 + 1) * fold, n % 2 * half :][:, :, :half] for n in range(3)]
        other = jnp.concatenate([one[:, top:low, width:], jnp.concatenate(folded, axis=1)], axis=2)
        out_output = scatter(other.reshape(model, width)).T
        out_gain_one = scatter(one[:, low + fold, half : half + krows].reshape(model))
        out_gain_two = scatter(one[:, low + fold + 1, half : half + krows].reshape(model))
    ffn = jnp.concatenate([ffn_one, ffn_two])
    ffn_other = jnp.concatenate([one_other, two_other])
    output = (jnp.concatenate(resids) + (ffn.astype(F32) + ffn_other.astype(F32))).astype(BF)
    written = []
    for part, (mine, other) in enumerate(zip((part_one, part_two), part_other)):
        written = [token_grads(mine, other, gres[part], tokens, gains, part, written)]
    (grad_tokens,) = written
    return (
        output,
        grad_tokens,
        out_gain_one,
        out_gain_two,
        out_scores,
        out_value,
        out_output,
        out_up,
        out_down,
    )


def solution(mesh):
    in_specs = (
        P("dp", None),
        P("dp", None),
        P("dp"),
        P("dp"),
        P("mp", "dp", None),
        P("dp", "mp"),
        P("mp", "dp"),
        P("dp", "mp"),
        P("mp", "dp"),
        P("dp", None),
    )
    out_specs = (
        P("dp", None),
        P("dp", None),
        P("dp"),
        P("dp"),
        P("mp", "dp", None),
        P("dp", "mp"),
        P("mp", "dp"),
        P("dp", "mp"),
        P("mp", "dp"),
    )
    return jax.shard_map(shards, mesh=mesh, in_specs=in_specs, out_specs=out_specs, check_vma=False)
```

```python
import jax
import jax.numpy as jnp
from jax import lax
from jax.experimental import pallas as pl
from jax.experimental.pallas import tpu as pltpu
from jax.sharding import PartitionSpec as P

EPSILON = 1e-06
NEGATIVE = -1e30
BF = jnp.bfloat16
F32 = jnp.float32
UNITS = 16
LANES = 128
PARTS = 2
RING_CHIPS = 8
VMEM_BYTES = 20 * 1024 * 1024
NT = (((1,), (1,)), ((), ()))
TN = (((0,), (0,)), ((), ()))
NN = (((1,), (0,)), ((), ()))


def mm(a, b, dims=NN):
    return lax.dot_general(a, b, dims, preferred_element_type=F32)


def run(kernel, name, scalars, arrays, outs, scratch=(), loose=(), loose_outs=(), aliases=None, near=0):
    held = [pltpu.with_memory_space_constraint(one, pltpu.VMEM) for one in arrays]
    results = [pltpu.VMEM(*one) for one in outs] + [jax.ShapeDtypeStruct(*one) for one in loose_outs]
    specs = [pl.BlockSpec(memory_space=pltpu.SMEM)] * len(scalars)
    specs += [pl.BlockSpec(memory_space=pltpu.VMEM)] * len(arrays)
    far = len(loose) - near
    specs += [pl.BlockSpec(memory_space=pltpu.HBM)] * far + [pl.BlockSpec(memory_space=pl.ANY)] * near
    loose = [pltpu.with_memory_space_constraint(one, pltpu.HBM) for one in loose[:far]] + list(loose[far:])
    out_specs = [pl.BlockSpec(memory_space=pltpu.VMEM)] * len(outs)
    out_specs += [pl.BlockSpec(memory_space=pl.ANY)] * len(loose_outs)
    return pl.pallas_call(
        kernel,
        out_shape=tuple(results),
        in_specs=specs,
        out_specs=tuple(out_specs),
        scratch_shapes=list(scratch),
        compiler_params=pltpu.CompilerParams(vmem_limit_bytes=VMEM_BYTES),
        cost_estimate=pl.CostEstimate(flops=1, bytes_accessed=1, transcendentals=0),
        input_output_aliases=aliases or {},
        name=name,
    )(*scalars, *held, *loose)


def gelu_pair(x):
    c = 0.7978845608028654
    a = 0.044715
    square = x * x
    t = jnp.tanh(c * x * (1.0 + a * square))
    half = 0.5 * (1.0 + t)
    return x * half, half + 0.5 * x * (1.0 - t * t) * (c * (1.0 + 3.0 * a * square))


def multiple(value, of):
    return pl.multiple_of(value, of)


class Unit:
    def __init__(self, heads, rows, krows, length, model, width, hidden):
        self.scores = heads * rows
        self.krows = krows
        self.length = length
        self.width = width
        self.hidden = hidden
        self.wide = width + model
        self.blocks = [("ffn", n * length) for n in range(2 * hidden // length)]
        self.blocks += [("proj", n * length) for n in range(self.wide // length)]
        self.tail = self.wide % length
        self.last = self.scores + krows * len(self.blocks)
        self.fold = krows // 3
        self.deep = self.last + self.fold
        self.cut = self.scores + krows * (2 * hidden // length // 3)
        self.gain_lane = 3 * self.tail
        self.head = self.value_row()

    def projection_parts(self):
        parts = []
        for n, (kind, first) in enumerate(self.blocks):
            at = self.scores + n * self.krows
            if kind == "proj":
                skip = max(self.width - first, 0)
                parts.append((at, skip, 0, first + skip - self.width, self.krows, self.length - skip))
        for n in range(3):
            column = self.wide - self.tail - self.width
            parts.append((self.last, n * self.tail, n * self.fold, column, self.fold, self.tail))
        return parts

    def ffn_blocks(self, first, rows):
        inside = [
            n
            for n, (kind, _) in enumerate(self.blocks)
            if kind == "ffn" and first <= self.scores + n * self.krows < first + rows
        ]
        return (inside[0], len(inside)) if inside else (0, 0)

    def value_row(self):
        return self.scores + [kind for kind, _ in self.blocks].index("proj") * self.krows


def other_parts(plan, first):
    begin = plan.width + first * plan.width
    parts = []
    for n, (kind, column) in enumerate(plan.blocks):
        low, high = max(begin, column), min(begin + plan.width, column + plan.length)
        if kind == "proj" and low < high:
            parts.append((plan.scores + n * plan.krows, low - column, 0, low - begin, plan.krows, high - low))
    low = max(begin, plan.wide - plan.tail)
    if low < begin + plan.width:
        for n in range(3):
            lanes = n * plan.tail + low - (plan.wide - plan.tail)
            parts.append((plan.last, lanes, n * plan.fold, low - begin, plan.fold, begin + plan.width - low))
    return parts


def put_half(plan, low, half_ref, first):
    for row, lane, at, column, rows, lanes in other_parts(plan, first):
        row = row - plan.head
        low[row : row + rows, lane : lane + lanes] = half_ref[at : at + rows, column : column + lanes]


def pack_unit(plan, second, scores, wv, gain_one, gain_two, w_up, w_down, wo):
    inputs = (scores, wv, gain_one.reshape(1, -1), gain_two.reshape(1, -1), w_up, w_down, wo)
    count = len(inputs)
    krows, length, width = plan.krows, plan.length, plan.width
    per = plan.hidden // length
    assert plan.tail <= width

    def kernel(second_ref, *rest):
        out, low, wo_out, gains = rest[count : count + 4]
        held, sem = rest[count + 4 : -1], rest[-1]
        fetch(rest[:count], held, sem)
        s_ref, wv_ref, ga_ref, gf_ref, up_ref, down_ref, own_ref = held
        out[: plan.scores, :] = s_ref[...].reshape(plan.scores, length).astype(BF)
        for n, (kind, column) in enumerate(plan.blocks):
            at = slice(plan.scores + n * krows, plan.scores + (n + 1) * krows)
            if kind == "ffn":
                ref, first = (up_ref, column) if n < per else (down_ref, column - plan.hidden)
                out[at, :] = ref[:, first : first + length].astype(BF)
        low[...] = jnp.zeros_like(low)
        low[:krows, :width] = wv_ref[...].astype(BF)
        wo_out[...] = own_ref[...].astype(BF)
        for place in range(2):

            @pl.when(second_ref[0] == place)
            def _():
                put_half(plan, low, wo_out, place)

        gains[...] = jnp.zeros_like(gains)
        gains[0:1, :krows] = ga_ref[...]
        gains[1:2, :krows] = gf_ref[...]
        low[plan.last - plan.head :, plan.gain_lane :] = gains[...].astype(BF)

    return run(
        kernel,
        "pack_unit",
        (second,),
        (),
        (((plan.head, length), BF), ((plan.deep - plan.head, length), BF), ((krows, width), BF)),
        (
            pltpu.VMEM((plan.fold, length - plan.gain_lane), F32),
            *[pltpu.VMEM(one.shape, one.dtype) for one in inputs],
            pltpu.SemaphoreType.DMA((count,)),
        ),
        loose=inputs,
    )


def fill_low(plan, second, low, other):
    def kernel(second_ref, old, other_ref, out):
        for place in range(2):

            @pl.when(second_ref[0] == 1 - place)
            def _():
                put_half(plan, out, other_ref, place)

    return run(kernel, "fill_low", (second,), (low, other), ((low.shape, BF),), aliases={1: 0})[0]


def join_units(plan, uppers, lowers):
    count = len(uppers)

    def kernel(*refs):
        for n in range(count):
            out = refs[2 * count + n]
            out[: plan.head, :] = refs[n][...]
            out[plan.head :, :] = refs[count + n][...]

    return run(kernel, "join_units", (), (*uppers, *lowers), [((plan.deep, plan.length), BF)] * count)


def fetch(refs, held, sem):
    copies = [pltpu.make_async_copy(ref, to, sem.at[n]) for n, (ref, to) in enumerate(zip(refs, held))]
    for copy in copies:
        copy.start()
    for copy in copies:
        copy.wait()


def pick(units, shares, where_ref, parts, target, sem):
    copies = []
    for n, (u, first, rows) in enumerate(shares):
        owner = where_ref[u]
        for m, part in enumerate(parts):
            row, column, count, columns = part[0], part[1], part[-2], part[-1]
            if first <= row and row + count <= first + rows:
                source = units[n].at[pl.ds(row - first, count), pl.ds(column, columns)]
                copies.append(pltpu.make_async_copy(source, target(m, owner), sem.at[u, m]))
                copies[-1].start()
    return copies


def document_mask(seg_ref, same):
    length = same.shape[0]
    documents = (seg_ref[...] == lax.broadcasted_iota(jnp.int32, (LANES, length), 0)).astype(BF)
    same[...] = mm(documents, documents, TN)


def exponentials(where_ref, shares, sources, e_ref, same):
    heads, length, _ = e_ref.shape
    rows = length // UNITS

    def one_head(h, carry):
        for (u, _, _), (ref, first) in zip(shares, sources):
            at = pl.ds(multiple(where_ref[u] * rows, rows), rows)
            s = ref[pl.ds(multiple(first + h * rows, rows), rows), :].astype(F32)
            e_ref[h, at, :] = (jnp.exp(s) * same[at, :]).astype(BF)
        return carry

    lax.fori_loop(0, heads, one_head, 0)


def low_parts(plan):
    return [
        (plan.value_row(), 0, plan.krows, plan.width),
        (plan.last, plan.gain_lane, plan.fold, LANES),
    ]


def bring_low(plan, units, shares, where_ref, wv_ref, low_ref, sem):
    krows = plan.krows

    def target(m, owner):
        if m == 0:
            return wv_ref.at[pl.ds(multiple(owner * krows, 16), krows), :]
        return low_ref.at[owner]

    return pick(units, shares, where_ref, low_parts(plan), target, sem)


def mixer_first(plan, where, tokens, segments, units, shares, heads):
    length, model = tokens.shape
    rows = length // UNITS

    def kernel(where_ref, tok_ref, seg_ref, *rest):
        e_ref, wv_ref, low_ref, hat_ref, same, unit, sem, more = rest[len(units) :]
        top = heads * rows

        def target(m, owner):
            return unit.at[pl.ds(multiple(owner * top, top), top), :]

        came = pick(rest[: len(units)], shares, where_ref, [(0, 0, top, length)], target, sem)
        copies = bring_low(plan, rest[: len(units)], shares, where_ref, wv_ref, low_ref, more)
        document_mask(seg_ref, same)
        x = tok_ref[...].astype(F32)
        hat_ref[...] = x * lax.rsqrt(jnp.mean(x * x, axis=-1, keepdims=True) + EPSILON)
        for copy in came:
            copy.wait()
        sources = [(unit, where_ref[u] * top) for u, _, _ in shares]
        exponentials(where_ref, shares, sources, e_ref, same)
        for copy in copies:
            copy.wait()

    return run(
        kernel,
        "mixer_first",
        (where,),
        (tokens, segments),
        (
            ((heads, length, length), BF),
            ((model, plan.width), BF),
            ((UNITS, plan.fold, LANES), BF),
            ((length, model), F32),
            ((length, length), F32),
        ),
        (
            pltpu.VMEM((heads * length, length), BF),
            pltpu.SemaphoreType.DMA((UNITS, 1)),
            pltpu.SemaphoreType.DMA((UNITS, 2)),
        ),
        loose=units,
    )


def take_late(plan, where_ref, shares, refs, e_ref, wv_ref, low, same):
    krows = plan.krows
    for (u, first, rows), ref in zip(shares, refs):
        for m, (row, lane, deep, lanes) in enumerate(low_parts(plan)):
            if first <= row < first + rows:
                part = ref[row - first : row - first + deep, lane : lane + lanes]
                if m == 0:
                    wv_ref[pl.ds(multiple(where_ref[u] * krows, 16), krows), :] = part
                else:
                    low[where_ref[u]] = part
    scored = [n for n in range(len(shares)) if shares[n][1] == 0]
    exponentials(where_ref, [shares[n] for n in scored], [(refs[n], 0) for n in scored], e_ref, same)


def mixer_next(plan, where, early, units, shares):
    e, wv, low, hat, same = early
    count = len(units)

    def kernel(where_ref, same_ref, e_old, wv_old, low_old, *rest):
        take_late(plan, where_ref, shares, rest[:count], *rest[count:], same_ref)

    outs = [(one.shape, one.dtype) for one in (e, wv, low)]
    more = run(
        kernel, "mixer_next", (where,), (same, e, wv, low, *units), outs, aliases={2: 0, 3: 1, 4: 2}
    )
    return [*more, hat, same]


def mixer_forward(plan, where, early, units, shares, heads, width):
    length, model = early[3].shape
    size = width // heads
    krows = model // UNITS
    wide = heads * LANES
    count = len(units)

    def kernel(where_ref, e_old, wv_old, low_old, hat_ref, same, *rest):
        e_ref, wv_ref, low, va_ref, sums_ref, n1_ref, gains_ref, *mixed, pieces = rest[count:]
        take_late(plan, where_ref, shares, rest[:count], e_ref, wv_ref, low, same)
        for d in range(UNITS):
            some = low[d].astype(F32)
            pieces[0, d : d + 1, :] = some[0:1, :]
            pieces[1, d : d + 1, :] = some[1:2, :]
        spread = (
            lax.broadcasted_iota(jnp.int32, (LANES, model), 1) % krows
            == lax.broadcasted_iota(jnp.int32, (LANES, model), 0)
        ).astype(BF)
        own = (
            lax.broadcasted_iota(jnp.int32, (UNITS, model), 1) // krows
            == lax.broadcasted_iota(jnp.int32, (UNITS, model), 0)
        )
        gains = []
        for t in range(2):
            full = jnp.where(own, mm(pieces[t].astype(BF), spread), 0.0)
            gains.append(jnp.sum(full, axis=0, keepdims=True))
            gains_ref[t : t + 1, :] = gains[t]
        n1_ref[...] = (hat_ref[...] * gains[0]).astype(BF)
        values = mm(n1_ref[...], wv_ref[...]).astype(BF)
        tail = (lax.broadcasted_iota(jnp.int32, (length, LANES - size), 1) < 2).astype(BF)
        for h in range(heads):
            va_ref[:, h * LANES : h * LANES + size] = values[:, h * size : (h + 1) * size]
            va_ref[:, h * LANES + size : (h + 1) * LANES] = tail

        for h in range(heads):
            lanes = slice(h * LANES, (h + 1) * LANES)
            sums = mm(e_ref[h], va_ref[:, lanes])
            sums_ref[:, lanes] = sums
            values = (sums * (1.0 / sums[:, size : size + 1]))[:, :size].astype(BF)
            for part, mixed_ref in enumerate(mixed):
                some = slice(part * (length // PARTS), (part + 1) * (length // PARTS))
                mixed_ref[:, h * size : (h + 1) * size] = values[some, :]

    return run(
        kernel,
        "mixer_forward",
        (where,),
        (*early, *units),
        (
            ((heads, length, length), BF),
            ((model, width), BF),
            ((UNITS, plan.fold, LANES), BF),
            ((length, wide), BF),
            ((length, wide), F32),
            ((length, model), BF),
            ((2, model), F32),
            *[((length // PARTS, width), BF)] * PARTS,
        ),
        (
            pltpu.VMEM((2, UNITS, LANES), F32),
        ),
        aliases={1: 0, 2: 1, 3: 2},
    )


def second_weights(plan, where, second, cotangent, sums, units, shares, near, size):
    length, model = cotangent.shape
    wide = sums.shape[1]
    hidden, krows, width = plan.hidden, plan.krows, plan.width
    parts = plan.projection_parts()
    blocks = 2 * hidden // length

    def kernel(where_ref, second_ref, cot_ref, sums_ref, *rest):
        out, wo_ref, gact, mixf_ref, rb_ref, own_ref, sem, more = rest[len(units) :]

        def target(m, owner):
            _, _, row, column, rows, columns = parts[m]
            return wo_ref.at[pl.ds(multiple(owner * krows + row, 16), rows), pl.ds(column, columns)]

        copies = []
        for n, (u, first, rows) in enumerate(shares):
            begin, count = plan.ffn_blocks(first, rows)
            if count:
                source = rest[n].at[pl.ds(plan.scores + begin * krows - first, count * krows), :]
                to = out.at[pl.ds(begin, count), pl.ds(multiple(where_ref[u] * krows, 16), krows), :]
                copies.append(pltpu.make_async_copy(source.reshape(count, krows, length), to, more.at[n]))
                copies[-1].start()
        copies += pick(rest[: len(units)], shares, where_ref, parts, target, sem)
        inside = lax.broadcasted_iota(jnp.int32, (length, LANES), 1) < size
        for h in range(wide // LANES):
            lanes = slice(h * LANES, (h + 1) * LANES)
            inverse = jnp.broadcast_to(1.0 / sums_ref[:, h * LANES + size : h * LANES + size + 1], (length, LANES))
            rb_ref[:, lanes] = inverse
            mixf_ref[:, lanes] = jnp.where(inside, sums_ref[:, lanes] * inverse, 0.0)
        for copy in copies:
            copy.wait()
        for j in range(blocks // 2):
            gact[:, j * length : (j + 1) * length] = mm(cot_ref[...], out[blocks // 2 + j])
        own = wo_ref[:, pl.ds(multiple(second_ref[0] * width, LANES), width)]
        own_ref[...] = jnp.zeros_like(own_ref)
        for h in range(width // size):
            own_ref[:, h * LANES : h * LANES + size] = own[:, h * size : (h + 1) * size]

    return run(
        kernel,
        "second_weights",
        (where, second),
        (cotangent, sums),
        (
            ((blocks, model, length), BF),
            ((model, model), BF),
            ((length, hidden), F32),
            (sums.shape, F32),
            (sums.shape, F32),
            ((model, wide), BF),
        ),
        (pltpu.SemaphoreType.DMA((UNITS, len(parts))), pltpu.SemaphoreType.DMA((len(units),))),
        loose=units,
        near=near,
    )


def ffn_main(second, tokens, mixed_own, mixed_other, gact, gains, w, wo, part, parts, before):
    length, model = tokens.shape
    width = mixed_own.shape[1]
    hidden = gact.shape[1]
    chunk = length // parts
    piece = w.shape[2]
    at = slice(part * chunk, (part + 1) * chunk)

    def kernel(second_ref, tok_ref, own_ref, other_ref, gact_ref, gains_ref, w_ref, wo_ref, *rest):
        back_ref, resid_ref, n2_ref, act_ref, gpre_ref, mixed = rest[len(before) :]
        first = second_ref[0]
        mixed[:, pl.ds(multiple(first * width, LANES), width)] = own_ref[...]
        mixed[:, pl.ds(multiple((1 - first) * width, LANES), width)] = other_ref[...]
        attn = mm(mixed[...], wo_ref[...], NT)
        resid = tok_ref[at, :].astype(F32) + attn
        resid_ref[...] = resid
        inv = lax.rsqrt(jnp.mean(resid * resid, axis=-1, keepdims=True) + EPSILON)
        n2 = (resid * inv * gains_ref[1:2, :]).astype(BF)
        n2_ref[at, :] = n2
        terms = []
        pres = [mm(n2, w_ref[j]) for j in range(hidden // piece)]
        for j in range(hidden // piece):
            cols = slice(j * piece, (j + 1) * piece)
            act, slope = gelu_pair(pres[j])
            act_ref[at, cols] = act.astype(BF)
            gpre = (gact_ref[at, cols] * slope).astype(BF)
            gpre_ref[at, cols] = gpre
            terms.append(mm(gpre, w_ref[j], NT))
        back_ref[...] = sum(terms).astype(BF)

    return run(
        kernel,
        "ffn_main",
        (second,),
        (tokens, mixed_own, mixed_other, gact, gains, w, wo, *before),
        (
            ((chunk, model), BF),
            ((chunk, model), F32),
            ((length, model), BF),
            ((length, hidden), BF),
            ((length, hidden), BF),
        ),
        (
            pltpu.VMEM((chunk, 2 * width), BF),
        ),
        aliases={8 + n: 2 + n for n in range(len(before))},
    )


def late_units(first):
    return [k for k in range(UNITS // 2) if k not in first]


def slots(refs, first, pieces):
    half = UNITS // 2
    count = len(first) * pieces
    keep, early, later = refs[0], refs[1 : 1 + count], refs[1 + count :]
    late = late_units(first)

    def slot(u):
        if u < half:
            return [keep.at[u]]
        k = u - half
        if k in first:
            at = first.index(k) * pieces
            return early[at : at + pieces]
        n = late.index(k)
        return [later[0].at[n] if len(later) == 1 else later[n]]

    return slot


def slot_shapes(rows, columns, first, pieces, apart):
    half = UNITS // 2
    early = [((rows, columns), BF)] * (len(first) * pieces)
    count = half - len(first)
    later = [((rows, columns), BF)] * count if apart else [((count, rows, columns), BF)]
    return [((half, rows, columns), BF), *early, *later]


FFN_FIRST = [UNITS // 4, UNITS // 4 - 1]
MIXER_FIRST = [UNITS // 4]


def result_kernel(name, keep, own, up, down, shapes, cut):
    def kernel(keep_ref, own_ref, up_ref, down_ref, *rest):
        outs, held, sem = rest[: len(shapes)], rest[len(shapes) : -1], rest[-1]

        def total(rows, columns):
            value = keep_ref[0, rows, columns].astype(F32) + own_ref[rows, columns].astype(F32)
            return value + up_ref[rows, columns].astype(F32) + down_ref[rows, columns].astype(F32)

        copies = []

        def send(source, to, n, m):
            copies.append(pltpu.make_async_copy(source, to, sem.at[n, m]))
            copies[-1].start()

        for n, (out, to) in reversed(list(enumerate(zip(outs, held)))):
            if len(shapes[n]) < 3:
                cut(n, to, total)
                send(to, out, n, 0)
            else:
                half = shapes[n][0] // 2
                for m, some in enumerate((range(half), range(half, shapes[n][0]))):
                    cut(n, to, total, some)
                    at = pl.ds(some.start, len(some))
                    send(to.at[at], out.at[at], n, m)
        for copy in copies:
            copy.wait()

    return run(
        kernel,
        name,
        (),
        (keep, own, up, down),
        (),
        (*[pltpu.VMEM(shape, F32) for shape in shapes], pltpu.SemaphoreType.DMA((len(shapes), 2))),
        loose_outs=[(shape, F32) for shape in shapes],
    )


def ffn_result(keep, own, up, down):
    _, rows, columns = keep.shape
    half = columns // 2

    def cut(n, to, total):
        to[...] = total(slice(None), slice(n * half, (n + 1) * half))

    return result_kernel("ffn_result", keep, own, up, down, [(rows, half)] * 2, cut)


def mixer_result(keep, own, up, down, heads, krows, width):
    _, deep, length = keep.shape
    top = deep - low_rows(krows)
    rows = top // heads
    lead, half, fold = length - width, length // 2, krows // 3
    shapes = [(heads, rows, length), (krows, width), (krows, width), (1, krows), (1, krows)]

    def cut(n, to, total, some=()):
        low = top + krows
        if n == 0:
            for h in some:
                to[h] = total(slice(h * rows, (h + 1) * rows), slice(None))
        elif n == 1:
            to[...] = total(slice(top, low), slice(0, width))
        elif n == 2:
            to[:, :lead] = total(slice(top, low), slice(width, length))
            for m in range(3):
                some = slice(low + m // 2 * fold, low + (m // 2 + 1) * fold)
                to[m * fold : (m + 1) * fold, lead:] = total(some, slice(m % 2 * half, (m % 2 + 1) * half))
        else:
            to[...] = total(slice(low + fold, low + 2 * fold), slice(half, half + LANES))[n - 3 : n - 2, :krows]

    return result_kernel("mixer_result", keep, own, up, down, shapes, cut)


def ffn_out(act, w, cut):
    length, hidden = act.shape
    blocks, model, piece = w.shape

    def kernel(act_ref, w_ref, one, two):
        for out, at in ((one, slice(0, cut)), (two, slice(cut, length))):
            terms = [
                mm(act_ref[at, j * piece : (j + 1) * piece], w_ref[blocks // 2 + j], NT) for j in range(blocks // 2)
            ]
            out[...] = sum(terms).astype(BF)

    return run(kernel, "ffn_out", (), (act, w), (((cut, model), BF), ((length - cut, model), BF)))


def ffn_grads(where, n2, gpre, act, cotangent):
    model, hidden = n2.shape[1], act.shape[1]
    krows = model // UNITS

    def kernel(where_ref, cot_ref, n2_ref, gpre_ref, act_ref, *rest):
        slot = slots(rest[:-2], FFN_FIRST, 1)
        scr, sem = rest[-2:]
        piece = hidden // 3
        for j in range(3):
            cols = slice(j * piece, (j + 1) * piece)
            down = slice(hidden + j * piece, hidden + (j + 1) * piece)
            scr[:, cols] = mm(n2_ref[...], gpre_ref[:, cols], TN).astype(BF)
            scr[:, down] = mm(cot_ref[...], act_ref[:, cols], TN).astype(BF)
        for u in range(UNITS):
            at = pl.ds(multiple(where_ref[u] * krows, 16), krows)
            (to,) = slot(u)
            to[...] = scr[at, :]

    return run(
        kernel,
        "ffn_grads",
        (where,),
        (cotangent, n2, gpre, act),
        slot_shapes(krows, 2 * hidden, FFN_FIRST, 1, False),
        (pltpu.VMEM((model, 2 * hidden), BF), pltpu.SemaphoreType.DMA((UNITS,))),
    )


def cut_gain(row, krows):
    model = row.shape[1]
    take = (
        lax.broadcasted_iota(jnp.int32, (model, LANES), 0) % krows
        == lax.broadcasted_iota(jnp.int32, (model, LANES), 1)
    ).astype(BF)
    own = (
        lax.broadcasted_iota(jnp.int32, (UNITS, model), 1) // krows
        == lax.broadcasted_iota(jnp.int32, (UNITS, model), 0)
    )
    high = row.astype(BF).astype(F32)
    pieces = mm(jnp.where(own, high, 0.0).astype(BF), take)
    return pieces + mm(jnp.where(own, row - high, 0.0).astype(BF), take)


def resid_back(back, other, resid, cotangent, gains, wo, mixf, part, heads, size, before):
    chunk, model = resid.shape
    wide = heads * LANES
    at = slice(part * chunk, (part + 1) * chunk)

    def kernel(cot_ref, gains_ref, wo_ref, mixf_ref, back_ref, other_ref, res_ref, *rest):
        gres_ref, gat_ref, xh_ref, gain_ref, gm = rest[len(before) :]
        g2 = back_ref[...].astype(F32) + other_ref[...].astype(F32)
        res = res_ref[...]
        inv = lax.rsqrt(jnp.mean(res * res, axis=-1, keepdims=True) + EPSILON)
        hat = res * inv
        total = jnp.sum((g2 * hat).reshape(chunk // 8, 8, model), axis=0)
        gain_ref[...] = total + rest[0][...] if before else total
        z = gains_ref[1:2, :] * g2
        corr = jnp.mean(z * hat, axis=-1, keepdims=True)
        gres = cot_ref[at, :].astype(F32) + inv * (z - hat * corr)
        gres_ref[...] = gres
        gat_ref[...] = gres.astype(BF)
        gm[...] = mm(gat_ref[...], wo_ref[...]).astype(BF)
        lane = lax.broadcasted_iota(jnp.int32, (chunk, LANES), 1)
        for h in range(heads):
            lanes = slice(h * LANES, (h + 1) * LANES)
            here = gm[:, lanes].astype(F32)
            inner = -jnp.sum(here * mixf_ref[at, lanes], axis=-1, keepdims=True)
            high = inner.astype(BF).astype(F32)
            xh_ref[:, lanes] = jnp.where(
                lane == size, high, jnp.where(lane == size + 1, inner - high, here)
            ).astype(BF)

    return run(
        kernel,
        "resid_back",
        (),
        (cotangent, gains, wo, mixf, back, other, resid, *before),
        (
            ((chunk, model), F32),
            ((chunk, model), BF),
            ((chunk, wide), BF),
            ((8, model), F32),
        ),
        (pltpu.VMEM((chunk, wide), BF),),
    )


def value_terms(xh_ref, rb_ref, e_ref, at, h):
    lanes = slice(h * LANES, (h + 1) * LANES)
    scaled = (xh_ref[:, lanes].astype(F32) * rb_ref[at, lanes]).astype(BF)
    return mm(e_ref[h, at, :], scaled, TN)


def value_first(xh, rb, e, size):
    heads, length, _ = e.shape
    at = slice(0, xh.shape[0])

    def kernel(xh_ref, rb_ref, e_ref, out):
        for h in range(heads):
            out[:, h * size : (h + 1) * size] = value_terms(xh_ref, rb_ref, e_ref, at, h)[:, :size]

    return run(kernel, "value_first", (), (xh, rb, e), (((length, heads * size), F32),))[0]


def value_back(xh, first, rb, e, wv, tokens, size, cut):
    length, model = tokens.shape
    heads = e.shape[0]
    width = heads * size
    krows = model // UNITS
    last = slice(length - xh.shape[0], length)

    def kernel(xh_ref, first_ref, rb_ref, e_ref, wv_ref, tok_ref, gv_ref, part_one, part_two, ga_ref, acc):
        acc[...] = jnp.zeros_like(acc)
        for h in range(heads):
            cols = slice(h * size, (h + 1) * size)
            term = value_terms(xh_ref, rb_ref, e_ref, last, h)[:, :size]
            gv_ref[:, cols] = (first_ref[:, cols] + term).astype(BF)

        for at, part_ref in ((slice(0, cut), part_one), (slice(cut, length), part_two)):
            part = mm(gv_ref[at, :], wv_ref[...], NT)
            part_ref[...] = part.astype(BF)
            x = tok_ref[at, :].astype(F32)
            inv = lax.rsqrt(jnp.mean(x * x, axis=-1, keepdims=True) + EPSILON)
            acc[...] += jnp.sum((part * (x * inv)).reshape((at.stop - at.start) // 8, 8, model), axis=0)

        ga_ref[...] = jnp.zeros_like(ga_ref)
        ga_ref[:UNITS, :] = cut_gain(jnp.sum(acc[...], axis=0, keepdims=True), krows)

    return run(
        kernel,
        "value_back",
        (),
        (xh, first, rb, e, wv, tokens),
        (
            ((length, width), BF),
            ((cut, model), BF),
            ((length - cut, model), BF),
            ((4 * UNITS, LANES), F32),
        ),
        (pltpu.VMEM((8, model), F32),),
    )


def token_grads(mine, other, gres, tokens, gains, part, before):
    chunk, model = mine.shape
    length = tokens.shape[0]
    at = slice(part * chunk, (part + 1) * chunk)

    def kernel(mine_ref, other_ref, gres_ref, tok_ref, gains_ref, *rest):
        out, held, sem = rest[len(before) :]
        x = tok_ref[at, :].astype(F32)
        inv = lax.rsqrt(jnp.mean(x * x, axis=-1, keepdims=True) + EPSILON)
        hat = x * inv
        z = gains_ref[0:1, :] * (mine_ref[...].astype(F32) + other_ref[...].astype(F32))
        held[...] = (gres_ref[...] + inv * (z - hat * jnp.mean(z * hat, axis=-1, keepdims=True))).astype(BF)
        copy = pltpu.make_async_copy(held, out.at[at, :], sem)
        copy.start()
        copy.wait()

    return run(
        kernel,
        "token_grads",
        (),
        (mine, other, gres, tokens, gains),
        (),
        (pltpu.VMEM((chunk, model), BF), pltpu.SemaphoreType.DMA),
        loose=before,
        loose_outs=(((length, model), BF),),
        aliases={5: 0} if before else None,
    )[0]


def low_rows(krows):
    return krows + 2 * (krows // 3)


def mixer_grads(where, xh, va, e, rb, krows, part, before):
    heads, length, _ = e.shape
    rows = length // UNITS
    chunk = xh.shape[0]
    owners = chunk // rows
    at = slice(part * chunk, (part + 1) * chunk)
    deep = heads * rows + low_rows(krows)

    def kernel(where_ref, xh_ref, va_ref, e_ref, rb_ref, *rest):
        outs, ds = rest[len(before) : -1], rest[-1]
        slot = slots(outs, MIXER_FIRST, 1)

        for h in range(heads):
            lanes = slice(h * LANES, (h + 1) * LANES)
            d = mm(xh_ref[:, lanes], va_ref[:, lanes], NT)
            inverse = rb_ref[at, lanes]
            for q in range(length // LANES):
                cols = slice(q * LANES, (q + 1) * LANES)
                ds[h, :, cols] = (e_ref[h, at, cols].astype(F32) * inverse * d[:, cols]).astype(BF)
        for u in range(UNITS):
            owner = where_ref[u] - part * owners

            @pl.when((owner >= 0) & (owner < owners))
            def _(u=u, owner=owner):
                some = pl.ds(multiple(owner * rows, rows), rows)
                for h in range(heads):
                    slot(u)[0][h * rows : (h + 1) * rows, :] = ds[h, some, :]

    return run(
        kernel,
        "mixer_grads",
        (where,),
        (xh, va, e, rb, *before),
        slot_shapes(deep, length, MIXER_FIRST, 1, False),
        (pltpu.VMEM((heads, chunk, length), BF),),
        aliases={5 + n: n for n in range(len(before))},
    )


def weight_grads(where, parts, n1, gv, gats, mixed, ga, ga_other, gain):
    length = n1.shape[0]
    model = n1.shape[1]
    width = gv.shape[1]
    krows = model // UNITS
    deep, length = parts[0].shape[1:]
    top = deep - low_rows(krows)
    lead, half, fold = length - width, length // 2, krows // 3
    assert width - lead == half

    def kernel(where_ref, n1_ref, gv_ref, ga_ref, gb_ref, gain_ref, *rest):
        gat_refs, mixed_refs, rest = rest[: len(mixed)], rest[len(mixed) : 2 * len(mixed)], rest[2 * len(mixed) :]
        slot = slots(rest[len(parts) : 2 * len(parts)], MIXER_FIRST, 1)
        wide, other, folded, pieces = rest[2 * len(parts) :]
        wide[:, :width] = mm(n1_ref[...], gv_ref[...], TN).astype(BF)
        some = [mm(gat_ref[...], one[...], TN) for gat_ref, one in zip(gat_refs, mixed_refs)]
        other[...] = sum(some).astype(BF)
        wide[:, width:] = other[:, :lead]
        pieces[0] = ga_ref[:UNITS, :] + gb_ref[:UNITS, :]
        pieces[1] = cut_gain(jnp.sum(gain_ref[...], axis=0, keepdims=True), krows)
        sub = lax.broadcasted_iota(jnp.int32, (fold, LANES), 0)
        for d in range(UNITS):
            for n in range(3):
                at = slice(d * krows + n * fold, d * krows + (n + 1) * fold)
                to = slice((2 * d + n // 2) * fold, (2 * d + n // 2 + 1) * fold)
                folded[to, (n % 2) * half : (n % 2 + 1) * half] = other[at, lead:]
            both = jnp.where(
                sub == 0, pieces[0, d : d + 1, :], jnp.where(sub == 1, pieces[1, d : d + 1, :], 0.0)
            )
            at = slice((2 * d + 1) * fold, (2 * d + 2) * fold)
            folded[at, half : half + LANES] = both.astype(BF)
            folded[at, half + LANES :] = jnp.zeros((fold, half - LANES), BF)
        for u in range(UNITS):
            (to,) = slot(u)
            to[top : top + krows, :] = wide[pl.ds(multiple(where_ref[u] * krows, 16), krows), :]
            to[top + krows :, :] = folded[pl.ds(multiple(where_ref[u] * 2 * fold, 16), 2 * fold), :]

    return run(
        kernel,
        "weight_grads",
        (where,),
        (n1, gv, ga, ga_other, gain, *gats, *mixed, *parts),
        slot_shapes(deep, length, MIXER_FIRST, 1, False),
        (
            pltpu.VMEM((model, length), BF),
            pltpu.VMEM((model, width), BF),
            pltpu.VMEM((UNITS * 2 * fold, length), BF),
            pltpu.VMEM((2, UNITS, LANES), F32),
        ),
        aliases={6 + 2 * len(mixed) + n: n for n in range(len(parts))},
    )


class Ring:
    def __init__(self, size):
        self.size = size
        self.chips = size // 2
        n = self.chips
        self.order = list(range(0, n, 2)) + list(range(n - 1, 0, -2))
        me = lax.axis_index("dp")
        self.core = me % 2
        chip = me // 2
        self.at = jnp.where(chip % 2 == 0, chip // 2, n - 1 - chip // 2)
        self.up = self.pairs(1)
        self.down = self.pairs(-1)
        self.swap = [(d, d ^ 1) for d in range(size)]

    def pairs(self, step):
        n = self.chips
        return [
            (self.order[p] * 2 + c, self.order[(p + step) % n] * 2 + c) for p in range(n) for c in range(2)
        ]

    def device(self, offset, core):
        n = self.chips
        p = (self.at + jnp.asarray(offset, jnp.int32) + n) % n
        chip = jnp.where(p < (n + 1) // 2, 2 * p, 2 * (n - 1 - p) + 1)
        return chip * 2 + core

    def gathered(self):
        n = self.chips
        offsets = [0]
        for s in range(1, n // 2):
            offsets += [-s, s]
        offsets.append(n // 2)
        return jnp.concatenate([self.device(offsets, self.core), self.device(offsets, 1 - self.core)])

    def scattered(self):
        offsets = list(range(self.chips))
        return jnp.concatenate([self.device(offsets, self.core), self.device(offsets, 1 - self.core)])


class Gather:
    def __init__(self, ring, unit, cut):
        self.ring = ring
        self.rows = unit.shape[0]
        self.cut = cut
        self.last = [unit, unit]
        self.hops = 0
        self.mine = []
        self.theirs = []
        self.here = [unit]

    def values(self):
        return self.last

    def take(self, values):
        self.last = list(values)

    def arrived(self, units):
        self.hops = 1
        self.last = self.here = list(units)

    def hop(self):
        ring = self.ring
        self.hops += 1
        up, down = self.last
        if self.hops == ring.chips // 2:
            up, down = up[: self.cut], down[self.cut :]
        self.last = [lax.ppermute(up, "dp", ring.up), lax.ppermute(down, "dp", ring.down)]
        self.swap()
        self.here = self.last

    def swap(self):
        self.theirs += [lax.ppermute(one, "dp", self.ring.swap) for one in self.here]
        self.mine += self.here
        self.here = []

    def finish(self):
        self.swap()
        return self.mine + self.theirs

    def shares(self):
        n = self.ring.chips
        own = [(u, 0, self.rows) for u in range(n - 1)]
        own += [(n - 1, 0, self.cut), (n - 1, self.cut, self.rows - self.cut)]
        return own + [(u + n, first, rows) for u, first, rows in own]


class Scatter:
    def __init__(self, ring, first, pieces, keep, *give):
        self.ring = ring
        self.keep = keep
        count = len(first) * pieces
        swapped = [lax.ppermute(one, "dp", ring.swap) for one in give[:count]]
        self.early = {k: swapped[n * pieces : (n + 1) * pieces] for n, k in enumerate(first)}
        self.first = first
        self.late = late_units(first)
        self.later = give[count:]
        self.got = {}
        self.last = {}

    def values(self):
        return list(self.last.values()) if self.last else [one for k in self.first for one in self.early[k]]

    def take(self, values):
        if self.last:
            self.last = dict(zip(self.last, values))
        else:
            pieces = len(values) // len(self.first)
            self.early = {k: values[n * pieces : (n + 1) * pieces] for n, k in enumerate(self.first)}

    def swap_all(self, *after):
        stack = lax.ppermute(tie(self.later[0], *after), "dp", self.ring.swap)
        self.got = {k: stack[n] for n, k in enumerate(self.late)}

    def hop(self, way, k):
        got = self.early[k][0] if k in self.early else self.got[k]
        value = self.keep[k].astype(F32) + got.astype(F32)
        if way in self.last:
            value = value + self.last[way].astype(F32)
        value = value.astype(BF)
        self.last[way] = lax.ppermute(value, "dp", self.ring.up if way == "up" else self.ring.down)
        return value

    def result(self):
        return self.keep, self.got[0], self.last["up"], self.last["down"]


def together(chains, *more):
    values = [one for chain in chains for one in chain.values()]
    tied = lax.optimization_barrier(tuple(values) + more)
    at = 0
    for chain in chains:
        count = len(chain.values())
        chain.take(tied[at : at + count])
        at += count
    return tied[at:]


def tie(value, *after):
    return lax.optimization_barrier((value,) + after)[0] if after else value


def shards(
    tokens,
    segment_ids,
    gain_attn,
    gain_ffn,
    random_scores,
    w_value,
    w_output,
    w_up,
    w_down,
    cotangent,
):
    devices = lax.axis_size("dp")
    second = lax.axis_index("mp")
    length = segment_ids.shape[1]
    heads = random_scores.shape[0]
    model = tokens.shape[1]
    width = w_value.shape[1]
    size = width // heads
    rows = length // UNITS
    krows = model // UNITS
    ring = devices == UNITS and devices // 2 <= RING_CHIPS
    flip = [(0, 1), (1, 0)]
    second_at = jnp.reshape(second, (1,)).astype(jnp.int32)
    plan = Unit(heads, rows, krows, length, model, width, w_up.shape[1])

    if ring:
        net = Ring(devices)
        far = net.chips // 2
        where_in = net.gathered().astype(jnp.int32)
        where_out = net.scattered().astype(jnp.int32)
        upper, lower, wo_own = pack_unit(
            plan, second_at, random_scores, w_value, gain_attn, gain_ffn, w_up, w_down.T, w_output.T
        )
        ways = (net.up, net.down)
        uppers = [lax.ppermute(upper, "dp", way) for way in ways]
        wo_other = lax.ppermute(tie(wo_own, where_in, where_out), "mp", flip)
        lower = fill_low(plan, second_at, lower, wo_other)
        lowers = [lax.ppermute(lower, "dp", way) for way in ways]
        (unit,) = join_units(plan, [upper], [lower])
        one = Gather(net, unit, plan.cut)
        one.swap()
        uppers[0], uppers[1], *lowers = lax.optimization_barrier((*uppers, *lowers))
        one.arrived(join_units(plan, uppers, lowers))
        for step in range(1, far - 1):
            one.hop()
            together([one])
            one.here = one.last
        there = one.mine + one.theirs
        shares = one.shares()
        half = len(shares) // 2
        early = [n for n in range(len(one.mine))] + [half + n for n in range(len(one.theirs))]
        one.hop()
        begun = mixer_first(plan, where_in, tokens, segment_ids, there, [shares[n] for n in early], heads)
        begun = together([one], *begun)
        one.here = one.last
        units = one.finish()
        late = [n for n in range(len(shares)) if n not in early]
        near = late
        order = [n for n in range(len(shares)) if n not in near] + near
        units, shares = [units[n] for n in order], [shares[n] for n in order]
        late = [n for n, old in enumerate(order) if old in late]
    else:
        where_in = jnp.arange(UNITS, dtype=jnp.int32)
        where_out = where_in

        def gather(one, axis=0):
            return lax.all_gather(one.astype(BF), "dp", axis=axis, tiled=True)

        wo_own = w_output.T.astype(BF)
        wo_other = lax.ppermute(wo_own, "mp", flip)
        halves = [jnp.where(second == n, wo_own, wo_other) for n in range(2)]
        scores = gather(random_scores, 1).reshape(heads, UNITS, rows, length).transpose(1, 0, 2, 3)
        wide = [gather(one) for one in (w_value, *halves)]
        wide = jnp.concatenate(wide, axis=1).reshape(UNITS, krows, plan.wide)
        ffn = jnp.concatenate([gather(w_up), gather(w_down.T)], axis=1).reshape(UNITS, krows, -1)
        stack = [scores.reshape(UNITS, heads * rows, length)]
        for kind, column in plan.blocks:
            stack.append((ffn if kind == "ffn" else wide)[:, :, column : column + length])
        gains = jnp.stack([gather(gain_attn), gather(gain_ffn)]).reshape(2, UNITS, krows).transpose(1, 0, 2)
        gains = jnp.pad(gains, ((0, 0), (0, plan.fold - 2), (0, length - plan.gain_lane - krows)))
        tail = wide[:, :, plan.wide - plan.tail :].reshape(UNITS, 3, plan.fold, plan.tail)
        stack.append(jnp.concatenate([tail[:, 0], tail[:, 1], tail[:, 2], gains], axis=2))
        whole = jnp.concatenate(stack, axis=1)
        units = [whole[u] for u in range(UNITS)]
        shares = [(u, 0, plan.deep) for u in range(UNITS)]
        early, late, near = list(range(UNITS // 2)), list(range(UNITS // 2, UNITS)), []
        begun = mixer_first(plan, where_in, tokens, segment_ids, units[: UNITS // 2], shares[: UNITS // 2], heads)

    own = [n for n in late if shares[n][0] < UNITS // 2] if ring else late[:1]
    late = [n for n in late if n not in own]
    begun = mixer_next(plan, where_in, begun, [units[n] for n in own], [shares[n] for n in own])
    e, wv, _, va, sums, n1, gains, *mixed = mixer_forward(
        plan, where_in, begun, [units[n] for n in late], [shares[n] for n in late], heads, width
    )
    mixed_other = [lax.ppermute(one, "mp", flip) for one in mixed]
    w, wo_whole, gact, mixf, rb, wo = second_weights(plan, where_in, second_at, cotangent, sums, units, shares, len(near), size)
    backs, others, resids, kept = [], [], [], []
    for part in range(PARTS):
        back, resid, *kept = ffn_main(
            second_at, tokens, mixed[part], mixed_other[part], gact, gains, w, wo_whole, part, PARTS, kept
        )
        backs.append(back)
        others.append(lax.ppermute(tie(back, *others[-1:]), "mp", flip))
        resids.append(resid)
    n2, act, gpre = kept
    parts_two = ffn_grads(where_out, n2, gpre, act, cotangent)
    early = resid_back(backs[0], others[0], resids[0], cotangent, gains, wo, mixf, 0, heads, size, [])
    ffn_one, ffn_two = ffn_out(tie(act, *early), w, 3 * length // 8)
    first_values = value_first(early[2], rb, e, size)
    parts_one = mixer_grads(where_out, early[2], va, e, rb, krows, 0, [])
    if ring:
        ffn_sum = Scatter(net, FFN_FIRST, 1, *parts_two)
        ffn_sum.swap_all(others[0], *ffn_sum.values())
        for step in range(2):
            ffn_sum.hop("down", far + step)
            ffn_sum.hop("up", far - 1 - step)
            if step == 0:
                ffn_one, ffn_two, first_values, *more = together(
                    [ffn_sum], ffn_one, ffn_two, first_values, *early, *parts_one
                )
                early, parts_one = more[: len(early)], more[len(early) :]
    cot_late = tie(cotangent, first_values, *parts_one)
    final = resid_back(backs[1], others[1], resids[1], cot_late, gains, wo, mixf, 1, heads, size, early[3:])
    gres, gats = (early[0], final[0]), (early[1], final[1])
    xh = final[2]
    gv, part_one, part_two, ga = value_back(xh, first_values, rb, e, wv, tokens, size, length // 2)
    ga_other = lax.ppermute(ga, "mp", flip)
    one_other = lax.ppermute(tie(ffn_one, ga), "mp", flip)
    if ring:
        together([ffn_sum])
        for step in range(2, far - 1):
            ffn_sum.hop("down", far + step)
            ffn_sum.hop("up", far - 1 - step)
    parts_one = mixer_grads(where_out, xh, va, e, rb, krows, 1, parts_one)
    parts_one = weight_grads(where_out, parts_one, n1, gv, gats, mixed, ga, ga_other, final[3])

    top = heads * rows
    if ring:
        score_sum = Scatter(net, MIXER_FIRST, 1, *parts_one)
        one_other, ffn_two = together([ffn_sum, score_sum], one_other, ffn_two)
        value = score_sum.hop("up", far)
        ffn_sum.hop("down", 2 * far - 1)
        score_sum.swap_all(value)
        two_other = lax.ppermute(ffn_two, "mp", flip)
        part_one, part_two = together([score_sum], part_one, part_two)
        for step in range(1, far):
            score_sum.hop("up", far - step)
            score_sum.hop("down", far + step)
            if step == 1:
                part_other = [lax.ppermute(part_one, "mp", flip)]
                two_other, part_two = together([ffn_sum, score_sum], two_other, part_two)
            elif step < far - 1:
                part_other.append(lax.ppermute(part_two, "mp", flip))
                (part_other[0],) = together([score_sum], part_other[0])
        out_up, out_down = ffn_result(*ffn_sum.result())
        out_scores, out_value, out_output, *out_gains = mixer_result(*score_sum.result(), heads, krows, width)
        out_down, out_output = out_down.T, out_output.T
        out_gain_one, out_gain_two = [one.reshape(krows) for one in out_gains]
    else:
        two_other = lax.ppermute(ffn_two, "mp", flip)
        part_other = [lax.ppermute(one, "mp", flip) for one in (part_one, part_two)]

        def scatter(one, axis=0):
            return lax.psum_scatter(one, "dp", scatter_dimension=axis, tiled=True)

        def whole(first, pieces, keep, *give):
            late = late_units(first)
            early, later = give[: len(first) * pieces], give[len(first) * pieces :]
            given = []
            for k in range(UNITS // 2):
                if k in first:
                    at = first.index(k) * pieces
                    given.append(jnp.concatenate(early[at : at + pieces]))
                else:
                    given.append(later[0][late.index(k)] if len(later) == 1 else later[late.index(k)])
            return jnp.concatenate([keep, jnp.stack(given)]).astype(F32)

        two = whole(FFN_FIRST, 1, *parts_two).reshape(model, -1)
        one = whole(MIXER_FIRST, 1, *parts_one)
        out_up = scatter(two[:, : two.shape[1] // 2])
        out_down = scatter(two[:, two.shape[1] // 2 :]).T
        scores = one[:, :top].reshape(UNITS, heads, rows, length).transpose(1, 0, 2, 3)
        out_scores = scatter(scores.reshape(heads, length, length), 1)
        out_value = scatter(one[:, top : top + krows, :width].reshape(model, width))
        low, fold, half = top + krows, krows // 3, length // 2
        folded = [one[:, low + n // 2 * fold : low + (n // 2 + 1) * fold, n % 2 * half :][:, :, :half] for n in range(3)]
        other = jnp.concatenate([one[:, top:low, width:], jnp.concatenate(folded, axis=1)], axis=2)
        out_output = scatter(other.reshape(model, width)).T
        out_gain_one = scatter(one[:, low + fold, half : half + krows].reshape(model))
        out_gain_two = scatter(one[:, low + fold + 1, half : half + krows].reshape(model))
    ffn = jnp.concatenate([ffn_one, ffn_two])
    ffn_other = jnp.concatenate([one_other, two_other])
    output = (jnp.concatenate(resids) + (ffn.astype(F32) + ffn_other.astype(F32))).astype(BF)
    written = []
    for part, (mine, other) in enumerate(zip((part_one, part_two), part_other)):
        written = [token_grads(mine, other, gres[part], tokens, gains, part, written)]
    (grad_tokens,) = written
    return (
        output,
        grad_tokens,
        out_gain_one,
        out_gain_two,
        out_scores,
        out_value,
        out_output,
        out_up,
        out_down,
    )


def solution(mesh):
    in_specs = (
        P("dp", None),
        P("dp", None),
        P("dp"),
        P("dp"),
        P("mp", "dp", None),
        P("dp", "mp"),
        P("mp", "dp"),
        P("dp", "mp"),
        P("mp", "dp"),
        P("dp", None),
    )
    out_specs = (
        P("dp", None),
        P("dp", None),
        P("dp"),
        P("dp"),
        P("mp", "dp", None),
        P("dp", "mp"),
        P("mp", "dp"),
        P("dp", "mp"),
        P("mp", "dp"),
    )
    return jax.shard_map(shards, mesh=mesh, in_specs=in_specs, out_specs=out_specs, check_vma=False)
```

```python
import jax
import jax.numpy as jnp
from jax import lax
from jax.experimental import pallas as pl
from jax.experimental.pallas import tpu as pltpu
from jax.sharding import PartitionSpec as P

EPSILON = 1e-06
NEGATIVE = -1e30
BF = jnp.bfloat16
F32 = jnp.float32
UNITS = 16
LANES = 128
PARTS = 2
RING_CHIPS = 8
VMEM_BYTES = 20 * 1024 * 1024
NT = (((1,), (1,)), ((), ()))
TN = (((0,), (0,)), ((), ()))
NN = (((1,), (0,)), ((), ()))


def mm(a, b, dims=NN):
    return lax.dot_general(a, b, dims, preferred_element_type=F32)


def run(kernel, name, scalars, arrays, outs, scratch=(), loose=(), loose_outs=(), aliases=None, near=0):
    held = [pltpu.with_memory_space_constraint(one, pltpu.VMEM) for one in arrays]
    results = [pltpu.VMEM(*one) for one in outs] + [jax.ShapeDtypeStruct(*one) for one in loose_outs]
    specs = [pl.BlockSpec(memory_space=pltpu.SMEM)] * len(scalars)
    specs += [pl.BlockSpec(memory_space=pltpu.VMEM)] * len(arrays)
    far = len(loose) - near
    specs += [pl.BlockSpec(memory_space=pltpu.HBM)] * far + [pl.BlockSpec(memory_space=pl.ANY)] * near
    loose = [pltpu.with_memory_space_constraint(one, pltpu.HBM) for one in loose[:far]] + list(loose[far:])
    out_specs = [pl.BlockSpec(memory_space=pltpu.VMEM)] * len(outs)
    out_specs += [pl.BlockSpec(memory_space=pl.ANY)] * len(loose_outs)
    return pl.pallas_call(
        kernel,
        out_shape=tuple(results),
        in_specs=specs,
        out_specs=tuple(out_specs),
        scratch_shapes=list(scratch),
        compiler_params=pltpu.CompilerParams(vmem_limit_bytes=VMEM_BYTES),
        cost_estimate=pl.CostEstimate(flops=1, bytes_accessed=1, transcendentals=0),
        input_output_aliases=aliases or {},
        name=name,
    )(*scalars, *held, *loose)


def gelu_pair(x):
    c = 0.7978845608028654
    a = 0.044715
    square = x * x
    t = jnp.tanh(c * x * (1.0 + a * square))
    half = 0.5 * (1.0 + t)
    return x * half, half + 0.5 * x * (1.0 - t * t) * (c * (1.0 + 3.0 * a * square))


def multiple(value, of):
    return pl.multiple_of(value, of)


class Unit:
    def __init__(self, heads, rows, krows, length, model, width, hidden):
        self.scores = heads * rows
        self.krows = krows
        self.length = length
        self.width = width
        self.hidden = hidden
        self.wide = width + model
        self.blocks = [("ffn", n * length) for n in range(2 * hidden // length)]
        self.blocks += [("proj", n * length) for n in range(self.wide // length)]
        self.tail = self.wide % length
        self.last = self.scores + krows * len(self.blocks)
        self.fold = krows // 3
        self.deep = self.last + self.fold
        self.cut = self.scores + krows * (2 * hidden // length // 3)
        self.gain_lane = 3 * self.tail
        self.head = self.value_row()

    def projection_parts(self):
        parts = []
        for n, (kind, first) in enumerate(self.blocks):
            at = self.scores + n * self.krows
            if kind == "proj":
                skip = max(self.width - first, 0)
                parts.append((at, skip, 0, first + skip - self.width, self.krows, self.length - skip))
        for n in range(3):
            column = self.wide - self.tail - self.width
            parts.append((self.last, n * self.tail, n * self.fold, column, self.fold, self.tail))
        return parts

    def ffn_blocks(self, first, rows):
        inside = [
            n
            for n, (kind, _) in enumerate(self.blocks)
            if kind == "ffn" and first <= self.scores + n * self.krows < first + rows
        ]
        return (inside[0], len(inside)) if inside else (0, 0)

    def value_row(self):
        return self.scores + [kind for kind, _ in self.blocks].index("proj") * self.krows


def other_parts(plan, first):
    begin = plan.width + first * plan.width
    parts = []
    for n, (kind, column) in enumerate(plan.blocks):
        low, high = max(begin, column), min(begin + plan.width, column + plan.length)
        if kind == "proj" and low < high:
            parts.append((plan.scores + n * plan.krows, low - column, 0, low - begin, plan.krows, high - low))
    low = max(begin, plan.wide - plan.tail)
    if low < begin + plan.width:
        for n in range(3):
            lanes = n * plan.tail + low - (plan.wide - plan.tail)
            parts.append((plan.last, lanes, n * plan.fold, low - begin, plan.fold, begin + plan.width - low))
    return parts


def put_half(plan, low, half_ref, first):
    for row, lane, at, column, rows, lanes in other_parts(plan, first):
        row = row - plan.head
        low[row : row + rows, lane : lane + lanes] = half_ref[at : at + rows, column : column + lanes]


def pack_unit(plan, second, scores, wv, gain_one, gain_two, w_up, w_down, wo):
    inputs = (scores, wv, gain_one.reshape(1, -1), gain_two.reshape(1, -1), w_up, w_down, wo)
    count = len(inputs)
    krows, length, width = plan.krows, plan.length, plan.width
    per = plan.hidden // length
    assert plan.tail <= width

    def kernel(second_ref, *rest):
        out, low, wo_out, gains = rest[count : count + 4]
        held, sem = rest[count + 4 : -1], rest[-1]
        fetch(rest[:count], held, sem)
        s_ref, wv_ref, ga_ref, gf_ref, up_ref, down_ref, own_ref = held
        out[: plan.scores, :] = s_ref[...].reshape(plan.scores, length).astype(BF)
        for n, (kind, column) in enumerate(plan.blocks):
            at = slice(plan.scores + n * krows, plan.scores + (n + 1) * krows)
            if kind == "ffn":
                ref, first = (up_ref, column) if n < per else (down_ref, column - plan.hidden)
                out[at, :] = ref[:, first : first + length].astype(BF)
        low[...] = jnp.zeros_like(low)
        low[:krows, :width] = wv_ref[...].astype(BF)
        wo_out[...] = own_ref[...].astype(BF)
        for place in range(2):

            @pl.when(second_ref[0] == place)
            def _():
                put_half(plan, low, wo_out, place)

        gains[...] = jnp.zeros_like(gains)
        gains[0:1, :krows] = ga_ref[...]
        gains[1:2, :krows] = gf_ref[...]
        low[plan.last - plan.head :, plan.gain_lane :] = gains[...].astype(BF)

    return run(
        kernel,
        "pack_unit",
        (second,),
        (),
        (((plan.head, length), BF), ((plan.deep - plan.head, length), BF), ((krows, width), BF)),
        (
            pltpu.VMEM((plan.fold, length - plan.gain_lane), F32),
            *[pltpu.VMEM(one.shape, one.dtype) for one in inputs],
            pltpu.SemaphoreType.DMA((count,)),
        ),
        loose=inputs,
    )


def fill_low(plan, second, low, other):
    def kernel(second_ref, old, other_ref, out):
        for place in range(2):

            @pl.when(second_ref[0] == 1 - place)
            def _():
                put_half(plan, out, other_ref, place)

    return run(kernel, "fill_low", (second,), (low, other), ((low.shape, BF),), aliases={1: 0})[0]


def join_units(plan, uppers, lowers):
    count = len(uppers)

    def kernel(*refs):
        for n in range(count):
            out = refs[2 * count + n]
            out[: plan.head, :] = refs[n][...]
            out[plan.head :, :] = refs[count + n][...]

    return run(kernel, "join_units", (), (*uppers, *lowers), [((plan.deep, plan.length), BF)] * count)


def fetch(refs, held, sem):
    copies = [pltpu.make_async_copy(ref, to, sem.at[n]) for n, (ref, to) in enumerate(zip(refs, held))]
    for copy in copies:
        copy.start()
    for copy in copies:
        copy.wait()


def pick(units, shares, where_ref, parts, target, sem):
    copies = []
    for n, (u, first, rows) in enumerate(shares):
        owner = where_ref[u]
        for m, part in enumerate(parts):
            row, column, count, columns = part[0], part[1], part[-2], part[-1]
            if first <= row and row + count <= first + rows:
                source = units[n].at[pl.ds(row - first, count), pl.ds(column, columns)]
                copies.append(pltpu.make_async_copy(source, target(m, owner), sem.at[u, m]))
                copies[-1].start()
    return copies


def document_mask(seg_ref, same):
    length = same.shape[0]
    documents = (seg_ref[...] == lax.broadcasted_iota(jnp.int32, (LANES, length), 0)).astype(BF)
    same[...] = mm(documents, documents, TN)


def exponentials(where_ref, shares, sources, e_ref, same):
    heads, length, _ = e_ref.shape
    rows = length // UNITS

    def one_head(h, carry):
        for (u, _, _), (ref, first) in zip(shares, sources):
            at = pl.ds(multiple(where_ref[u] * rows, rows), rows)
            s = ref[pl.ds(multiple(first + h * rows, rows), rows), :].astype(F32)
            e_ref[h, at, :] = (jnp.exp(s) * same[at, :]).astype(BF)
        return carry

    lax.fori_loop(0, heads, one_head, 0)


def low_parts(plan):
    return [
        (plan.value_row(), 0, plan.krows, plan.width),
        (plan.last, plan.gain_lane, plan.fold, LANES),
    ]


def bring_low(plan, units, shares, where_ref, wv_ref, low_ref, sem):
    krows = plan.krows

    def target(m, owner):
        if m == 0:
            return wv_ref.at[pl.ds(multiple(owner * krows, 16), krows), :]
        return low_ref.at[owner]

    return pick(units, shares, where_ref, low_parts(plan), target, sem)


def mixer_first(plan, where, tokens, segments, units, shares, heads):
    length, model = tokens.shape
    rows = length // UNITS

    def kernel(where_ref, tok_ref, seg_ref, *rest):
        e_ref, wv_ref, low_ref, hat_ref, same, unit, sem, more = rest[len(units) :]
        top = heads * rows

        def target(m, owner):
            return unit.at[pl.ds(multiple(owner * top, top), top), :]

        came = pick(rest[: len(units)], shares, where_ref, [(0, 0, top, length)], target, sem)
        copies = bring_low(plan, rest[: len(units)], shares, where_ref, wv_ref, low_ref, more)
        document_mask(seg_ref, same)
        x = tok_ref[...].astype(F32)
        hat_ref[...] = x * lax.rsqrt(jnp.mean(x * x, axis=-1, keepdims=True) + EPSILON)
        for copy in came:
            copy.wait()
        sources = [(unit, where_ref[u] * top) for u, _, _ in shares]
        exponentials(where_ref, shares, sources, e_ref, same)
        for copy in copies:
            copy.wait()

    return run(
        kernel,
        "mixer_first",
        (where,),
        (tokens, segments),
        (
            ((heads, length, length), BF),
            ((model, plan.width), BF),
            ((UNITS, plan.fold, LANES), BF),
            ((length, model), F32),
            ((length, length), F32),
        ),
        (
            pltpu.VMEM((heads * length, length), BF),
            pltpu.SemaphoreType.DMA((UNITS, 1)),
            pltpu.SemaphoreType.DMA((UNITS, 2)),
        ),
        loose=units,
    )


def take_late(plan, where_ref, shares, refs, e_ref, wv_ref, low, same):
    krows = plan.krows
    for (u, first, rows), ref in zip(shares, refs):
        for m, (row, lane, deep, lanes) in enumerate(low_parts(plan)):
            if first <= row < first + rows:
                part = ref[row - first : row - first + deep, lane : lane + lanes]
                if m == 0:
                    wv_ref[pl.ds(multiple(where_ref[u] * krows, 16), krows), :] = part
                else:
                    low[where_ref[u]] = part
    scored = [n for n in range(len(shares)) if shares[n][1] == 0]
    exponentials(where_ref, [shares[n] for n in scored], [(refs[n], 0) for n in scored], e_ref, same)


def mixer_next(plan, where, early, units, shares):
    e, wv, low, hat, same = early
    count = len(units)

    def kernel(where_ref, same_ref, e_old, wv_old, low_old, *rest):
        take_late(plan, where_ref, shares, rest[:count], *rest[count:], same_ref)

    outs = [(one.shape, one.dtype) for one in (e, wv, low)]
    more = run(
        kernel, "mixer_next", (where,), (same, e, wv, low, *units), outs, aliases={2: 0, 3: 1, 4: 2}
    )
    return [*more, hat, same]


def mixer_forward(plan, where, early, units, shares, heads, width):
    length, model = early[3].shape
    size = width // heads
    krows = model // UNITS
    wide = heads * LANES
    count = len(units)

    def kernel(where_ref, e_old, wv_old, low_old, hat_ref, same, *rest):
        e_ref, wv_ref, low, va_ref, sums_ref, n1_ref, gains_ref, *mixed, pieces = rest[count:]
        take_late(plan, where_ref, shares, rest[:count], e_ref, wv_ref, low, same)
        for d in range(UNITS):
            some = low[d].astype(F32)
            pieces[0, d : d + 1, :] = some[0:1, :]
            pieces[1, d : d + 1, :] = some[1:2, :]
        spread = (
            lax.broadcasted_iota(jnp.int32, (LANES, model), 1) % krows
            == lax.broadcasted_iota(jnp.int32, (LANES, model), 0)
        ).astype(BF)
        own = (
            lax.broadcasted_iota(jnp.int32, (UNITS, model), 1) // krows
            == lax.broadcasted_iota(jnp.int32, (UNITS, model), 0)
        )
        gains = []
        for t in range(2):
            full = jnp.where(own, mm(pieces[t].astype(BF), spread), 0.0)
            gains.append(jnp.sum(full, axis=0, keepdims=True))
            gains_ref[t : t + 1, :] = gains[t]
        n1_ref[...] = (hat_ref[...] * gains[0]).astype(BF)
        values = mm(n1_ref[...], wv_ref[...]).astype(BF)
        tail = (lax.broadcasted_iota(jnp.int32, (length, LANES - size), 1) < 2).astype(BF)
        for h in range(heads):
            va_ref[:, h * LANES : h * LANES + size] = values[:, h * size : (h + 1) * size]
            va_ref[:, h * LANES + size : (h + 1) * LANES] = tail

        for h in range(heads):
            lanes = slice(h * LANES, (h + 1) * LANES)
            sums = mm(e_ref[h], va_ref[:, lanes])
            sums_ref[:, lanes] = sums
            values = (sums * (1.0 / sums[:, size : size + 1]))[:, :size].astype(BF)
            for part, mixed_ref in enumerate(mixed):
                some = slice(part * (length // PARTS), (part + 1) * (length // PARTS))
                mixed_ref[:, h * size : (h + 1) * size] = values[some, :]

    return run(
        kernel,
        "mixer_forward",
        (where,),
        (*early, *units),
        (
            ((heads, length, length), BF),
            ((model, width), BF),
            ((UNITS, plan.fold, LANES), BF),
            ((length, wide), BF),
            ((length, wide), F32),
            ((length, model), BF),
            ((2, model), F32),
            *[((length // PARTS, width), BF)] * PARTS,
        ),
        (
            pltpu.VMEM((2, UNITS, LANES), F32),
        ),
        aliases={1: 0, 2: 1, 3: 2},
    )


def second_weights(plan, where, second, cotangent, sums, units, shares, near, size):
    length, model = cotangent.shape
    wide = sums.shape[1]
    hidden, krows, width = plan.hidden, plan.krows, plan.width
    parts = plan.projection_parts()
    blocks = 2 * hidden // length

    def kernel(where_ref, second_ref, cot_ref, sums_ref, *rest):
        out, wo_ref, gact, mixf_ref, rb_ref, own_ref, sem, more = rest[len(units) :]

        def target(m, owner):
            _, _, row, column, rows, columns = parts[m]
            return wo_ref.at[pl.ds(multiple(owner * krows + row, 16), rows), pl.ds(column, columns)]

        copies = []
        for n, (u, first, rows) in enumerate(shares):
            begin, count = plan.ffn_blocks(first, rows)
            if count:
                source = rest[n].at[pl.ds(plan.scores + begin * krows - first, count * krows), :]
                to = out.at[pl.ds(begin, count), pl.ds(multiple(where_ref[u] * krows, 16), krows), :]
                copies.append(pltpu.make_async_copy(source.reshape(count, krows, length), to, more.at[n]))
                copies[-1].start()
        copies += pick(rest[: len(units)], shares, where_ref, parts, target, sem)
        inside = lax.broadcasted_iota(jnp.int32, (length, LANES), 1) < size
        for h in range(wide // LANES):
            lanes = slice(h * LANES, (h + 1) * LANES)
            inverse = jnp.broadcast_to(1.0 / sums_ref[:, h * LANES + size : h * LANES + size + 1], (length, LANES))
            rb_ref[:, lanes] = inverse
            mixf_ref[:, lanes] = jnp.where(inside, sums_ref[:, lanes] * inverse, 0.0)
        for copy in copies:
            copy.wait()
        for j in range(blocks // 2):
            gact[:, j * length : (j + 1) * length] = mm(cot_ref[...], out[blocks // 2 + j])
        own = wo_ref[:, pl.ds(multiple(second_ref[0] * width, LANES), width)]
        own_ref[...] = jnp.zeros_like(own_ref)
        for h in range(width // size):
            own_ref[:, h * LANES : h * LANES + size] = own[:, h * size : (h + 1) * size]

    return run(
        kernel,
        "second_weights",
        (where, second),
        (cotangent, sums),
        (
            ((blocks, model, length), BF),
            ((model, model), BF),
            ((length, hidden), F32),
            (sums.shape, F32),
            (sums.shape, F32),
            ((model, wide), BF),
        ),
        (pltpu.SemaphoreType.DMA((UNITS, len(parts))), pltpu.SemaphoreType.DMA((len(units),))),
        loose=units,
        near=near,
    )


def ffn_main(second, tokens, mixed_own, mixed_other, gact, gains, w, wo, part, parts, before):
    length, model = tokens.shape
    width = mixed_own.shape[1]
    hidden = gact.shape[1]
    chunk = length // parts
    piece = w.shape[2]
    at = slice(part * chunk, (part + 1) * chunk)

    def kernel(second_ref, tok_ref, own_ref, other_ref, gact_ref, gains_ref, w_ref, wo_ref, *rest):
        back_ref, resid_ref, n2_ref, act_ref, gpre_ref, mixed = rest[len(before) :]
        first = second_ref[0]
        mixed[:, pl.ds(multiple(first * width, LANES), width)] = own_ref[...]
        mixed[:, pl.ds(multiple((1 - first) * width, LANES), width)] = other_ref[...]
        attn = mm(mixed[...], wo_ref[...], NT)
        resid = tok_ref[at, :].astype(F32) + attn
        resid_ref[...] = resid
        inv = lax.rsqrt(jnp.mean(resid * resid, axis=-1, keepdims=True) + EPSILON)
        n2 = (resid * inv * gains_ref[1:2, :]).astype(BF)
        n2_ref[at, :] = n2
        terms = []
        pres = [mm(n2, w_ref[j]) for j in range(hidden // piece)]
        for j in range(hidden // piece):
            cols = slice(j * piece, (j + 1) * piece)
            act, slope = gelu_pair(pres[j])
            act_ref[at, cols] = act.astype(BF)
            gpre = (gact_ref[at, cols] * slope).astype(BF)
            gpre_ref[at, cols] = gpre
            terms.append(mm(gpre, w_ref[j], NT))
        back_ref[...] = sum(terms).astype(BF)

    return run(
        kernel,
        "ffn_main",
        (second,),
        (tokens, mixed_own, mixed_other, gact, gains, w, wo, *before),
        (
            ((chunk, model), BF),
            ((chunk, model), F32),
            ((length, model), BF),
            ((length, hidden), BF),
            ((length, hidden), BF),
        ),
        (
            pltpu.VMEM((chunk, 2 * width), BF),
        ),
        aliases={8 + n: 2 + n for n in range(len(before))},
    )


def late_units(first):
    return [k for k in range(UNITS // 2) if k not in first]


def slots(refs, first, pieces):
    half = UNITS // 2
    count = len(first) * pieces
    keep, early, later = refs[0], refs[1 : 1 + count], refs[1 + count :]
    late = late_units(first)

    def slot(u):
        if u < half:
            return [keep.at[u]]
        k = u - half
        if k in first:
            at = first.index(k) * pieces
            return early[at : at + pieces]
        n = late.index(k)
        return [later[0].at[n] if len(later) == 1 else later[n]]

    return slot


def slot_shapes(rows, columns, first, pieces, apart):
    half = UNITS // 2
    early = [((rows, columns), BF)] * (len(first) * pieces)
    count = half - len(first)
    later = [((rows, columns), BF)] * count if apart else [((count, rows, columns), BF)]
    return [((half, rows, columns), BF), *early, *later]


FFN_FIRST = [UNITS // 4, UNITS // 4 - 1]
MIXER_FIRST = [UNITS // 4]


def result_kernel(name, keep, own, up, down, shapes, cut):
    def kernel(keep_ref, own_ref, up_ref, down_ref, *rest):
        outs, held, sem = rest[: len(shapes)], rest[len(shapes) : -1], rest[-1]

        def total(rows, columns):
            value = keep_ref[0, rows, columns].astype(F32) + own_ref[rows, columns].astype(F32)
            return value + up_ref[rows, columns].astype(F32) + down_ref[rows, columns].astype(F32)

        copies = []

        def send(source, to, n, m):
            copies.append(pltpu.make_async_copy(source, to, sem.at[n, m]))
            copies[-1].start()

        for n, (out, to) in reversed(list(enumerate(zip(outs, held)))):
            if len(shapes[n]) < 3:
                cut(n, to, total)
                send(to, out, n, 0)
            else:
                half = shapes[n][0] // 2
                for m, some in enumerate((range(half), range(half, shapes[n][0]))):
                    cut(n, to, total, some)
                    at = pl.ds(some.start, len(some))
                    send(to.at[at], out.at[at], n, m)
        for copy in copies:
            copy.wait()

    return run(
        kernel,
        name,
        (),
        (keep, own, up, down),
        (),
        (*[pltpu.VMEM(shape, F32) for shape in shapes], pltpu.SemaphoreType.DMA((len(shapes), 2))),
        loose_outs=[(shape, F32) for shape in shapes],
    )


def ffn_result(keep, own, up, down):
    _, rows, columns = keep.shape
    half = columns // 2

    def cut(n, to, total):
        to[...] = total(slice(None), slice(n * half, (n + 1) * half))

    return result_kernel("ffn_result", keep, own, up, down, [(rows, half)] * 2, cut)


def mixer_result(keep, own, up, down, heads, krows, width):
    _, deep, length = keep.shape
    top = deep - low_rows(krows)
    rows = top // heads
    lead, half, fold = length - width, length // 2, krows // 3
    shapes = [(heads, rows, length), (krows, width), (krows, width), (1, krows), (1, krows)]

    def cut(n, to, total, some=()):
        low = top + krows
        if n == 0:
            for h in some:
                to[h] = total(slice(h * rows, (h + 1) * rows), slice(None))
        elif n == 1:
            to[...] = total(slice(top, low), slice(0, width))
        elif n == 2:
            to[:, :lead] = total(slice(top, low), slice(width, length))
            for m in range(3):
                some = slice(low + m // 2 * fold, low + (m // 2 + 1) * fold)
                to[m * fold : (m + 1) * fold, lead:] = total(some, slice(m % 2 * half, (m % 2 + 1) * half))
        else:
            to[...] = total(slice(low + fold, low + 2 * fold), slice(half, half + LANES))[n - 3 : n - 2, :krows]

    return result_kernel("mixer_result", keep, own, up, down, shapes, cut)


def ffn_out(act, w, cut):
    length, hidden = act.shape
    blocks, model, piece = w.shape

    def kernel(act_ref, w_ref, one, two):
        for out, at in ((one, slice(0, cut)), (two, slice(cut, length))):
            terms = [
                mm(act_ref[at, j * piece : (j + 1) * piece], w_ref[blocks // 2 + j], NT) for j in range(blocks // 2)
            ]
            out[...] = sum(terms).astype(BF)

    return run(kernel, "ffn_out", (), (act, w), (((cut, model), BF), ((length - cut, model), BF)))


def ffn_grads(where, n2, gpre, act, cotangent):
    model, hidden = n2.shape[1], act.shape[1]
    krows = model // UNITS

    def kernel(where_ref, cot_ref, n2_ref, gpre_ref, act_ref, *rest):
        slot = slots(rest[:-2], FFN_FIRST, 1)
        scr, sem = rest[-2:]
        piece = hidden // 3
        for j in range(3):
            cols = slice(j * piece, (j + 1) * piece)
            down = slice(hidden + j * piece, hidden + (j + 1) * piece)
            scr[:, cols] = mm(n2_ref[...], gpre_ref[:, cols], TN).astype(BF)
            scr[:, down] = mm(cot_ref[...], act_ref[:, cols], TN).astype(BF)
        for u in range(UNITS):
            at = pl.ds(multiple(where_ref[u] * krows, 16), krows)
            (to,) = slot(u)
            to[...] = scr[at, :]

    return run(
        kernel,
        "ffn_grads",
        (where,),
        (cotangent, n2, gpre, act),
        slot_shapes(krows, 2 * hidden, FFN_FIRST, 1, False),
        (pltpu.VMEM((model, 2 * hidden), BF), pltpu.SemaphoreType.DMA((UNITS,))),
    )


def cut_gain(row, krows):
    model = row.shape[1]
    take = (
        lax.broadcasted_iota(jnp.int32, (model, LANES), 0) % krows
        == lax.broadcasted_iota(jnp.int32, (model, LANES), 1)
    ).astype(BF)
    own = (
        lax.broadcasted_iota(jnp.int32, (UNITS, model), 1) // krows
        == lax.broadcasted_iota(jnp.int32, (UNITS, model), 0)
    )
    high = row.astype(BF).astype(F32)
    pieces = mm(jnp.where(own, high, 0.0).astype(BF), take)
    return pieces + mm(jnp.where(own, row - high, 0.0).astype(BF), take)


def resid_back(back, other, resid, cotangent, gains, wo, mixf, part, heads, size, before):
    chunk, model = resid.shape
    wide = heads * LANES
    at = slice(part * chunk, (part + 1) * chunk)

    def kernel(cot_ref, gains_ref, wo_ref, mixf_ref, back_ref, other_ref, res_ref, *rest):
        gres_ref, gat_ref, xh_ref, gain_ref, gm = rest[len(before) :]
        g2 = back_ref[...].astype(F32) + other_ref[...].astype(F32)
        res = res_ref[...]
        inv = lax.rsqrt(jnp.mean(res * res, axis=-1, keepdims=True) + EPSILON)
        hat = res * inv
        total = jnp.sum((g2 * hat).reshape(chunk // 8, 8, model), axis=0)
        gain_ref[...] = total + rest[0][...] if before else total
        z = gains_ref[1:2, :] * g2
        corr = jnp.mean(z * hat, axis=-1, keepdims=True)
        gres = cot_ref[at, :].astype(F32) + inv * (z - hat * corr)
        gres_ref[...] = gres
        gat_ref[...] = gres.astype(BF)
        gm[...] = mm(gat_ref[...], wo_ref[...]).astype(BF)
        lane = lax.broadcasted_iota(jnp.int32, (chunk, LANES), 1)
        for h in range(heads):
            lanes = slice(h * LANES, (h + 1) * LANES)
            here = gm[:, lanes].astype(F32)
            inner = -jnp.sum(here * mixf_ref[at, lanes], axis=-1, keepdims=True)
            high = inner.astype(BF).astype(F32)
            xh_ref[:, lanes] = jnp.where(
                lane == size, high, jnp.where(lane == size + 1, inner - high, here)
            ).astype(BF)

    return run(
        kernel,
        "resid_back",
        (),
        (cotangent, gains, wo, mixf, back, other, resid, *before),
        (
            ((chunk, model), F32),
            ((chunk, model), BF),
            ((chunk, wide), BF),
            ((8, model), F32),
        ),
        (pltpu.VMEM((chunk, wide), BF),),
    )


def value_terms(xh_ref, rb_ref, e_ref, at, h):
    lanes = slice(h * LANES, (h + 1) * LANES)
    scaled = (xh_ref[:, lanes].astype(F32) * rb_ref[at, lanes]).astype(BF)
    return mm(e_ref[h, at, :], scaled, TN)


def value_first(xh, rb, e, size):
    heads, length, _ = e.shape
    at = slice(0, xh.shape[0])

    def kernel(xh_ref, rb_ref, e_ref, out):
        for h in range(heads):
            out[:, h * size : (h + 1) * size] = value_terms(xh_ref, rb_ref, e_ref, at, h)[:, :size]

    return run(kernel, "value_first", (), (xh, rb, e), (((length, heads * size), F32),))[0]


def value_back(xh, first, rb, e, wv, tokens, size, cut):
    length, model = tokens.shape
    heads = e.shape[0]
    width = heads * size
    krows = model // UNITS
    last = slice(length - xh.shape[0], length)

    def kernel(xh_ref, first_ref, rb_ref, e_ref, wv_ref, tok_ref, gv_ref, part_one, part_two, ga_ref, acc):
        acc[...] = jnp.zeros_like(acc)
        for h in range(heads):
            cols = slice(h * size, (h + 1) * size)
            term = value_terms(xh_ref, rb_ref, e_ref, last, h)[:, :size]
            gv_ref[:, cols] = (first_ref[:, cols] + term).astype(BF)

        for at, part_ref in ((slice(0, cut), part_one), (slice(cut, length), part_two)):
            part = mm(gv_ref[at, :], wv_ref[...], NT)
            part_ref[...] = part.astype(BF)
            x = tok_ref[at, :].astype(F32)
            inv = lax.rsqrt(jnp.mean(x * x, axis=-1, keepdims=True) + EPSILON)
            acc[...] += jnp.sum((part * (x * inv)).reshape((at.stop - at.start) // 8, 8, model), axis=0)

        ga_ref[...] = jnp.zeros_like(ga_ref)
        ga_ref[:UNITS, :] = cut_gain(jnp.sum(acc[...], axis=0, keepdims=True), krows)

    return run(
        kernel,
        "value_back",
        (),
        (xh, first, rb, e, wv, tokens),
        (
            ((length, width), BF),
            ((cut, model), BF),
            ((length - cut, model), BF),
            ((4 * UNITS, LANES), F32),
        ),
        (pltpu.VMEM((8, model), F32),),
    )


def token_grads(mine, other, gres, tokens, gains, part, before):
    chunk, model = mine.shape
    length = tokens.shape[0]
    at = slice(part * chunk, (part + 1) * chunk)

    def kernel(mine_ref, other_ref, gres_ref, tok_ref, gains_ref, *rest):
        out, held, sem = rest[len(before) :]
        x = tok_ref[at, :].astype(F32)
        inv = lax.rsqrt(jnp.mean(x * x, axis=-1, keepdims=True) + EPSILON)
        hat = x * inv
        z = gains_ref[0:1, :] * (mine_ref[...].astype(F32) + other_ref[...].astype(F32))
        held[...] = (gres_ref[...] + inv * (z - hat * jnp.mean(z * hat, axis=-1, keepdims=True))).astype(BF)
        copy = pltpu.make_async_copy(held, out.at[at, :], sem)
        copy.start()
        copy.wait()

    return run(
        kernel,
        "token_grads",
        (),
        (mine, other, gres, tokens, gains),
        (),
        (pltpu.VMEM((chunk, model), BF), pltpu.SemaphoreType.DMA),
        loose=before,
        loose_outs=(((length, model), BF),),
        aliases={5: 0} if before else None,
    )[0]


def low_rows(krows):
    return krows + 2 * (krows // 3)


def mixer_grads(where, xh, va, e, rb, krows, part, before):
    heads, length, _ = e.shape
    rows = length // UNITS
    chunk = xh.shape[0]
    owners = chunk // rows
    at = slice(part * chunk, (part + 1) * chunk)
    deep = heads * rows + low_rows(krows)

    def kernel(where_ref, xh_ref, va_ref, e_ref, rb_ref, *rest):
        outs, ds = rest[len(before) : -1], rest[-1]
        slot = slots(outs, MIXER_FIRST, 1)

        for h in range(heads):
            lanes = slice(h * LANES, (h + 1) * LANES)
            d = mm(xh_ref[:, lanes], va_ref[:, lanes], NT)
            inverse = rb_ref[at, lanes]
            for q in range(length // LANES):
                cols = slice(q * LANES, (q + 1) * LANES)
                ds[h, :, cols] = (e_ref[h, at, cols].astype(F32) * inverse * d[:, cols]).astype(BF)
        for u in range(UNITS):
            owner = where_ref[u] - part * owners

            @pl.when((owner >= 0) & (owner < owners))
            def _(u=u, owner=owner):
                some = pl.ds(multiple(owner * rows, rows), rows)
                for h in range(heads):
                    slot(u)[0][h * rows : (h + 1) * rows, :] = ds[h, some, :]

    return run(
        kernel,
        "mixer_grads",
        (where,),
        (xh, va, e, rb, *before),
        slot_shapes(deep, length, MIXER_FIRST, 1, False),
        (pltpu.VMEM((heads, chunk, length), BF),),
        aliases={5 + n: n for n in range(len(before))},
    )


def weight_grads(where, parts, n1, gv, gats, mixed, ga, ga_other, gain):
    length = n1.shape[0]
    model = n1.shape[1]
    width = gv.shape[1]
    krows = model // UNITS
    deep, length = parts[0].shape[1:]
    top = deep - low_rows(krows)
    lead, half, fold = length - width, length // 2, krows // 3
    assert width - lead == half

    def kernel(where_ref, n1_ref, gv_ref, ga_ref, gb_ref, gain_ref, *rest):
        gat_refs, mixed_refs, rest = rest[: len(mixed)], rest[len(mixed) : 2 * len(mixed)], rest[2 * len(mixed) :]
        slot = slots(rest[len(parts) : 2 * len(parts)], MIXER_FIRST, 1)
        wide, other, folded, pieces = rest[2 * len(parts) :]
        wide[:, :width] = mm(n1_ref[...], gv_ref[...], TN).astype(BF)
        some = [mm(gat_ref[...], one[...], TN) for gat_ref, one in zip(gat_refs, mixed_refs)]
        other[...] = sum(some).astype(BF)
        wide[:, width:] = other[:, :lead]
        pieces[0] = ga_ref[:UNITS, :] + gb_ref[:UNITS, :]
        pieces[1] = cut_gain(jnp.sum(gain_ref[...], axis=0, keepdims=True), krows)
        sub = lax.broadcasted_iota(jnp.int32, (fold, LANES), 0)
        for d in range(UNITS):
            for n in range(3):
                at = slice(d * krows + n * fold, d * krows + (n + 1) * fold)
                to = slice((2 * d + n // 2) * fold, (2 * d + n // 2 + 1) * fold)
                folded[to, (n % 2) * half : (n % 2 + 1) * half] = other[at, lead:]
            both = jnp.where(
                sub == 0, pieces[0, d : d + 1, :], jnp.where(sub == 1, pieces[1, d : d + 1, :], 0.0)
            )
            at = slice((2 * d + 1) * fold, (2 * d + 2) * fold)
            folded[at, half : half + LANES] = both.astype(BF)
            folded[at, half + LANES :] = jnp.zeros((fold, half - LANES), BF)
        for u in range(UNITS):
            (to,) = slot(u)
            to[top : top + krows, :] = wide[pl.ds(multiple(where_ref[u] * krows, 16), krows), :]
            to[top + krows :, :] = folded[pl.ds(multiple(where_ref[u] * 2 * fold, 16), 2 * fold), :]

    return run(
        kernel,
        "weight_grads",
        (where,),
        (n1, gv, ga, ga_other, gain, *gats, *mixed, *parts),
        slot_shapes(deep, length, MIXER_FIRST, 1, False),
        (
            pltpu.VMEM((model, length), BF),
            pltpu.VMEM((model, width), BF),
            pltpu.VMEM((UNITS * 2 * fold, length), BF),
            pltpu.VMEM((2, UNITS, LANES), F32),
        ),
        aliases={6 + 2 * len(mixed) + n: n for n in range(len(parts))},
    )


class Ring:
    def __init__(self, size):
        self.size = size
        self.chips = size // 2
        n = self.chips
        self.order = list(range(0, n, 2)) + list(range(n - 1, 0, -2))
        me = lax.axis_index("dp")
        self.core = me % 2
        chip = me // 2
        self.at = jnp.where(chip % 2 == 0, chip // 2, n - 1 - chip // 2)
        self.up = self.pairs(1)
        self.down = self.pairs(-1)
        self.swap = [(d, d ^ 1) for d in range(size)]

    def pairs(self, step):
        n = self.chips
        return [
            (self.order[p] * 2 + c, self.order[(p + step) % n] * 2 + c) for p in range(n) for c in range(2)
        ]

    def device(self, offset, core):
        n = self.chips
        p = (self.at + jnp.asarray(offset, jnp.int32) + n) % n
        chip = jnp.where(p < (n + 1) // 2, 2 * p, 2 * (n - 1 - p) + 1)
        return chip * 2 + core

    def gathered(self):
        n = self.chips
        offsets = [0]
        for s in range(1, n // 2):
            offsets += [-s, s]
        offsets.append(n // 2)
        return jnp.concatenate([self.device(offsets, self.core), self.device(offsets, 1 - self.core)])

    def scattered(self):
        offsets = list(range(self.chips))
        return jnp.concatenate([self.device(offsets, self.core), self.device(offsets, 1 - self.core)])


class Gather:
    def __init__(self, ring, unit, cut):
        self.ring = ring
        self.rows = unit.shape[0]
        self.cut = cut
        self.last = [unit, unit]
        self.hops = 0
        self.mine = []
        self.theirs = []
        self.here = [unit]

    def values(self):
        return self.last

    def take(self, values):
        self.last = list(values)

    def arrived(self, units):
        self.hops = 1
        self.last = self.here = list(units)

    def hop(self):
        ring = self.ring
        self.hops += 1
        up, down = self.last
        if self.hops == ring.chips // 2:
            up, down = up[: self.cut], down[self.cut :]
        self.last = [lax.ppermute(up, "dp", ring.up), lax.ppermute(down, "dp", ring.down)]
        self.swap()
        self.here = self.last

    def swap(self):
        self.theirs += [lax.ppermute(one, "dp", self.ring.swap) for one in self.here]
        self.mine += self.here
        self.here = []

    def finish(self):
        self.swap()
        return self.mine + self.theirs

    def shares(self):
        n = self.ring.chips
        own = [(u, 0, self.rows) for u in range(n - 1)]
        own += [(n - 1, 0, self.cut), (n - 1, self.cut, self.rows - self.cut)]
        return own + [(u + n, first, rows) for u, first, rows in own]


class Scatter:
    def __init__(self, ring, first, pieces, keep, *give):
        self.ring = ring
        self.keep = keep
        count = len(first) * pieces
        swapped = [lax.ppermute(one, "dp", ring.swap) for one in give[:count]]
        self.early = {k: swapped[n * pieces : (n + 1) * pieces] for n, k in enumerate(first)}
        self.first = first
        self.late = late_units(first)
        self.later = give[count:]
        self.got = {}
        self.last = {}

    def values(self):
        return list(self.last.values()) if self.last else [one for k in self.first for one in self.early[k]]

    def take(self, values):
        if self.last:
            self.last = dict(zip(self.last, values))
        else:
            pieces = len(values) // len(self.first)
            self.early = {k: values[n * pieces : (n + 1) * pieces] for n, k in enumerate(self.first)}

    def swap_all(self, *after):
        stack = lax.ppermute(tie(self.later[0], *after), "dp", self.ring.swap)
        self.got = {k: stack[n] for n, k in enumerate(self.late)}

    def hop(self, way, k):
        got = self.early[k][0] if k in self.early else self.got[k]
        value = self.keep[k].astype(F32) + got.astype(F32)
        if way in self.last:
            value = value + self.last[way].astype(F32)
        value = value.astype(BF)
        self.last[way] = lax.ppermute(value, "dp", self.ring.up if way == "up" else self.ring.down)
        return value

    def result(self):
        return self.keep, self.got[0], self.last["up"], self.last["down"]


def together(chains, *more):
    values = [one for chain in chains for one in chain.values()]
    tied = lax.optimization_barrier(tuple(values) + more)
    at = 0
    for chain in chains:
        count = len(chain.values())
        chain.take(tied[at : at + count])
        at += count
    return tied[at:]


def tie(value, *after):
    return lax.optimization_barrier((value,) + after)[0] if after else value


def shards(
    tokens,
    segment_ids,
    gain_attn,
    gain_ffn,
    random_scores,
    w_value,
    w_output,
    w_up,
    w_down,
    cotangent,
):
    devices = lax.axis_size("dp")
    second = lax.axis_index("mp")
    length = segment_ids.shape[1]
    heads = random_scores.shape[0]
    model = tokens.shape[1]
    width = w_value.shape[1]
    size = width // heads
    rows = length // UNITS
    krows = model // UNITS
    ring = devices == UNITS and devices // 2 <= RING_CHIPS
    flip = [(0, 1), (1, 0)]
    second_at = jnp.reshape(second, (1,)).astype(jnp.int32)
    plan = Unit(heads, rows, krows, length, model, width, w_up.shape[1])

    if ring:
        net = Ring(devices)
        far = net.chips // 2
        where_in = net.gathered().astype(jnp.int32)
        where_out = net.scattered().astype(jnp.int32)
        upper, lower, wo_own = pack_unit(
            plan, second_at, random_scores, w_value, gain_attn, gain_ffn, w_up, w_down.T, w_output.T
        )
        ways = (net.up, net.down)
        uppers = [lax.ppermute(upper, "dp", way) for way in ways]
        wo_other = lax.ppermute(tie(wo_own, where_in, where_out), "mp", flip)
        lower = fill_low(plan, second_at, lower, wo_other)
        lowers = [lax.ppermute(lower, "dp", way) for way in ways]
        (unit,) = join_units(plan, [upper], [lower])
        one = Gather(net, unit, plan.cut)
        one.swap()
        uppers[0], uppers[1], *lowers = lax.optimization_barrier((*uppers, *lowers))
        one.arrived(join_units(plan, uppers, lowers))
        for step in range(1, far - 1):
            one.hop()
            together([one])
            one.here = one.last
        there = one.mine + one.theirs
        shares = one.shares()
        half = len(shares) // 2
        early = [n for n in range(len(one.mine))] + [half + n for n in range(len(one.theirs))]
        one.hop()
        begun = mixer_first(plan, where_in, tokens, segment_ids, there, [shares[n] for n in early], heads)
        begun = together([one], *begun)
        one.here = one.last
        units = one.finish()
        late = [n for n in range(len(shares)) if n not in early]
        near = late
        order = [n for n in range(len(shares)) if n not in near] + near
        units, shares = [units[n] for n in order], [shares[n] for n in order]
        late = [n for n, old in enumerate(order) if old in late]
    else:
        where_in = jnp.arange(UNITS, dtype=jnp.int32)
        where_out = where_in

        def gather(one, axis=0):
            return lax.all_gather(one.astype(BF), "dp", axis=axis, tiled=True)

        wo_own = w_output.T.astype(BF)
        wo_other = lax.ppermute(wo_own, "mp", flip)
        halves = [jnp.where(second == n, wo_own, wo_other) for n in range(2)]
        scores = gather(random_scores, 1).reshape(heads, UNITS, rows, length).transpose(1, 0, 2, 3)
        wide = [gather(one) for one in (w_value, *halves)]
        wide = jnp.concatenate(wide, axis=1).reshape(UNITS, krows, plan.wide)
        ffn = jnp.concatenate([gather(w_up), gather(w_down.T)], axis=1).reshape(UNITS, krows, -1)
        stack = [scores.reshape(UNITS, heads * rows, length)]
        for kind, column in plan.blocks:
            stack.append((ffn if kind == "ffn" else wide)[:, :, column : column + length])
        gains = jnp.stack([gather(gain_attn), gather(gain_ffn)]).reshape(2, UNITS, krows).transpose(1, 0, 2)
        gains = jnp.pad(gains, ((0, 0), (0, plan.fold - 2), (0, length - plan.gain_lane - krows)))
        tail = wide[:, :, plan.wide - plan.tail :].reshape(UNITS, 3, plan.fold, plan.tail)
        stack.append(jnp.concatenate([tail[:, 0], tail[:, 1], tail[:, 2], gains], axis=2))
        whole = jnp.concatenate(stack, axis=1)
        units = [whole[u] for u in range(UNITS)]
        shares = [(u, 0, plan.deep) for u in range(UNITS)]
        early, late, near = list(range(UNITS // 2)), list(range(UNITS // 2, UNITS)), []
        begun = mixer_first(plan, where_in, tokens, segment_ids, units[: UNITS // 2], shares[: UNITS // 2], heads)

    own = [n for n in late if shares[n][0] < UNITS // 2 or shares[n][2] == plan.deep] if ring else late[:1]
    late = [n for n in late if n not in own]
    begun = mixer_next(plan, where_in, begun, [units[n] for n in own], [shares[n] for n in own])
    e, wv, _, va, sums, n1, gains, *mixed = mixer_forward(
        plan, where_in, begun, [units[n] for n in late], [shares[n] for n in late], heads, width
    )
    mixed_other = [lax.ppermute(one, "mp", flip) for one in mixed]
    w, wo_whole, gact, mixf, rb, wo = second_weights(plan, where_in, second_at, cotangent, sums, units, shares, len(near), size)
    backs, others, resids, kept = [], [], [], []
    for part in range(PARTS):
        back, resid, *kept = ffn_main(
            second_at, tokens, mixed[part], mixed_other[part], gact, gains, w, wo_whole, part, PARTS, kept
        )
        backs.append(back)
        others.append(lax.ppermute(tie(back, *others[-1:]), "mp", flip))
        resids.append(resid)
    n2, act, gpre = kept
    parts_two = ffn_grads(where_out, n2, gpre, act, cotangent)
    early = resid_back(backs[0], others[0], resids[0], cotangent, gains, wo, mixf, 0, heads, size, [])
    ffn_one, ffn_two = ffn_out(tie(act, *early), w, 3 * length // 8)
    first_values = value_first(early[2], rb, e, size)
    parts_one = mixer_grads(where_out, early[2], va, e, rb, krows, 0, [])
    if ring:
        ffn_sum = Scatter(net, FFN_FIRST, 1, *parts_two)
        ffn_sum.swap_all(others[0], *ffn_sum.values())
        for step in range(2):
            ffn_sum.hop("down", far + step)
            ffn_sum.hop("up", far - 1 - step)
            if step == 0:
                ffn_one, ffn_two, first_values, *more = together(
                    [ffn_sum], ffn_one, ffn_two, first_values, *early, *parts_one
                )
                early, parts_one = more[: len(early)], more[len(early) :]
    cot_late = tie(cotangent, first_values, *parts_one)
    final = resid_back(backs[1], others[1], resids[1], cot_late, gains, wo, mixf, 1, heads, size, early[3:])
    gres, gats = (early[0], final[0]), (early[1], final[1])
    xh = final[2]
    gv, part_one, part_two, ga = value_back(xh, first_values, rb, e, wv, tokens, size, length // 2)
    ga_other = lax.ppermute(ga, "mp", flip)
    one_other = lax.ppermute(tie(ffn_one, ga), "mp", flip)
    if ring:
        together([ffn_sum])
        for step in range(2, far - 1):
            ffn_sum.hop("down", far + step)
            ffn_sum.hop("up", far - 1 - step)
    parts_one = mixer_grads(where_out, xh, va, e, rb, krows, 1, parts_one)
    parts_one = weight_grads(where_out, parts_one, n1, gv, gats, mixed, ga, ga_other, final[3])

    top = heads * rows
    if ring:
        score_sum = Scatter(net, MIXER_FIRST, 1, *parts_one)
        one_other, ffn_two = together([ffn_sum, score_sum], one_other, ffn_two)
        value = score_sum.hop("up", far)
        ffn_sum.hop("down", 2 * far - 1)
        score_sum.swap_all(value)
        two_other = lax.ppermute(ffn_two, "mp", flip)
        part_one, part_two = together([score_sum], part_one, part_two)
        for step in range(1, far):
            score_sum.hop("up", far - step)
            score_sum.hop("down", far + step)
            if step == 1:
                part_other = [lax.ppermute(part_one, "mp", flip)]
                two_other, part_two = together([ffn_sum, score_sum], two_other, part_two)
            elif step < far - 1:
                part_other.append(lax.ppermute(part_two, "mp", flip))
                (part_other[0],) = together([score_sum], part_other[0])
        out_up, out_down = ffn_result(*ffn_sum.result())
        out_scores, out_value, out_output, *out_gains = mixer_result(*score_sum.result(), heads, krows, width)
        out_down, out_output = out_down.T, out_output.T
        out_gain_one, out_gain_two = [one.reshape(krows) for one in out_gains]
    else:
        two_other = lax.ppermute(ffn_two, "mp", flip)
        part_other = [lax.ppermute(one, "mp", flip) for one in (part_one, part_two)]

        def scatter(one, axis=0):
            return lax.psum_scatter(one, "dp", scatter_dimension=axis, tiled=True)

        def whole(first, pieces, keep, *give):
            late = late_units(first)
            early, later = give[: len(first) * pieces], give[len(first) * pieces :]
            given = []
            for k in range(UNITS // 2):
                if k in first:
                    at = first.index(k) * pieces
                    given.append(jnp.concatenate(early[at : at + pieces]))
                else:
                    given.append(later[0][late.index(k)] if len(later) == 1 else later[late.index(k)])
            return jnp.concatenate([keep, jnp.stack(given)]).astype(F32)

        two = whole(FFN_FIRST, 1, *parts_two).reshape(model, -1)
        one = whole(MIXER_FIRST, 1, *parts_one)
        out_up = scatter(two[:, : two.shape[1] // 2])
        out_down = scatter(two[:, two.shape[1] // 2 :]).T
        scores = one[:, :top].reshape(UNITS, heads, rows, length).transpose(1, 0, 2, 3)
        out_scores = scatter(scores.reshape(heads, length, length), 1)
        out_value = scatter(one[:, top : top + krows, :width].reshape(model, width))
        low, fold, half = top + krows, krows // 3, length // 2
        folded = [one[:, low + n // 2 * fold : low + (n // 2 + 1) * fold, n % 2 * half :][:, :, :half] for n in range(3)]
        other = jnp.concatenate([one[:, top:low, width:], jnp.concatenate(folded, axis=1)], axis=2)
        out_output = scatter(other.reshape(model, width)).T
        out_gain_one = scatter(one[:, low + fold, half : half + krows].reshape(model))
        out_gain_two = scatter(one[:, low + fold + 1, half : half + krows].reshape(model))
    ffn = jnp.concatenate([ffn_one, ffn_two])
    ffn_other = jnp.concatenate([one_other, two_other])
    output = (jnp.concatenate(resids) + (ffn.astype(F32) + ffn_other.astype(F32))).astype(BF)
    written = []
    for part, (mine, other) in enumerate(zip((part_one, part_two), part_other)):
        written = [token_grads(mine, other, gres[part], tokens, gains, part, written)]
    (grad_tokens,) = written
    return (
        output,
        grad_tokens,
        out_gain_one,
        out_gain_two,
        out_scores,
        out_value,
        out_output,
        out_up,
        out_down,
    )


def solution(mesh):
    in_specs = (
        P("dp", None),
        P("dp", None),
        P("dp"),
        P("dp"),
        P("mp", "dp", None),
        P("dp", "mp"),
        P("mp", "dp"),
        P("dp", "mp"),
        P("mp", "dp"),
        P("dp", None),
    )
    out_specs = (
        P("dp", None),
        P("dp", None),
        P("dp"),
        P("dp"),
        P("mp", "dp", None),
        P("dp", "mp"),
        P("mp", "dp"),
        P("dp", "mp"),
        P("mp", "dp"),
    )
    return jax.shard_map(shards, mesh=mesh, in_specs=in_specs, out_specs=out_specs, check_vma=False)
```

```python
import jax
import jax.numpy as jnp
from jax import lax
from jax.experimental import pallas as pl
from jax.experimental.pallas import tpu as pltpu
from jax.sharding import PartitionSpec as P

EPSILON = 1e-06
NEGATIVE = -1e30
BF = jnp.bfloat16
F32 = jnp.float32
UNITS = 16
LANES = 128
PARTS = 2
RING_CHIPS = 8
VMEM_BYTES = 20 * 1024 * 1024
NT = (((1,), (1,)), ((), ()))
TN = (((0,), (0,)), ((), ()))
NN = (((1,), (0,)), ((), ()))


def mm(a, b, dims=NN):
    return lax.dot_general(a, b, dims, preferred_element_type=F32)


def run(kernel, name, scalars, arrays, outs, scratch=(), loose=(), loose_outs=(), aliases=None, near=0):
    held = [pltpu.with_memory_space_constraint(one, pltpu.VMEM) for one in arrays]
    results = [pltpu.VMEM(*one) for one in outs] + [jax.ShapeDtypeStruct(*one) for one in loose_outs]
    specs = [pl.BlockSpec(memory_space=pltpu.SMEM)] * len(scalars)
    specs += [pl.BlockSpec(memory_space=pltpu.VMEM)] * len(arrays)
    far = len(loose) - near
    specs += [pl.BlockSpec(memory_space=pltpu.HBM)] * far + [pl.BlockSpec(memory_space=pl.ANY)] * near
    loose = [pltpu.with_memory_space_constraint(one, pltpu.HBM) for one in loose[:far]] + list(loose[far:])
    out_specs = [pl.BlockSpec(memory_space=pltpu.VMEM)] * len(outs)
    out_specs += [pl.BlockSpec(memory_space=pl.ANY)] * len(loose_outs)
    return pl.pallas_call(
        kernel,
        out_shape=tuple(results),
        in_specs=specs,
        out_specs=tuple(out_specs),
        scratch_shapes=list(scratch),
        compiler_params=pltpu.CompilerParams(vmem_limit_bytes=VMEM_BYTES),
        cost_estimate=pl.CostEstimate(flops=1, bytes_accessed=1, transcendentals=0),
        input_output_aliases=aliases or {},
        name=name,
    )(*scalars, *held, *loose)


def gelu_pair(x):
    c = 0.7978845608028654
    a = 0.044715
    square = x * x
    t = jnp.tanh(c * x * (1.0 + a * square))
    half = 0.5 * (1.0 + t)
    return x * half, half + 0.5 * x * (1.0 - t * t) * (c * (1.0 + 3.0 * a * square))


def multiple(value, of):
    return pl.multiple_of(value, of)


class Unit:
    def __init__(self, heads, rows, krows, length, model, width, hidden):
        self.scores = heads * rows
        self.krows = krows
        self.length = length
        self.width = width
        self.hidden = hidden
        self.wide = width + model
        self.blocks = [("ffn", n * length) for n in range(2 * hidden // length)]
        self.blocks += [("proj", n * length) for n in range(self.wide // length)]
        self.tail = self.wide % length
        self.last = self.scores + krows * len(self.blocks)
        self.fold = krows // 3
        self.deep = self.last + self.fold
        self.cut = self.scores + krows * (2 * hidden // length // 3)
        self.gain_lane = 3 * self.tail
        self.head = self.value_row()

    def projection_parts(self):
        parts = []
        for n, (kind, first) in enumerate(self.blocks):
            at = self.scores + n * self.krows
            if kind == "proj":
                skip = max(self.width - first, 0)
                parts.append((at, skip, 0, first + skip - self.width, self.krows, self.length - skip))
        for n in range(3):
            column = self.wide - self.tail - self.width
            parts.append((self.last, n * self.tail, n * self.fold, column, self.fold, self.tail))
        return parts

    def ffn_blocks(self, first, rows):
        inside = [
            n
            for n, (kind, _) in enumerate(self.blocks)
            if kind == "ffn" and first <= self.scores + n * self.krows < first + rows
        ]
        return (inside[0], len(inside)) if inside else (0, 0)

    def value_row(self):
        return self.scores + [kind for kind, _ in self.blocks].index("proj") * self.krows


def other_parts(plan, first):
    begin = plan.width + first * plan.width
    parts = []
    for n, (kind, column) in enumerate(plan.blocks):
        low, high = max(begin, column), min(begin + plan.width, column + plan.length)
        if kind == "proj" and low < high:
            parts.append((plan.scores + n * plan.krows, low - column, 0, low - begin, plan.krows, high - low))
    low = max(begin, plan.wide - plan.tail)
    if low < begin + plan.width:
        for n in range(3):
            lanes = n * plan.tail + low - (plan.wide - plan.tail)
            parts.append((plan.last, lanes, n * plan.fold, low - begin, plan.fold, begin + plan.width - low))
    return parts


def put_half(plan, low, half_ref, first):
    for row, lane, at, column, rows, lanes in other_parts(plan, first):
        row = row - plan.head
        low[row : row + rows, lane : lane + lanes] = half_ref[at : at + rows, column : column + lanes]


def pack_unit(plan, second, scores, wv, gain_one, gain_two, w_up, w_down, wo):
    inputs = (scores, wv, gain_one.reshape(1, -1), gain_two.reshape(1, -1), w_up, w_down, wo)
    count = len(inputs)
    krows, length, width = plan.krows, plan.length, plan.width
    per = plan.hidden // length
    assert plan.tail <= width

    def kernel(second_ref, *rest):
        out, low, wo_out, gains = rest[count : count + 4]
        held, sem = rest[count + 4 : -1], rest[-1]
        copies = [pltpu.make_async_copy(rest[n], held[n], sem.at[n]) for n in range(count)]
        for copy in copies:
            copy.start()
        s_ref, wv_ref, ga_ref, gf_ref, up_ref, down_ref, own_ref = held
        copies[0].wait()
        out[: plan.scores, :] = s_ref[...].reshape(plan.scores, length).astype(BF)
        for copy in copies[1:]:
            copy.wait()
        for n, (kind, column) in enumerate(plan.blocks):
            at = slice(plan.scores + n * krows, plan.scores + (n + 1) * krows)
            if kind == "ffn":
                ref, first = (up_ref, column) if n < per else (down_ref, column - plan.hidden)
                out[at, :] = ref[:, first : first + length].astype(BF)
        low[...] = jnp.zeros_like(low)
        low[:krows, :width] = wv_ref[...].astype(BF)
        wo_out[...] = own_ref[...].astype(BF)
        for place in range(2):

            @pl.when(second_ref[0] == place)
            def _():
                put_half(plan, low, wo_out, place)

        gains[...] = jnp.zeros_like(gains)
        gains[0:1, :krows] = ga_ref[...]
        gains[1:2, :krows] = gf_ref[...]
        low[plan.last - plan.head :, plan.gain_lane :] = gains[...].astype(BF)

    return run(
        kernel,
        "pack_unit",
        (second,),
        (),
        (((plan.head, length), BF), ((plan.deep - plan.head, length), BF), ((krows, width), BF)),
        (
            pltpu.VMEM((plan.fold, length - plan.gain_lane), F32),
            *[pltpu.VMEM(one.shape, one.dtype) for one in inputs],
            pltpu.SemaphoreType.DMA((count,)),
        ),
        loose=inputs,
    )


def fill_low(plan, second, low, other):
    def kernel(second_ref, old, other_ref, out):
        for place in range(2):

            @pl.when(second_ref[0] == 1 - place)
            def _():
                put_half(plan, out, other_ref, place)

    return run(kernel, "fill_low", (second,), (low, other), ((low.shape, BF),), aliases={1: 0})[0]


def join_units(plan, uppers, lowers):
    count = len(uppers)

    def kernel(*refs):
        for n in range(count):
            out = refs[2 * count + n]
            out[: plan.head, :] = refs[n][...]
            out[plan.head :, :] = refs[count + n][...]

    return run(kernel, "join_units", (), (*uppers, *lowers), [((plan.deep, plan.length), BF)] * count)


def pick(units, shares, where_ref, parts, target, sem):
    copies = []
    for n, (u, first, rows) in enumerate(shares):
        owner = where_ref[u]
        for m, part in enumerate(parts):
            row, column, count, columns = part[0], part[1], part[-2], part[-1]
            if first <= row and row + count <= first + rows:
                source = units[n].at[pl.ds(row - first, count), pl.ds(column, columns)]
                copies.append(pltpu.make_async_copy(source, target(m, owner), sem.at[u, m]))
                copies[-1].start()
    return copies


def document_mask(seg_ref, same):
    length = same.shape[0]
    documents = (seg_ref[...] == lax.broadcasted_iota(jnp.int32, (LANES, length), 0)).astype(BF)
    same[...] = mm(documents, documents, TN)


def exponentials(where_ref, shares, sources, e_ref, same):
    heads, length, _ = e_ref.shape
    rows = length // UNITS

    def one_head(h, carry):
        for (u, _, _), (ref, first) in zip(shares, sources):
            at = pl.ds(multiple(where_ref[u] * rows, rows), rows)
            s = ref[pl.ds(multiple(first + h * rows, rows), rows), :].astype(F32)
            e_ref[h, at, :] = (jnp.exp(s) * same[at, :]).astype(BF)
        return carry

    lax.fori_loop(0, heads, one_head, 0)


def low_parts(plan):
    return [
        (plan.value_row(), 0, plan.krows, plan.width),
        (plan.last, plan.gain_lane, plan.fold, LANES),
    ]


def bring_low(plan, units, shares, where_ref, wv_ref, low_ref, sem):
    krows = plan.krows

    def target(m, owner):
        if m == 0:
            return wv_ref.at[pl.ds(multiple(owner * krows, 16), krows), :]
        return low_ref.at[owner]

    return pick(units, shares, where_ref, low_parts(plan), target, sem)


def mixer_first(plan, where, tokens, segments, units, shares, heads):
    length, model = tokens.shape
    rows = length // UNITS

    def kernel(where_ref, tok_ref, seg_ref, *rest):
        e_ref, wv_ref, low_ref, hat_ref, same, unit, sem, more = rest[len(units) :]
        top = heads * rows

        def target(m, owner):
            return unit.at[pl.ds(multiple(owner * top, top), top), :]

        came = pick(rest[: len(units)], shares, where_ref, [(0, 0, top, length)], target, sem)
        copies = bring_low(plan, rest[: len(units)], shares, where_ref, wv_ref, low_ref, more)
        document_mask(seg_ref, same)
        x = tok_ref[...].astype(F32)
        hat_ref[...] = x * lax.rsqrt(jnp.mean(x * x, axis=-1, keepdims=True) + EPSILON)
        for copy in came:
            copy.wait()
        sources = [(unit, where_ref[u] * top) for u, _, _ in shares]
        exponentials(where_ref, shares, sources, e_ref, same)
        for copy in copies:
            copy.wait()

    return run(
        kernel,
        "mixer_first",
        (where,),
        (tokens, segments),
        (
            ((heads, length, length), BF),
            ((model, plan.width), BF),
            ((UNITS, plan.fold, LANES), BF),
            ((length, model), F32),
            ((length, length), F32),
        ),
        (
            pltpu.VMEM((heads * length, length), BF),
            pltpu.SemaphoreType.DMA((UNITS, 1)),
            pltpu.SemaphoreType.DMA((UNITS, 2)),
        ),
        loose=units,
    )


def take_late(plan, where_ref, shares, refs, e_ref, wv_ref, low, same):
    krows = plan.krows
    for (u, first, rows), ref in zip(shares, refs):
        for m, (row, lane, deep, lanes) in enumerate(low_parts(plan)):
            if first <= row < first + rows:
                part = ref[row - first : row - first + deep, lane : lane + lanes]
                if m == 0:
                    wv_ref[pl.ds(multiple(where_ref[u] * krows, 16), krows), :] = part
                else:
                    low[where_ref[u]] = part
    scored = [n for n in range(len(shares)) if shares[n][1] == 0]
    exponentials(where_ref, [shares[n] for n in scored], [(refs[n], 0) for n in scored], e_ref, same)


def mixer_next(plan, where, early, units, shares):
    e, wv, low, hat, same = early
    count = len(units)

    def kernel(where_ref, same_ref, e_old, wv_old, low_old, *rest):
        take_late(plan, where_ref, shares, rest[:count], *rest[count:], same_ref)

    outs = [(one.shape, one.dtype) for one in (e, wv, low)]
    more = run(
        kernel, "mixer_next", (where,), (same, e, wv, low, *units), outs, aliases={2: 0, 3: 1, 4: 2}
    )
    return [*more, hat, same]


def mixer_forward(plan, where, early, units, shares, heads, width):
    length, model = early[3].shape
    size = width // heads
    krows = model // UNITS
    wide = heads * LANES
    count = len(units)

    def kernel(where_ref, e_old, wv_old, low_old, hat_ref, same, *rest):
        e_ref, wv_ref, low, va_ref, sums_ref, n1_ref, gains_ref, *mixed, pieces = rest[count:]
        take_late(plan, where_ref, shares, rest[:count], e_ref, wv_ref, low, same)
        for d in range(UNITS):
            some = low[d].astype(F32)
            pieces[0, d : d + 1, :] = some[0:1, :]
            pieces[1, d : d + 1, :] = some[1:2, :]
        spread = (
            lax.broadcasted_iota(jnp.int32, (LANES, model), 1) % krows
            == lax.broadcasted_iota(jnp.int32, (LANES, model), 0)
        ).astype(BF)
        own = (
            lax.broadcasted_iota(jnp.int32, (UNITS, model), 1) // krows
            == lax.broadcasted_iota(jnp.int32, (UNITS, model), 0)
        )
        gains = []
        for t in range(2):
            full = jnp.where(own, mm(pieces[t].astype(BF), spread), 0.0)
            gains.append(jnp.sum(full, axis=0, keepdims=True))
            gains_ref[t : t + 1, :] = gains[t]
        n1_ref[...] = (hat_ref[...] * gains[0]).astype(BF)
        values = mm(n1_ref[...], wv_ref[...]).astype(BF)
        tail = (lax.broadcasted_iota(jnp.int32, (length, LANES - size), 1) < 2).astype(BF)
        for h in range(heads):
            va_ref[:, h * LANES : h * LANES + size] = values[:, h * size : (h + 1) * size]
            va_ref[:, h * LANES + size : (h + 1) * LANES] = tail

        for h in range(heads):
            lanes = slice(h * LANES, (h + 1) * LANES)
            sums = mm(e_ref[h], va_ref[:, lanes])
            sums_ref[:, lanes] = sums
            values = (sums * (1.0 / sums[:, size : size + 1]))[:, :size].astype(BF)
            for part, mixed_ref in enumerate(mixed):
                some = slice(part * (length // PARTS), (part + 1) * (length // PARTS))
                mixed_ref[:, h * size : (h + 1) * size] = values[some, :]

    return run(
        kernel,
        "mixer_forward",
        (where,),
        (*early, *units),
        (
            ((heads, length, length), BF),
            ((model, width), BF),
            ((UNITS, plan.fold, LANES), BF),
            ((length, wide), BF),
            ((length, wide), F32),
            ((length, model), BF),
            ((2, model), F32),
            *[((length // PARTS, width), BF)] * PARTS,
        ),
        (
            pltpu.VMEM((2, UNITS, LANES), F32),
        ),
        aliases={1: 0, 2: 1, 3: 2},
    )


def second_weights(plan, where, second, cotangent, sums, units, shares, near, size):
    length, model = cotangent.shape
    wide = sums.shape[1]
    hidden, krows, width = plan.hidden, plan.krows, plan.width
    parts = plan.projection_parts()
    blocks = 2 * hidden // length

    def kernel(where_ref, second_ref, cot_ref, sums_ref, *rest):
        out, wo_ref, gact, mixf_ref, rb_ref, own_ref, sem, more = rest[len(units) :]

        def target(m, owner):
            _, _, row, column, rows, columns = parts[m]
            return wo_ref.at[pl.ds(multiple(owner * krows + row, 16), rows), pl.ds(column, columns)]

        copies = []
        for n, (u, first, rows) in enumerate(shares):
            begin, count = plan.ffn_blocks(first, rows)
            if count:
                source = rest[n].at[pl.ds(plan.scores + begin * krows - first, count * krows), :]
                to = out.at[pl.ds(begin, count), pl.ds(multiple(where_ref[u] * krows, 16), krows), :]
                copies.append(pltpu.make_async_copy(source.reshape(count, krows, length), to, more.at[n]))
                copies[-1].start()
        copies += pick(rest[: len(units)], shares, where_ref, parts, target, sem)
        inside = lax.broadcasted_iota(jnp.int32, (length, LANES), 1) < size
        for h in range(wide // LANES):
            lanes = slice(h * LANES, (h + 1) * LANES)
            inverse = jnp.broadcast_to(1.0 / sums_ref[:, h * LANES + size : h * LANES + size + 1], (length, LANES))
            rb_ref[:, lanes] = inverse
            mixf_ref[:, lanes] = jnp.where(inside, sums_ref[:, lanes] * inverse, 0.0)
        for copy in copies:
            copy.wait()
        for j in range(blocks // 2):
            gact[:, j * length : (j + 1) * length] = mm(cot_ref[...], out[blocks // 2 + j])
        own = wo_ref[:, pl.ds(multiple(second_ref[0] * width, LANES), width)]
        own_ref[...] = jnp.zeros_like(own_ref)
        for h in range(width // size):
            own_ref[:, h * LANES : h * LANES + size] = own[:, h * size : (h + 1) * size]

    return run(
        kernel,
        "second_weights",
        (where, second),
        (cotangent, sums),
        (
            ((blocks, model, length), BF),
            ((model, model), BF),
            ((length, hidden), F32),
            (sums.shape, F32),
            (sums.shape, F32),
            ((model, wide), BF),
        ),
        (pltpu.SemaphoreType.DMA((UNITS, len(parts))), pltpu.SemaphoreType.DMA((len(units),))),
        loose=units,
        near=near,
    )


def ffn_main(second, tokens, mixed_own, mixed_other, gact, gains, w, wo, part, parts, before):
    length, model = tokens.shape
    width = mixed_own.shape[1]
    hidden = gact.shape[1]
    chunk = length // parts
    piece = w.shape[2]
    at = slice(part * chunk, (part + 1) * chunk)

    def kernel(second_ref, tok_ref, own_ref, other_ref, gact_ref, gains_ref, w_ref, wo_ref, *rest):
        back_ref, resid_ref, n2_ref, act_ref, gpre_ref, mixed = rest[len(before) :]
        first = second_ref[0]
        mixed[:, pl.ds(multiple(first * width, LANES), width)] = own_ref[...]
        mixed[:, pl.ds(multiple((1 - first) * width, LANES), width)] = other_ref[...]
        attn = mm(mixed[...], wo_ref[...], NT)
        resid = tok_ref[at, :].astype(F32) + attn
        resid_ref[...] = resid
        inv = lax.rsqrt(jnp.mean(resid * resid, axis=-1, keepdims=True) + EPSILON)
        n2 = (resid * inv * gains_ref[1:2, :]).astype(BF)
        n2_ref[at, :] = n2
        terms = []
        pres = [mm(n2, w_ref[j]) for j in range(hidden // piece)]
        for j in range(hidden // piece):
            cols = slice(j * piece, (j + 1) * piece)
            act, slope = gelu_pair(pres[j])
            act_ref[at, cols] = act.astype(BF)
            gpre = (gact_ref[at, cols] * slope).astype(BF)
            gpre_ref[at, cols] = gpre
            terms.append(mm(gpre, w_ref[j], NT))
        back_ref[...] = sum(terms).astype(BF)

    return run(
        kernel,
        "ffn_main",
        (second,),
        (tokens, mixed_own, mixed_other, gact, gains, w, wo, *before),
        (
            ((chunk, model), BF),
            ((chunk, model), F32),
            ((length, model), BF),
            ((length, hidden), BF),
            ((length, hidden), BF),
        ),
        (
            pltpu.VMEM((chunk, 2 * width), BF),
        ),
        aliases={8 + n: 2 + n for n in range(len(before))},
    )


def late_units(first):
    return [k for k in range(UNITS // 2) if k not in first]


def slots(refs, first, pieces):
    half = UNITS // 2
    count = len(first) * pieces
    keep, early, later = refs[0], refs[1 : 1 + count], refs[1 + count :]
    late = late_units(first)

    def slot(u):
        if u < half:
            return [keep.at[u]]
        k = u - half
        if k in first:
            at = first.index(k) * pieces
            return early[at : at + pieces]
        n = late.index(k)
        return [later[0].at[n] if len(later) == 1 else later[n]]

    return slot


def slot_shapes(rows, columns, first, pieces, apart):
    half = UNITS // 2
    early = [((rows, columns), BF)] * (len(first) * pieces)
    count = half - len(first)
    later = [((rows, columns), BF)] * count if apart else [((count, rows, columns), BF)]
    return [((half, rows, columns), BF), *early, *later]


FFN_FIRST = [UNITS // 4, UNITS // 4 - 1]
MIXER_FIRST = [UNITS // 4]


def result_kernel(name, keep, own, up, down, shapes, cut):
    def kernel(keep_ref, own_ref, up_ref, down_ref, *rest):
        outs, held, sem = rest[: len(shapes)], rest[len(shapes) : -1], rest[-1]

        def total(rows, columns):
            value = keep_ref[0, rows, columns].astype(F32) + own_ref[rows, columns].astype(F32)
            return value + up_ref[rows, columns].astype(F32) + down_ref[rows, columns].astype(F32)

        copies = []

        def send(source, to, n, m):
            copies.append(pltpu.make_async_copy(source, to, sem.at[n, m]))
            copies[-1].start()

        for n, (out, to) in reversed(list(enumerate(zip(outs, held)))):
            if len(shapes[n]) < 3:
                cut(n, to, total)
                send(to, out, n, 0)
            else:
                half = shapes[n][0] // 2
                for m, some in enumerate((range(half), range(half, shapes[n][0]))):
                    cut(n, to, total, some)
                    at = pl.ds(some.start, len(some))
                    send(to.at[at], out.at[at], n, m)
        for copy in copies:
            copy.wait()

    return run(
        kernel,
        name,
        (),
        (keep, own, up, down),
        (),
        (*[pltpu.VMEM(shape, F32) for shape in shapes], pltpu.SemaphoreType.DMA((len(shapes), 2))),
        loose_outs=[(shape, F32) for shape in shapes],
    )


def ffn_result(keep, own, up, down):
    _, rows, columns = keep.shape
    half = columns // 2

    def cut(n, to, total):
        to[...] = total(slice(None), slice(n * half, (n + 1) * half))

    return result_kernel("ffn_result", keep, own, up, down, [(rows, half)] * 2, cut)


def mixer_result(keep, own, up, down, heads, krows, width):
    _, deep, length = keep.shape
    top = deep - low_rows(krows)
    rows = top // heads
    lead, half, fold = length - width, length // 2, krows // 3
    shapes = [(heads, rows, length), (krows, width), (krows, width), (1, krows), (1, krows)]

    def cut(n, to, total, some=()):
        low = top + krows
        if n == 0:
            for h in some:
                to[h] = total(slice(h * rows, (h + 1) * rows), slice(None))
        elif n == 1:
            to[...] = total(slice(top, low), slice(0, width))
        elif n == 2:
            to[:, :lead] = total(slice(top, low), slice(width, length))
            for m in range(3):
                some = slice(low + m // 2 * fold, low + (m // 2 + 1) * fold)
                to[m * fold : (m + 1) * fold, lead:] = total(some, slice(m % 2 * half, (m % 2 + 1) * half))
        else:
            to[...] = total(slice(low + fold, low + 2 * fold), slice(half, half + LANES))[n - 3 : n - 2, :krows]

    return result_kernel("mixer_result", keep, own, up, down, shapes, cut)


def ffn_out(act, w, cut):
    length, hidden = act.shape
    blocks, model, piece = w.shape

    def kernel(act_ref, w_ref, one, two):
        for out, at in ((one, slice(0, cut)), (two, slice(cut, length))):
            terms = [
                mm(act_ref[at, j * piece : (j + 1) * piece], w_ref[blocks // 2 + j], NT) for j in range(blocks // 2)
            ]
            out[...] = sum(terms).astype(BF)

    return run(kernel, "ffn_out", (), (act, w), (((cut, model), BF), ((length - cut, model), BF)))


def ffn_grads(where, n2, gpre, act, cotangent):
    model, hidden = n2.shape[1], act.shape[1]
    krows = model // UNITS

    def kernel(where_ref, cot_ref, n2_ref, gpre_ref, act_ref, *rest):
        slot = slots(rest[:-2], FFN_FIRST, 1)
        scr, sem = rest[-2:]
        piece = hidden // 3
        for j in range(3):
            cols = slice(j * piece, (j + 1) * piece)
            down = slice(hidden + j * piece, hidden + (j + 1) * piece)
            scr[:, cols] = mm(n2_ref[...], gpre_ref[:, cols], TN).astype(BF)
            scr[:, down] = mm(cot_ref[...], act_ref[:, cols], TN).astype(BF)
        for u in range(UNITS):
            at = pl.ds(multiple(where_ref[u] * krows, 16), krows)
            (to,) = slot(u)
            to[...] = scr[at, :]

    return run(
        kernel,
        "ffn_grads",
        (where,),
        (cotangent, n2, gpre, act),
        slot_shapes(krows, 2 * hidden, FFN_FIRST, 1, False),
        (pltpu.VMEM((model, 2 * hidden), BF), pltpu.SemaphoreType.DMA((UNITS,))),
    )


def cut_gain(row, krows):
    model = row.shape[1]
    take = (
        lax.broadcasted_iota(jnp.int32, (model, LANES), 0) % krows
        == lax.broadcasted_iota(jnp.int32, (model, LANES), 1)
    ).astype(BF)
    own = (
        lax.broadcasted_iota(jnp.int32, (UNITS, model), 1) // krows
        == lax.broadcasted_iota(jnp.int32, (UNITS, model), 0)
    )
    high = row.astype(BF).astype(F32)
    pieces = mm(jnp.where(own, high, 0.0).astype(BF), take)
    return pieces + mm(jnp.where(own, row - high, 0.0).astype(BF), take)


def resid_back(back, other, resid, cotangent, gains, wo, mixf, part, heads, size, before):
    chunk, model = resid.shape
    wide = heads * LANES
    at = slice(part * chunk, (part + 1) * chunk)

    def kernel(cot_ref, gains_ref, wo_ref, mixf_ref, back_ref, other_ref, res_ref, *rest):
        gres_ref, gat_ref, xh_ref, gain_ref, gm = rest[len(before) :]
        g2 = back_ref[...].astype(F32) + other_ref[...].astype(F32)
        res = res_ref[...]
        inv = lax.rsqrt(jnp.mean(res * res, axis=-1, keepdims=True) + EPSILON)
        hat = res * inv
        total = jnp.sum((g2 * hat).reshape(chunk // 8, 8, model), axis=0)
        gain_ref[...] = total + rest[0][...] if before else total
        z = gains_ref[1:2, :] * g2
        corr = jnp.mean(z * hat, axis=-1, keepdims=True)
        gres = cot_ref[at, :].astype(F32) + inv * (z - hat * corr)
        gres_ref[...] = gres
        gat_ref[...] = gres.astype(BF)
        gm[...] = mm(gat_ref[...], wo_ref[...]).astype(BF)
        lane = lax.broadcasted_iota(jnp.int32, (chunk, LANES), 1)
        for h in range(heads):
            lanes = slice(h * LANES, (h + 1) * LANES)
            here = gm[:, lanes].astype(F32)
            inner = -jnp.sum(here * mixf_ref[at, lanes], axis=-1, keepdims=True)
            high = inner.astype(BF).astype(F32)
            xh_ref[:, lanes] = jnp.where(
                lane == size, high, jnp.where(lane == size + 1, inner - high, here)
            ).astype(BF)

    return run(
        kernel,
        "resid_back",
        (),
        (cotangent, gains, wo, mixf, back, other, resid, *before),
        (
            ((chunk, model), F32),
            ((chunk, model), BF),
            ((chunk, wide), BF),
            ((8, model), F32),
        ),
        (pltpu.VMEM((chunk, wide), BF),),
    )


def value_terms(xh_ref, rb_ref, e_ref, at, h):
    lanes = slice(h * LANES, (h + 1) * LANES)
    scaled = (xh_ref[:, lanes].astype(F32) * rb_ref[at, lanes]).astype(BF)
    return mm(e_ref[h, at, :], scaled, TN)


def value_first(xh, rb, e, size):
    heads, length, _ = e.shape
    at = slice(0, xh.shape[0])

    def kernel(xh_ref, rb_ref, e_ref, out):
        for h in range(heads):
            out[:, h * size : (h + 1) * size] = value_terms(xh_ref, rb_ref, e_ref, at, h)[:, :size]

    return run(kernel, "value_first", (), (xh, rb, e), (((length, heads * size), F32),))[0]


def value_back(xh, first, rb, e, wv, tokens, size, cut):
    length, model = tokens.shape
    heads = e.shape[0]
    width = heads * size
    krows = model // UNITS
    last = slice(length - xh.shape[0], length)

    def kernel(xh_ref, first_ref, rb_ref, e_ref, wv_ref, tok_ref, gv_ref, part_one, part_two, ga_ref, acc):
        acc[...] = jnp.zeros_like(acc)
        for h in range(heads):
            cols = slice(h * size, (h + 1) * size)
            term = value_terms(xh_ref, rb_ref, e_ref, last, h)[:, :size]
            gv_ref[:, cols] = (first_ref[:, cols] + term).astype(BF)

        for at, part_ref in ((slice(0, cut), part_one), (slice(cut, length), part_two)):
            part = mm(gv_ref[at, :], wv_ref[...], NT)
            part_ref[...] = part.astype(BF)
            x = tok_ref[at, :].astype(F32)
            inv = lax.rsqrt(jnp.mean(x * x, axis=-1, keepdims=True) + EPSILON)
            acc[...] += jnp.sum((part * (x * inv)).reshape((at.stop - at.start) // 8, 8, model), axis=0)

        ga_ref[...] = jnp.zeros_like(ga_ref)
        ga_ref[:UNITS, :] = cut_gain(jnp.sum(acc[...], axis=0, keepdims=True), krows)

    return run(
        kernel,
        "value_back",
        (),
        (xh, first, rb, e, wv, tokens),
        (
            ((length, width), BF),
            ((cut, model), BF),
            ((length - cut, model), BF),
            ((4 * UNITS, LANES), F32),
        ),
        (pltpu.VMEM((8, model), F32),),
    )


def token_grads(mine, other, gres, tokens, gains, part, before):
    chunk, model = mine.shape
    length = tokens.shape[0]
    at = slice(part * chunk, (part + 1) * chunk)

    def kernel(mine_ref, other_ref, gres_ref, tok_ref, gains_ref, *rest):
        out, held, sem = rest[len(before) :]
        x = tok_ref[at, :].astype(F32)
        inv = lax.rsqrt(jnp.mean(x * x, axis=-1, keepdims=True) + EPSILON)
        hat = x * inv
        z = gains_ref[0:1, :] * (mine_ref[...].astype(F32) + other_ref[...].astype(F32))
        held[...] = (gres_ref[...] + inv * (z - hat * jnp.mean(z * hat, axis=-1, keepdims=True))).astype(BF)
        copy = pltpu.make_async_copy(held, out.at[at, :], sem)
        copy.start()
        copy.wait()

    return run(
        kernel,
        "token_grads",
        (),
        (mine, other, gres, tokens, gains),
        (),
        (pltpu.VMEM((chunk, model), BF), pltpu.SemaphoreType.DMA),
        loose=before,
        loose_outs=(((length, model), BF),),
        aliases={5: 0} if before else None,
    )[0]


def low_rows(krows):
    return krows + 2 * (krows // 3)


def mixer_grads(where, xh, va, e, rb, krows, part, before):
    heads, length, _ = e.shape
    rows = length // UNITS
    chunk = xh.shape[0]
    owners = chunk // rows
    at = slice(part * chunk, (part + 1) * chunk)
    deep = heads * rows + low_rows(krows)

    def kernel(where_ref, xh_ref, va_ref, e_ref, rb_ref, *rest):
        outs, ds = rest[len(before) : -1], rest[-1]
        slot = slots(outs, MIXER_FIRST, 1)

        for h in range(heads):
            lanes = slice(h * LANES, (h + 1) * LANES)
            d = mm(xh_ref[:, lanes], va_ref[:, lanes], NT)
            inverse = rb_ref[at, lanes]
            for q in range(length // LANES):
                cols = slice(q * LANES, (q + 1) * LANES)
                ds[h, :, cols] = (e_ref[h, at, cols].astype(F32) * inverse * d[:, cols]).astype(BF)
        for u in range(UNITS):
            owner = where_ref[u] - part * owners

            @pl.when((owner >= 0) & (owner < owners))
            def _(u=u, owner=owner):
                some = pl.ds(multiple(owner * rows, rows), rows)
                for h in range(heads):
                    slot(u)[0][h * rows : (h + 1) * rows, :] = ds[h, some, :]

    return run(
        kernel,
        "mixer_grads",
        (where,),
        (xh, va, e, rb, *before),
        slot_shapes(deep, length, MIXER_FIRST, 1, False),
        (pltpu.VMEM((heads, chunk, length), BF),),
        aliases={5 + n: n for n in range(len(before))},
    )


def weight_grads(where, parts, n1, gv, gats, mixed, ga, ga_other, gain):
    length = n1.shape[0]
    model = n1.shape[1]
    width = gv.shape[1]
    krows = model // UNITS
    deep, length = parts[0].shape[1:]
    top = deep - low_rows(krows)
    lead, half, fold = length - width, length // 2, krows // 3
    assert width - lead == half

    def kernel(where_ref, n1_ref, gv_ref, ga_ref, gb_ref, gain_ref, *rest):
        gat_refs, mixed_refs, rest = rest[: len(mixed)], rest[len(mixed) : 2 * len(mixed)], rest[2 * len(mixed) :]
        slot = slots(rest[len(parts) : 2 * len(parts)], MIXER_FIRST, 1)
        wide, other, folded, pieces = rest[2 * len(parts) :]
        wide[:, :width] = mm(n1_ref[...], gv_ref[...], TN).astype(BF)
        some = [mm(gat_ref[...], one[...], TN) for gat_ref, one in zip(gat_refs, mixed_refs)]
        other[...] = sum(some).astype(BF)
        wide[:, width:] = other[:, :lead]
        pieces[0] = ga_ref[:UNITS, :] + gb_ref[:UNITS, :]
        pieces[1] = cut_gain(jnp.sum(gain_ref[...], axis=0, keepdims=True), krows)
        sub = lax.broadcasted_iota(jnp.int32, (fold, LANES), 0)
        for d in range(UNITS):
            for n in range(3):
                at = slice(d * krows + n * fold, d * krows + (n + 1) * fold)
                to = slice((2 * d + n // 2) * fold, (2 * d + n // 2 + 1) * fold)
                folded[to, (n % 2) * half : (n % 2 + 1) * half] = other[at, lead:]
            both = jnp.where(
                sub == 0, pieces[0, d : d + 1, :], jnp.where(sub == 1, pieces[1, d : d + 1, :], 0.0)
            )
            at = slice((2 * d + 1) * fold, (2 * d + 2) * fold)
            folded[at, half : half + LANES] = both.astype(BF)
            folded[at, half + LANES :] = jnp.zeros((fold, half - LANES), BF)
        for u in range(UNITS):
            (to,) = slot(u)
            to[top : top + krows, :] = wide[pl.ds(multiple(where_ref[u] * krows, 16), krows), :]
            to[top + krows :, :] = folded[pl.ds(multiple(where_ref[u] * 2 * fold, 16), 2 * fold), :]

    return run(
        kernel,
        "weight_grads",
        (where,),
        (n1, gv, ga, ga_other, gain, *gats, *mixed, *parts),
        slot_shapes(deep, length, MIXER_FIRST, 1, False),
        (
            pltpu.VMEM((model, length), BF),
            pltpu.VMEM((model, width), BF),
            pltpu.VMEM((UNITS * 2 * fold, length), BF),
            pltpu.VMEM((2, UNITS, LANES), F32),
        ),
        aliases={6 + 2 * len(mixed) + n: n for n in range(len(parts))},
    )


class Ring:
    def __init__(self, size):
        self.size = size
        self.chips = size // 2
        n = self.chips
        self.order = list(range(0, n, 2)) + list(range(n - 1, 0, -2))
        me = lax.axis_index("dp")
        self.core = me % 2
        chip = me // 2
        self.at = jnp.where(chip % 2 == 0, chip // 2, n - 1 - chip // 2)
        self.up = self.pairs(1)
        self.down = self.pairs(-1)
        self.swap = [(d, d ^ 1) for d in range(size)]

    def pairs(self, step):
        n = self.chips
        return [
            (self.order[p] * 2 + c, self.order[(p + step) % n] * 2 + c) for p in range(n) for c in range(2)
        ]

    def device(self, offset, core):
        n = self.chips
        p = (self.at + jnp.asarray(offset, jnp.int32) + n) % n
        chip = jnp.where(p < (n + 1) // 2, 2 * p, 2 * (n - 1 - p) + 1)
        return chip * 2 + core

    def gathered(self):
        n = self.chips
        offsets = [0]
        for s in range(1, n // 2):
            offsets += [-s, s]
        offsets.append(n // 2)
        return jnp.concatenate([self.device(offsets, self.core), self.device(offsets, 1 - self.core)])

    def scattered(self):
        offsets = list(range(self.chips))
        return jnp.concatenate([self.device(offsets, self.core), self.device(offsets, 1 - self.core)])


class Gather:
    def __init__(self, ring, unit, cut):
        self.ring = ring
        self.rows = unit.shape[0]
        self.cut = cut
        self.last = [unit, unit]
        self.hops = 0
        self.mine = []
        self.theirs = []
        self.here = [unit]

    def values(self):
        return self.last

    def take(self, values):
        self.last = list(values)

    def arrived(self, units):
        self.hops = 1
        self.last = self.here = list(units)

    def hop(self):
        ring = self.ring
        self.hops += 1
        up, down = self.last
        if self.hops == ring.chips // 2:
            up, down = up[: self.cut], down[self.cut :]
        self.last = [lax.ppermute(up, "dp", ring.up), lax.ppermute(down, "dp", ring.down)]
        self.swap()
        self.here = self.last

    def swap(self):
        self.theirs += [lax.ppermute(one, "dp", self.ring.swap) for one in self.here]
        self.mine += self.here
        self.here = []

    def finish(self):
        self.swap()
        return self.mine + self.theirs

    def shares(self):
        n = self.ring.chips
        own = [(u, 0, self.rows) for u in range(n - 1)]
        own += [(n - 1, 0, self.cut), (n - 1, self.cut, self.rows - self.cut)]
        return own + [(u + n, first, rows) for u, first, rows in own]


class Scatter:
    def __init__(self, ring, first, pieces, keep, *give):
        self.ring = ring
        self.keep = keep
        count = len(first) * pieces
        swapped = [lax.ppermute(one, "dp", ring.swap) for one in give[:count]]
        self.early = {k: swapped[n * pieces : (n + 1) * pieces] for n, k in enumerate(first)}
        self.first = first
        self.late = late_units(first)
        self.later = give[count:]
        self.got = {}
        self.last = {}

    def values(self):
        return list(self.last.values()) if self.last else [one for k in self.first for one in self.early[k]]

    def take(self, values):
        if self.last:
            self.last = dict(zip(self.last, values))
        else:
            pieces = len(values) // len(self.first)
            self.early = {k: values[n * pieces : (n + 1) * pieces] for n, k in enumerate(self.first)}

    def swap_all(self, *after):
        stack = lax.ppermute(tie(self.later[0], *after), "dp", self.ring.swap)
        self.got = {k: stack[n] for n, k in enumerate(self.late)}

    def hop(self, way, k):
        got = self.early[k][0] if k in self.early else self.got[k]
        value = self.keep[k].astype(F32) + got.astype(F32)
        if way in self.last:
            value = value + self.last[way].astype(F32)
        value = value.astype(BF)
        self.last[way] = lax.ppermute(value, "dp", self.ring.up if way == "up" else self.ring.down)
        return value

    def result(self):
        return self.keep, self.got[0], self.last["up"], self.last["down"]


def together(chains, *more):
    values = [one for chain in chains for one in chain.values()]
    tied = lax.optimization_barrier(tuple(values) + more)
    at = 0
    for chain in chains:
        count = len(chain.values())
        chain.take(tied[at : at + count])
        at += count
    return tied[at:]


def tie(value, *after):
    return lax.optimization_barrier((value,) + after)[0] if after else value


def shards(
    tokens,
    segment_ids,
    gain_attn,
    gain_ffn,
    random_scores,
    w_value,
    w_output,
    w_up,
    w_down,
    cotangent,
):
    devices = lax.axis_size("dp")
    second = lax.axis_index("mp")
    length = segment_ids.shape[1]
    heads = random_scores.shape[0]
    model = tokens.shape[1]
    width = w_value.shape[1]
    size = width // heads
    rows = length // UNITS
    krows = model // UNITS
    ring = devices == UNITS and devices // 2 <= RING_CHIPS
    flip = [(0, 1), (1, 0)]
    second_at = jnp.reshape(second, (1,)).astype(jnp.int32)
    plan = Unit(heads, rows, krows, length, model, width, w_up.shape[1])

    if ring:
        net = Ring(devices)
        far = net.chips // 2
        where_in = net.gathered().astype(jnp.int32)
        where_out = net.scattered().astype(jnp.int32)
        upper, lower, wo_own = pack_unit(
            plan, second_at, random_scores, w_value, gain_attn, gain_ffn, w_up, w_down.T, w_output.T
        )
        ways = (net.up, net.down)
        uppers = [lax.ppermute(upper, "dp", way) for way in ways]
        wo_other = lax.ppermute(tie(wo_own, where_in, where_out), "mp", flip)
        lower = fill_low(plan, second_at, lower, wo_other)
        lowers = [lax.ppermute(lower, "dp", way) for way in ways]
        (unit,) = join_units(plan, [upper], [lower])
        one = Gather(net, unit, plan.cut)
        one.swap()
        uppers[0], uppers[1], *lowers = lax.optimization_barrier((*uppers, *lowers))
        one.arrived(join_units(plan, uppers, lowers))
        for step in range(1, far - 1):
            one.hop()
            together([one])
            one.here = one.last
        there = one.mine + one.theirs
        shares = one.shares()
        half = len(shares) // 2
        early = [n for n in range(len(one.mine))] + [half + n for n in range(len(one.theirs))]
        one.hop()
        begun = mixer_first(plan, where_in, tokens, segment_ids, there, [shares[n] for n in early], heads)
        begun = together([one], *begun)
        one.here = one.last
        units = one.finish()
        late = [n for n in range(len(shares)) if n not in early]
        near = late
        order = [n for n in range(len(shares)) if n not in near] + near
        units, shares = [units[n] for n in order], [shares[n] for n in order]
        late = [n for n, old in enumerate(order) if old in late]
    else:
        where_in = jnp.arange(UNITS, dtype=jnp.int32)
        where_out = where_in

        def gather(one, axis=0):
            return lax.all_gather(one.astype(BF), "dp", axis=axis, tiled=True)

        wo_own = w_output.T.astype(BF)
        wo_other = lax.ppermute(wo_own, "mp", flip)
        halves = [jnp.where(second == n, wo_own, wo_other) for n in range(2)]
        scores = gather(random_scores, 1).reshape(heads, UNITS, rows, length).transpose(1, 0, 2, 3)
        wide = [gather(one) for one in (w_value, *halves)]
        wide = jnp.concatenate(wide, axis=1).reshape(UNITS, krows, plan.wide)
        ffn = jnp.concatenate([gather(w_up), gather(w_down.T)], axis=1).reshape(UNITS, krows, -1)
        stack = [scores.reshape(UNITS, heads * rows, length)]
        for kind, column in plan.blocks:
            stack.append((ffn if kind == "ffn" else wide)[:, :, column : column + length])
        gains = jnp.stack([gather(gain_attn), gather(gain_ffn)]).reshape(2, UNITS, krows).transpose(1, 0, 2)
        gains = jnp.pad(gains, ((0, 0), (0, plan.fold - 2), (0, length - plan.gain_lane - krows)))
        tail = wide[:, :, plan.wide - plan.tail :].reshape(UNITS, 3, plan.fold, plan.tail)
        stack.append(jnp.concatenate([tail[:, 0], tail[:, 1], tail[:, 2], gains], axis=2))
        whole = jnp.concatenate(stack, axis=1)
        units = [whole[u] for u in range(UNITS)]
        shares = [(u, 0, plan.deep) for u in range(UNITS)]
        early, late, near = list(range(UNITS // 2)), list(range(UNITS // 2, UNITS)), []
        begun = mixer_first(plan, where_in, tokens, segment_ids, units[: UNITS // 2], shares[: UNITS // 2], heads)

    own = [n for n in late if shares[n][0] < UNITS // 2 or shares[n][2] == plan.deep] if ring else late[:1]
    late = [n for n in late if n not in own]
    begun = mixer_next(plan, where_in, begun, [units[n] for n in own], [shares[n] for n in own])
    e, wv, _, va, sums, n1, gains, *mixed = mixer_forward(
        plan, where_in, begun, [units[n] for n in late], [shares[n] for n in late], heads, width
    )
    mixed_other = [lax.ppermute(one, "mp", flip) for one in mixed]
    w, wo_whole, gact, mixf, rb, wo = second_weights(plan, where_in, second_at, cotangent, sums, units, shares, len(near), size)
    backs, others, resids, kept = [], [], [], []
    for part in range(PARTS):
        back, resid, *kept = ffn_main(
            second_at, tokens, mixed[part], mixed_other[part], gact, gains, w, wo_whole, part, PARTS, kept
        )
        backs.append(back)
        others.append(lax.ppermute(tie(back, *others[-1:]), "mp", flip))
        resids.append(resid)
    n2, act, gpre = kept
    parts_two = ffn_grads(where_out, n2, gpre, act, cotangent)
    early = resid_back(backs[0], others[0], resids[0], cotangent, gains, wo, mixf, 0, heads, size, [])
    ffn_one, ffn_two = ffn_out(tie(act, *early), w, 3 * length // 8)
    first_values = value_first(early[2], rb, e, size)
    parts_one = mixer_grads(where_out, early[2], va, e, rb, krows, 0, [])
    if ring:
        ffn_sum = Scatter(net, FFN_FIRST, 1, *parts_two)
        ffn_sum.swap_all(others[0], *ffn_sum.values())
        for step in range(2):
            ffn_sum.hop("down", far + step)
            ffn_sum.hop("up", far - 1 - step)
            if step == 0:
                ffn_one, ffn_two, first_values, *more = together(
                    [ffn_sum], ffn_one, ffn_two, first_values, *early, *parts_one
                )
                early, parts_one = more[: len(early)], more[len(early) :]
    cot_late = tie(cotangent, first_values, *parts_one)
    final = resid_back(backs[1], others[1], resids[1], cot_late, gains, wo, mixf, 1, heads, size, early[3:])
    gres, gats = (early[0], final[0]), (early[1], final[1])
    xh = final[2]
    gv, part_one, part_two, ga = value_back(xh, first_values, rb, e, wv, tokens, size, length // 2)
    ga_other = lax.ppermute(ga, "mp", flip)
    one_other = lax.ppermute(tie(ffn_one, ga), "mp", flip)
    if ring:
        together([ffn_sum])
        for step in range(2, far - 1):
            ffn_sum.hop("down", far + step)
            ffn_sum.hop("up", far - 1 - step)
    parts_one = mixer_grads(where_out, xh, va, e, rb, krows, 1, parts_one)
    parts_one = weight_grads(where_out, parts_one, n1, gv, gats, mixed, ga, ga_other, final[3])

    top = heads * rows
    if ring:
        score_sum = Scatter(net, MIXER_FIRST, 1, *parts_one)
        one_other, ffn_two = together([ffn_sum, score_sum], one_other, ffn_two)
        value = score_sum.hop("up", far)
        ffn_sum.hop("down", 2 * far - 1)
        score_sum.swap_all(value)
        two_other = lax.ppermute(ffn_two, "mp", flip)
        part_one, part_two = together([score_sum], part_one, part_two)
        for step in range(1, far):
            score_sum.hop("up", far - step)
            score_sum.hop("down", far + step)
            if step == 1:
                part_other = [lax.ppermute(part_one, "mp", flip)]
                two_other, part_two = together([ffn_sum, score_sum], two_other, part_two)
            elif step < far - 1:
                part_other.append(lax.ppermute(part_two, "mp", flip))
                (part_other[0],) = together([score_sum], part_other[0])
        out_up, out_down = ffn_result(*ffn_sum.result())
        out_scores, out_value, out_output, *out_gains = mixer_result(*score_sum.result(), heads, krows, width)
        out_down, out_output = out_down.T, out_output.T
        out_gain_one, out_gain_two = [one.reshape(krows) for one in out_gains]
    else:
        two_other = lax.ppermute(ffn_two, "mp", flip)
        part_other = [lax.ppermute(one, "mp", flip) for one in (part_one, part_two)]

        def scatter(one, axis=0):
            return lax.psum_scatter(one, "dp", scatter_dimension=axis, tiled=True)

        def whole(first, pieces, keep, *give):
            late = late_units(first)
            early, later = give[: len(first) * pieces], give[len(first) * pieces :]
            given = []
            for k in range(UNITS // 2):
                if k in first:
                    at = first.index(k) * pieces
                    given.append(jnp.concatenate(early[at : at + pieces]))
                else:
                    given.append(later[0][late.index(k)] if len(later) == 1 else later[late.index(k)])
            return jnp.concatenate([keep, jnp.stack(given)]).astype(F32)

        two = whole(FFN_FIRST, 1, *parts_two).reshape(model, -1)
        one = whole(MIXER_FIRST, 1, *parts_one)
        out_up = scatter(two[:, : two.shape[1] // 2])
        out_down = scatter(two[:, two.shape[1] // 2 :]).T
        scores = one[:, :top].reshape(UNITS, heads, rows, length).transpose(1, 0, 2, 3)
        out_scores = scatter(scores.reshape(heads, length, length), 1)
        out_value = scatter(one[:, top : top + krows, :width].reshape(model, width))
        low, fold, half = top + krows, krows // 3, length // 2
        folded = [one[:, low + n // 2 * fold : low + (n // 2 + 1) * fold, n % 2 * half :][:, :, :half] for n in range(3)]
        other = jnp.concatenate([one[:, top:low, width:], jnp.concatenate(folded, axis=1)], axis=2)
        out_output = scatter(other.reshape(model, width)).T
        out_gain_one = scatter(one[:, low + fold, half : half + krows].reshape(model))
        out_gain_two = scatter(one[:, low + fold + 1, half : half + krows].reshape(model))
    ffn = jnp.concatenate([ffn_one, ffn_two])
    ffn_other = jnp.concatenate([one_other, two_other])
    output = (jnp.concatenate(resids) + (ffn.astype(F32) + ffn_other.astype(F32))).astype(BF)
    written = []
    for part, (mine, other) in enumerate(zip((part_one, part_two), part_other)):
        written = [token_grads(mine, other, gres[part], tokens, gains, part, written)]
    (grad_tokens,) = written
    return (
        output,
        grad_tokens,
        out_gain_one,
        out_gain_two,
        out_scores,
        out_value,
        out_output,
        out_up,
        out_down,
    )


def solution(mesh):
    in_specs = (
        P("dp", None),
        P("dp", None),
        P("dp"),
        P("dp"),
        P("mp", "dp", None),
        P("dp", "mp"),
        P("mp", "dp"),
        P("dp", "mp"),
        P("mp", "dp"),
        P("dp", None),
    )
    out_specs = (
        P("dp", None),
        P("dp", None),
        P("dp"),
        P("dp"),
        P("mp", "dp", None),
        P("dp", "mp"),
        P("mp", "dp"),
        P("dp", "mp"),
        P("mp", "dp"),
    )
    return jax.shard_map(shards, mesh=mesh, in_specs=in_specs, out_specs=out_specs, check_vma=False)
```
